32 devices in a mesh: wide: 8 (over y, x, core), narrow: 4 (over z).
Axes of the slice: x: 2, y: 2, z: 4, core: 2. Of those that a mesh axis runs over, the one named last changes fastest.
Arguments:
- tokens: bfloat16 [32, 128, 2048], P(('wide', 'narrow')), may hold values from -6 to 6
- lengths: int32 [32, 5], P(('wide', 'narrow')), may hold values from 1 to 96, as said below
- gain: bfloat16 [2048], P(('wide', 'narrow')), may hold values from 0.5 to 1.5
- w_in: bfloat16 [2048, 8192], P(('wide', 'narrow')), may hold values from -0.125 to 0.125
- conv_w: bfloat16 [4096, 4], P(('wide', 'narrow')), may hold values from -3 to 3
- conv_b: bfloat16 [4096], P(('wide', 'narrow')), may hold values from -3 to 3
- w_x: bfloat16 [4096, 160], P(('wide', 'narrow')), may hold values from -0.09375 to 0.09375
- w_dt: bfloat16 [4096, 128], P(('wide', 'narrow')), may hold values from -0.5 to 0.5
- dt_bias: bfloat16 [4096], P(('wide', 'narrow')), may hold values from -4 to 1
- skip: bfloat16 [4096], P(('wide', 'narrow')), may hold values from 0.099609375 to 1.8984375
- w_out: bfloat16 [4096, 2048], P(('wide', 'narrow')), may hold values from -0.09375 to 0.09375
- grad_out: bfloat16 [32, 128, 2048], P(('wide', 'narrow')), may hold values from -6 to 6
Outputs:
- block_out: bfloat16 [32, 128, 2048], P(('wide', 'narrow'))
- grad_tokens: bfloat16 [32, 128, 2048], P(('wide', 'narrow'))
- grad_gain: float32 [2048], P(('wide', 'narrow'))
- grad_w_in: float32 [2048, 8192], P(('wide', 'narrow'))
- grad_conv_w: float32 [4096, 4], P(('wide', 'narrow'))
- grad_conv_b: float32 [4096], P(('wide', 'narrow'))
- grad_w_x: float32 [4096, 160], P(('wide', 'narrow'))
- grad_w_dt: float32 [4096, 128], P(('wide', 'narrow'))
- grad_dt_bias: float32 [4096], P(('wide', 'narrow'))
- grad_skip: float32 [4096], P(('wide', 'narrow'))
- grad_w_out: float32 [4096, 2048], P(('wide', 'narrow'))
- beta_mean: float32 [], replicated
- beta_max: float32 [], replicated
The draws below stay inside these ranges and needn't reach their ends.
Inputs may be any that keep to these rules, and one draw needn't show every extreme that they name: Each row's entries sum to 128; the first 4 are its documents' lengths, the last the length of its padding at the row's end.
All inputs are finite; a program needn't handle non-finite values.
Results may differ from the reference program's by a relative error of at most 0.0096.
Values may be sent and summed in bfloat16 or wider, within the bound.
A program may use at most 384 MiB of HBM per device.

```python
import jax
import jax.numpy as jnp
from jax import lax

D = 2048
E = 4096
STATE = 16
RANK = 128
KERNEL = 4
TOK = 128
DOCS = 4
ROWS = 32


def draw_lengths(key, part):
    rows = jnp.arange(ROWS, dtype=jnp.int32)
    live = TOK // 4 + TOK // 2 * rows // max(ROWS - 1, 1)
    raw = jax.random.randint(key, (ROWS, DOCS), 0, 16, dtype=jnp.int32)
    weights = 1 + raw * raw
    spare = live - DOCS
    parts = 1 + spare[:, None] * weights // jnp.sum(weights, axis=1, keepdims=True)
    leading = parts[:, :-1]
    final = live - jnp.sum(leading, axis=1)
    padding = TOK - live
    return jnp.concatenate([leading, final[:, None], padding[:, None]], axis=1).astype(jnp.int32)


def block_scale(own_key, dims, cuts, least, top_value):
    level, own = 1.0, jax.random.fold_in(own_key, 6)
    for position, blocks in cuts:
        steps = jnp.exp(jax.random.uniform(jax.random.fold_in(own, position), (blocks,), jnp.float32, least / len(cuts), top_value / len(cuts)))
        level = level * jnp.repeat(steps, dims[position] // blocks).reshape([-1 if axis == position else 1 for axis in range(len(dims))])
    return level


def normal_values(key, shape, deviation, limit, split=(), held_as=jnp.bfloat16):
    array = deviation * jax.random.normal(key, shape, jnp.float32)
    if split:
        array = array * block_scale(key, shape, split, -0.22, 0.18)
    return jnp.clip(array, -limit, limit).astype(held_as)


def setup_inputs(seed: int = 0) -> dict:
    arg_keys = jax.random.split(jax.random.key(seed), 13)
    return {
        "tokens": normal_values(arg_keys[0], (ROWS, TOK, D), 1.0, 6.0, ((0, 32),)),
        "lengths": draw_lengths(jax.random.fold_in(arg_keys[12], 71), 0),
        "gain": jnp.clip(1.0 + 0.1 * jax.random.normal(arg_keys[2], (D,), jnp.float32), 0.5, 1.5).astype(jnp.bfloat16),
        "w_in": normal_values(arg_keys[3], (D, 2 * E), D ** -0.5, 0.125, ((0, 32),)),
        "conv_w": normal_values(arg_keys[4], (E, KERNEL), KERNEL ** -0.5, 3.0, ((0, 32),)),
        "conv_b": normal_values(arg_keys[5], (E,), 0.5, 3.0, ((0, 32),)),
        "w_x": normal_values(arg_keys[6], (E, RANK + 2 * STATE), E ** -0.5, 0.09375, ((0, 32),)),
        "w_dt": normal_values(arg_keys[7], (E, RANK), RANK ** -0.5, 0.5, ((0, 32),)),
        "dt_bias": jnp.clip(-4.0 + 5.0 * jax.random.uniform(arg_keys[8], (E,), jnp.float32) ** block_scale(arg_keys[8], (E,), ((0, 32),), -0.2, 0.2), -4.0, 1.0).astype(jnp.bfloat16),
        "skip": jnp.clip(1.0 + 0.18 * jax.random.normal(arg_keys[9], (E,), jnp.float32), 0.099609375, 1.8984375).astype(jnp.bfloat16),
        "w_out": normal_values(arg_keys[10], (E, D), E ** -0.5, 0.09375, ((0, 32),)),
        "grad_out": normal_values(arg_keys[11], (ROWS, TOK, D), 1.0, 6.0, ((0, 32),)),
    }


@jax.custom_vjp
def low(v):
    return lax.optimization_barrier(v.astype(jnp.bfloat16)).astype(jnp.float32)

@jax.custom_vjp
def low_back(v):
    return v

def low_keep(v):
    return (low(v), None)

def low_pass(kept, grad):
    return (grad,)

def back_keep(v):
    return (v, None)

def back_low(kept, grad):
    return (low(grad),)
low.defvjp(low_keep, low_pass)
low_back.defvjp(back_keep, back_low)
highest = lax.Precision.HIGHEST
norm_eps = 1e-05

def segment_ids(lengths_row, count):
    ends = jnp.cumsum(lengths_row).astype(jnp.int32)
    places = jnp.arange(count, dtype=jnp.int32)
    return lax.optimization_barrier(jnp.sum((places[:, None] >= ends[None, :]).astype(jnp.int32), axis=1)).astype(jnp.int32)

def keep_flags(segment):
    earlier = jnp.concatenate([jnp.full((1,), -1, jnp.int32), segment[:-1].astype(jnp.int32)])
    return (earlier == segment).astype(jnp.float32)

def convolve(inputs, conv_w, conv_b, segment):
    count = inputs.shape[0]
    width = conv_w.shape[1]
    total = conv_b[None, :] + conv_w[:, width - 1][None, :] * inputs
    for offset in range(1, width):
        earlier = jnp.pad(inputs, ((offset, 0), (0, 0)))[:count]
        before = jnp.pad(segment, (offset, 0), constant_values=-1)[:count]
        same = (before == segment).astype(jnp.float32)
        total = total + conv_w[:, width - 1 - offset][None, :] * earlier * same[:, None]
    return total

def longhorn(beta, keys, queries, inputs, keep):
    squares = keys * keys
    rates = beta / (1.0 + beta * lax.optimization_barrier(jnp.sum(squares, axis=1, keepdims=True)))

    def advance(state, item):
        rate, square, key, query, value, held = item
        decay = held * (1.0 - rate[:, None] * square[None, :])
        state = decay * state + (rate * value)[:, None] * key[None, :]
        return (state, jnp.dot(state, query, precision=highest))
    start = jnp.zeros((beta.shape[1], keys.shape[1]), jnp.float32)
    _, outputs = lax.scan(advance, start, (rates, squares, keys, queries, inputs, keep))
    return outputs

def block_row(inputs, lengths_row, weights):
    gain, w_in, conv_w, conv_b, w_x, w_dt, dt_bias, skip, w_out = weights
    count = inputs.shape[0]
    inner = w_in.shape[1] // 2
    rank = w_dt.shape[1]
    states = (w_x.shape[1] - rank) // 2
    segment = segment_ids(lengths_row, count)
    keep = keep_flags(segment)
    live = (segment < DOCS).astype(jnp.float32)
    scale = lax.rsqrt(lax.optimization_barrier(jnp.mean(inputs * inputs, axis=1, keepdims=True)) + norm_eps)
    normed = low(inputs * scale * gain)
    mixed_in = low_back(jnp.dot(normed, w_in, precision=highest))
    conv_in = mixed_in[:, :inner]
    gate = mixed_in[:, inner:]
    activated = low(jax.nn.silu(convolve(conv_in, conv_w, conv_b, segment)))
    projected = low_back(jnp.dot(activated, w_x, precision=highest))
    delta = low(projected[:, :rank])
    keys = projected[:, rank:rank + states]
    queries = projected[:, rank + states:]
    pre = low_back(jnp.dot(delta, w_dt.T, precision=highest) + dt_bias)
    beta = jax.nn.sigmoid(pre)
    mixed_out = longhorn(beta, keys, queries, activated, keep) + skip * activated
    mixed = low(mixed_out * jax.nn.silu(gate) * live[:, None])
    result = inputs + jnp.dot(mixed, w_out, precision=highest)
    live_beta = beta * live[:, None]
    return (result, (jnp.sum(live_beta), jnp.max(live_beta)))

def reference(tokens, lengths, gain, w_in, conv_w, conv_b, w_x, w_dt, dt_bias, skip, w_out, grad_out):
    weights = tuple((member.astype(jnp.float32) for member in (gain, w_in, conv_w, conv_b, w_x, w_dt, dt_bias, skip, w_out)))
    inputs = tokens.astype(jnp.float32)

    def forward(values, params):

        def per_row(carry, item):
            row_out, stats = jax.checkpoint(block_row)(item[0], item[1], params)
            return (carry, (row_out, stats))
        _, (outs, stats) = lax.scan(per_row, jnp.zeros((), jnp.float32), (values, lengths))
        return (outs, stats)
    outs, pullback, stats = jax.vjp(forward, inputs, weights, has_aux=True)
    grad_inputs, grad_weights = pullback(grad_out.astype(jnp.float32))
    sums, peaks = stats
    inner = w_in.shape[1] // 2
    slots = float(tokens.shape[0] * tokens.shape[1] * inner)
    beta_mean = jnp.sum(sums) / slots
    beta_max = jnp.max(peaks)
    return (outs.astype(jnp.bfloat16), grad_inputs.astype(jnp.bfloat16), grad_weights[0], grad_weights[1], grad_weights[2], grad_weights[3], grad_weights[4], grad_weights[5], grad_weights[6], grad_weights[7], grad_weights[8], beta_mean, beta_max)
```

```python
import functools
import jax, jax.numpy as jnp
from jax import lax
from jax.experimental import pallas as pl
from jax.experimental.pallas import tpu as pltpu
from jax.sharding import Mesh, PartitionSpec as P

DOCS = 4
EPS = 1e-05
ALL = ("dp", "core", "z")
TP = ("core", "z")

f32 = jnp.float32
bf16 = jnp.bfloat16

def fold(x):
    total = x[:, :128]
    for at in range(128, x.shape[1], 128):
        total = total + x[:, at:at+128]
    return total

def mixer_kernel(states, unroll, chunk, flags_ref, kq3_ref, sk_ref, pre_ref, v_ref, g_ref, dm_ref, skip_ref,
                 m_ref, dg_ref, dpre_ref, dv_ref, dkq_ref, stat_ref, s_ref, h_ref, rate_ref, rv_ref, kb_ref, drr_ref):
    rows = pre_ref.shape[0]
    width = pre_ref.shape[1]
    steps = rows // 8
    wide = states * 128
    spread_rows = kq3_ref.shape[1]
    def spread(i, c):
        r = pl.ds(pl.multiple_of(i * chunk, chunk), chunk)
        left = kq3_ref[r, :]
        for part in range(0, 2 * wide, 512):
            ids = lax.broadcasted_iota(jnp.int32, (spread_rows, 512), 0) % (2 * states)
            col = lax.broadcasted_iota(jnp.int32, (spread_rows, 512), 1) // 128 + part // 128
            hot = jnp.where(ids == col, 1.0, 0.0).astype(bf16)
            kb_ref[r, part:part+512] = jnp.dot(left, hot, preferred_element_type=f32)
        return c
    lax.fori_loop(0, rows // chunk, spread, 0)

    def before(i, c):
        r = pl.ds(pl.multiple_of(i * 64, 64), 64)
        live = flags_ref[r, 1:2]
        beta = jax.nn.sigmoid(pre_ref[r, :])
        part = 1.0 / (1.0 + beta * sk_ref[r, 0:1])
        rate = beta * part
        rate_ref[r, :] = rate
        v = v_ref[r, :]
        rv_ref[r, :] = rate * v
        dpre_ref[r, :] = part * part * beta * (1.0 - beta)
        g = g_ref[r, :]
        sg = jax.nn.sigmoid(g)
        dm = dm_ref[r, :] * live
        dv_ref[r, :] = dm * (g * sg)
        dg_ref[r, :] = dm * (sg * (1.0 + g * (1.0 - sg)))
        return c
    lax.fori_loop(0, rows // 64, before, 0)

    s_ref[0, 0] = jnp.zeros(s_ref.shape[2:], f32)

    group = unroll
    tile = lambda x: jnp.concatenate([x] * (width // 128), axis=1)
    span = group * 8
    at = [slice(j * 8, j * 8 + 8) for j in range(group)]
    def view(ref, i):
        return ref.at[pl.ds(pl.multiple_of(i * span, span), span)]

    def forward(i, carry):
        flags, rates, rvs, vs, kbs, ms = [view(x, i) for x in (flags_ref, rate_ref, rv_ref, v_ref, kb_ref, m_ref)]
        keep = [jnp.broadcast_to(flags[r, 0:1], (8, 128)) for r in at]
        rate = [rates[r, :] for r in at]
        rv = [rvs[r, :] for r in at]
        y = [skip_ref[...] * vs[r, :] for r in at]
        for n in range(states):
            state = s_ref[i, 0, n]
            for j, r in enumerate(at):
                kb = kbs[r, n*128:(n+1)*128]
                qb = kbs[r, wide+n*128:wide+(n+1)*128]
                state = (tile(keep[j]) - rate[j] * tile(kb * kb * keep[j])) * state + rv[j] * tile(kb)
                if j < group - 1:
                    s_ref[i, j + 1, n] = state
                else:
                    s_ref[i + 1, 0, n] = state
                y[j] = y[j] + state * tile(qb)
        for j, r in enumerate(at):
            ms[r, :] = y[j]
        return carry

    lax.fori_loop(0, steps // group, forward, 0)
    h_ref[...] = jnp.zeros_like(h_ref)

    def backward(step, carry):
        i = steps // group - 1 - step
        flags, rates, rvs, vs, kbs, dvs, dpres, drrs = [view(x, i) for x in (flags_ref, rate_ref, rv_ref, v_ref, kb_ref, dv_ref, dpre_ref, drr_ref)]
        keep = [jnp.broadcast_to(flags[r, 0:1], (8, 128)) for r in at]
        rate = [rates[r, :] for r in at]
        rv = [rvs[r, :] for r in at]
        dy = [dvs[r, :] for r in at]
        hk = [jnp.zeros((8, width), f32) for r in at]
        hs2 = [jnp.zeros((8, width), f32) for r in at]
        for n in range(states):
            ah = h_ref[n]
            after_ = s_ref[i + 1, 0, n]
            for j in range(group - 1, -1, -1):
                r = at[j]
                kb = kbs[r, n*128:(n+1)*128]
                qb = kbs[r, wide+n*128:wide+(n+1)*128]
                kk = kb * keep[j]
                held = tile(kb * kk)
                h = dy[j] * tile(qb) + ah
                prior = s_ref[i, j, n]
                hs = h * prior
                hk[j] = hk[j] + h * tile(kb)
                hs2[j] = hs2[j] + hs * held
                kbs[r, n*128:(n+1)*128] = fold(h * rv[j]) - 2.0 * kk * fold(hs * rate[j])
                kbs[r, wide+n*128:wide+(n+1)*128] = fold(dy[j] * after_)
                after_ = prior
                ah = (tile(keep[j]) - rate[j] * held) * h
            h_ref[n] = ah
        for j, r in enumerate(at):
            v = vs[r, :]
            drate = v * hk[j] - hs2[j]
            drrs[r, :] = fold(drate * rate[j] * rate[j]) * (-2.0)
            dpres[r, :] = drate * dpres[r, :]
            dvs[r, :] = rate[j] * hk[j] + skip_ref[...] * dy[j]
            stat_ref[0, 0] += dy[j] * v
        return carry

    stat_ref[...] = jnp.zeros_like(stat_ref)
    lax.fori_loop(0, steps // group, backward, 0)

    first = pl.program_id(0) == 0
    def gather(i, c):
        r = pl.ds(pl.multiple_of(i * chunk, chunk), chunk)
        total = jnp.zeros((chunk, 128), f32)
        for part in range(0, 2 * wide, 512):
            row = lax.broadcasted_iota(jnp.int32, (512, 128), 0) // 128 + part // 128
            col = lax.broadcasted_iota(jnp.int32, (512, 128), 1)
            hot = jnp.where(row == col, 1.0, 0.0).astype(bf16)
            total += jnp.dot(kb_ref[r, part:part+512].astype(bf16), hot, preferred_element_type=f32)
        col = lax.broadcasted_iota(jnp.int32, (128, 128), 1)
        hot = jnp.where(col == 2 * states, 1.0, 0.0).astype(bf16)
        total += jnp.dot(drr_ref[r, :].astype(bf16), hot, preferred_element_type=f32)
        dkq_ref[r, :] = jnp.where(first, total, dkq_ref[r, :] + total)
        return c
    lax.fori_loop(0, rows // chunk, gather, 0)

    def after(i, c):
        r = pl.ds(pl.multiple_of(i * 64, 64), 64)
        live = flags_ref[r, 1:2]
        y = m_ref[r, :]
        g = g_ref[r, :]
        m_ref[r, :] = y * (g * jax.nn.sigmoid(g)) * live
        dg_ref[r, :] = y * dg_ref[r, :]
        shown = (jax.nn.sigmoid(pre_ref[r, :]) * live).reshape(8, 8, width)
        stat_ref[0, 1] += jnp.sum(shown, axis=0)
        stat_ref[0, 2] = jnp.maximum(stat_ref[0, 2], jnp.max(shown, axis=0))
        return c
    lax.fori_loop(0, rows // 64, after, 0)

def mixer(flags, kq3, sk, pre, v, g, dm, skip, states=16, width=256, unroll=1):
    rows, total = pre.shape
    steps = rows // 8
    tiles = total // width
    big = jax.ShapeDtypeStruct((rows, total), f32)
    cut = pl.BlockSpec((rows, width), lambda h: (0, h))
    whole = lambda a: pl.BlockSpec(a.shape, lambda h: (0,) * a.ndim)
    return pl.pallas_call(
        functools.partial(mixer_kernel, states, unroll, min(256, rows)),
        grid=(tiles,),
        out_shape=(big, big, big, big, jax.ShapeDtypeStruct((rows, 128), f32), jax.ShapeDtypeStruct((tiles, 3, 8, width), f32)),
        in_specs=[whole(flags), whole(kq3), whole(sk), cut, cut, cut, cut, pl.BlockSpec((1, width), lambda h: (0, h))],
        out_specs=(cut, cut, cut, cut, pl.BlockSpec((rows, 128), lambda h: (0, 0)), pl.BlockSpec((1, 3, 8, width), lambda h: (h, 0, 0, 0))),
        scratch_shapes=[pltpu.VMEM((steps//unroll+1, unroll, states, 8, width), f32), pltpu.VMEM((states, 8, width), f32)] + [pltpu.VMEM((rows, width), f32)]*2
          + [pltpu.VMEM((rows, 2*states*128), f32), pltpu.VMEM((rows, 128), f32)],
        compiler_params=pltpu.CompilerParams(vmem_limit_bytes=60*1024*1024),
    )(flags, kq3, sk, pre, v, g, dm, skip)


def masks(lengths, count):
    ends = jnp.cumsum(lengths, axis=1)
    places = jnp.arange(count, dtype=jnp.int32)
    segment = jnp.sum((places[:, None, None] >= ends[None, :, :]).astype(jnp.int32), axis=2)
    same = []
    for offset in range(1, 4):
        before = jnp.pad(segment, ((offset, 0), (0, 0)), constant_values=-1)[:count]
        same.append((before == segment).astype(f32))
    return same, (segment < DOCS).astype(f32)


def columns(weights, ways):
    rows, total = weights.shape
    return weights.reshape(rows, 2, total // (2 * ways * 128), ways, 128)


def on_device(tokens, lengths, gain, w_in, conv_w, conv_b, w_x, w_dt, dt_bias, skip, w_out, grad_out):
    ways = lax.axis_size("core") * lax.axis_size("z")
    groups = lax.axis_size("dp")
    length, model = tokens.shape[1:]
    own_d = w_in.shape[0]
    own_e = conv_w.shape[0]
    inner = w_in.shape[1] // 2
    channels = inner // ways
    rank = w_dt.shape[1]
    states = (w_x.shape[1] - rank) // 2
    cols = w_in.reshape(own_d, 2, groups, ways, own_e).transpose(3, 0, 1, 2, 4).reshape(ways, own_d, 2 * channels)
    cols = lax.all_to_all(cols, TP, split_axis=0, concat_axis=0, tiled=True)
    win = lax.all_gather(cols, "dp", axis=0, tiled=True).reshape(model, 2 * channels)
    small = jnp.concatenate([w_x, w_dt, conv_w, conv_b[:, None], dt_bias[:, None], skip[:, None]], axis=1)
    small_width = small.shape[1]
    small = lax.all_gather(small, "dp", axis=0, tiled=True)
    wx = small[:, :rank + 2 * states]
    wdt = small[:, rank + 2 * states:2 * rank + 2 * states]
    rest = small[:, 2 * rank + 2 * states:].astype(f32)
    taps, bias, dtb, skips = rest[:, :4], rest[:, 4], rest[:, 5], rest[:, 6]
    wout = lax.all_gather(w_out, "dp", axis=0, tiled=True)
    gains = lax.all_gather(gain, ALL, axis=0, tiled=True).astype(f32)
    x = tokens[0].astype(f32)
    scale = lax.rsqrt(jnp.mean(x * x, axis=1, keepdims=True) + EPS)
    xn = (x * scale * gains).astype(bf16)
    xns = lax.all_gather(xn, TP, axis=0, tiled=True)
    ups = lax.all_gather(grad_out[0], TP, axis=0, tiled=True)
    lens = lax.all_gather(lengths, TP, axis=0, tiled=True)
    rows = lens.shape[0]
    tall = rows * length

    def time_major(a):
        return a.reshape(rows, length, -1).transpose(1, 0, 2).reshape(tall, -1)

    def row_major(a):
        return a.reshape(length, rows, -1).transpose(1, 0, 2).reshape(tall, -1)

    same, live = masks(lens, length)
    zz = time_major(jnp.dot(xns, win, preferred_element_type=f32))
    u = zz[:, :channels].reshape(length, rows, channels)
    g = zz[:, channels:]
    c = bias + taps[:, 3] * u
    shifted = []
    for offset in range(1, 4):
        earlier = jnp.pad(u, ((offset, 0), (0, 0), (0, 0)))[:length] * same[offset - 1][:, :, None]
        shifted.append(earlier)
        c = c + taps[:, 3 - offset] * earlier
    sig = jax.nn.sigmoid(c)
    v16 = (c * sig).astype(bf16).reshape(tall, channels)
    v = v16.astype(f32)
    p = lax.psum(jnp.dot(v16, wx, preferred_element_type=f32), TP)
    dl = p[:, :rank].astype(bf16)
    kq = p[:, rank:]
    dims_cols = (((1,), (1,)), ((), ()))
    dims_rows = (((0,), (0,)), ((), ()))
    pre = lax.dot_general(dl, wdt, dims_cols, preferred_element_type=f32) + dtb
    dm = time_major(lax.dot_general(ups, wout, dims_cols, preferred_element_type=f32))
    flags = jnp.pad(jnp.stack([same[0].reshape(tall), live.reshape(tall)], axis=1), ((0, 0), (0, 126)))
    hi = kq.astype(bf16)
    mid = (kq - hi.astype(f32)).astype(bf16)
    low = (kq - hi.astype(f32) - mid.astype(f32)).astype(bf16)
    kq3 = jnp.concatenate([hi, mid, low], axis=1)
    keys = kq[:, :states]
    sk = jnp.broadcast_to(jnp.sum(keys * keys, axis=1, keepdims=True), (tall, 8))
    m, dg, dpre, dv, dkq, stats = mixer(flags, kq3, sk, pre, v, g, dm, skips[None], states=states, width=256, unroll=4)
    stats = stats.transpose(1, 2, 0, 3).reshape(3, 8, channels)
    dskip = jnp.sum(stats[0], axis=0)
    total = lax.psum(jnp.sum(stats[1]), ALL)
    peak = lax.pmax(jnp.max(stats[2]), ALL)
    beta_mean = total / float(groups * ways * length * inner)
    m16 = row_major(m).astype(bf16)
    out = jnp.dot(m16, wout, preferred_element_type=f32).astype(bf16)
    out = lax.psum_scatter(out, TP, scatter_dimension=0, tiled=True)
    block_out = (x + out.astype(f32)).astype(bf16)
    grad_wout = lax.dot_general(m16, ups, dims_rows, preferred_element_type=f32).astype(bf16)
    grad_wout = lax.psum_scatter(grad_wout, "dp", scatter_dimension=0, tiled=True)
    dpre16 = dpre.astype(bf16)
    grad_dtb = jnp.sum(dpre16.astype(f32), axis=0)
    grad_wdt = lax.dot_general(dpre16, dl, dims_rows, preferred_element_type=f32)
    ddl = jnp.dot(dpre16, wdt, preferred_element_type=f32)
    dkq = dkq[:, :2 * states] + dkq[:, 2 * states:2 * states + 1] * jnp.pad(keys, ((0, 0), (0, states)))
    dp16 = lax.psum(jnp.concatenate([ddl, dkq], axis=1), TP).astype(bf16)
    grad_wx = lax.dot_general(v16, dp16, dims_rows, preferred_element_type=f32)
    dvt = dv + lax.dot_general(dp16, wx, dims_cols, preferred_element_type=f32)
    dc = (dvt * (sig.reshape(tall, channels) * (1.0 + c.reshape(tall, channels) * (1.0 - sig.reshape(tall, channels))))).reshape(length, rows, channels)
    du = taps[:, 3] * dc
    grad_taps = [jnp.sum(dc * u, axis=(0, 1))]
    for offset in range(1, 4):
        grad_taps.append(jnp.sum(dc * shifted[offset - 1], axis=(0, 1)))
        du = du + taps[:, 3 - offset] * jnp.pad((dc * same[offset - 1][:, :, None])[offset:], ((0, offset), (0, 0), (0, 0)))
    grad_conv = jnp.stack(grad_taps[::-1] + [jnp.sum(dc, axis=(0, 1)), grad_dtb, dskip], axis=1)
    dz = row_major(jnp.concatenate([du.reshape(tall, channels), dg], axis=1)).astype(bf16)
    gwin = lax.dot_general(xns, dz, dims_rows, preferred_element_type=f32).astype(bf16)
    gwin = lax.psum_scatter(gwin, "dp", scatter_dimension=0, tiled=True)
    gwin = lax.all_to_all(gwin.reshape(ways, own_d, 2 * channels), TP, split_axis=0, concat_axis=0, tiled=True)
    grad_win = gwin.reshape(ways, own_d, 2, groups, own_e).transpose(1, 2, 3, 0, 4).reshape(own_d, 2 * inner).astype(f32)
    dxn = lax.dot_general(dz, win, dims_cols, preferred_element_type=f32).astype(bf16)
    dxn = lax.psum_scatter(dxn, TP, scatter_dimension=0, tiled=True).astype(f32)
    small_grad = lax.psum_scatter(jnp.concatenate([grad_wx, grad_wdt, grad_conv], axis=1), "dp", scatter_dimension=0, tiled=True)
    inner_grad = dxn * gains
    dxx = scale * inner_grad - x * (scale * scale * scale) * (jnp.sum(inner_grad * x, axis=1, keepdims=True) / model)
    grad_tokens = (grad_out[0].astype(f32) + dxx).astype(bf16)
    grad_gain = lax.psum_scatter(jnp.sum(dxn * x * scale, axis=0), ALL, scatter_dimension=0, tiled=True)
    at = rank + 2 * states
    return (
        block_out[None],
        grad_tokens[None],
        grad_gain,
        grad_win,
        small_grad[:, at + rank:at + rank + 4],
        small_grad[:, at + rank + 4],
        small_grad[:, :at],
        small_grad[:, at:at + rank],
        small_grad[:, at + rank + 5],
        small_grad[:, at + rank + 6],
        grad_wout.astype(f32),
        beta_mean,
        peak,
    )


def solution(mesh):
    wide, narrow = mesh.devices.shape
    fine = Mesh(mesh.devices.reshape(wide // 2, 2, narrow), ALL)
    cut = (P(ALL, None), P(ALL))
    in_specs = (P(ALL, None, None), cut[0], cut[1], cut[0], cut[0], cut[1], cut[0], cut[0], cut[1], cut[1], cut[0], P(ALL, None, None))
    out_specs = (P(ALL, None, None), P(ALL, None, None), cut[1], cut[0], cut[0], cut[1], cut[0], cut[0], cut[1], cut[1], cut[0], P(), P())
    return jax.shard_map(on_device, mesh=fine, in_specs=in_specs, out_specs=out_specs, check_vma=False)
```

```python
import functools
import jax, jax.numpy as jnp
from jax import lax
from jax.experimental import pallas as pl
from jax.experimental.pallas import tpu as pltpu
from jax.sharding import Mesh, PartitionSpec as P

DOCS = 4
EPS = 1e-05
ALL = ("dp", "core", "z")
TP = ("core", "z")

f32 = jnp.float32
bf16 = jnp.bfloat16

def fold(x):
    total = x[:, :128]
    for at in range(128, x.shape[1], 128):
        total = total + x[:, at:at+128]
    return total

def mixer_kernel(states, unroll, chunk, flags_ref, kq3_ref, sk_ref, pre_ref, v_ref, g_ref, dm_ref, skip_ref,
                 m_ref, dg_ref, dpre_ref, dv_ref, dkq_ref, stat_ref, s_ref, h_ref, rate_ref, rv_ref, kb_ref, drr_ref):
    rows = pre_ref.shape[0]
    width = pre_ref.shape[1]
    steps = rows // 8
    wide = states * 128
    spread_rows = kq3_ref.shape[1]
    def spread(i, c):
        r = pl.ds(pl.multiple_of(i * chunk, chunk), chunk)
        left = kq3_ref[r, :]
        for part in range(0, 2 * wide, 512):
            ids = lax.broadcasted_iota(jnp.int32, (spread_rows, 512), 0) % (2 * states)
            col = lax.broadcasted_iota(jnp.int32, (spread_rows, 512), 1) // 128 + part // 128
            hot = jnp.where(ids == col, 1.0, 0.0).astype(bf16)
            kb_ref[r, part:part+512] = jnp.dot(left, hot, preferred_element_type=f32)
        return c
    lax.fori_loop(0, rows // chunk, spread, 0)

    def before(i, c):
        r = pl.ds(pl.multiple_of(i * 64, 64), 64)
        live = flags_ref[r, 1:2]
        beta = jax.nn.sigmoid(pre_ref[r, :])
        part = 1.0 / (1.0 + beta * sk_ref[r, 0:1])
        rate = beta * part
        rate_ref[r, :] = rate
        v = v_ref[r, :]
        rv_ref[r, :] = rate * v
        dpre_ref[r, :] = part * part * beta * (1.0 - beta)
        g = g_ref[r, :]
        sg = jax.nn.sigmoid(g)
        dm = dm_ref[r, :] * live
        dv_ref[r, :] = dm * (g * sg)
        dg_ref[r, :] = dm * (sg * (1.0 + g * (1.0 - sg)))
        return c
    lax.fori_loop(0, rows // 64, before, 0)

    s_ref[0, 0] = jnp.zeros(s_ref.shape[2:], f32)

    group = unroll
    tile = lambda x: jnp.concatenate([x] * (width // 128), axis=1)
    span = group * 8
    at = [slice(j * 8, j * 8 + 8) for j in range(group)]
    def view(ref, i):
        return ref.at[pl.ds(pl.multiple_of(i * span, span), span)]

    def forward(i, carry):
        flags, rates, rvs, vs, kbs, ms = [view(x, i) for x in (flags_ref, rate_ref, rv_ref, v_ref, kb_ref, m_ref)]
        keep = [jnp.broadcast_to(flags[r, 0:1], (8, 128)) for r in at]
        rate = [rates[r, :] for r in at]
        rv = [rvs[r, :] for r in at]
        y = [skip_ref[...] * vs[r, :] for r in at]
        for n in range(states):
            state = s_ref[i, 0, n]
            for j, r in enumerate(at):
                kb = kbs[r, n*128:(n+1)*128]
                qb = kbs[r, wide+n*128:wide+(n+1)*128]
                state = (tile(keep[j]) - rate[j] * tile(kb * kb * keep[j])) * state + rv[j] * tile(kb)
                if j < group - 1:
                    s_ref[i, j + 1, n] = state
                else:
                    s_ref[i + 1, 0, n] = state
                y[j] = y[j] + state * tile(qb)
        for j, r in enumerate(at):
            ms[r, :] = y[j]
        return carry

    lax.fori_loop(0, steps // group, forward, 0)
    h_ref[...] = jnp.zeros_like(h_ref)

    def backward(step, carry):
        i = steps // group - 1 - step
        flags, rates, rvs, vs, kbs, dvs, dpres, drrs = [view(x, i) for x in (flags_ref, rate_ref, rv_ref, v_ref, kb_ref, dv_ref, dpre_ref, drr_ref)]
        keep = [jnp.broadcast_to(flags[r, 0:1], (8, 128)) for r in at]
        rate = [rates[r, :] for r in at]
        rv = [rvs[r, :] for r in at]
        dy = [dvs[r, :] for r in at]
        hk = [jnp.zeros((8, width), f32) for r in at]
        hs2 = [jnp.zeros((8, width), f32) for r in at]
        for n in range(states):
            ah = h_ref[n]
            after_ = s_ref[i + 1, 0, n]
            for j in range(group - 1, -1, -1):
                r = at[j]
                kb = kbs[r, n*128:(n+1)*128]
                qb = kbs[r, wide+n*128:wide+(n+1)*128]
                kk = kb * keep[j]
                held = tile(kb * kk)
                h = dy[j] * tile(qb) + ah
                prior = s_ref[i, j, n]
                hs = h * prior
                hk[j] = hk[j] + h * tile(kb)
                hs2[j] = hs2[j] + hs * held
                kbs[r, n*128:(n+1)*128] = fold(h * rv[j]) - 2.0 * kk * fold(hs * rate[j])
                kbs[r, wide+n*128:wide+(n+1)*128] = fold(dy[j] * after_)
                after_ = prior
                ah = (tile(keep[j]) - rate[j] * held) * h
            h_ref[n] = ah
        for j, r in enumerate(at):
            v = vs[r, :]
            drate = v * hk[j] - hs2[j]
            drrs[r, :] = fold(drate * rate[j] * rate[j]) * (-2.0)
            dpres[r, :] = drate * dpres[r, :]
            dvs[r, :] = rate[j] * hk[j] + skip_ref[...] * dy[j]
            stat_ref[0, 0] += dy[j] * v
        return carry

    stat_ref[...] = jnp.zeros_like(stat_ref)
    lax.fori_loop(0, steps // group, backward, 0)

    first = pl.program_id(0) == 0
    def gather(i, c):
        r = pl.ds(pl.multiple_of(i * chunk, chunk), chunk)
        total = jnp.zeros((chunk, 128), f32)
        for part in range(0, 2 * wide, 512):
            row = lax.broadcasted_iota(jnp.int32, (512, 128), 0) // 128 + part // 128
            col = lax.broadcasted_iota(jnp.int32, (512, 128), 1)
            hot = jnp.where(row == col, 1.0, 0.0).astype(bf16)
            total += jnp.dot(kb_ref[r, part:part+512].astype(bf16), hot, preferred_element_type=f32)
        col = lax.broadcasted_iota(jnp.int32, (128, 128), 1)
        hot = jnp.where(col == 2 * states, 1.0, 0.0).astype(bf16)
        total += jnp.dot(drr_ref[r, :].astype(bf16), hot, preferred_element_type=f32)
        dkq_ref[r, :] = jnp.where(first, total, dkq_ref[r, :] + total)
        return c
    lax.fori_loop(0, rows // chunk, gather, 0)

    def after(i, c):
        r = pl.ds(pl.multiple_of(i * 64, 64), 64)
        live = flags_ref[r, 1:2]
        y = m_ref[r, :]
        g = g_ref[r, :]
        m_ref[r, :] = y * (g * jax.nn.sigmoid(g)) * live
        dg_ref[r, :] = y * dg_ref[r, :]
        shown = (jax.nn.sigmoid(pre_ref[r, :]) * live).reshape(8, 8, width)
        stat_ref[0, 1] += jnp.sum(shown, axis=0)
        stat_ref[0, 2] = jnp.maximum(stat_ref[0, 2], jnp.max(shown, axis=0))
        return c
    lax.fori_loop(0, rows // 64, after, 0)

def mixer(flags, kq3, sk, pre, v, g, dm, skip, states=16, width=256, unroll=1):
    rows, total = pre.shape
    steps = rows // 8
    tiles = total // width
    big = jax.ShapeDtypeStruct((rows, total), f32)
    cut = pl.BlockSpec((rows, width), lambda h: (0, h))
    whole = lambda a: pl.BlockSpec(a.shape, lambda h: (0,) * a.ndim)
    return pl.pallas_call(
        functools.partial(mixer_kernel, states, unroll, min(256, rows)),
        grid=(tiles,),
        out_shape=(big, big, big, big, jax.ShapeDtypeStruct((rows, 128), f32), jax.ShapeDtypeStruct((tiles, 3, 8, width), f32)),
        in_specs=[whole(flags), whole(kq3), whole(sk), cut, cut, cut, cut, pl.BlockSpec((1, width), lambda h: (0, h))],
        out_specs=(cut, cut, cut, cut, pl.BlockSpec((rows, 128), lambda h: (0, 0)), pl.BlockSpec((1, 3, 8, width), lambda h: (h, 0, 0, 0))),
        scratch_shapes=[pltpu.VMEM((steps//unroll+1, unroll, states, 8, width), f32), pltpu.VMEM((states, 8, width), f32)] + [pltpu.VMEM((rows, width), f32)]*2
          + [pltpu.VMEM((rows, 2*states*128), f32), pltpu.VMEM((rows, 128), f32)],
        compiler_params=pltpu.CompilerParams(vmem_limit_bytes=60*1024*1024),
    )(flags, kq3, sk, pre, v, g, dm, skip)


MESH = pl.DeviceIdType.MESH


def flip(value, bit):
    return value + bit * (1 - 2 * ((value // bit) % 2))


def place():
    d, c, z = lax.axis_index("dp"), lax.axis_index("core"), lax.axis_index("z")
    return d, c, z


def put(src, dst, send, recv, device):
    copy = pltpu.make_async_remote_copy(src_ref=src, dst_ref=dst, send_sem=send, recv_sem=recv, device_id=device, device_id_type=MESH)
    copy.start()
    return copy


def landed(slot, sem, device):
    pltpu.make_async_remote_copy(src_ref=slot, dst_ref=slot, send_sem=sem, recv_sem=sem, device_id=device, device_id_type=MESH).wait_recv()


def sent(slot, sem, device):
    pltpu.make_async_remote_copy(src_ref=slot, dst_ref=slot, send_sem=sem, recv_sem=sem, device_id=device, device_id_type=MESH).wait_send()


def greet(devices):
    barrier = pltpu.get_barrier_semaphore()
    for device in devices:
        pl.semaphore_signal(barrier, inc=1, device_id=device, device_id_type=MESH)
    pl.semaphore_wait(barrier, len(devices))


def mates():
    return [(a, k) for k in (0, 1, 3, 2) for a in (1, 0) if (a, k) != (0, 0)]


def mate(step, sign=1):
    d, c, z = place()
    a, k = step
    return d, (flip(c, 1) if a else c), lax.rem(z + sign * k + 4, 4)


def rank_of(device):
    return device[1] * 4 + device[2]


def front_kernel(tok_ref, up_ref, cols_ref, wout_ref, small_ref, meta_ref,
                 xs_ref, ups_ref, win_ref, wouts_ref, smalls_ref, metas_ref,
                 own_sem, ms, mr, qs, qr, xls, xlr, xrs, xrr, xcs, xcr, as_, ar, ps, pr, rs, rr, ws, wr):
    d, c, z = place()
    j = c * 4 + z
    me = (d, c, z)
    dx, dy, dd = flip(d, 1), flip(d, 2), flip(flip(d, 1), 2)
    xn, yn, dn = (dx, c, z), (dy, c, z), (dd, c, z)
    sib = (d, flip(c, 1), z)
    left = (d, c, lax.rem(z + 3, 4))
    right = (d, c, lax.rem(z + 1, 4))
    steps = mates()
    greet([mate(s) for s in steps] + [xn, yn, dn])
    half = cols_ref.shape[1]
    own = [
        pltpu.make_async_copy(tok_ref.at[0], xs_ref.at[j], own_sem.at[0]),
        pltpu.make_async_copy(up_ref.at[0], ups_ref.at[j], own_sem.at[1]),
        pltpu.make_async_copy(cols_ref.at[j], win_ref.at[d, j], own_sem.at[2]),
        pltpu.make_async_copy(wout_ref, wouts_ref.at[d], own_sem.at[3]),
        pltpu.make_async_copy(small_ref, smalls_ref.at[d], own_sem.at[4]),
        pltpu.make_async_copy(meta_ref, metas_ref.at[d, j], own_sem.at[5]),
    ]
    for copy in own:
        copy.start()
    pending = []
    for i, s in enumerate(steps):
        to = mate(s)
        pending.append(put(meta_ref, metas_ref.at[d, j], ms.at[i], mr.at[i], to))
    for i, to in enumerate((xn, yn, dn)):
        pending.append(put(small_ref, smalls_ref.at[d], ps.at[16 + i], pr.at[16 + i], to))
    for i, s in enumerate(steps):
        to = mate(s)
        pending.append(put(cols_ref.at[rank_of(to)], win_ref.at[d, j], as_.at[i], ar.at[i], to))
    own[2].wait()
    pending.append(put(win_ref.at[d, j], win_ref.at[d, j], ps.at[7], pr.at[7], xn))
    pending.append(put(win_ref.at[d, j], win_ref.at[d, j], ps.at[15], pr.at[15], yn))

    def row_start(ref, out, base):
        pending.append(put(ref.at[0], out.at[j], xcs.at[base + z], xcr.at[base + z], sib))

        @pl.when(z < 3)
        def _():
            put(ref.at[0], out.at[j], xls.at[base], xlr.at[base], right)

        @pl.when(z > 0)
        def _():
            put(ref.at[0], out.at[j], xrs.at[base], xrr.at[base], left)

    def row_hop(out, base, i):
        @pl.when(z > i)
        def _():
            at = z - 1 - i
            slot = out.at[c * 4 + at]
            landed(slot, xlr.at[base + i], left)
            if i < 2:
                @pl.when(z < 3)
                def _():
                    put(slot, slot, xls.at[base + i + 1], xlr.at[base + i + 1], right)
            put(slot, slot, xcs.at[base + at], xcr.at[base + at], sib)

        @pl.when(z < 3 - i)
        def _():
            at = z + 1 + i
            slot = out.at[c * 4 + at]
            landed(slot, xrr.at[base + i], right)
            if i < 2:
                @pl.when(z > 0)
                def _():
                    put(slot, slot, xrs.at[base + i + 1], xrr.at[base + i + 1], left)
            put(slot, slot, xcs.at[base + at], xcr.at[base + at], sib)

    def row_end(out, base):
        for i in range(3):
            @pl.when((z < 3) & (z >= i))
            def _():
                sent(out.at[j], xls.at[base + i], right)

            @pl.when((z > 0) & (z <= 3 - i))
            def _():
                sent(out.at[j], xrs.at[base + i], left)
        for at in range(4):
            landed(out.at[flip(c, 1) * 4 + at], xcr.at[base + at], sib)

            @pl.when(z != at)
            def _():
                sent(out.at[j], xcs.at[base + at], sib)

    row_start(tok_ref, xs_ref, 0)
    own[5].wait()
    for i, s in enumerate(steps):
        landed(metas_ref.at[d, rank_of(mate(s, -1))], mr.at[i], xn)
    for i, to in enumerate((xn, yn, dn)):
        pending.append(put(metas_ref.at[d], metas_ref.at[d], qs.at[i], qr.at[i], to))
    for i, s in enumerate(steps):
        src = mate(s, -1)
        slot = win_ref.at[d, rank_of(src)]
        landed(slot, ar.at[i], src)
        pending.append(put(slot, slot, ps.at[i], pr.at[i], xn))
        pending.append(put(slot, slot, ps.at[8 + i], pr.at[8 + i], yn))
    row_hop(xs_ref, 0, 0)
    row_start(up_ref, ups_ref, 4)
    halves = wout_ref.shape[0] // 2
    pending.append(put(wout_ref, wouts_ref.at[d], ws.at[0], wr.at[0], xn))
    pending.append(put(wout_ref, wouts_ref.at[d], ws.at[1], wr.at[1], yn))
    order = [7] + list(range(7))
    slots = {7: j}
    for i, s in enumerate(steps):
        slots[i] = rank_of(mate(s, -1))
    for k, i in enumerate(order):
        slot = win_ref.at[dx, slots[i]]
        landed(slot, pr.at[i], xn)
        if k % 2 == 0:
            pending.append(put(slot, slot, rs.at[k // 2], rr.at[k // 2], yn))
        slot = win_ref.at[dy, slots[i]]
        landed(slot, pr.at[8 + i], yn)
        if k % 2 == 1:
            pending.append(put(slot, slot, rs.at[4 + k // 2], rr.at[4 + k // 2], xn))
        if k == 3:
            row_hop(xs_ref, 0, 1)
            row_hop(ups_ref, 4, 0)
    row_hop(xs_ref, 0, 2)
    row_hop(ups_ref, 4, 1)
    slot = wouts_ref.at[dx]
    landed(slot, wr.at[0], xn)
    slot = wouts_ref.at[dx, pl.ds(0, halves)]
    pending.append(put(slot, slot, ws.at[2], wr.at[2], yn))
    slot = wouts_ref.at[dy]
    landed(slot, wr.at[1], yn)
    slot = wouts_ref.at[dy, pl.ds(halves, halves)]
    pending.append(put(slot, slot, ws.at[3], wr.at[3], xn))
    row_hop(ups_ref, 4, 2)
    for k, i in enumerate(order):
        slot = win_ref.at[dd, slots[i]]
        if k % 2 == 0:
            landed(slot, rr.at[k // 2], yn)
        else:
            landed(slot, rr.at[4 + k // 2], xn)
    landed(wouts_ref.at[dd, pl.ds(0, halves)], wr.at[2], yn)
    landed(wouts_ref.at[dd, pl.ds(halves, halves)], wr.at[3], xn)
    for i, (to, at) in enumerate(((xn, dx), (yn, dy), (dn, dd))):
        landed(smalls_ref.at[at], pr.at[16 + i], to)
        landed(metas_ref.at[at], qr.at[i], to)
    row_end(xs_ref, 0)
    row_end(ups_ref, 4)
    for copy in own[:2] + own[3:5]:
        copy.wait()
    for copy in pending:
        copy.wait_send()


def front(tokens, upstream, cols, w_out, small, meta):
    groups, ways = lax.axis_size("dp"), cols.shape[0]
    like = jax.ShapeDtypeStruct
    length, model = tokens.shape[1:]
    dma = lambda n: pltpu.SemaphoreType.DMA((n,))
    some = pl.BlockSpec(memory_space=pl.ANY)
    return pl.pallas_call(
        front_kernel,
        out_shape=(
            like((ways, length, model), bf16),
            like((ways, length, model), bf16),
            like((groups,) + cols.shape, bf16),
            like((groups,) + w_out.shape, bf16),
            like((groups,) + small.shape, bf16),
            like((groups, ways) + meta.shape, bf16),
        ),
        in_specs=[some] * 6,
        out_specs=(some,) * 6,
        scratch_shapes=[dma(6), dma(7), dma(7), dma(3), dma(3), dma(8), dma(8), dma(8), dma(8), dma(8), dma(8), dma(7), dma(7), dma(19), dma(19), dma(8), dma(8), dma(4), dma(4)],
        compiler_params=pltpu.CompilerParams(collective_id=0, has_side_effects=True, vmem_limit_bytes=16 * 1024 * 1024),
    )(tokens, upstream, cols, w_out, small, meta)


PIECES = 4


def total_kernel(part_ref, out_ref, sib_ref, base_ref, left_ref, right_ref, tor_ref, tol_ref, ss, sr, ls, lr, rs, rr, os_, or_):
    d, c, z = place()
    sib = (d, flip(c, 1), z)
    left = (d, c, lax.rem(z + 3, 4))
    right = (d, c, lax.rem(z + 1, 4))
    rows = part_ref.shape[0] // 2
    piece = rows // PIECES
    mine, theirs = c * rows, flip(c, 1) * rows
    barrier = pltpu.get_barrier_semaphore()
    pl.semaphore_signal(barrier, inc=1, device_id=sib, device_id_type=MESH)
    pl.semaphore_signal(barrier, inc=1, device_id=left, device_id_type=MESH)
    pl.semaphore_signal(barrier, inc=1, device_id=right, device_id_type=MESH)
    pl.semaphore_wait(barrier, 3)

    def cut(p):
        return pl.ds(p * piece, piece)

    def far(base, p):
        return pl.ds(pl.multiple_of(base + p * piece, 8), piece)

    for p in range(PIECES):
        put(part_ref.at[far(theirs, p)], sib_ref.at[cut(p)], ss.at[p], sr.at[p], sib)
    for p in range(PIECES):
        landed(sib_ref.at[cut(p)], sr.at[p], sib)
        base_ref[cut(p), :] = part_ref[far(mine, p), :] + sib_ref[cut(p), :]

        @pl.when(z == 0)
        def _():
            put(base_ref.at[cut(p)], left_ref.at[cut(p)], rs.at[p], lr.at[p], right)

        @pl.when(z == 3)
        def _():
            put(base_ref.at[cut(p)], right_ref.at[cut(p)], ls.at[p], rr.at[p], left)

    def from_left(p):
        landed(left_ref.at[cut(p)], lr.at[p], left)

        @pl.when(z < 3)
        def _():
            tor_ref[cut(p), :] = base_ref[cut(p), :] + left_ref[cut(p), :]
            put(tor_ref.at[cut(p)], left_ref.at[cut(p)], rs.at[p], lr.at[p], right)

    def from_right(p):
        landed(right_ref.at[cut(p)], rr.at[p], right)

        @pl.when(z > 0)
        def _():
            tol_ref[cut(p), :] = base_ref[cut(p), :] + right_ref[cut(p), :]
            put(tol_ref.at[cut(p)], right_ref.at[cut(p)], ls.at[p], rr.at[p], left)

    def finish(p):
        value = base_ref[cut(p), :]
        out_ref[far(mine, p), :] = value

        @pl.when(z > 0)
        def _():
            out_ref[far(mine, p), :] += left_ref[cut(p), :]

        @pl.when(z < 3)
        def _():
            out_ref[far(mine, p), :] += right_ref[cut(p), :]

        put(out_ref.at[far(mine, p)], out_ref.at[far(mine, p)], os_.at[p], or_.at[p], sib)

    @pl.when(z == 1)
    def _():
        for p in range(PIECES):
            from_left(p)

    @pl.when(z < 3)
    def _():
        for p in range(PIECES):
            from_right(p)

    @pl.when(z >= 2)
    def _():
        for p in range(PIECES):
            from_left(p)

    for p in range(PIECES):
        finish(p)
    for p in range(PIECES):
        landed(out_ref.at[far(theirs, p)], or_.at[p], sib)
        sent(out_ref.at[far(mine, p)], os_.at[p], sib)
        sent(part_ref.at[far(theirs, p)], ss.at[p], sib)

        @pl.when(z < 3)
        def _():
            sent(base_ref.at[cut(p)], rs.at[p], right)

        @pl.when(z > 0)
        def _():
            sent(base_ref.at[cut(p)], ls.at[p], left)


def group_total(part, which):
    rows = part.shape[0] // 2
    dma = lambda: pltpu.SemaphoreType.DMA((PIECES,))
    here = pl.BlockSpec(memory_space=pltpu.VMEM)
    return pl.pallas_call(
        total_kernel,
        out_shape=jax.ShapeDtypeStruct(part.shape, f32),
        in_specs=[here],
        out_specs=here,
        scratch_shapes=[pltpu.VMEM((rows, 128), f32)] * 6 + [dma() for _ in range(8)],
        compiler_params=pltpu.CompilerParams(collective_id=which, has_side_effects=True, vmem_limit_bytes=16 * 1024 * 1024),
    )(part)


def add_rows(dst, sources):
    rows = dst.shape[0]
    step = 16

    def body(i, carry):
        r = pl.ds(pl.multiple_of(i * step, step), step)
        value = sources[0][r, :].astype(f32)
        for more in sources[1:]:
            value = value + more[r, :].astype(f32)
        dst[r, :] = value.astype(dst.dtype)
        return carry

    lax.fori_loop(0, rows // step, body, 0)


class Line:
    def __init__(self, part, out, sib, send, left, right, sems):
        self.part, self.out, self.sib, self.send, self.left, self.right = part, out, sib, send, left, right
        self.ss, self.sr, self.gs, self.lr, self.rr = sems
        d, c, z = place()
        self.c = c
        self.other = (d, flip(c, 1), z)
        self.to_left = (d, c, lax.rem(z + 3, 4))
        self.to_right = (d, c, lax.rem(z + 1, 4))

    def start(self):
        for zp in (3, 0, 2, 1):
            put(self.part.at[flip(self.c, 1), zp], self.sib.at[zp], self.ss.at[zp], self.sr.at[zp], self.other)

    def step(self, zs, k):
        for zp in range(4):
            if zp > zs and k == 3 - zp + zs:
                landed(self.sib.at[zp], self.sr.at[zp], self.other)
                terms = [self.part.at[self.c, zp], self.sib.at[zp]]
                if zs > 0:
                    landed(self.left.at[zp], self.lr.at[zp], self.to_left)
                    terms.append(self.left.at[zp])
                add_rows(self.send.at[zp], terms)
                put(self.send.at[zp], self.left.at[zp], self.gs.at[zp], self.lr.at[zp], self.to_right)
            if zp < zs and k == zp + 3 - zs:
                landed(self.sib.at[zp], self.sr.at[zp], self.other)
                terms = [self.part.at[self.c, zp], self.sib.at[zp]]
                if zs < 3:
                    landed(self.right.at[zp], self.rr.at[zp], self.to_right)
                    terms.append(self.right.at[zp])
                add_rows(self.send.at[zp], terms)
                put(self.send.at[zp], self.right.at[zp], self.gs.at[zp], self.rr.at[zp], self.to_left)

    def finish(self, zs):
        landed(self.sib.at[zs], self.sr.at[zs], self.other)
        terms = [self.part.at[self.c, zs], self.sib.at[zs]]
        if zs > 0:
            landed(self.left.at[zs], self.lr.at[zs], self.to_left)
            terms.append(self.left.at[zs])
        if zs < 3:
            landed(self.right.at[zs], self.rr.at[zs], self.to_right)
            terms.append(self.right.at[zs])
        add_rows(self.out, terms)

    def close(self, zs):
        for zp in range(4):
            sent(self.sib.at[zp], self.ss.at[zp], self.other)
            if zp != zs:
                sent(self.send.at[zp], self.gs.at[zp], self.other)


class Plane:
    def __init__(self, part, out, xa, yb, sx, sy, rx, ry, sems):
        self.part, self.out, self.xa, self.yb, self.sx, self.sy, self.rx, self.ry = part, out, xa, yb, sx, sy, rx, ry
        self.ss, self.rs = sems
        d, c, z = place()
        self.d, self.dx, self.dy, self.dd = d, flip(d, 1), flip(d, 2), flip(flip(d, 1), 2)
        self.xn, self.yn = (self.dx, c, z), (self.dy, c, z)
        half = part.shape[1] // 2
        self.a, self.b = pl.ds(0, half), pl.ds(half, half)

    def start(self):
        p = self.part
        self.sends = [
            put(p.at[self.dd, self.a], self.xa, self.ss.at[0], self.rs.at[0], self.xn),
            put(p.at[self.dd, self.b], self.yb, self.ss.at[1], self.rs.at[1], self.yn),
            put(p.at[self.dx, self.a], self.rx.at[self.a], self.ss.at[2], self.rs.at[2], self.xn),
            put(p.at[self.dy, self.b], self.ry.at[self.b], self.ss.at[3], self.rs.at[3], self.yn),
        ]

    def middle(self):
        p = self.part
        landed(self.xa, self.rs.at[0], self.xn)
        add_rows(self.sy, [p.at[self.dy, self.a], self.xa])
        self.sends.append(put(self.sy, self.ry.at[self.a], self.ss.at[4], self.rs.at[4], self.yn))
        landed(self.yb, self.rs.at[1], self.yn)
        add_rows(self.sx, [p.at[self.dx, self.b], self.yb])
        self.sends.append(put(self.sx, self.rx.at[self.b], self.ss.at[5], self.rs.at[5], self.xn))

    def finish(self):
        landed(self.rx.at[self.a], self.rs.at[2], self.xn)
        landed(self.ry.at[self.b], self.rs.at[3], self.yn)
        landed(self.ry.at[self.a], self.rs.at[4], self.yn)
        landed(self.rx.at[self.b], self.rs.at[5], self.xn)
        add_rows(self.out, [self.part.at[self.d], self.rx, self.ry])

    def close(self):
        for copy in self.sends:
            copy.wait_send()


def plane_scratch(rows, columns, dtype):
    half = pltpu.VMEM((rows // 2, columns), dtype)
    full = pltpu.VMEM((rows, columns), dtype)
    return [half, half, half, half, full, full, pltpu.SemaphoreType.DMA((6,)), pltpu.SemaphoreType.DMA((6,))]


def line_scratch(rows, columns, dtype):
    four = pltpu.VMEM((4, rows, columns), dtype)
    return [four] * 4 + [pltpu.SemaphoreType.DMA((4,))] * 5


def back_kernel(dxn_ref, outp_ref, gwin_ref, gwout_ref, small_ref,
                dxns_ref, outs_ref, gwins_ref, gwouts_ref, smalls_ref, *scratch):
    lines = [Line(dxn_ref, dxns_ref, *scratch[0:4], scratch[4:9]), Line(outp_ref, outs_ref, *scratch[9:13], scratch[13:18])]
    scratch = scratch[18:]
    fin, own, as_, ar = scratch[:4]
    scratch = scratch[4:]
    planes = []
    for part, out in ((gwin_ref, fin), (gwout_ref, gwouts_ref), (small_ref, smalls_ref)):
        planes.append(Plane(part, out, *scratch[:6], scratch[6:8]))
        scratch = scratch[8:]
    d, c, z = place()
    j = c * 4 + z
    steps = mates()
    greet([mate(s) for s in steps] + [planes[0].xn, planes[0].yn])
    lines[0].start()
    planes[0].start()
    lines[1].start()

    def along(line, k):
        for zs in range(4):
            @pl.when(z == zs)
            def _():
                if k < 3:
                    line.step(zs, k)
                else:
                    line.finish(zs)
                    line.close(zs)

    along(lines[0], 0)
    along(lines[1], 0)
    planes[1].start()
    planes[2].start()
    along(lines[0], 1)
    planes[0].middle()
    along(lines[0], 2)
    planes[0].finish()
    block = fin.shape[0] // 8
    def rows_of(rank):
        return fin.at[pl.ds(pl.multiple_of(rank * block, 16), block)]
    keep = pltpu.make_async_copy(rows_of(j), gwins_ref.at[j], own)
    keep.start()
    pending = []
    for i, s in enumerate(steps):
        to = mate(s)
        pending.append(put(rows_of(rank_of(to)), gwins_ref.at[j], as_.at[i], ar.at[i], to))
    along(lines[0], 3)
    planes[1].middle()
    planes[2].middle()
    along(lines[1], 1)
    planes[1].finish()
    planes[2].finish()
    along(lines[1], 2)
    for i, s in enumerate(steps):
        src = mate(s, -1)
        landed(gwins_ref.at[rank_of(src)], ar.at[i], src)
    along(lines[1], 3)
    keep.wait()
    for copy in pending:
        copy.wait_send()
    for plane in planes:
        plane.close()


def back(dxn, outp, gwin, gwout, small):
    like = jax.ShapeDtypeStruct
    here = pl.BlockSpec(memory_space=pltpu.VMEM)
    rows, columns = dxn.shape[2:]
    return pl.pallas_call(
        back_kernel,
        out_shape=(
            like((rows, columns), f32),
            like((rows, columns), f32),
            like((8, gwin.shape[1] // 8, gwin.shape[2]), bf16),
            like(gwout.shape[1:], f32),
            like(small.shape[1:], f32),
        ),
        in_specs=[here] * 5,
        out_specs=(here,) * 5,
        scratch_shapes=line_scratch(rows, columns, bf16) + line_scratch(rows, columns, bf16)
        + [pltpu.VMEM(gwin.shape[1:], bf16), pltpu.SemaphoreType.DMA(()), pltpu.SemaphoreType.DMA((7,)), pltpu.SemaphoreType.DMA((7,))]
        + plane_scratch(*gwin.shape[1:], bf16) + plane_scratch(*gwout.shape[1:], bf16) + plane_scratch(*small.shape[1:], f32),
        compiler_params=pltpu.CompilerParams(collective_id=3, has_side_effects=True, vmem_limit_bytes=60 * 1024 * 1024),
    )(dxn, outp, gwin, gwout, small)


def tiny_kernel(part_ref, out_ref, near_ref, sum_ref, far_ref, ns, nr, fs, fr):
    d, c, z = place()
    j = c * 4 + z
    steps = mates()
    planes = [(flip(d, 1), c, z), (flip(d, 2), c, z), (flip(flip(d, 1), 2), c, z)]
    greet([mate(s) for s in steps] + planes)
    for i, s in enumerate(steps):
        to = mate(s)
        put(part_ref.at[rank_of(to)], near_ref.at[i], ns.at[i], nr.at[i], to)
    row = lax.broadcasted_iota(jnp.int32, (8, 128), 0)
    lane = lax.broadcasted_iota(jnp.int32, (8, 128), 1)
    peak = (row == 4) & (lane == 1)

    def join(a, b):
        return jnp.where(peak, jnp.maximum(a, b), a + b)

    value = part_ref[j]
    for i, s in enumerate(steps):
        landed(near_ref.at[i], nr.at[i], mate(s, -1))
        value = join(value, near_ref[i])
    sum_ref[...] = value
    for i, to in enumerate(planes):
        put(sum_ref, far_ref.at[i], fs.at[i], fr.at[i], to)
    for i, to in enumerate(planes):
        landed(far_ref.at[i], fr.at[i], to)
        value = join(value, far_ref[i])
    out_ref[...] = value
    for i, to in enumerate(planes):
        sent(sum_ref, fs.at[i], to)
    for i, s in enumerate(steps):
        sent(near_ref.at[i], ns.at[i], mate(s))


def tiny(part):
    here = pl.BlockSpec(memory_space=pltpu.VMEM)
    dma = lambda n: pltpu.SemaphoreType.DMA((n,))
    return pl.pallas_call(
        tiny_kernel,
        out_shape=jax.ShapeDtypeStruct((8, 128), f32),
        in_specs=[here],
        out_specs=here,
        scratch_shapes=[pltpu.VMEM((7, 8, 128), f32), pltpu.VMEM((8, 128), f32), pltpu.VMEM((3, 8, 128), f32), dma(7), dma(7), dma(3), dma(3)],
        compiler_params=pltpu.CompilerParams(collective_id=4, has_side_effects=True),
    )(part)


def masks(lengths, count):
    ends = jnp.cumsum(lengths, axis=1)
    places = jnp.arange(count, dtype=jnp.int32)
    segment = jnp.sum((places[:, None, None] >= ends[None, :, :]).astype(jnp.int32), axis=2)
    same = []
    for offset in range(1, 4):
        before = jnp.pad(segment, ((offset, 0), (0, 0)), constant_values=-1)[:count]
        same.append((before == segment).astype(f32))
    return same, (segment < DOCS).astype(f32)


def columns(weights, ways):
    rows, total = weights.shape
    return weights.reshape(rows, 2, total // (2 * ways * 128), ways, 128)


def group_sum(part, rank, direct, which):
    if not direct:
        return lax.psum(part, TP)
    count, rest = part.shape[0], part.shape[1] - rank
    packed = jnp.concatenate([part[:, :rank], part[:, rank:].T.reshape(-1, rank)], axis=0)
    packed = group_total(packed, which)
    return jnp.concatenate([packed[:count], packed[count:].reshape(rest, count).T], axis=1)


def on_device(tokens, lengths, gain, w_in, conv_w, conv_b, w_x, w_dt, dt_bias, skip, w_out, grad_out):
    ways = lax.axis_size("core") * lax.axis_size("z")
    groups = lax.axis_size("dp")
    length, model = tokens.shape[1:]
    own_d = w_in.shape[0]
    own_e = conv_w.shape[0]
    inner = w_in.shape[1] // 2
    channels = inner // ways
    rank = w_dt.shape[1]
    states = (w_x.shape[1] - rank) // 2
    cols = w_in.reshape(own_d, 2, groups, ways, own_e).transpose(3, 0, 1, 2, 4).reshape(ways, own_d, 2 * channels)
    small = jnp.concatenate([w_x, w_dt, conv_w, conv_b[:, None], dt_bias[:, None], skip[:, None]], axis=1)
    small_width = small.shape[1]
    direct = groups == 4 and lax.axis_size("z") == 4
    x = tokens[0].astype(f32)
    scale = lax.rsqrt(jnp.mean(x * x, axis=1, keepdims=True) + EPS)
    if direct:
        padded = -small_width % 128
        meta = jnp.zeros((16, 128), bf16).at[0, :own_d].set(gain).at[1, :5].set(lengths[0].astype(bf16))
        xs, ups, win, wout, small, metas = front(tokens, grad_out, cols, w_out, jnp.pad(small, ((0, 0), (0, padded))), meta)
        gains = metas[:, :, 0, :own_d].reshape(model).astype(f32)
        lens = lax.dynamic_index_in_dim(metas, lax.axis_index("dp"), keepdims=False)[:, 1, :5].astype(jnp.int32)
    else:
        cols = lax.all_to_all(cols, TP, split_axis=0, concat_axis=0, tiled=True)
        win = lax.all_gather(cols, "dp", axis=0, tiled=True)
        small = lax.all_gather(small, "dp", axis=0, tiled=True)
        wout = lax.all_gather(w_out, "dp", axis=0, tiled=True)
        gains = lax.all_gather(gain, ALL, axis=0, tiled=True).astype(f32)
        xs = lax.all_gather(tokens, TP, axis=0, tiled=True)
        ups = lax.all_gather(grad_out, TP, axis=0, tiled=True)
        lens = lax.all_gather(lengths, TP, axis=0, tiled=True)
    rows = lens.shape[0]
    tall = rows * length
    win = win.reshape(model, 2 * channels)
    wout = wout.reshape(channels, model)
    small = small.reshape(channels, -1)
    ups = ups.reshape(tall, model)
    wide_x = xs.reshape(tall, model).astype(f32)
    xns = (wide_x * lax.rsqrt(jnp.mean(wide_x * wide_x, axis=1, keepdims=True) + EPS) * gains).astype(bf16)
    wx = small[:, :rank + 2 * states]
    wdt = small[:, rank + 2 * states:2 * rank + 2 * states]
    rest = small[:, 2 * rank + 2 * states:small_width].astype(f32)
    taps, bias, dtb, skips = rest[:, :4], rest[:, 4], rest[:, 5], rest[:, 6]

    def time_major(a):
        return a.reshape(rows, length, -1).transpose(1, 0, 2).reshape(tall, -1)

    def row_major(a):
        return a.reshape(length, rows, -1).transpose(1, 0, 2).reshape(tall, -1)

    same, live = masks(lens, length)
    zz = time_major(jnp.dot(xns, win, preferred_element_type=f32))
    u = zz[:, :channels].reshape(length, rows, channels)
    g = zz[:, channels:]
    c = bias + taps[:, 3] * u
    shifted = []
    for offset in range(1, 4):
        earlier = jnp.pad(u, ((offset, 0), (0, 0), (0, 0)))[:length] * same[offset - 1][:, :, None]
        shifted.append(earlier)
        c = c + taps[:, 3 - offset] * earlier
    sig = jax.nn.sigmoid(c)
    v16 = (c * sig).astype(bf16).reshape(tall, channels)
    v = v16.astype(f32)
    whole = group_sum(jnp.dot(v16, wx, preferred_element_type=f32), rank, direct, 1)
    p = whole
    dl = p[:, :rank].astype(bf16)
    kq = p[:, rank:]
    dims_cols = (((1,), (1,)), ((), ()))
    dims_rows = (((0,), (0,)), ((), ()))
    pre = lax.dot_general(dl, wdt, dims_cols, preferred_element_type=f32) + dtb
    dm = time_major(lax.dot_general(ups, wout, dims_cols, preferred_element_type=f32))
    flags = jnp.pad(jnp.stack([same[0].reshape(tall), live.reshape(tall)], axis=1), ((0, 0), (0, 126)))
    hi = kq.astype(bf16)
    mid = (kq - hi.astype(f32)).astype(bf16)
    low = (kq - hi.astype(f32) - mid.astype(f32)).astype(bf16)
    kq3 = jnp.concatenate([hi, mid, low], axis=1)
    keys = kq[:, :states]
    sk = jnp.broadcast_to(jnp.sum(keys * keys, axis=1, keepdims=True), (tall, 8))
    m, dg, dpre, dv, dkq, stats = mixer(flags, kq3, sk, pre, v, g, dm, skips[None], states=states, width=256, unroll=4)
    stats = stats.transpose(1, 2, 0, 3).reshape(3, 8, channels)
    dskip = jnp.sum(stats[0], axis=0)
    m16 = row_major(m).astype(bf16)
    out = jnp.dot(m16, wout, preferred_element_type=f32).astype(bf16)
    grad_wout = lax.dot_general(m16, ups, dims_rows, preferred_element_type=f32).astype(bf16)
    dpre16 = dpre.astype(bf16)
    grad_dtb = jnp.sum(dpre16.astype(f32), axis=0)
    grad_wdt = lax.dot_general(dpre16, dl, dims_rows, preferred_element_type=f32)
    ddl = jnp.dot(dpre16, wdt, preferred_element_type=f32)
    dkq = dkq[:, :2 * states] + dkq[:, 2 * states:2 * states + 1] * jnp.pad(keys, ((0, 0), (0, states)))
    dp16 = group_sum(jnp.concatenate([ddl, dkq], axis=1), rank, direct, 2).astype(bf16)
    grad_wx = lax.dot_general(v16, dp16, dims_rows, preferred_element_type=f32)
    dvt = dv + lax.dot_general(dp16, wx, dims_cols, preferred_element_type=f32)
    dc = (dvt * (sig.reshape(tall, channels) * (1.0 + c.reshape(tall, channels) * (1.0 - sig.reshape(tall, channels))))).reshape(length, rows, channels)
    du = taps[:, 3] * dc
    grad_taps = [jnp.sum(dc * u, axis=(0, 1))]
    for offset in range(1, 4):
        grad_taps.append(jnp.sum(dc * shifted[offset - 1], axis=(0, 1)))
        du = du + taps[:, 3 - offset] * jnp.pad((dc * same[offset - 1][:, :, None])[offset:], ((0, offset), (0, 0), (0, 0)))
    grad_conv = jnp.stack(grad_taps[::-1] + [jnp.sum(dc, axis=(0, 1)), grad_dtb, dskip], axis=1)
    dz = row_major(jnp.concatenate([du.reshape(tall, channels), dg], axis=1)).astype(bf16)
    gwin = lax.dot_general(xns, dz, dims_rows, preferred_element_type=f32).astype(bf16)
    dxn = lax.dot_general(dz, win, dims_cols, preferred_element_type=f32).astype(bf16)
    small_grad = jnp.concatenate([grad_wx, grad_wdt, grad_conv], axis=1)
    if direct:
        small_grad = jnp.pad(small_grad, ((0, 0), (0, padded)))
        dxn, out, gwin, grad_wout, small_grad = back(
            dxn.reshape(2, 4, length, model), out.reshape(2, 4, length, model), gwin.reshape(groups, ways * own_d, 2 * channels),
            grad_wout.reshape(groups, own_e, model), small_grad.reshape(groups, own_e, -1))
    else:
        out = lax.psum_scatter(out, TP, scatter_dimension=0, tiled=True).astype(f32)
        grad_wout = lax.psum_scatter(grad_wout, "dp", scatter_dimension=0, tiled=True).astype(f32)
        gwin = lax.psum_scatter(gwin, "dp", scatter_dimension=0, tiled=True)
        gwin = lax.all_to_all(gwin.reshape(ways, own_d, 2 * channels), TP, split_axis=0, concat_axis=0, tiled=True)
        dxn = lax.psum_scatter(dxn, TP, scatter_dimension=0, tiled=True).astype(f32)
        small_grad = lax.psum_scatter(small_grad, "dp", scatter_dimension=0, tiled=True)
    block_out = (x + out).astype(bf16)
    grad_win = gwin.reshape(ways, own_d, 2, groups, own_e).transpose(1, 2, 3, 0, 4).reshape(own_d, 2 * inner).astype(f32)
    inner_grad = dxn * gains
    dxx = scale * inner_grad - x * (scale * scale * scale) * (jnp.sum(inner_grad * x, axis=1, keepdims=True) / model)
    grad_tokens = (grad_out[0].astype(f32) + dxx).astype(bf16)
    grad_gain = jnp.sum(dxn * x * scale, axis=0)
    seen, peak = jnp.sum(stats[1]), jnp.max(stats[2])
    if direct:
        part = grad_gain.reshape(groups, ways, own_d).transpose(1, 0, 2)
        part = jnp.pad(part, ((0, 0), (0, 8 - groups), (0, 128 - own_d)))
        part = part.at[:, 4, 0].set(seen).at[:, 4, 1].set(peak)
        part = tiny(part)
        grad_gain = lax.dynamic_index_in_dim(part, lax.axis_index("dp"), keepdims=False)[:own_d]
        seen, peak = part[4, 0], part[4, 1]
    else:
        grad_gain = lax.psum_scatter(grad_gain, ALL, scatter_dimension=0, tiled=True)
        seen, peak = lax.psum(seen, ALL), lax.pmax(peak, ALL)
    beta_mean = seen / float(groups * ways * length * inner)
    at = rank + 2 * states
    return (
        block_out[None],
        grad_tokens[None],
        grad_gain,
        grad_win,
        small_grad[:, at + rank:at + rank + 4],
        small_grad[:, at + rank + 4],
        small_grad[:, :at],
        small_grad[:, at:at + rank],
        small_grad[:, at + rank + 5],
        small_grad[:, at + rank + 6],
        grad_wout,
        beta_mean,
        peak,
    )


def solution(mesh):
    wide, narrow = mesh.devices.shape
    fine = Mesh(mesh.devices.reshape(wide // 2, 2, narrow), ALL)
    cut = (P(ALL, None), P(ALL))
    in_specs = (P(ALL, None, None), cut[0], cut[1], cut[0], cut[0], cut[1], cut[0], cut[0], cut[1], cut[1], cut[0], P(ALL, None, None))
    out_specs = (P(ALL, None, None), P(ALL, None, None), cut[1], cut[0], cut[0], cut[1], cut[0], cut[0], cut[1], cut[1], cut[0], P(), P())
    return jax.shard_map(on_device, mesh=fine, in_specs=in_specs, out_specs=out_specs, check_vma=False)
```

```python
import functools
import jax, jax.numpy as jnp
from jax import lax
from jax.experimental import pallas as pl
from jax.experimental.pallas import tpu as pltpu
from jax.sharding import Mesh, PartitionSpec as P

DOCS = 4
EPS = 1e-05
ALL = ("dp", "core", "z")
TP = ("core", "z")

f32 = jnp.float32
bf16 = jnp.bfloat16

def fold(x):
    total = x[:, :128]
    for at in range(128, x.shape[1], 128):
        total = total + x[:, at:at+128]
    return total

def mixer_kernel(states, unroll, chunk, flags_ref, kq3_ref, sk_ref, pre_ref, v_ref, g_ref, dm_ref, skip_ref,
                 m_ref, dg_ref, dpre_ref, dv_ref, dkq_ref, stat_ref, s_ref, h_ref, rate_ref, rv_ref, kb_ref, drr_ref):
    rows = pre_ref.shape[0]
    width = pre_ref.shape[1]
    steps = rows // 8
    wide = states * 128
    spread_rows = kq3_ref.shape[1]
    def spread(i, c):
        r = pl.ds(pl.multiple_of(i * chunk, chunk), chunk)
        left = kq3_ref[r, :]
        for part in range(0, 2 * wide, 512):
            ids = lax.broadcasted_iota(jnp.int32, (spread_rows, 512), 0) % (2 * states)
            col = lax.broadcasted_iota(jnp.int32, (spread_rows, 512), 1) // 128 + part // 128
            hot = jnp.where(ids == col, 1.0, 0.0).astype(bf16)
            kb_ref[r, part:part+512] = jnp.dot(left, hot, preferred_element_type=f32)
        return c
    lax.fori_loop(0, rows // chunk, spread, 0)

    def before(i, c):
        r = pl.ds(pl.multiple_of(i * 64, 64), 64)
        live = flags_ref[r, 1:2]
        beta = jax.nn.sigmoid(pre_ref[r, :])
        part = 1.0 / (1.0 + beta * sk_ref[r, 0:1])
        rate = beta * part
        rate_ref[r, :] = rate
        v = v_ref[r, :]
        rv_ref[r, :] = rate * v
        dpre_ref[r, :] = part * part * beta * (1.0 - beta)
        g = g_ref[r, :]
        sg = jax.nn.sigmoid(g)
        dm = dm_ref[r, :] * live
        dv_ref[r, :] = dm * (g * sg)
        dg_ref[r, :] = dm * (sg * (1.0 + g * (1.0 - sg)))
        return c
    lax.fori_loop(0, rows // 64, before, 0)

    s_ref[0, 0] = jnp.zeros(s_ref.shape[2:], f32)

    group = unroll
    tile = lambda x: jnp.concatenate([x] * (width // 128), axis=1)
    span = group * 8
    at = [slice(j * 8, j * 8 + 8) for j in range(group)]
    def view(ref, i):
        return ref.at[pl.ds(pl.multiple_of(i * span, span), span)]

    def forward(i, carry):
        flags, rates, rvs, vs, kbs, ms = [view(x, i) for x in (flags_ref, rate_ref, rv_ref, v_ref, kb_ref, m_ref)]
        keep = [jnp.broadcast_to(flags[r, 0:1], (8, 128)) for r in at]
        rate = [rates[r, :] for r in at]
        rv = [rvs[r, :] for r in at]
        y = [skip_ref[...] * vs[r, :] for r in at]
        for n in range(states):
            state = s_ref[i, 0, n]
            for j, r in enumerate(at):
                kb = kbs[r, n*128:(n+1)*128]
                qb = kbs[r, wide+n*128:wide+(n+1)*128]
                state = (tile(keep[j]) - rate[j] * tile(kb * kb * keep[j])) * state + rv[j] * tile(kb)
                if j < group - 1:
                    s_ref[i, j + 1, n] = state
                else:
                    s_ref[i + 1, 0, n] = state
                y[j] = y[j] + state * tile(qb)
        for j, r in enumerate(at):
            ms[r, :] = y[j]
        return carry

    lax.fori_loop(0, steps // group, forward, 0)
    h_ref[...] = jnp.zeros_like(h_ref)

    def backward(step, carry):
        i = steps // group - 1 - step
        flags, rates, rvs, vs, kbs, dvs, dpres, drrs = [view(x, i) for x in (flags_ref, rate_ref, rv_ref, v_ref, kb_ref, dv_ref, dpre_ref, drr_ref)]
        keep = [jnp.broadcast_to(flags[r, 0:1], (8, 128)) for r in at]
        rate = [rates[r, :] for r in at]
        rv = [rvs[r, :] for r in at]
        dy = [dvs[r, :] for r in at]
        hk = [jnp.zeros((8, width), f32) for r in at]
        hs2 = [jnp.zeros((8, width), f32) for r in at]
        for n in range(states):
            ah = h_ref[n]
            after_ = s_ref[i + 1, 0, n]
            for j in range(group - 1, -1, -1):
                r = at[j]
                kb = kbs[r, n*128:(n+1)*128]
                qb = kbs[r, wide+n*128:wide+(n+1)*128]
                kk = kb * keep[j]
                held = tile(kb * kk)
                h = dy[j] * tile(qb) + ah
                prior = s_ref[i, j, n]
                hs = h * prior
                hk[j] = hk[j] + h * tile(kb)
                hs2[j] = hs2[j] + hs * held
                kbs[r, n*128:(n+1)*128] = fold(h * rv[j]) - 2.0 * kk * fold(hs * rate[j])
                kbs[r, wide+n*128:wide+(n+1)*128] = fold(dy[j] * after_)
                after_ = prior
                ah = (tile(keep[j]) - rate[j] * held) * h
            h_ref[n] = ah
        for j, r in enumerate(at):
            v = vs[r, :]
            drate = v * hk[j] - hs2[j]
            drrs[r, :] = fold(drate * rate[j] * rate[j]) * (-2.0)
            dpres[r, :] = drate * dpres[r, :]
            dvs[r, :] = rate[j] * hk[j] + skip_ref[...] * dy[j]
            stat_ref[0, 0] += dy[j] * v
        return carry

    stat_ref[...] = jnp.zeros_like(stat_ref)
    lax.fori_loop(0, steps // group, backward, 0)

    first = pl.program_id(0) == 0
    def gather(i, c):
        r = pl.ds(pl.multiple_of(i * chunk, chunk), chunk)
        total = jnp.zeros((chunk, 128), f32)
        for part in range(0, 2 * wide, 512):
            row = lax.broadcasted_iota(jnp.int32, (512, 128), 0) // 128 + part // 128
            col = lax.broadcasted_iota(jnp.int32, (512, 128), 1)
            hot = jnp.where(row == col, 1.0, 0.0).astype(bf16)
            total += jnp.dot(kb_ref[r, part:part+512].astype(bf16), hot, preferred_element_type=f32)
        col = lax.broadcasted_iota(jnp.int32, (128, 128), 1)
        hot = jnp.where(col == 2 * states, 1.0, 0.0).astype(bf16)
        total += jnp.dot(drr_ref[r, :].astype(bf16), hot, preferred_element_type=f32)
        dkq_ref[r, :] = jnp.where(first, total, dkq_ref[r, :] + total)
        return c
    lax.fori_loop(0, rows // chunk, gather, 0)

    def after(i, c):
        r = pl.ds(pl.multiple_of(i * 64, 64), 64)
        live = flags_ref[r, 1:2]
        y = m_ref[r, :]
        g = g_ref[r, :]
        m_ref[r, :] = y * (g * jax.nn.sigmoid(g)) * live
        dg_ref[r, :] = y * dg_ref[r, :]
        shown = (jax.nn.sigmoid(pre_ref[r, :]) * live).reshape(8, 8, width)
        stat_ref[0, 1] += jnp.sum(shown, axis=0)
        stat_ref[0, 2] = jnp.maximum(stat_ref[0, 2], jnp.max(shown, axis=0))
        return c
    lax.fori_loop(0, rows // 64, after, 0)

def mixer(flags, kq3, sk, pre, v, g, dm, skip, states=16, width=256, unroll=1):
    rows, total = pre.shape
    steps = rows // 8
    tiles = total // width
    big = jax.ShapeDtypeStruct((rows, total), f32)
    cut = pl.BlockSpec((rows, width), lambda h: (0, h))
    whole = lambda a: pl.BlockSpec(a.shape, lambda h: (0,) * a.ndim)
    return pl.pallas_call(
        functools.partial(mixer_kernel, states, unroll, min(256, rows)),
        grid=(tiles,),
        out_shape=(big, big, big, big, jax.ShapeDtypeStruct((rows, 128), f32), jax.ShapeDtypeStruct((tiles, 3, 8, width), f32)),
        in_specs=[whole(flags), whole(kq3), whole(sk), cut, cut, cut, cut, pl.BlockSpec((1, width), lambda h: (0, h))],
        out_specs=(cut, cut, cut, cut, pl.BlockSpec((rows, 128), lambda h: (0, 0)), pl.BlockSpec((1, 3, 8, width), lambda h: (h, 0, 0, 0))),
        scratch_shapes=[pltpu.VMEM((steps//unroll+1, unroll, states, 8, width), f32), pltpu.VMEM((states, 8, width), f32)] + [pltpu.VMEM((rows, width), f32)]*2
          + [pltpu.VMEM((rows, 2*states*128), f32), pltpu.VMEM((rows, 128), f32)],
        compiler_params=pltpu.CompilerParams(vmem_limit_bytes=60*1024*1024),
    )(flags, kq3, sk, pre, v, g, dm, skip)


MESH = pl.DeviceIdType.MESH


def flip(value, bit):
    return value + bit * (1 - 2 * ((value // bit) % 2))


def place():
    d, c, z = lax.axis_index("dp"), lax.axis_index("core"), lax.axis_index("z")
    return d, c, z


def put(src, dst, send, recv, device):
    copy = pltpu.make_async_remote_copy(src_ref=src, dst_ref=dst, send_sem=send, recv_sem=recv, device_id=device, device_id_type=MESH)
    copy.start()
    return copy


def landed(slot, sem, device):
    pltpu.make_async_remote_copy(src_ref=slot, dst_ref=slot, send_sem=sem, recv_sem=sem, device_id=device, device_id_type=MESH).wait_recv()


def sent(slot, sem, device):
    pltpu.make_async_remote_copy(src_ref=slot, dst_ref=slot, send_sem=sem, recv_sem=sem, device_id=device, device_id_type=MESH).wait_send()


def greet(devices):
    barrier = pltpu.get_barrier_semaphore()
    for device in devices:
        pl.semaphore_signal(barrier, inc=1, device_id=device, device_id_type=MESH)
    pl.semaphore_wait(barrier, len(devices))


def mates():
    return [(a, k) for k in (0, 1, 3, 2) for a in (1, 0) if (a, k) != (0, 0)]


def mate(step, sign=1):
    d, c, z = place()
    a, k = step
    return d, (flip(c, 1) if a else c), lax.rem(z + sign * k + 4, 4)


def rank_of(device):
    return device[1] * 4 + device[2]


PIECES = 4


def total_kernel(part_ref, out_ref, sib_ref, base_ref, left_ref, right_ref, tor_ref, tol_ref, ss, sr, ls, lr, rs, rr, os_, or_):
    d, c, z = place()
    sib = (d, flip(c, 1), z)
    left = (d, c, lax.rem(z + 3, 4))
    right = (d, c, lax.rem(z + 1, 4))
    rows = part_ref.shape[0] // 2
    piece = rows // PIECES
    mine, theirs = c * rows, flip(c, 1) * rows
    barrier = pltpu.get_barrier_semaphore()
    pl.semaphore_signal(barrier, inc=1, device_id=sib, device_id_type=MESH)
    pl.semaphore_signal(barrier, inc=1, device_id=left, device_id_type=MESH)
    pl.semaphore_signal(barrier, inc=1, device_id=right, device_id_type=MESH)
    pl.semaphore_wait(barrier, 3)

    def cut(p):
        return pl.ds(p * piece, piece)

    def far(base, p):
        return pl.ds(pl.multiple_of(base + p * piece, 8), piece)

    for p in range(PIECES):
        put(part_ref.at[far(theirs, p)], sib_ref.at[cut(p)], ss.at[p], sr.at[p], sib)
    for p in range(PIECES):
        landed(sib_ref.at[cut(p)], sr.at[p], sib)
        base_ref[cut(p), :] = part_ref[far(mine, p), :] + sib_ref[cut(p), :]

        @pl.when(z == 0)
        def _():
            put(base_ref.at[cut(p)], left_ref.at[cut(p)], rs.at[p], lr.at[p], right)

        @pl.when(z == 3)
        def _():
            put(base_ref.at[cut(p)], right_ref.at[cut(p)], ls.at[p], rr.at[p], left)

    def from_left(p):
        landed(left_ref.at[cut(p)], lr.at[p], left)

        @pl.when(z < 3)
        def _():
            tor_ref[cut(p), :] = base_ref[cut(p), :] + left_ref[cut(p), :]
            put(tor_ref.at[cut(p)], left_ref.at[cut(p)], rs.at[p], lr.at[p], right)

    def from_right(p):
        landed(right_ref.at[cut(p)], rr.at[p], right)

        @pl.when(z > 0)
        def _():
            tol_ref[cut(p), :] = base_ref[cut(p), :] + right_ref[cut(p), :]
            put(tol_ref.at[cut(p)], right_ref.at[cut(p)], ls.at[p], rr.at[p], left)

    def finish(p):
        value = base_ref[cut(p), :]
        out_ref[far(mine, p), :] = value

        @pl.when(z > 0)
        def _():
            out_ref[far(mine, p), :] += left_ref[cut(p), :]

        @pl.when(z < 3)
        def _():
            out_ref[far(mine, p), :] += right_ref[cut(p), :]

        put(out_ref.at[far(mine, p)], out_ref.at[far(mine, p)], os_.at[p], or_.at[p], sib)

    @pl.when(z == 1)
    def _():
        for p in range(PIECES):
            from_left(p)

    @pl.when(z < 3)
    def _():
        for p in range(PIECES):
            from_right(p)

    @pl.when(z >= 2)
    def _():
        for p in range(PIECES):
            from_left(p)

    for p in range(PIECES):
        finish(p)
    for p in range(PIECES):
        landed(out_ref.at[far(theirs, p)], or_.at[p], sib)
        sent(out_ref.at[far(mine, p)], os_.at[p], sib)
        sent(part_ref.at[far(theirs, p)], ss.at[p], sib)

        @pl.when(z < 3)
        def _():
            sent(base_ref.at[cut(p)], rs.at[p], right)

        @pl.when(z > 0)
        def _():
            sent(base_ref.at[cut(p)], ls.at[p], left)


def group_total(part, which):
    rows = part.shape[0] // 2
    dma = lambda: pltpu.SemaphoreType.DMA((PIECES,))
    here = pl.BlockSpec(memory_space=pltpu.VMEM)
    return pl.pallas_call(
        total_kernel,
        out_shape=jax.ShapeDtypeStruct(part.shape, f32),
        in_specs=[here],
        out_specs=here,
        scratch_shapes=[pltpu.VMEM((rows, 128), f32)] * 6 + [dma() for _ in range(8)],
        compiler_params=pltpu.CompilerParams(collective_id=which, has_side_effects=True, vmem_limit_bytes=16 * 1024 * 1024),
    )(part)


def k1_kernel(tok_ref, up_ref, cols_ref, wout_ref, small_ref, meta_ref,
              xn_out, ups_ref, win_out, wouts_ref, smalls_ref, vecs_ref, gains_ref, masks_ref,
              u_ref, g_ref, v_ref, slope_ref, dl_ref, kq_ref,
              xs_ref, xn_ref, win_ref, metas_ref, part_ref, out_ref, sib_ref, base_ref, left_ref, right_ref, tor_ref, tol_ref,
              own_sem, ms, mr, qs, qr, xls, xlr, xrs, xrr, xcs, xcr, as_, ar, ps, pr, rs, rr, ws, wr, ts, tr, tls, tlr, trs, trr, tos, tor):
    d, c, z = place()
    j = c * 4 + z
    dx, dy, dd = flip(d, 1), flip(d, 2), flip(flip(d, 1), 2)
    xn, yn, dn = (dx, c, z), (dy, c, z), (dd, c, z)
    sib = (d, flip(c, 1), z)
    left = (d, c, lax.rem(z + 3, 4))
    right = (d, c, lax.rem(z + 1, 4))
    steps = mates()
    greet([mate(s) for s in steps] + [xn, yn, dn])
    length = tok_ref.shape[1]
    model = tok_ref.shape[2]
    depth = cols_ref.shape[1]
    tiles = u_ref.shape[0]
    width = tiles * 128
    count = g_ref.shape[1]

    def rows(rank):
        return pl.ds(pl.multiple_of(rank * length, length), length)

    def block(group, rank):
        return pl.ds(pl.multiple_of((group * 8 + rank) * depth, depth), depth)

    own_e = wout_ref.shape[0]

    def part_e(group, start=0, size=own_e):
        return pl.ds(pl.multiple_of(group * own_e + start, 16), size)

    own = [
        pltpu.make_async_copy(tok_ref.at[0], xs_ref.at[rows(j)], own_sem.at[0]),
        pltpu.make_async_copy(up_ref.at[0], ups_ref.at[rows(j)], own_sem.at[1]),
        pltpu.make_async_copy(cols_ref.at[j], win_ref.at[block(d, j)], own_sem.at[2]),
        pltpu.make_async_copy(wout_ref, wouts_ref.at[part_e(d)], own_sem.at[3]),
        pltpu.make_async_copy(small_ref, smalls_ref.at[part_e(d)], own_sem.at[4]),
        pltpu.make_async_copy(meta_ref, metas_ref.at[d, j], own_sem.at[5]),
    ]
    for copy in own:
        copy.start()
    pending = []
    for i, s in enumerate(steps):
        to = mate(s)
        pending.append(put(meta_ref, metas_ref.at[d, j], ms.at[i], mr.at[i], to))
    for i, s in enumerate(steps):
        to = mate(s)
        pending.append(put(cols_ref.at[rank_of(to)], win_ref.at[block(d, j)], as_.at[i], ar.at[i], to))
    for i, to in enumerate((xn, yn, dn)):
        pending.append(put(small_ref, smalls_ref.at[part_e(d)], ps.at[16 + i], pr.at[16 + i], to))
    own[2].wait()
    slot = win_ref.at[block(d, j)]
    pending.append(put(slot, slot, ps.at[7], pr.at[7], xn))
    pending.append(put(slot, slot, ps.at[15], pr.at[15], yn))

    def row_start(ref, out, base):
        pending.append(put(ref.at[0], out.at[rows(j)], xcs.at[base + z], xcr.at[base + z], sib))

        @pl.when(z < 3)
        def _():
            put(ref.at[0], out.at[rows(j)], xls.at[base], xlr.at[base], right)

        @pl.when(z > 0)
        def _():
            put(ref.at[0], out.at[rows(j)], xrs.at[base], xrr.at[base], left)

    def row_hop(out, base, i, then=None):
        @pl.when(z > i)
        def _():
            at = z - 1 - i
            slot = out.at[rows(c * 4 + at)]
            landed(slot, xlr.at[base + i], left)
            if i < 2:
                @pl.when(z < 3)
                def _():
                    put(slot, slot, xls.at[base + i + 1], xlr.at[base + i + 1], right)
            put(slot, slot, xcs.at[base + at], xcr.at[base + at], sib)
            if then is not None:
                then(c * 4 + at)

        @pl.when(z < 3 - i)
        def _():
            at = z + 1 + i
            slot = out.at[rows(c * 4 + at)]
            landed(slot, xrr.at[base + i], right)
            if i < 2:
                @pl.when(z > 0)
                def _():
                    put(slot, slot, xrs.at[base + i + 1], xrr.at[base + i + 1], left)
            put(slot, slot, xcs.at[base + at], xcr.at[base + at], sib)
            if then is not None:
                then(c * 4 + at)

    def row_end(out, base):
        for i in range(3):
            @pl.when((z < 3) & (z >= i))
            def _():
                sent(out.at[rows(j)], xls.at[base + i], right)

            @pl.when((z > 0) & (z <= 3 - i))
            def _():
                sent(out.at[rows(j)], xrs.at[base + i], left)
        for at in range(4):
            @pl.when(z != at)
            def _():
                sent(out.at[rows(j)], xcs.at[base + at], sib)

    row_start(tok_ref, xs_ref, 0)
    own[5].wait()
    for i, s in enumerate(steps):
        landed(metas_ref.at[d, rank_of(mate(s, -1))], mr.at[i], xn)
    for i, to in enumerate((xn, yn, dn)):
        pending.append(put(metas_ref.at[d], metas_ref.at[d], qs.at[i], qr.at[i], to))
    slots = {7: j}
    for i, s in enumerate(steps):
        slots[i] = rank_of(mate(s, -1))
    order = [7] + list(range(7))

    def pass_on(i):
        src = mate(steps[i], -1)
        slot = win_ref.at[block(d, slots[i])]
        landed(slot, ar.at[i], src)
        pending.append(put(slot, slot, ps.at[i], pr.at[i], xn))
        pending.append(put(slot, slot, ps.at[8 + i], pr.at[8 + i], yn))

    def relay(k):
        i = order[k]
        slot = win_ref.at[block(dx, slots[i])]
        landed(slot, pr.at[i], xn)
        if k % 2 == 0:
            pending.append(put(slot, slot, rs.at[k // 2], rr.at[k // 2], yn))
        slot = win_ref.at[block(dy, slots[i])]
        landed(slot, pr.at[8 + i], yn)
        if k % 2 == 1:
            pending.append(put(slot, slot, rs.at[4 + k // 2], rr.at[4 + k // 2], xn))

    pass_on(0)
    for i, (to, at) in enumerate(((xn, dx), (yn, dy), (dn, dd))):
        landed(metas_ref.at[at], qr.at[i], to)
    lens = jnp.concatenate([metas_ref[d, r, 1:2, :] for r in range(8)], axis=0)
    ends = []
    last = jnp.zeros((8, 1), f32)
    for i in range(5):
        last = last + lens[:, i:i + 1]
        ends.append(jnp.broadcast_to(last, (8, 128)))

    def mask_step(t, carry):
        here = t.astype(f32)

        def segment(at):
            total = jnp.zeros((8, 128), f32)
            for end in ends:
                total = total + jnp.where(end <= at, 1.0, 0.0)
            return total

        now = segment(here)
        r = pl.ds(pl.multiple_of(t * 8, 8), 8)
        for o in range(1, 4):
            same = jnp.where(segment(here - o) == now, 1.0, 0.0)
            masks_ref[o - 1, r, :] = jnp.where(here >= o, same, 0.0)
        masks_ref[3, r, :] = jnp.where(now < DOCS, 1.0, 0.0)
        return carry

    lax.fori_loop(0, length, mask_step, 0)
    lane = lax.broadcasted_iota(jnp.int32, (1, 128), 1)
    for group in range(4):
        for pair in range(4):
            at = group * 512 + pair * 128
            gains_ref[:, at:at + 128] = jnp.where(lane < depth, metas_ref[group, 2 * pair, 0:1, :], metas_ref[group, 2 * pair + 1, 0:1, :])
        vecs_ref[:, group * own_e:(group + 1) * own_e] = metas_ref[group, j, 8:16, :]

    def normalize(rank):
        def body(i, carry):
            r = pl.ds(pl.multiple_of(rank * length + i * 16, 16), 16)
            x = xs_ref[r, :].astype(f32)
            scale = lax.rsqrt(jnp.sum(x * x, axis=1, keepdims=True) * (1.0 / model) + EPS)
            xn_ref[r, :] = (x * scale * gains_ref[...]).astype(bf16)
            return carry

        lax.fori_loop(0, length // 16, body, 0)

    for i in range(1, 7):
        pass_on(i)
    own[0].wait()
    normalize(j)
    row_hop(xs_ref, 0, 0, normalize)
    row_start(up_ref, ups_ref, 4)
    halves = own_e // 2
    pending.append(put(wout_ref, wouts_ref.at[part_e(d)], ws.at[0], wr.at[0], xn))
    pending.append(put(wout_ref, wouts_ref.at[part_e(d)], ws.at[1], wr.at[1], yn))
    for k in range(4):
        relay(k)
    row_hop(xs_ref, 0, 1, normalize)
    for k in range(4, 8):
        relay(k)
    row_hop(xs_ref, 0, 2, normalize)
    for at in range(4):
        rank = flip(c, 1) * 4 + at
        landed(xs_ref.at[rows(rank)], xcr.at[at], sib)
        normalize(rank)
    for k, i in enumerate(order):
        slot = win_ref.at[block(dd, slots[i])]
        if k % 2 == 0:
            landed(slot, rr.at[k // 2], yn)
        else:
            landed(slot, rr.at[4 + k // 2], xn)
    own += [pltpu.make_async_copy(xn_ref, xn_out, own_sem.at[6]), pltpu.make_async_copy(win_ref, win_out, own_sem.at[7])]
    own[6].start()
    own[7].start()
    row_hop(ups_ref, 4, 0)
    lead = u_ref.shape[1] - count
    u_ref[:, 0:lead, :] = jnp.zeros((tiles, lead, 128), f32)

    tile = 256

    def spread(out, first, start):
        def body(i, carry):
            product = jnp.dot(xn_ref[...], win_ref[:, pl.ds(pl.multiple_of(start + i * tile, tile), tile)], preferred_element_type=f32)
            for r in range(8):
                for part in range(0, tile, 128):
                    out[i * (tile // 128) + part // 128, pl.ds(first + r, length, stride=8), :] = product[r * length:(r + 1) * length, part:part + 128]
            return carry

        lax.fori_loop(0, width // tile, body, 0)

    spread(u_ref, lead, 0)
    taps = [vecs_ref[o:o + 1, :] for o in range(4)]
    bias = vecs_ref[4:5, :]

    def conv_step(i, carry):
        r = pl.ds(pl.multiple_of(i * 32, 32), 32)
        for n in range(tiles):
            lanes = slice(n * 128, n * 128 + 128)
            total = bias[:, lanes] + taps[3][:, lanes] * u_ref[n, pl.ds(pl.multiple_of(lead + i * 32, 8), 32), :]
            for o in range(1, 4):
                total = total + taps[3 - o][:, lanes] * (u_ref[n, pl.ds(pl.multiple_of(lead + i * 32 - 8 * o, 8), 32), :] * masks_ref[o - 1, r, :])
            sig = jax.nn.sigmoid(total)
            v_ref[n, r, :] = (total * sig).astype(bf16).astype(f32)
            slope_ref[n, r, :] = sig * (1.0 + total * (1.0 - sig))
        return carry

    lax.fori_loop(0, count // 32, conv_step, 0)
    for copy in own[3:5]:
        copy.wait()
    for i, (to, at) in enumerate(((xn, dx), (yn, dy), (dn, dd))):
        landed(smalls_ref.at[part_e(at)], pr.at[16 + i], to)
    quarter = count // 4
    narrow = smalls_ref[:, 128:256].astype(f32)
    packed = jnp.zeros((quarter, 128), f32)
    for b in range(4):
        r = slice(b * quarter, (b + 1) * quarter)
        values = jnp.concatenate([v_ref[n, r, :].astype(bf16) for n in range(tiles)], axis=1)
        part_ref[r, :] = jnp.dot(values, smalls_ref[:, 0:128], preferred_element_type=f32)
        turned = pltpu.roll(narrow, 32 * b, 1) if b else narrow
        packed = packed + jnp.dot(values, turned.astype(bf16), preferred_element_type=f32)
    part_ref[count:count + quarter, :] = packed
    slot = wouts_ref.at[part_e(dx)]
    landed(slot, wr.at[0], xn)
    slot = wouts_ref.at[part_e(dx, 0, halves)]
    pending.append(put(slot, slot, ws.at[2], wr.at[2], yn))
    slot = wouts_ref.at[part_e(dy)]
    landed(slot, wr.at[1], yn)
    slot = wouts_ref.at[part_e(dy, halves, halves)]
    pending.append(put(slot, slot, ws.at[3], wr.at[3], xn))

    def between():
        spread(g_ref, 0, width)
        row_hop(ups_ref, 4, 1)

    line_total(part_ref, out_ref, sib_ref, base_ref, left_ref, right_ref, tor_ref, tol_ref, ts, tr, tls, tlr, trs, trr, tos, tor, between)
    dl_ref[...] = out_ref[0:count, :].astype(bf16)
    for b in range(4):
        packed = out_ref[count:count + quarter, :]
        kq_ref[b * quarter:(b + 1) * quarter, :] = pltpu.roll(packed, 128 - 32 * b, 1) if b else packed
    row_hop(ups_ref, 4, 2)
    for at in range(4):
        landed(ups_ref.at[rows(flip(c, 1) * 4 + at)], xcr.at[4 + at], sib)
    landed(wouts_ref.at[part_e(dd, 0, halves)], wr.at[2], yn)
    landed(wouts_ref.at[part_e(dd, halves, halves)], wr.at[3], xn)
    row_end(xs_ref, 0)
    row_end(ups_ref, 4)
    own[1].wait()
    own[6].wait()
    own[7].wait()
    for copy in pending:
        copy.wait_send()


def line_total(part_ref, out_ref, sib_ref, base_ref, left_ref, right_ref, tor_ref, tol_ref, ss, sr, ls, lr, rs, rr, os_, or_, between):
    d, c, z = place()
    sib = (d, flip(c, 1), z)
    left = (d, c, lax.rem(z + 3, 4))
    right = (d, c, lax.rem(z + 1, 4))
    rows = part_ref.shape[0] // 2
    piece = rows // PIECES
    mine, theirs = c * rows, flip(c, 1) * rows

    def cut(p):
        return pl.ds(p * piece, piece)

    def far(base, p):
        return pl.ds(pl.multiple_of(base + p * piece, 8), piece)

    for p in range(PIECES):
        put(part_ref.at[far(theirs, p)], sib_ref.at[cut(p)], ss.at[p], sr.at[p], sib)
    for p in range(PIECES):
        landed(sib_ref.at[cut(p)], sr.at[p], sib)
        base_ref[cut(p), :] = part_ref[far(mine, p), :] + sib_ref[cut(p), :]

        @pl.when(z == 0)
        def _():
            put(base_ref.at[cut(p)], left_ref.at[cut(p)], rs.at[p], lr.at[p], right)

        @pl.when(z == 3)
        def _():
            put(base_ref.at[cut(p)], right_ref.at[cut(p)], ls.at[p], rr.at[p], left)

    def from_left(p):
        landed(left_ref.at[cut(p)], lr.at[p], left)

        @pl.when(z < 3)
        def _():
            tor_ref[cut(p), :] = base_ref[cut(p), :] + left_ref[cut(p), :]
            put(tor_ref.at[cut(p)], left_ref.at[cut(p)], rs.at[p], lr.at[p], right)

    def from_right(p):
        landed(right_ref.at[cut(p)], rr.at[p], right)

        @pl.when(z > 0)
        def _():
            tol_ref[cut(p), :] = base_ref[cut(p), :] + right_ref[cut(p), :]
            put(tol_ref.at[cut(p)], right_ref.at[cut(p)], ls.at[p], rr.at[p], left)

    @pl.when(z == 1)
    def _():
        for p in range(PIECES):
            from_left(p)

    @pl.when(z == 2)
    def _():
        for p in range(PIECES):
            from_right(p)

    if between is not None:
        between()

    @pl.when(z < 2)
    def _():
        for p in range(PIECES):
            from_right(p)

    @pl.when(z >= 2)
    def _():
        for p in range(PIECES):
            from_left(p)

    for p in range(PIECES):
        out_ref[far(mine, p), :] = base_ref[cut(p), :]

        @pl.when(z > 0)
        def _():
            out_ref[far(mine, p), :] += left_ref[cut(p), :]

        @pl.when(z < 3)
        def _():
            out_ref[far(mine, p), :] += right_ref[cut(p), :]

        put(out_ref.at[far(mine, p)], out_ref.at[far(mine, p)], os_.at[p], or_.at[p], sib)
    for p in range(PIECES):
        landed(out_ref.at[far(theirs, p)], or_.at[p], sib)
        sent(out_ref.at[far(mine, p)], os_.at[p], sib)
        sent(part_ref.at[far(theirs, p)], ss.at[p], sib)

        @pl.when(z < 3)
        def _():
            sent(base_ref.at[cut(p)], rs.at[p], right)

        @pl.when(z > 0)
        def _():
            sent(base_ref.at[cut(p)], ls.at[p], left)


def k1(tokens, upstream, cols, w_out, small, meta):
    groups, ways = 4, cols.shape[0]
    like = jax.ShapeDtypeStruct
    length, model = tokens.shape[1:]
    count = ways * length
    channels = groups * w_out.shape[0]
    dma = lambda n: pltpu.SemaphoreType.DMA((n,))
    some = pl.BlockSpec(memory_space=pl.ANY)
    far = pl.BlockSpec(memory_space=pltpu.HBM)
    here = pl.BlockSpec(memory_space=pltpu.VMEM)
    packed = count + count // 4
    return pl.pallas_call(
        k1_kernel,
        out_shape=(
            like((count, model), bf16),
            like((count, model), bf16),
            like((groups * ways * cols.shape[1], cols.shape[2]), bf16),
            like((channels, model), bf16),
            like((channels, small.shape[1]), bf16),
            like((8, channels), f32),
            like((1, model), f32),
            like((4, count, 128), f32),
            like((channels // 128, count + 24, 128), f32),
            like((channels // 128, count, 128), f32),
            like((channels // 128, count, 128), f32),
            like((channels // 128, count, 128), f32),
            like((count, 128), bf16),
            like((count, 128), f32),
        ),
        in_specs=[some] * 6,
        out_specs=(far,) * 4 + (here,) * 10,
        scratch_shapes=[
            pltpu.VMEM((count, model), bf16),
            pltpu.VMEM((count, model), bf16),
            pltpu.VMEM((groups * ways * cols.shape[1], cols.shape[2]), bf16),
            pltpu.VMEM((groups, ways) + meta.shape, f32),
            pltpu.VMEM((packed, 128), f32),
            pltpu.VMEM((packed, 128), f32),
        ] + [pltpu.VMEM((packed // 2, 128), f32)] * 6
        + [dma(8), dma(7), dma(7), dma(3), dma(3), dma(8), dma(8), dma(8), dma(8), dma(8), dma(8), dma(7), dma(7), dma(19), dma(19), dma(8), dma(8), dma(4), dma(4)]
        + [dma(PIECES) for _ in range(8)],
        compiler_params=pltpu.CompilerParams(collective_id=0, has_side_effects=True, vmem_limit_bytes=56 * 1024 * 1024),
    )(tokens, upstream, cols, w_out, small, meta)


GROUP = 4


def k2_kernel(states, dl_ref, kq_ref, wdt_ref, vecs_ref, keep_ref, live_ref, v_ref, g_ref, ups_ref, wout_ref,
              m_ref, dg_ref, dpre_ref, dv_ref, part_ref, stat_ref,
              s_ref, h_ref, rate_ref, w_ref, y_ref, dm_ref, kb_ref, hot_ref, drr_ref):
    tiles, count = v_ref.shape[:2]
    steps = count // 8
    wide = states * 128
    chunk = 256
    first = pl.program_id(0) == 0
    half = pl.program_id(0)
    both = range(tiles)
    rank = wdt_ref.shape[1]

    @pl.when(first)
    def _():
        row = lax.broadcasted_iota(jnp.int32, (128, 512), 0)
        col = lax.broadcasted_iota(jnp.int32, (128, 512), 1) // 128
        for part in range(0, 2 * wide, 512):
            hot_ref[:, part:part + 512] = jnp.where((row % 32 == col + part // 128) & (row < 96), 1.0, 0.0).astype(bf16)

    lane = lax.broadcasted_iota(jnp.int32, (chunk, 128), 1)

    def spread(i, carry):
        r = pl.ds(pl.multiple_of(i * chunk, chunk), chunk)
        value = jnp.where(lane < 2 * states, kq_ref[r, :], 0.0)
        hi = value.astype(bf16).astype(f32)
        mid = (value - hi).astype(bf16).astype(f32)
        low = value - hi - mid
        left = (hi + pltpu.roll(mid, 32, 1) + pltpu.roll(low, 64, 1)).astype(bf16)
        for part in range(0, 2 * wide, 512):
            kb_ref[r, part:part + 512] = jnp.dot(left, hot_ref[:, part:part + 512], preferred_element_type=f32)
        return carry

    lax.fori_loop(0, count // chunk, spread, 0)
    cols = (((1,), (1,)), ((), ()))
    length = count // 8

    def gate_step(i, carry):
        r = pl.ds(pl.multiple_of(i * chunk, chunk), chunk)
        product = lax.dot_general(ups_ref[r, :], wout_ref[...], cols, preferred_element_type=f32)
        for j in range(chunk // length):
            for n in both:
                dm_ref[n, pl.ds(i * (chunk // length) + j, length, stride=8), :] = product[j * length:(j + 1) * length, n * 128:(n + 1) * 128]
        return carry

    lax.fori_loop(0, count // chunk, gate_step, 0)
    bias = vecs_ref[5:6, :]
    skip = vecs_ref[6:7, :]
    tile_of = lambda x, n: x[:, n * 128:(n + 1) * 128]
    ks = lax.broadcasted_iota(jnp.int32, (128, 128), 1)

    def before(i, carry):
        seen = list(carry)
        r = pl.ds(pl.multiple_of(i * 128, 128), 128)
        live = live_ref[0, r, :]
        k = jnp.where(ks < states, kq_ref[r, :], 0.0)
        sk = jnp.sum(k * k, axis=1, keepdims=True)
        pre = lax.dot_general(dl_ref[r, :], wdt_ref[...], cols, preferred_element_type=f32) + bias
        for n in both:
            beta = jax.nn.sigmoid(tile_of(pre, n))
            part = 1.0 / (1.0 + beta * sk)
            rate_ref[n, r, :] = beta * part
            w_ref[n, r, :] = part * part * beta * (1.0 - beta)
            g = g_ref[n, r, :]
            sg = jax.nn.sigmoid(g)
            dm = dm_ref[n, r, :] * live
            dv_ref[n, r, :] = dm * (g * sg)
            dm_ref[n, r, :] = dm * (sg * (1.0 + g * (1.0 - sg)))
            shown = (beta * live).reshape(16, 8, 128)
            seen[n] = seen[n] + jnp.sum(shown, axis=0)
            seen[tiles + n] = jnp.maximum(seen[tiles + n], jnp.max(shown, axis=0))
        return tuple(seen)

    blank = jnp.zeros((8, 128), f32)
    seen = lax.fori_loop(0, count // 128, before, (blank,) * (2 * tiles))
    s_ref[0, 0] = jnp.zeros(s_ref.shape[2:], f32)
    span = GROUP * 8
    at = [slice(j * 8, j * 8 + 8) for j in range(GROUP)]

    def view(ref, i):
        r = pl.ds(pl.multiple_of(i * span, span), span)
        return ref.at[:, r] if len(ref.shape) == 3 else ref.at[r]

    def pair(ref, r):
        return jnp.concatenate([ref[n, r, :] for n in both], axis=1)

    def keep_pair(ref, r, value):
        for n in both:
            ref[n, r, :] = tile_of(value, n)

    tile = lambda x: jnp.concatenate([x] * tiles, axis=1)

    def fold(x):
        total = tile_of(x, 0)
        for n in range(1, tiles):
            total = total + tile_of(x, n)
        return total

    def forward(i, carry):
        keeps, rates, vs, kbs, ys = [view(x, i) for x in (keep_ref, rate_ref, v_ref, kb_ref, y_ref)]
        keep = [keeps[0, r, :] for r in at]
        rate = [pair(rates, r) for r in at]
        value = [pair(vs, r) for r in at]
        rv = [a * b for a, b in zip(rate, value)]
        y = [skip * b for b in value]
        for n in range(states):
            state = s_ref[i, 0, n]
            for j, r in enumerate(at):
                kb = kbs[r, n * 128:(n + 1) * 128]
                qb = kbs[r, wide + n * 128:wide + (n + 1) * 128]
                state = (tile(keep[j]) - rate[j] * tile(kb * kb * keep[j])) * state + rv[j] * tile(kb)
                if j < GROUP - 1:
                    s_ref[i, j + 1, n] = state
                else:
                    s_ref[i + 1, 0, n] = state
                y[j] = y[j] + state * tile(qb)
        for j, r in enumerate(at):
            keep_pair(ys, r, y[j])
        return carry

    lax.fori_loop(0, steps // GROUP, forward, 0)
    h_ref[...] = jnp.zeros_like(h_ref)

    def backward(step, carry):
        i = steps // GROUP - 1 - step
        keeps, rates, vs, kbs, dvs, ws, drrs = [view(x, i) for x in (keep_ref, rate_ref, v_ref, kb_ref, dv_ref, w_ref, drr_ref)]
        keep = [keeps[0, r, :] for r in at]
        rate = [pair(rates, r) for r in at]
        value = [pair(vs, r) for r in at]
        rv = [a * b for a, b in zip(rate, value)]
        dy = [pair(dvs, r) for r in at]
        hk = [jnp.zeros((8, tiles * 128), f32) for r in at]
        hs2 = [jnp.zeros((8, tiles * 128), f32) for r in at]
        for n in range(states):
            ah = h_ref[n]
            later = s_ref[i + 1, 0, n]
            for j in range(GROUP - 1, -1, -1):
                r = at[j]
                kb = kbs[r, n * 128:(n + 1) * 128]
                qb = kbs[r, wide + n * 128:wide + (n + 1) * 128]
                kk = kb * keep[j]
                held = tile(kb * kk)
                h = dy[j] * tile(qb) + ah
                prior = s_ref[i, j, n]
                hs = h * prior
                hk[j] = hk[j] + h * tile(kb)
                hs2[j] = hs2[j] + hs * held
                kbs[r, n * 128:(n + 1) * 128] = fold(h * rv[j]) - 2.0 * kk * fold(hs * rate[j])
                kbs[r, wide + n * 128:wide + (n + 1) * 128] = fold(dy[j] * later)
                later = prior
                ah = (tile(keep[j]) - rate[j] * held) * h
            h_ref[n] = ah
        dskip = carry
        for j, r in enumerate(at):
            drate = value[j] * hk[j] - hs2[j]
            drrs[r, :] = fold(drate * rate[j] * rate[j]) * (-2.0)
            keep_pair(ws, r, drate * pair(ws, r))
            keep_pair(dvs, r, rate[j] * hk[j] + skip * dy[j])
            dskip = dskip + dy[j] * value[j]
        return dskip

    dskip = lax.fori_loop(0, steps // GROUP, backward, jnp.zeros((8, tiles * 128), f32))

    quarter = count // 4
    packed = jnp.zeros((quarter, 128), f32)
    for b in range(4):
        r = slice(b * quarter, (b + 1) * quarter)
        total = jnp.zeros((quarter, 128), f32)
        for part in range(0, 2 * wide, 512):
            total = total + lax.dot_general(kb_ref[r, part:part + 512].astype(bf16), hot_ref[:, part:part + 512], cols, preferred_element_type=f32)
        drr = jnp.sum(drr_ref[r, :], axis=1, keepdims=True)
        k = kq_ref[r, :]
        low = lax.broadcasted_iota(jnp.int32, (quarter, 128), 1)
        total = jnp.where(low < 2 * states, total, 0.0) + jnp.where(low < states, k * drr, 0.0)
        packed = packed + (pltpu.roll(total, 32 * b, 1) if b else total)

    tail = pl.ds(count, quarter)
    part_ref[tail, :] = jnp.where(first, packed, part_ref[tail, :] + packed)

    def after(i, carry):
        r = pl.ds(pl.multiple_of(i * 128, 128), 128)
        live = live_ref[0, r, :]
        sums = list(carry)
        for n in both:
            y = y_ref[n, r, :]
            g = g_ref[n, r, :]
            y_ref[n, r, :] = y * (g * jax.nn.sigmoid(g)) * live
            dm_ref[n, r, :] = y * dm_ref[n, r, :]
            low = w_ref[n, r, :].astype(bf16)
            dpre_ref[r, n * 128:(n + 1) * 128] = low
            sums[n] = sums[n] + jnp.sum(low.astype(f32).reshape(16, 8, 128), axis=0)
        ddl = jnp.dot(dpre_ref[r, :], wdt_ref[...], preferred_element_type=f32)
        part_ref[r, :] = jnp.where(first, ddl, part_ref[r, :] + ddl)
        return tuple(sums)

    sums = lax.fori_loop(0, count // 128, after, (blank,) * tiles)

    def by_row(j, carry):
        r = pl.ds(pl.multiple_of(j * length, length), length)
        for n in both:
            m_ref[r, n * 128:(n + 1) * 128] = y_ref[n, pl.ds(j, length, stride=8), :].astype(bf16)
            dg_ref[r, n * 128:(n + 1) * 128] = dm_ref[n, pl.ds(j, length, stride=8), :].astype(bf16)
        return carry

    lax.fori_loop(0, 8, by_row, 0)
    stat_ref[...] = jnp.zeros_like(stat_ref)
    for n in both:
        lanes = slice(n * 128, (n + 1) * 128)
        stat_ref[0:1, lanes] = jnp.sum(seen[n], axis=0, keepdims=True)
        stat_ref[1:2, lanes] = jnp.max(seen[tiles + n], axis=0, keepdims=True)
        stat_ref[5:6, lanes] = jnp.sum(sums[n], axis=0, keepdims=True)
        stat_ref[6:7, lanes] = jnp.sum(tile_of(dskip, n), axis=0, keepdims=True)


def k2(dl, kq, smalls, vecs, masks, v, g, ups, wout, states):
    count, rank = dl.shape
    channels, model = wout.shape
    tiles = 2
    width = tiles * 128
    like = jax.ShapeDtypeStruct
    once = pl.Buffered(buffer_count=1)
    whole = lambda a: pl.BlockSpec(a.shape, lambda h: (0,) * a.ndim, pipeline_mode=once)
    deep = pl.BlockSpec((tiles, count, 128), lambda h: (h, 0, 0))
    flat = pl.BlockSpec((count, width), lambda h: (0, h))
    return pl.pallas_call(
        functools.partial(k2_kernel, states),
        grid=(channels // width,),
        out_shape=(
            like((count, channels), bf16),
            like((count, channels), bf16),
            like((count, channels), bf16),
            like(v.shape, f32),
            like((count + count // 4, 128), f32),
            like((8, channels), f32),
        ),
        in_specs=[
            whole(dl), whole(kq),
            pl.BlockSpec((width, 128), lambda h: (h, 2)),
            pl.BlockSpec((8, width), lambda h: (0, h)),
            pl.BlockSpec((1, count, 128), lambda h: (0, 0, 0), pipeline_mode=once),
            pl.BlockSpec((1, count, 128), lambda h: (3, 0, 0), pipeline_mode=once),
            deep, deep, whole(ups),
            pl.BlockSpec((width, model), lambda h: (h, 0)),
        ],
        out_specs=(flat, flat, flat, deep, pl.BlockSpec((count + count // 4, 128), lambda h: (0, 0)), pl.BlockSpec((8, width), lambda h: (0, h))),
        scratch_shapes=[
            pltpu.VMEM((count // 8 // GROUP + 1, GROUP, states, 8, width), f32),
            pltpu.VMEM((states, 8, width), f32),
        ] + [pltpu.VMEM((tiles, count, 128), f32)] * 4
        + [pltpu.VMEM((count, 2 * states * 128), f32), pltpu.VMEM((128, 2 * states * 128), bf16), pltpu.VMEM((count, 128), f32)],
        compiler_params=pltpu.CompilerParams(vmem_limit_bytes=60 * 1024 * 1024),
    )(dl, kq, smalls, vecs, masks, masks, v, g, ups, wout)


def add_rows(dst, sources):
    rows = dst.shape[0]
    step = 16

    def body(i, carry):
        r = pl.ds(pl.multiple_of(i * step, step), step)
        value = sources[0][r, :].astype(f32)
        for more in sources[1:]:
            value = value + more[r, :].astype(f32)
        dst[r, :] = value.astype(dst.dtype)
        return carry

    lax.fori_loop(0, rows // step, body, 0)


class Line:
    def __init__(self, part, out, sib, send, left, right, sems):
        self.part, self.out, self.sib, self.send, self.left, self.right = part, out, sib, send, left, right
        self.ss, self.sr, self.gs, self.lr, self.rr = sems
        d, c, z = place()
        self.c = c
        self.other = (d, flip(c, 1), z)
        self.to_left = (d, c, lax.rem(z + 3, 4))
        self.to_right = (d, c, lax.rem(z + 1, 4))

    def start(self):
        for zp in (3, 0, 2, 1):
            put(self.part.at[flip(self.c, 1), zp], self.sib.at[zp], self.ss.at[zp], self.sr.at[zp], self.other)

    def step(self, zs, k):
        for zp in range(4):
            if zp > zs and k == 3 - zp + zs:
                landed(self.sib.at[zp], self.sr.at[zp], self.other)
                terms = [self.part.at[self.c, zp], self.sib.at[zp]]
                if zs > 0:
                    landed(self.left.at[zp], self.lr.at[zp], self.to_left)
                    terms.append(self.left.at[zp])
                add_rows(self.send.at[zp], terms)
                put(self.send.at[zp], self.left.at[zp], self.gs.at[zp], self.lr.at[zp], self.to_right)
            if zp < zs and k == zp + 3 - zs:
                landed(self.sib.at[zp], self.sr.at[zp], self.other)
                terms = [self.part.at[self.c, zp], self.sib.at[zp]]
                if zs < 3:
                    landed(self.right.at[zp], self.rr.at[zp], self.to_right)
                    terms.append(self.right.at[zp])
                add_rows(self.send.at[zp], terms)
                put(self.send.at[zp], self.right.at[zp], self.gs.at[zp], self.rr.at[zp], self.to_left)

    def finish(self, zs):
        landed(self.sib.at[zs], self.sr.at[zs], self.other)
        terms = [self.part.at[self.c, zs], self.sib.at[zs]]
        if zs > 0:
            landed(self.left.at[zs], self.lr.at[zs], self.to_left)
            terms.append(self.left.at[zs])
        if zs < 3:
            landed(self.right.at[zs], self.rr.at[zs], self.to_right)
            terms.append(self.right.at[zs])
        add_rows(self.out, terms)

    def close(self, zs):
        for zp in range(4):
            sent(self.sib.at[zp], self.ss.at[zp], self.other)
            if zp != zs:
                sent(self.send.at[zp], self.gs.at[zp], self.other)


class Plane:
    def __init__(self, part, out, xa, yb, sx, sy, rx, ry, sems):
        self.part, self.out, self.xa, self.yb, self.sx, self.sy, self.rx, self.ry = part, out, xa, yb, sx, sy, rx, ry
        self.ss, self.rs = sems
        d, c, z = place()
        self.d, self.dx, self.dy, self.dd = d, flip(d, 1), flip(d, 2), flip(flip(d, 1), 2)
        self.xn, self.yn = (self.dx, c, z), (self.dy, c, z)
        half = part.shape[1] // 2
        self.a, self.b = pl.ds(0, half), pl.ds(half, half)

    def start(self):
        p = self.part
        self.sends = [
            put(p.at[self.dd, self.a], self.xa, self.ss.at[0], self.rs.at[0], self.xn),
            put(p.at[self.dd, self.b], self.yb, self.ss.at[1], self.rs.at[1], self.yn),
            put(p.at[self.dx, self.a], self.rx.at[self.a], self.ss.at[2], self.rs.at[2], self.xn),
            put(p.at[self.dy, self.b], self.ry.at[self.b], self.ss.at[3], self.rs.at[3], self.yn),
        ]

    def middle(self):
        p = self.part
        landed(self.xa, self.rs.at[0], self.xn)
        add_rows(self.sy, [p.at[self.dy, self.a], self.xa])
        self.sends.append(put(self.sy, self.ry.at[self.a], self.ss.at[4], self.rs.at[4], self.yn))
        landed(self.yb, self.rs.at[1], self.yn)
        add_rows(self.sx, [p.at[self.dx, self.b], self.yb])
        self.sends.append(put(self.sx, self.rx.at[self.b], self.ss.at[5], self.rs.at[5], self.xn))

    def finish(self):
        landed(self.rx.at[self.a], self.rs.at[2], self.xn)
        landed(self.ry.at[self.b], self.rs.at[3], self.yn)
        landed(self.ry.at[self.a], self.rs.at[4], self.yn)
        landed(self.rx.at[self.b], self.rs.at[5], self.xn)
        add_rows(self.out, [self.part.at[self.d], self.rx, self.ry])

    def close(self):
        for copy in self.sends:
            copy.wait_send()


def plane_scratch(rows, columns, dtype):
    half = pltpu.VMEM((rows // 2, columns), dtype)
    full = pltpu.VMEM((rows, columns), dtype)
    return [half, half, half, half, full, full, pltpu.SemaphoreType.DMA((6,)), pltpu.SemaphoreType.DMA((6,))]


def line_scratch(rows, columns, dtype):
    four = pltpu.VMEM((4, rows, columns), dtype)
    return [four] * 4 + [pltpu.SemaphoreType.DMA((4,))] * 5


def back_kernel(dxn_ref, outp_ref, gwin_ref, gwout_ref, small_ref,
                dxns_ref, outs_ref, gwins_ref, gwouts_ref, smalls_ref, *scratch):
    lines = [Line(dxn_ref, dxns_ref, *scratch[0:4], scratch[4:9]), Line(outp_ref, outs_ref, *scratch[9:13], scratch[13:18])]
    scratch = scratch[18:]
    fin, own, as_, ar = scratch[:4]
    scratch = scratch[4:]
    planes = []
    for part, out in ((gwin_ref, fin), (gwout_ref, gwouts_ref), (small_ref, smalls_ref)):
        planes.append(Plane(part, out, *scratch[:6], scratch[6:8]))
        scratch = scratch[8:]
    d, c, z = place()
    j = c * 4 + z
    steps = mates()
    greet([mate(s) for s in steps] + [planes[0].xn, planes[0].yn])
    lines[0].start()
    planes[0].start()
    lines[1].start()

    def along(line, k):
        for zs in range(4):
            @pl.when(z == zs)
            def _():
                if k < 3:
                    line.step(zs, k)
                else:
                    line.finish(zs)
                    line.close(zs)

    along(lines[0], 0)
    along(lines[1], 0)
    planes[1].start()
    planes[2].start()
    along(lines[0], 1)
    planes[0].middle()
    along(lines[0], 2)
    planes[0].finish()
    block = fin.shape[0] // 8
    def rows_of(rank):
        return fin.at[pl.ds(pl.multiple_of(rank * block, 16), block)]
    keep = pltpu.make_async_copy(rows_of(j), gwins_ref.at[j], own)
    keep.start()
    pending = []
    for i, s in enumerate(steps):
        to = mate(s)
        pending.append(put(rows_of(rank_of(to)), gwins_ref.at[j], as_.at[i], ar.at[i], to))
    along(lines[0], 3)
    planes[1].middle()
    planes[2].middle()
    along(lines[1], 1)
    planes[1].finish()
    planes[2].finish()
    along(lines[1], 2)
    for i, s in enumerate(steps):
        src = mate(s, -1)
        landed(gwins_ref.at[rank_of(src)], ar.at[i], src)
    along(lines[1], 3)
    keep.wait()
    for copy in pending:
        copy.wait_send()
    for plane in planes:
        plane.close()


def back(dxn, outp, gwin, gwout, small):
    like = jax.ShapeDtypeStruct
    here = pl.BlockSpec(memory_space=pltpu.VMEM)
    rows, columns = dxn.shape[2:]
    return pl.pallas_call(
        back_kernel,
        out_shape=(
            like((rows, columns), f32),
            like((rows, columns), f32),
            like((8, gwin.shape[1] // 8, gwin.shape[2]), bf16),
            like(gwout.shape[1:], f32),
            like(small.shape[1:], f32),
        ),
        in_specs=[here] * 5,
        out_specs=(here,) * 5,
        scratch_shapes=line_scratch(rows, columns, bf16) + line_scratch(rows, columns, bf16)
        + [pltpu.VMEM(gwin.shape[1:], bf16), pltpu.SemaphoreType.DMA(()), pltpu.SemaphoreType.DMA((7,)), pltpu.SemaphoreType.DMA((7,))]
        + plane_scratch(*gwin.shape[1:], bf16) + plane_scratch(*gwout.shape[1:], bf16) + plane_scratch(*small.shape[1:], f32),
        compiler_params=pltpu.CompilerParams(collective_id=3, has_side_effects=True, vmem_limit_bytes=60 * 1024 * 1024),
    )(dxn, outp, gwin, gwout, small)


def tiny_kernel(part_ref, out_ref, near_ref, sum_ref, far_ref, ns, nr, fs, fr):
    d, c, z = place()
    j = c * 4 + z
    steps = mates()
    planes = [(flip(d, 1), c, z), (flip(d, 2), c, z), (flip(flip(d, 1), 2), c, z)]
    greet([mate(s) for s in steps] + planes)
    for i, s in enumerate(steps):
        to = mate(s)
        put(part_ref.at[rank_of(to)], near_ref.at[i], ns.at[i], nr.at[i], to)
    row = lax.broadcasted_iota(jnp.int32, (8, 128), 0)
    lane = lax.broadcasted_iota(jnp.int32, (8, 128), 1)
    peak = (row == 4) & (lane == 1)

    def join(a, b):
        return jnp.where(peak, jnp.maximum(a, b), a + b)

    value = part_ref[j]
    for i, s in enumerate(steps):
        landed(near_ref.at[i], nr.at[i], mate(s, -1))
        value = join(value, near_ref[i])
    sum_ref[...] = value
    for i, to in enumerate(planes):
        put(sum_ref, far_ref.at[i], fs.at[i], fr.at[i], to)
    for i, to in enumerate(planes):
        landed(far_ref.at[i], fr.at[i], to)
        value = join(value, far_ref[i])
    out_ref[...] = value
    for i, to in enumerate(planes):
        sent(sum_ref, fs.at[i], to)
    for i, s in enumerate(steps):
        sent(near_ref.at[i], ns.at[i], mate(s))


def tiny(part):
    here = pl.BlockSpec(memory_space=pltpu.VMEM)
    dma = lambda n: pltpu.SemaphoreType.DMA((n,))
    return pl.pallas_call(
        tiny_kernel,
        out_shape=jax.ShapeDtypeStruct((8, 128), f32),
        in_specs=[here],
        out_specs=here,
        scratch_shapes=[pltpu.VMEM((7, 8, 128), f32), pltpu.VMEM((8, 128), f32), pltpu.VMEM((3, 8, 128), f32), dma(7), dma(7), dma(3), dma(3)],
        compiler_params=pltpu.CompilerParams(collective_id=4, has_side_effects=True),
    )(part)

def masks(lengths, count):
    ends = jnp.cumsum(lengths, axis=1)
    places = jnp.arange(count, dtype=jnp.int32)
    segment = jnp.sum((places[:, None, None] >= ends[None, :, :]).astype(jnp.int32), axis=2)
    same = []
    for offset in range(1, 4):
        before = jnp.pad(segment, ((offset, 0), (0, 0)), constant_values=-1)[:count]
        same.append((before == segment).astype(f32))
    return same, (segment < DOCS).astype(f32)


def columns(weights, ways):
    rows, total = weights.shape
    return weights.reshape(rows, 2, total // (2 * ways * 128), ways, 128)


def on_device(tokens, lengths, gain, w_in, conv_w, conv_b, w_x, w_dt, dt_bias, skip, w_out, grad_out):
    ways = lax.axis_size("core") * lax.axis_size("z")
    groups = lax.axis_size("dp")
    length, model = tokens.shape[1:]
    own_d = w_in.shape[0]
    own_e = conv_w.shape[0]
    inner = w_in.shape[1] // 2
    channels = inner // ways
    rank = w_dt.shape[1]
    states = (w_x.shape[1] - rank) // 2
    cols = w_in.reshape(own_d, 2, groups, ways, own_e).transpose(3, 0, 1, 2, 4).reshape(ways, own_d, 2 * channels)
    cols = lax.all_to_all(cols, TP, split_axis=0, concat_axis=0, tiled=True)
    win = lax.all_gather(cols, "dp", axis=0, tiled=True).reshape(model, 2 * channels)
    small = jnp.concatenate([w_x, w_dt, conv_w, conv_b[:, None], dt_bias[:, None], skip[:, None]], axis=1)
    small_width = small.shape[1]
    small = lax.all_gather(small, "dp", axis=0, tiled=True)
    wx = small[:, :rank + 2 * states]
    wdt = small[:, rank + 2 * states:2 * rank + 2 * states]
    rest = small[:, 2 * rank + 2 * states:].astype(f32)
    taps, bias, dtb, skips = rest[:, :4], rest[:, 4], rest[:, 5], rest[:, 6]
    wout = lax.all_gather(w_out, "dp", axis=0, tiled=True)
    gains = lax.all_gather(gain, ALL, axis=0, tiled=True).astype(f32)
    x = tokens[0].astype(f32)
    scale = lax.rsqrt(jnp.mean(x * x, axis=1, keepdims=True) + EPS)
    xn = (x * scale * gains).astype(bf16)
    xns = lax.all_gather(xn, TP, axis=0, tiled=True)
    ups = lax.all_gather(grad_out[0], TP, axis=0, tiled=True)
    lens = lax.all_gather(lengths, TP, axis=0, tiled=True)
    rows = lens.shape[0]
    tall = rows * length

    def time_major(a):
        return a.reshape(rows, length, -1).transpose(1, 0, 2).reshape(tall, -1)

    def row_major(a):
        return a.reshape(length, rows, -1).transpose(1, 0, 2).reshape(tall, -1)

    same, live = masks(lens, length)
    zz = time_major(jnp.dot(xns, win, preferred_element_type=f32))
    u = zz[:, :channels].reshape(length, rows, channels)
    g = zz[:, channels:]
    c = bias + taps[:, 3] * u
    shifted = []
    for offset in range(1, 4):
        earlier = jnp.pad(u, ((offset, 0), (0, 0), (0, 0)))[:length] * same[offset - 1][:, :, None]
        shifted.append(earlier)
        c = c + taps[:, 3 - offset] * earlier
    sig = jax.nn.sigmoid(c)
    v16 = (c * sig).astype(bf16).reshape(tall, channels)
    v = v16.astype(f32)
    p = lax.psum(jnp.dot(v16, wx, preferred_element_type=f32), TP)
    dl = p[:, :rank].astype(bf16)
    kq = p[:, rank:]
    dims_cols = (((1,), (1,)), ((), ()))
    dims_rows = (((0,), (0,)), ((), ()))
    pre = lax.dot_general(dl, wdt, dims_cols, preferred_element_type=f32) + dtb
    dm = time_major(lax.dot_general(ups, wout, dims_cols, preferred_element_type=f32))
    flags = jnp.pad(jnp.stack([same[0].reshape(tall), live.reshape(tall)], axis=1), ((0, 0), (0, 126)))
    hi = kq.astype(bf16)
    mid = (kq - hi.astype(f32)).astype(bf16)
    low = (kq - hi.astype(f32) - mid.astype(f32)).astype(bf16)
    kq3 = jnp.concatenate([hi, mid, low], axis=1)
    keys = kq[:, :states]
    sk = jnp.broadcast_to(jnp.sum(keys * keys, axis=1, keepdims=True), (tall, 8))
    m, dg, dpre, dv, dkq, stats = mixer(flags, kq3, sk, pre, v, g, dm, skips[None], states=states, width=256, unroll=4)
    stats = stats.transpose(1, 2, 0, 3).reshape(3, 8, channels)
    dskip = jnp.sum(stats[0], axis=0)
    total = lax.psum(jnp.sum(stats[1]), ALL)
    peak = lax.pmax(jnp.max(stats[2]), ALL)
    beta_mean = total / float(groups * ways * length * inner)
    m16 = row_major(m).astype(bf16)
    out = jnp.dot(m16, wout, preferred_element_type=f32).astype(bf16)
    out = lax.psum_scatter(out, TP, scatter_dimension=0, tiled=True)
    block_out = (x + out.astype(f32)).astype(bf16)
    grad_wout = lax.dot_general(m16, ups, dims_rows, preferred_element_type=f32).astype(bf16)
    grad_wout = lax.psum_scatter(grad_wout, "dp", scatter_dimension=0, tiled=True)
    dpre16 = dpre.astype(bf16)
    grad_dtb = jnp.sum(dpre16.astype(f32), axis=0)
    grad_wdt = lax.dot_general(dpre16, dl, dims_rows, preferred_element_type=f32)
    ddl = jnp.dot(dpre16, wdt, preferred_element_type=f32)
    dkq = dkq[:, :2 * states] + dkq[:, 2 * states:2 * states + 1] * jnp.pad(keys, ((0, 0), (0, states)))
    dp16 = lax.psum(jnp.concatenate([ddl, dkq], axis=1), TP).astype(bf16)
    grad_wx = lax.dot_general(v16, dp16, dims_rows, preferred_element_type=f32)
    dvt = dv + lax.dot_general(dp16, wx, dims_cols, preferred_element_type=f32)
    dc = (dvt * (sig.reshape(tall, channels) * (1.0 + c.reshape(tall, channels) * (1.0 - sig.reshape(tall, channels))))).reshape(length, rows, channels)
    du = taps[:, 3] * dc
    grad_taps = [jnp.sum(dc * u, axis=(0, 1))]
    for offset in range(1, 4):
        grad_taps.append(jnp.sum(dc * shifted[offset - 1], axis=(0, 1)))
        du = du + taps[:, 3 - offset] * jnp.pad((dc * same[offset - 1][:, :, None])[offset:], ((0, offset), (0, 0), (0, 0)))
    grad_conv = jnp.stack(grad_taps[::-1] + [jnp.sum(dc, axis=(0, 1)), grad_dtb, dskip], axis=1)
    dz = row_major(jnp.concatenate([du.reshape(tall, channels), dg], axis=1)).astype(bf16)
    gwin = lax.dot_general(xns, dz, dims_rows, preferred_element_type=f32).astype(bf16)
    gwin = lax.psum_scatter(gwin, "dp", scatter_dimension=0, tiled=True)
    gwin = lax.all_to_all(gwin.reshape(ways, own_d, 2 * channels), TP, split_axis=0, concat_axis=0, tiled=True)
    grad_win = gwin.reshape(ways, own_d, 2, groups, own_e).transpose(1, 2, 3, 0, 4).reshape(own_d, 2 * inner).astype(f32)
    dxn = lax.dot_general(dz, win, dims_cols, preferred_element_type=f32).astype(bf16)
    dxn = lax.psum_scatter(dxn, TP, scatter_dimension=0, tiled=True).astype(f32)
    small_grad = lax.psum_scatter(jnp.concatenate([grad_wx, grad_wdt, grad_conv], axis=1), "dp", scatter_dimension=0, tiled=True)
    inner_grad = dxn * gains
    dxx = scale * inner_grad - x * (scale * scale * scale) * (jnp.sum(inner_grad * x, axis=1, keepdims=True) / model)
    grad_tokens = (grad_out[0].astype(f32) + dxx).astype(bf16)
    grad_gain = lax.psum_scatter(jnp.sum(dxn * x * scale, axis=0), ALL, scatter_dimension=0, tiled=True)
    at = rank + 2 * states
    return (
        block_out[None],
        grad_tokens[None],
        grad_gain,
        grad_win,
        small_grad[:, at + rank:at + rank + 4],
        small_grad[:, at + rank + 4],
        small_grad[:, :at],
        small_grad[:, at:at + rank],
        small_grad[:, at + rank + 5],
        small_grad[:, at + rank + 6],
        grad_wout.astype(f32),
        beta_mean,
        peak,
    )


def prepare(gain, lengths, w_in, conv_w, conv_b, w_x, w_dt, dt_bias, skip, ways, groups):
    own_d, own_e = w_in.shape[0], conv_w.shape[0]
    channels = own_e * groups
    cols = w_in.reshape(own_d, 2, groups, ways, own_e).transpose(3, 0, 1, 2, 4).reshape(ways, own_d, 2 * channels)
    small = jnp.concatenate([jnp.pad(w_x, ((0, 0), (0, 256 - w_x.shape[1]))), w_dt], axis=1)
    top = jnp.concatenate([jnp.tile(gain.astype(f32), 2)[None], jnp.pad(lengths.astype(f32), ((0, 0), (0, 123))), jnp.zeros((6, 128), f32)])
    low = jnp.concatenate([conv_w.astype(f32).T, conv_b.astype(f32)[None], dt_bias.astype(f32)[None], skip.astype(f32)[None], jnp.zeros((1, own_e), f32)])
    return cols, small, jnp.concatenate([top, low])


def on_device_direct(tokens, lengths, gain, w_in, conv_w, conv_b, w_x, w_dt, dt_bias, skip, w_out, grad_out):
    groups, ways = 4, 8
    length, model = tokens.shape[1:]
    own_d = w_in.shape[0]
    own_e = conv_w.shape[0]
    inner = w_in.shape[1] // 2
    channels = inner // ways
    rank = w_dt.shape[1]
    states = (w_x.shape[1] - rank) // 2
    rows = ways
    tall = rows * length
    cols, small, meta = prepare(gain, lengths, w_in, conv_w, conv_b, w_x, w_dt, dt_bias, skip, ways, groups)
    xns, ups, win, wout, smalls, vecs, gains, masks, u_pad, g, v, slope, dl, kq_wide = k1(tokens, grad_out, cols, w_out, small, meta)
    wx = smalls[:, :rank + 2 * states]
    taps = vecs[:4].T
    x = tokens[0].astype(f32)
    scale = lax.rsqrt(jnp.mean(x * x, axis=1, keepdims=True) + EPS)

    def time_major(a):
        return a.reshape(rows, length, -1).transpose(1, 0, 2).reshape(tall, -1)

    def row_major(a):
        return a.reshape(length, rows, -1).transpose(1, 0, 2).reshape(tall, -1)

    v4, g4 = v, g
    u_pad, v, slope = [a.transpose(1, 0, 2).reshape(-1, channels) for a in (u_pad, v, slope)]
    u = u_pad[24:].reshape(length, rows, channels)
    same = [masks[o, :, 0].reshape(length, rows) for o in range(3)]
    shifted = []
    for offset in range(1, 4):
        shifted.append(jnp.pad(u, ((offset, 0), (0, 0), (0, 0)))[:length] * same[offset - 1][:, :, None])
    v16 = v.astype(bf16)
    dims_cols = (((1,), (1,)), ((), ()))
    dims_rows = (((0,), (0,)), ((), ()))
    m16, dg16, dpre16, dv, part, stat = k2(dl, kq_wide, smalls, vecs, masks, v4, g4, ups, wout, states)
    dv = dv.transpose(1, 0, 2).reshape(tall, channels)
    dskip, grad_dtb = stat[6], stat[5]
    out = jnp.dot(m16, wout, preferred_element_type=f32).astype(bf16)
    grad_wout = lax.dot_general(m16, ups, dims_rows, preferred_element_type=f32).astype(bf16)
    grad_wdt = lax.dot_general(dpre16, dl, dims_rows, preferred_element_type=f32)
    part = group_total(part, 2)
    dp16 = jnp.concatenate([part[:tall], part[tall:].reshape(tall // 4, 4, 32).transpose(1, 0, 2).reshape(tall, 32)], axis=1).astype(bf16)
    grad_wx = lax.dot_general(v16, dp16, dims_rows, preferred_element_type=f32)
    dvt = dv + lax.dot_general(dp16, wx, dims_cols, preferred_element_type=f32)
    dc = (dvt * slope).reshape(length, rows, channels)
    du = taps[:, 3] * dc
    grad_taps = [jnp.sum(dc * u, axis=(0, 1))]
    for offset in range(1, 4):
        grad_taps.append(jnp.sum(dc * shifted[offset - 1], axis=(0, 1)))
        du = du + taps[:, 3 - offset] * jnp.pad((dc * same[offset - 1][:, :, None])[offset:], ((0, offset), (0, 0), (0, 0)))
    grad_conv = jnp.stack(grad_taps[::-1] + [jnp.sum(dc, axis=(0, 1)), grad_dtb, dskip], axis=1)
    dz = jnp.concatenate([row_major(du.reshape(tall, channels)).astype(bf16), dg16], axis=1)
    gwin = lax.dot_general(xns, dz, dims_rows, preferred_element_type=f32).astype(bf16)
    dxn = lax.dot_general(dz, win, dims_cols, preferred_element_type=f32).astype(bf16)
    small_grad = jnp.concatenate([grad_wx, grad_wdt, grad_conv], axis=1)
    small_grad = jnp.pad(small_grad, ((0, 0), (0, -small_grad.shape[1] % 128)))
    dxn, out, gwin, grad_wout, small_grad = back(
        dxn.reshape(2, 4, length, model), out.reshape(2, 4, length, model), gwin.reshape(groups, ways * own_d, 2 * channels),
        grad_wout.reshape(groups, own_e, model), small_grad.reshape(groups, own_e, -1))
    block_out = (x + out).astype(bf16)
    grad_win = gwin.reshape(ways, own_d, 2, groups, own_e).transpose(1, 2, 3, 0, 4).reshape(own_d, 2 * inner).astype(f32)
    gains = gains[0]
    inner_grad = dxn * gains
    dxx = scale * inner_grad - x * (scale * scale * scale) * (jnp.sum(inner_grad * x, axis=1, keepdims=True) / model)
    grad_tokens = (grad_out[0].astype(f32) + dxx).astype(bf16)
    grad_gain = jnp.sum(dxn * x * scale, axis=0)
    seen, peak = jnp.sum(stat[0]), jnp.max(stat[1])
    part = grad_gain.reshape(groups, ways, own_d).transpose(1, 0, 2)
    part = jnp.pad(part, ((0, 0), (0, 8 - groups), (0, 128 - own_d)))
    part = part.at[:, 4, 0].set(seen).at[:, 4, 1].set(peak)
    part = tiny(part)
    grad_gain = lax.dynamic_index_in_dim(part, lax.axis_index("dp"), keepdims=False)[:own_d]
    seen, peak = part[4, 0], part[4, 1]
    beta_mean = seen / float(groups * ways * length * inner)
    at = rank + 2 * states
    return (
        block_out[None],
        grad_tokens[None],
        grad_gain,
        grad_win,
        small_grad[:, at + rank:at + rank + 4],
        small_grad[:, at + rank + 4],
        small_grad[:, :at],
        small_grad[:, at:at + rank],
        small_grad[:, at + rank + 5],
        small_grad[:, at + rank + 6],
        grad_wout,
        beta_mean,
        peak,
    )


def on_device_any(*args):
    if lax.axis_size("dp") == 4 and lax.axis_size("z") == 4:
        return on_device_direct(*args)
    return on_device(*args)


def solution(mesh):
    wide, narrow = mesh.devices.shape
    fine = Mesh(mesh.devices.reshape(wide // 2, 2, narrow), ALL)
    cut = (P(ALL, None), P(ALL))
    in_specs = (P(ALL, None, None), cut[0], cut[1], cut[0], cut[0], cut[1], cut[0], cut[0], cut[1], cut[1], cut[0], P(ALL, None, None))
    out_specs = (P(ALL, None, None), P(ALL, None, None), cut[1], cut[0], cut[0], cut[1], cut[0], cut[0], cut[1], cut[1], cut[0], P(), P())
    return jax.shard_map(on_device_any, mesh=fine, in_specs=in_specs, out_specs=out_specs, check_vma=False)
```

```python
import functools
import jax, jax.numpy as jnp
from jax import lax
from jax.experimental import pallas as pl
from jax.experimental.pallas import tpu as pltpu
from jax.sharding import Mesh, PartitionSpec as P

DOCS = 4
EPS = 1e-05
ALL = ("dp", "core", "z")
TP = ("core", "z")

f32 = jnp.float32
bf16 = jnp.bfloat16

def fold(x):
    total = x[:, :128]
    for at in range(128, x.shape[1], 128):
        total = total + x[:, at:at+128]
    return total

def mixer_kernel(states, unroll, chunk, flags_ref, kq3_ref, sk_ref, pre_ref, v_ref, g_ref, dm_ref, skip_ref,
                 m_ref, dg_ref, dpre_ref, dv_ref, dkq_ref, stat_ref, s_ref, h_ref, rate_ref, rv_ref, kb_ref, drr_ref):
    rows = pre_ref.shape[0]
    width = pre_ref.shape[1]
    steps = rows // 8
    wide = states * 128
    spread_rows = kq3_ref.shape[1]
    def spread(i, c):
        r = pl.ds(pl.multiple_of(i * chunk, chunk), chunk)
        left = kq3_ref[r, :]
        for part in range(0, 2 * wide, 512):
            ids = lax.broadcasted_iota(jnp.int32, (spread_rows, 512), 0) % (2 * states)
            col = lax.broadcasted_iota(jnp.int32, (spread_rows, 512), 1) // 128 + part // 128
            hot = jnp.where(ids == col, 1.0, 0.0).astype(bf16)
            kb_ref[r, part:part+512] = jnp.dot(left, hot, preferred_element_type=f32)
        return c
    lax.fori_loop(0, rows // chunk, spread, 0)

    def before(i, c):
        r = pl.ds(pl.multiple_of(i * 64, 64), 64)
        live = flags_ref[r, 1:2]
        beta = jax.nn.sigmoid(pre_ref[r, :])
        part = 1.0 / (1.0 + beta * sk_ref[r, 0:1])
        rate = beta * part
        rate_ref[r, :] = rate
        v = v_ref[r, :]
        rv_ref[r, :] = rate * v
        dpre_ref[r, :] = part * part * beta * (1.0 - beta)
        g = g_ref[r, :]
        sg = jax.nn.sigmoid(g)
        dm = dm_ref[r, :] * live
        dv_ref[r, :] = dm * (g * sg)
        dg_ref[r, :] = dm * (sg * (1.0 + g * (1.0 - sg)))
        return c
    lax.fori_loop(0, rows // 64, before, 0)

    s_ref[0, 0] = jnp.zeros(s_ref.shape[2:], f32)

    group = unroll
    tile = lambda x: jnp.concatenate([x] * (width // 128), axis=1)
    span = group * 8
    at = [slice(j * 8, j * 8 + 8) for j in range(group)]
    def view(ref, i):
        return ref.at[pl.ds(pl.multiple_of(i * span, span), span)]

    def forward(i, carry):
        flags, rates, rvs, vs, kbs, ms = [view(x, i) for x in (flags_ref, rate_ref, rv_ref, v_ref, kb_ref, m_ref)]
        keep = [jnp.broadcast_to(flags[r, 0:1], (8, 128)) for r in at]
        rate = [rates[r, :] for r in at]
        rv = [rvs[r, :] for r in at]
        y = [skip_ref[...] * vs[r, :] for r in at]
        for n in range(states):
            state = s_ref[i, 0, n]
            for j, r in enumerate(at):
                kb = kbs[r, n*128:(n+1)*128]
                qb = kbs[r, wide+n*128:wide+(n+1)*128]
                state = (tile(keep[j]) - rate[j] * tile(kb * kb * keep[j])) * state + rv[j] * tile(kb)
                if j < group - 1:
                    s_ref[i, j + 1, n] = state
                else:
                    s_ref[i + 1, 0, n] = state
                y[j] = y[j] + state * tile(qb)
        for j, r in enumerate(at):
            ms[r, :] = y[j]
        return carry

    lax.fori_loop(0, steps // group, forward, 0)
    h_ref[...] = jnp.zeros_like(h_ref)

    def backward(step, carry):
        i = steps // group - 1 - step
        flags, rates, rvs, vs, kbs, dvs, dpres, drrs = [view(x, i) for x in (flags_ref, rate_ref, rv_ref, v_ref, kb_ref, dv_ref, dpre_ref, drr_ref)]
        keep = [jnp.broadcast_to(flags[r, 0:1], (8, 128)) for r in at]
        rate = [rates[r, :] for r in at]
        rv = [rvs[r, :] for r in at]
        dy = [dvs[r, :] for r in at]
        hk = [jnp.zeros((8, width), f32) for r in at]
        hs2 = [jnp.zeros((8, width), f32) for r in at]
        for n in range(states):
            ah = h_ref[n]
            after_ = s_ref[i + 1, 0, n]
            for j in range(group - 1, -1, -1):
                r = at[j]
                kb = kbs[r, n*128:(n+1)*128]
                qb = kbs[r, wide+n*128:wide+(n+1)*128]
                kk = kb * keep[j]
                held = tile(kb * kk)
                h = dy[j] * tile(qb) + ah
                prior = s_ref[i, j, n]
                hs = h * prior
                hk[j] = hk[j] + h * tile(kb)
                hs2[j] = hs2[j] + hs * held
                kbs[r, n*128:(n+1)*128] = fold(h * rv[j]) - 2.0 * kk * fold(hs * rate[j])
                kbs[r, wide+n*128:wide+(n+1)*128] = fold(dy[j] * after_)
                after_ = prior
                ah = (tile(keep[j]) - rate[j] * held) * h
            h_ref[n] = ah
        for j, r in enumerate(at):
            v = vs[r, :]
            drate = v * hk[j] - hs2[j]
            drrs[r, :] = fold(drate * rate[j] * rate[j]) * (-2.0)
            dpres[r, :] = drate * dpres[r, :]
            dvs[r, :] = rate[j] * hk[j] + skip_ref[...] * dy[j]
            stat_ref[0, 0] += dy[j] * v
        return carry

    stat_ref[...] = jnp.zeros_like(stat_ref)
    lax.fori_loop(0, steps // group, backward, 0)

    first = pl.program_id(0) == 0
    def gather(i, c):
        r = pl.ds(pl.multiple_of(i * chunk, chunk), chunk)
        total = jnp.zeros((chunk, 128), f32)
        for part in range(0, 2 * wide, 512):
            row = lax.broadcasted_iota(jnp.int32, (512, 128), 0) // 128 + part // 128
            col = lax.broadcasted_iota(jnp.int32, (512, 128), 1)
            hot = jnp.where(row == col, 1.0, 0.0).astype(bf16)
            total += jnp.dot(kb_ref[r, part:part+512].astype(bf16), hot, preferred_element_type=f32)
        col = lax.broadcasted_iota(jnp.int32, (128, 128), 1)
        hot = jnp.where(col == 2 * states, 1.0, 0.0).astype(bf16)
        total += jnp.dot(drr_ref[r, :].astype(bf16), hot, preferred_element_type=f32)
        dkq_ref[r, :] = jnp.where(first, total, dkq_ref[r, :] + total)
        return c
    lax.fori_loop(0, rows // chunk, gather, 0)

    def after(i, c):
        r = pl.ds(pl.multiple_of(i * 64, 64), 64)
        live = flags_ref[r, 1:2]
        y = m_ref[r, :]
        g = g_ref[r, :]
        m_ref[r, :] = y * (g * jax.nn.sigmoid(g)) * live
        dg_ref[r, :] = y * dg_ref[r, :]
        shown = (jax.nn.sigmoid(pre_ref[r, :]) * live).reshape(8, 8, width)
        stat_ref[0, 1] += jnp.sum(shown, axis=0)
        stat_ref[0, 2] = jnp.maximum(stat_ref[0, 2], jnp.max(shown, axis=0))
        return c
    lax.fori_loop(0, rows // 64, after, 0)

def mixer(flags, kq3, sk, pre, v, g, dm, skip, states=16, width=256, unroll=1):
    rows, total = pre.shape
    steps = rows // 8
    tiles = total // width
    big = jax.ShapeDtypeStruct((rows, total), f32)
    cut = pl.BlockSpec((rows, width), lambda h: (0, h))
    whole = lambda a: pl.BlockSpec(a.shape, lambda h: (0,) * a.ndim)
    return pl.pallas_call(
        functools.partial(mixer_kernel, states, unroll, min(256, rows)),
        grid=(tiles,),
        out_shape=(big, big, big, big, jax.ShapeDtypeStruct((rows, 128), f32), jax.ShapeDtypeStruct((tiles, 3, 8, width), f32)),
        in_specs=[whole(flags), whole(kq3), whole(sk), cut, cut, cut, cut, pl.BlockSpec((1, width), lambda h: (0, h))],
        out_specs=(cut, cut, cut, cut, pl.BlockSpec((rows, 128), lambda h: (0, 0)), pl.BlockSpec((1, 3, 8, width), lambda h: (h, 0, 0, 0))),
        scratch_shapes=[pltpu.VMEM((steps//unroll+1, unroll, states, 8, width), f32), pltpu.VMEM((states, 8, width), f32)] + [pltpu.VMEM((rows, width), f32)]*2
          + [pltpu.VMEM((rows, 2*states*128), f32), pltpu.VMEM((rows, 128), f32)],
        compiler_params=pltpu.CompilerParams(vmem_limit_bytes=60*1024*1024),
    )(flags, kq3, sk, pre, v, g, dm, skip)


MESH = pl.DeviceIdType.MESH


def flip(value, bit):
    return value + bit * (1 - 2 * ((value // bit) % 2))


def place():
    d, c, z = lax.axis_index("dp"), lax.axis_index("core"), lax.axis_index("z")
    return d, c, z


def put(src, dst, send, recv, device):
    copy = pltpu.make_async_remote_copy(src_ref=src, dst_ref=dst, send_sem=send, recv_sem=recv, device_id=device, device_id_type=MESH)
    copy.start()
    return copy


def landed(slot, sem, device):
    pltpu.make_async_remote_copy(src_ref=slot, dst_ref=slot, send_sem=sem, recv_sem=sem, device_id=device, device_id_type=MESH).wait_recv()


def sent(slot, sem, device):
    pltpu.make_async_remote_copy(src_ref=slot, dst_ref=slot, send_sem=sem, recv_sem=sem, device_id=device, device_id_type=MESH).wait_send()


def greet(devices):
    barrier = pltpu.get_barrier_semaphore()
    for device in devices:
        pl.semaphore_signal(barrier, inc=1, device_id=device, device_id_type=MESH)
    pl.semaphore_wait(barrier, len(devices))


def mates():
    return [(a, k) for k in (0, 1, 3, 2) for a in (1, 0) if (a, k) != (0, 0)]


def mate(step, sign=1):
    d, c, z = place()
    a, k = step
    return d, (flip(c, 1) if a else c), lax.rem(z + sign * k + 4, 4)


def rank_of(device):
    return device[1] * 4 + device[2]


PIECES = 4


def k1_kernel(tok_ref, up_ref, cols_ref, wout_ref, small_ref, meta_ref,
              xnt_out, ups_ref, win_out, wouts_ref, smalls_ref, vecs_ref, gains_ref, masks_ref, live_ref,
              u_ref, g_ref, v_ref, vt_ref, slope_ref, dl_ref, kq_ref,
              xs_ref, xn_ref, xnt_ref, win_ref, metas_ref, part_ref, out_ref, sib_ref, base_ref, left_ref, right_ref, tor_ref, tol_ref,
              own_sem, ms, mr, qs, qr, xls, xlr, xrs, xrr, xcs, xcr, as_, ar, ps, pr, rs, rr, ws, wr, ts, tr, tls, tlr, trs, trr, tos, tor):
    d, c, z = place()
    j = c * 4 + z
    dx, dy, dd = flip(d, 1), flip(d, 2), flip(flip(d, 1), 2)
    xn, yn, dn = (dx, c, z), (dy, c, z), (dd, c, z)
    sib = (d, flip(c, 1), z)
    left = (d, c, lax.rem(z + 3, 4))
    right = (d, c, lax.rem(z + 1, 4))
    steps = mates()
    greet([mate(s) for s in steps] + [xn, yn, dn])
    length = tok_ref.shape[1]
    model = tok_ref.shape[2]
    depth = cols_ref.shape[1]
    tiles = u_ref.shape[0]
    width = tiles * 128
    count = g_ref.shape[1]

    def rows(rank):
        return pl.ds(pl.multiple_of(rank * length, length), length)

    def block(group, rank):
        return pl.ds(pl.multiple_of((group * 8 + rank) * depth, depth), depth)

    own_e = wout_ref.shape[0]

    def part_e(group, start=0, size=own_e):
        return pl.ds(pl.multiple_of(group * own_e + start, 16), size)

    own = [
        pltpu.make_async_copy(tok_ref.at[0], xs_ref.at[rows(j)], own_sem.at[0]),
        pltpu.make_async_copy(up_ref.at[0], ups_ref.at[rows(j)], own_sem.at[1]),
        pltpu.make_async_copy(cols_ref.at[j], win_ref.at[block(d, j)], own_sem.at[2]),
        pltpu.make_async_copy(wout_ref, wouts_ref.at[part_e(d)], own_sem.at[3]),
        pltpu.make_async_copy(small_ref, smalls_ref.at[part_e(d)], own_sem.at[4]),
        pltpu.make_async_copy(meta_ref, metas_ref.at[d, j], own_sem.at[5]),
    ]
    for copy in own:
        copy.start()
    pending = []
    for i, s in enumerate(steps):
        to = mate(s)
        pending.append(put(meta_ref, metas_ref.at[d, j], ms.at[i], mr.at[i], to))
    for i, s in enumerate(steps):
        to = mate(s)
        pending.append(put(cols_ref.at[rank_of(to)], win_ref.at[block(d, j)], as_.at[i], ar.at[i], to))
    for i, to in enumerate((xn, yn, dn)):
        pending.append(put(small_ref, smalls_ref.at[part_e(d)], ps.at[16 + i], pr.at[16 + i], to))
    own[2].wait()
    slot = win_ref.at[block(d, j)]
    pending.append(put(slot, slot, ps.at[7], pr.at[7], xn))
    pending.append(put(slot, slot, ps.at[15], pr.at[15], yn))

    def row_start(ref, out, base):
        pending.append(put(ref.at[0], out.at[rows(j)], xcs.at[base + z], xcr.at[base + z], sib))

        @pl.when(z < 3)
        def _():
            put(ref.at[0], out.at[rows(j)], xls.at[base], xlr.at[base], right)

        @pl.when(z > 0)
        def _():
            put(ref.at[0], out.at[rows(j)], xrs.at[base], xrr.at[base], left)

    def row_hop(out, base, i, then=None):
        @pl.when(z > i)
        def _():
            at = z - 1 - i
            slot = out.at[rows(c * 4 + at)]
            landed(slot, xlr.at[base + i], left)
            if i < 2:
                @pl.when(z < 3)
                def _():
                    put(slot, slot, xls.at[base + i + 1], xlr.at[base + i + 1], right)
            put(slot, slot, xcs.at[base + at], xcr.at[base + at], sib)
            if then is not None:
                then(c * 4 + at)

        @pl.when(z < 3 - i)
        def _():
            at = z + 1 + i
            slot = out.at[rows(c * 4 + at)]
            landed(slot, xrr.at[base + i], right)
            if i < 2:
                @pl.when(z > 0)
                def _():
                    put(slot, slot, xrs.at[base + i + 1], xrr.at[base + i + 1], left)
            put(slot, slot, xcs.at[base + at], xcr.at[base + at], sib)
            if then is not None:
                then(c * 4 + at)

    def row_end(out, base):
        for i in range(3):
            @pl.when((z < 3) & (z >= i))
            def _():
                sent(out.at[rows(j)], xls.at[base + i], right)

            @pl.when((z > 0) & (z <= 3 - i))
            def _():
                sent(out.at[rows(j)], xrs.at[base + i], left)
        for at in range(4):
            @pl.when(z != at)
            def _():
                sent(out.at[rows(j)], xcs.at[base + at], sib)

    row_start(tok_ref, xs_ref, 0)
    own[5].wait()
    for i, s in enumerate(steps):
        landed(metas_ref.at[d, rank_of(mate(s, -1))], mr.at[i], xn)
    for i, to in enumerate((xn, yn, dn)):
        pending.append(put(metas_ref.at[d], metas_ref.at[d], qs.at[i], qr.at[i], to))
    slots = {7: j}
    for i, s in enumerate(steps):
        slots[i] = rank_of(mate(s, -1))
    order = [7] + list(range(7))

    def pass_on(i):
        src = mate(steps[i], -1)
        slot = win_ref.at[block(d, slots[i])]
        landed(slot, ar.at[i], src)
        pending.append(put(slot, slot, ps.at[i], pr.at[i], xn))
        pending.append(put(slot, slot, ps.at[8 + i], pr.at[8 + i], yn))

    def relay(k):
        i = order[k]
        slot = win_ref.at[block(dx, slots[i])]
        landed(slot, pr.at[i], xn)
        if k % 2 == 0:
            pending.append(put(slot, slot, rs.at[k // 2], rr.at[k // 2], yn))
        slot = win_ref.at[block(dy, slots[i])]
        landed(slot, pr.at[8 + i], yn)
        if k % 2 == 1:
            pending.append(put(slot, slot, rs.at[4 + k // 2], rr.at[4 + k // 2], xn))

    pass_on(0)
    for i, (to, at) in enumerate(((xn, dx), (yn, dy), (dn, dd))):
        landed(metas_ref.at[at], qr.at[i], to)
    lens = jnp.concatenate([metas_ref[d, r, 1:2, :] for r in range(8)], axis=0)
    ends = []
    last = jnp.zeros((8, 1), f32)
    for i in range(5):
        last = last + lens[:, i:i + 1]
        ends.append(jnp.broadcast_to(last, (8, 128)))

    def mask_step(t, carry):
        here = t.astype(f32)

        def segment(at):
            total = jnp.zeros((8, 128), f32)
            for end in ends:
                total = total + jnp.where(end <= at, 1.0, 0.0)
            return total

        now = segment(here)
        r = pl.ds(pl.multiple_of(t * 8, 8), 8)
        for o in range(1, 4):
            same = jnp.where(segment(here - o) == now, 1.0, 0.0)
            masks_ref[o - 1, r, :] = jnp.where(here >= o, same, 0.0)
        live_ref[0, r, :] = jnp.where(now < DOCS, 1.0, 0.0)
        return carry

    lax.fori_loop(0, length, mask_step, 0)
    masks_ref[:, count:, :] = jnp.zeros((3, masks_ref.shape[1] - count, 128), f32)
    lane = lax.broadcasted_iota(jnp.int32, (1, 128), 1)
    for group in range(4):
        for pair in range(4):
            at = group * 512 + pair * 128
            gains_ref[:, at:at + 128] = jnp.where(lane < depth, metas_ref[group, 2 * pair, 0:1, :], metas_ref[group, 2 * pair + 1, 0:1, :])
        vecs_ref[:, group * own_e:(group + 1) * own_e] = metas_ref[group, j, 8:16, :]

    def normalize(rank):
        def body(i, carry):
            r = pl.ds(pl.multiple_of(rank * length + i * 16, 16), 16)
            x = xs_ref[r, :].astype(f32)
            scale = lax.rsqrt(jnp.sum(x * x, axis=1, keepdims=True) * (1.0 / model) + EPS)
            xn_ref[r, :] = (x * scale * gains_ref[...]).astype(bf16)
            return carry

        lax.fori_loop(0, length // 16, body, 0)

        def turn(i, carry):
            part = pl.ds(pl.multiple_of(i * 256, 256), 256)
            xnt_ref[part, rows(rank)] = xn_ref[rows(rank), part].T
            return carry

        lax.fori_loop(0, model // 256, turn, 0)

    for i in range(1, 7):
        pass_on(i)
    own[0].wait()
    normalize(j)
    row_hop(xs_ref, 0, 0, normalize)
    row_start(up_ref, ups_ref, 4)
    halves = own_e // 2
    pending.append(put(wout_ref, wouts_ref.at[part_e(d)], ws.at[0], wr.at[0], xn))
    pending.append(put(wout_ref, wouts_ref.at[part_e(d)], ws.at[1], wr.at[1], yn))
    for k in range(4):
        relay(k)
    row_hop(xs_ref, 0, 1, normalize)
    for k in range(4, 8):
        relay(k)
    row_hop(xs_ref, 0, 2, normalize)
    for at in range(4):
        rank = flip(c, 1) * 4 + at
        landed(xs_ref.at[rows(rank)], xcr.at[at], sib)
        normalize(rank)
    for k, i in enumerate(order):
        slot = win_ref.at[block(dd, slots[i])]
        if k % 2 == 0:
            landed(slot, rr.at[k // 2], yn)
        else:
            landed(slot, rr.at[4 + k // 2], xn)
    own += [pltpu.make_async_copy(xnt_ref, xnt_out, own_sem.at[6]), pltpu.make_async_copy(win_ref, win_out, own_sem.at[7])]
    own[6].start()
    own[7].start()
    row_hop(ups_ref, 4, 0)
    lead = u_ref.shape[1] - count
    u_ref[:, 0:lead, :] = jnp.zeros((tiles, lead, 128), f32)

    tile = 256

    def spread(out, first, start):
        def body(i, carry):
            product = jnp.dot(xn_ref[...], win_ref[:, pl.ds(pl.multiple_of(start + i * tile, tile), tile)], preferred_element_type=f32)
            for r in range(8):
                for part in range(0, tile, 128):
                    out[i * (tile // 128) + part // 128, pl.ds(first + r, length, stride=8), :] = product[r * length:(r + 1) * length, part:part + 128]
            return carry

        lax.fori_loop(0, width // tile, body, 0)

    spread(u_ref, lead, 0)
    taps = [vecs_ref[o:o + 1, :] for o in range(4)]
    bias = vecs_ref[4:5, :]

    def conv_step(i, carry):
        r = pl.ds(pl.multiple_of(i * 32, 32), 32)
        for n in range(tiles):
            lanes = slice(n * 128, n * 128 + 128)
            total = bias[:, lanes] + taps[3][:, lanes] * u_ref[n, pl.ds(pl.multiple_of(lead + i * 32, 8), 32), :]
            for o in range(1, 4):
                total = total + taps[3 - o][:, lanes] * (u_ref[n, pl.ds(pl.multiple_of(lead + i * 32 - 8 * o, 8), 32), :] * masks_ref[o - 1, r, :])
            sig = jax.nn.sigmoid(total)
            v_ref[n, r, :] = (total * sig).astype(bf16).astype(f32)
            slope_ref[n, r, :] = sig * (1.0 + total * (1.0 - sig))
        return carry

    lax.fori_loop(0, count // 32, conv_step, 0)
    for copy in own[3:5]:
        copy.wait()
    for i, (to, at) in enumerate(((xn, dx), (yn, dy), (dn, dd))):
        landed(smalls_ref.at[part_e(at)], pr.at[16 + i], to)
    quarter = count // 4
    narrow = smalls_ref[:, 128:256].astype(f32)
    packed = jnp.zeros((quarter, 128), f32)
    for b in range(4):
        r = slice(b * quarter, (b + 1) * quarter)
        values = jnp.concatenate([v_ref[n, r, :].astype(bf16) for n in range(tiles)], axis=1)
        part_ref[r, :] = jnp.dot(values, smalls_ref[:, 0:128], preferred_element_type=f32)
        turned = pltpu.roll(narrow, 32 * b, 1) if b else narrow
        packed = packed + jnp.dot(values, turned.astype(bf16), preferred_element_type=f32)
    part_ref[count:count + quarter, :] = packed
    slot = wouts_ref.at[part_e(dx)]
    landed(slot, wr.at[0], xn)
    slot = wouts_ref.at[part_e(dx, 0, halves)]
    pending.append(put(slot, slot, ws.at[2], wr.at[2], yn))
    slot = wouts_ref.at[part_e(dy)]
    landed(slot, wr.at[1], yn)
    slot = wouts_ref.at[part_e(dy, halves, halves)]
    pending.append(put(slot, slot, ws.at[3], wr.at[3], xn))

    def between():
        spread(g_ref, 0, width)
        row_hop(ups_ref, 4, 1)

        def turn(i, carry):
            r = pl.ds(pl.multiple_of(i * 128, 128), 128)
            for n in range(tiles):
                vt_ref[n * 128:(n + 1) * 128, r] = v_ref[n, r, :].T.astype(bf16)
            return carry

        lax.fori_loop(0, count // 128, turn, 0)

    line_total(part_ref, out_ref, sib_ref, base_ref, left_ref, right_ref, tor_ref, tol_ref, ts, tr, tls, tlr, trs, trr, tos, tor, between)
    dl_ref[...] = out_ref[0:count, :].astype(bf16)
    for b in range(4):
        packed = out_ref[count:count + quarter, :]
        kq_ref[b * quarter:(b + 1) * quarter, :] = pltpu.roll(packed, 128 - 32 * b, 1) if b else packed
    row_hop(ups_ref, 4, 2)
    for at in range(4):
        landed(ups_ref.at[rows(flip(c, 1) * 4 + at)], xcr.at[4 + at], sib)
    landed(wouts_ref.at[part_e(dd, 0, halves)], wr.at[2], yn)
    landed(wouts_ref.at[part_e(dd, halves, halves)], wr.at[3], xn)
    row_end(xs_ref, 0)
    row_end(ups_ref, 4)
    own[1].wait()
    own[6].wait()
    own[7].wait()
    for copy in pending:
        copy.wait_send()


def line_total(part_ref, out_ref, sib_ref, base_ref, left_ref, right_ref, tor_ref, tol_ref, ss, sr, ls, lr, rs, rr, os_, or_, between, early=None):
    d, c, z = place()
    sib = (d, flip(c, 1), z)
    left = (d, c, lax.rem(z + 3, 4))
    right = (d, c, lax.rem(z + 1, 4))
    rows = part_ref.shape[0] // 2
    piece = rows // PIECES
    mine, theirs = c * rows, flip(c, 1) * rows

    def cut(p):
        return pl.ds(p * piece, piece)

    def far(base, p):
        return pl.ds(pl.multiple_of(base + p * piece, 8), piece)

    for p in range(PIECES):
        put(part_ref.at[far(theirs, p)], sib_ref.at[cut(p)], ss.at[p], sr.at[p], sib)
    for p in range(PIECES):
        landed(sib_ref.at[cut(p)], sr.at[p], sib)
        base_ref[cut(p), :] = part_ref[far(mine, p), :] + sib_ref[cut(p), :]

        @pl.when(z == 0)
        def _():
            put(base_ref.at[cut(p)], left_ref.at[cut(p)], rs.at[p], lr.at[p], right)

        @pl.when(z == 3)
        def _():
            put(base_ref.at[cut(p)], right_ref.at[cut(p)], ls.at[p], rr.at[p], left)

    if early is not None:
        early()

    def from_left(p):
        landed(left_ref.at[cut(p)], lr.at[p], left)

        @pl.when(z < 3)
        def _():
            tor_ref[cut(p), :] = base_ref[cut(p), :] + left_ref[cut(p), :]
            put(tor_ref.at[cut(p)], left_ref.at[cut(p)], rs.at[p], lr.at[p], right)

    def from_right(p):
        landed(right_ref.at[cut(p)], rr.at[p], right)

        @pl.when(z > 0)
        def _():
            tol_ref[cut(p), :] = base_ref[cut(p), :] + right_ref[cut(p), :]
            put(tol_ref.at[cut(p)], right_ref.at[cut(p)], ls.at[p], rr.at[p], left)

    @pl.when(z == 1)
    def _():
        for p in range(PIECES):
            from_left(p)

    @pl.when(z == 2)
    def _():
        for p in range(PIECES):
            from_right(p)

    if between is not None:
        between()

    @pl.when(z < 2)
    def _():
        for p in range(PIECES):
            from_right(p)

    @pl.when(z >= 2)
    def _():
        for p in range(PIECES):
            from_left(p)

    for p in range(PIECES):
        out_ref[far(mine, p), :] = base_ref[cut(p), :]

        @pl.when(z > 0)
        def _():
            out_ref[far(mine, p), :] += left_ref[cut(p), :]

        @pl.when(z < 3)
        def _():
            out_ref[far(mine, p), :] += right_ref[cut(p), :]

        put(out_ref.at[far(mine, p)], out_ref.at[far(mine, p)], os_.at[p], or_.at[p], sib)
    for p in range(PIECES):
        landed(out_ref.at[far(theirs, p)], or_.at[p], sib)
        sent(out_ref.at[far(mine, p)], os_.at[p], sib)
        sent(part_ref.at[far(theirs, p)], ss.at[p], sib)

        @pl.when(z < 3)
        def _():
            sent(base_ref.at[cut(p)], rs.at[p], right)

        @pl.when(z > 0)
        def _():
            sent(base_ref.at[cut(p)], ls.at[p], left)


def k1(tokens, upstream, cols, w_out, small, meta):
    groups, ways = 4, cols.shape[0]
    like = jax.ShapeDtypeStruct
    length, model = tokens.shape[1:]
    count = ways * length
    channels = groups * w_out.shape[0]
    dma = lambda n: pltpu.SemaphoreType.DMA((n,))
    some = pl.BlockSpec(memory_space=pl.ANY)
    far = pl.BlockSpec(memory_space=pltpu.HBM)
    here = pl.BlockSpec(memory_space=pltpu.VMEM)
    packed = count + count // 4
    return pl.pallas_call(
        k1_kernel,
        out_shape=(
            like((model, count), bf16),
            like((count, model), bf16),
            like((groups * ways * cols.shape[1], cols.shape[2]), bf16),
            like((channels, model), bf16),
            like((channels, small.shape[1]), bf16),
            like((8, channels), f32),
            like((1, model), f32),
            like((3, count + 32, 128), f32),
            like((1, count, 128), f32),
            like((channels // 128, count + 24, 128), f32),
            like((channels // 128, count, 128), f32),
            like((channels // 128, count, 128), f32),
            like((channels, count), bf16),
            like((channels // 128, count, 128), f32),
            like((count, 128), bf16),
            like((count, 128), f32),
        ),
        in_specs=[some] * 6,
        out_specs=(far,) * 4 + (here,) * 12,
        scratch_shapes=[
            pltpu.VMEM((count, model), bf16),
            pltpu.VMEM((count, model), bf16),
            pltpu.VMEM((model, count), bf16),
            pltpu.VMEM((groups * ways * cols.shape[1], cols.shape[2]), bf16),
            pltpu.VMEM((groups, ways) + meta.shape, f32),
            pltpu.VMEM((packed, 128), f32),
            pltpu.VMEM((packed, 128), f32),
        ] + [pltpu.VMEM((packed // 2, 128), f32)] * 6
        + [dma(8), dma(7), dma(7), dma(3), dma(3), dma(8), dma(8), dma(8), dma(8), dma(8), dma(8), dma(7), dma(7), dma(19), dma(19), dma(8), dma(8), dma(4), dma(4)]
        + [dma(PIECES) for _ in range(8)],
        compiler_params=pltpu.CompilerParams(collective_id=0, has_side_effects=True, vmem_limit_bytes=56 * 1024 * 1024),
    )(tokens, upstream, cols, w_out, small, meta)


GROUP = 4


def k2_kernel(states, dl_ref, kq_ref, wdt_ref, vecs_ref, keep_ref, live_ref, v_ref, g_ref, ups_ref, wout_ref,
              m_ref, mt_ref, dg_ref, gwdt_ref, dv_ref, part_ref, stat_ref,
              dpre_ref, s_ref, h_ref, rate_ref, w_ref, y_ref, dm_ref, kb_ref, hot_ref, drr_ref):
    tiles, count = v_ref.shape[:2]
    steps = count // 8
    wide = states * 128
    chunk = 256
    first = pl.program_id(0) == 0
    half = pl.program_id(0)
    both = range(tiles)
    rank = wdt_ref.shape[1]

    @pl.when(first)
    def _():
        row = lax.broadcasted_iota(jnp.int32, (128, 512), 0)
        col = lax.broadcasted_iota(jnp.int32, (128, 512), 1) // 128
        for part in range(0, 2 * wide, 512):
            hot_ref[:, part:part + 512] = jnp.where((row % 32 == col + part // 128) & (row < 96), 1.0, 0.0).astype(bf16)

    lane = lax.broadcasted_iota(jnp.int32, (chunk, 128), 1)

    def spread(i, carry):
        r = pl.ds(pl.multiple_of(i * chunk, chunk), chunk)
        value = jnp.where(lane < 2 * states, kq_ref[r, :], 0.0)
        hi = value.astype(bf16).astype(f32)
        mid = (value - hi).astype(bf16).astype(f32)
        low = value - hi - mid
        left = (hi + pltpu.roll(mid, 32, 1) + pltpu.roll(low, 64, 1)).astype(bf16)
        for part in range(0, 2 * wide, 512):
            kb_ref[r, part:part + 512] = jnp.dot(left, hot_ref[:, part:part + 512], preferred_element_type=f32)
        return carry

    lax.fori_loop(0, count // chunk, spread, 0)
    cols = (((1,), (1,)), ((), ()))
    length = count // 8

    def gate_step(i, carry):
        r = pl.ds(pl.multiple_of(i * chunk, chunk), chunk)
        product = lax.dot_general(ups_ref[r, :], wout_ref[...], cols, preferred_element_type=f32)
        for j in range(chunk // length):
            for n in both:
                dm_ref[n, pl.ds(i * (chunk // length) + j, length, stride=8), :] = product[j * length:(j + 1) * length, n * 128:(n + 1) * 128]
        return carry

    lax.fori_loop(0, count // chunk, gate_step, 0)
    bias = vecs_ref[5:6, :]
    skip = vecs_ref[6:7, :]
    tile_of = lambda x, n: x[:, n * 128:(n + 1) * 128]
    ks = lax.broadcasted_iota(jnp.int32, (128, 128), 1)

    def before(i, carry):
        seen = list(carry)
        r = pl.ds(pl.multiple_of(i * 128, 128), 128)
        live = live_ref[0, r, :]
        k = jnp.where(ks < states, kq_ref[r, :], 0.0)
        sk = jnp.sum(k * k, axis=1, keepdims=True)
        pre = lax.dot_general(dl_ref[r, :], wdt_ref[...], cols, preferred_element_type=f32) + bias
        for n in both:
            beta = jax.nn.sigmoid(tile_of(pre, n))
            part = 1.0 / (1.0 + beta * sk)
            rate_ref[n, r, :] = beta * part
            w_ref[n, r, :] = part * part * beta * (1.0 - beta)
            g = g_ref[n, r, :]
            sg = jax.nn.sigmoid(g)
            dm = dm_ref[n, r, :] * live
            dv_ref[n, r, :] = dm * (g * sg)
            dm_ref[n, r, :] = dm * (sg * (1.0 + g * (1.0 - sg)))
            shown = (beta * live).reshape(16, 8, 128)
            seen[n] = seen[n] + jnp.sum(shown, axis=0)
            seen[tiles + n] = jnp.maximum(seen[tiles + n], jnp.max(shown, axis=0))
        return tuple(seen)

    blank = jnp.zeros((8, 128), f32)
    seen = lax.fori_loop(0, count // 128, before, (blank,) * (2 * tiles))
    s_ref[0, 0] = jnp.zeros(s_ref.shape[2:], f32)
    span = GROUP * 8
    at = [slice(j * 8, j * 8 + 8) for j in range(GROUP)]

    def view(ref, i):
        r = pl.ds(pl.multiple_of(i * span, span), span)
        return ref.at[:, r] if len(ref.shape) == 3 else ref.at[r]

    def pair(ref, r):
        return jnp.concatenate([ref[n, r, :] for n in both], axis=1)

    def keep_pair(ref, r, value):
        for n in both:
            ref[n, r, :] = tile_of(value, n)

    tile = lambda x: jnp.concatenate([x] * tiles, axis=1)

    def fold(x):
        total = tile_of(x, 0)
        for n in range(1, tiles):
            total = total + tile_of(x, n)
        return total

    def forward(i, carry):
        keeps, rates, vs, kbs, ys = [view(x, i) for x in (keep_ref, rate_ref, v_ref, kb_ref, y_ref)]
        keep = [keeps[0, r, :] for r in at]
        rate = [pair(rates, r) for r in at]
        value = [pair(vs, r) for r in at]
        rv = [a * b for a, b in zip(rate, value)]
        y = [skip * b for b in value]
        for n in range(states):
            state = s_ref[i, 0, n]
            for j, r in enumerate(at):
                kb = kbs[r, n * 128:(n + 1) * 128]
                qb = kbs[r, wide + n * 128:wide + (n + 1) * 128]
                state = (tile(keep[j]) - rate[j] * tile(kb * kb * keep[j])) * state + rv[j] * tile(kb)
                if j < GROUP - 1:
                    s_ref[i, j + 1, n] = state
                else:
                    s_ref[i + 1, 0, n] = state
                y[j] = y[j] + state * tile(qb)
        for j, r in enumerate(at):
            keep_pair(ys, r, y[j])
        return carry

    lax.fori_loop(0, steps // GROUP, forward, 0)
    h_ref[...] = jnp.zeros_like(h_ref)

    def backward(step, carry):
        i = steps // GROUP - 1 - step
        keeps, rates, vs, kbs, dvs, ws, drrs = [view(x, i) for x in (keep_ref, rate_ref, v_ref, kb_ref, dv_ref, w_ref, drr_ref)]
        keep = [keeps[0, r, :] for r in at]
        rate = [pair(rates, r) for r in at]
        value = [pair(vs, r) for r in at]
        rv = [a * b for a, b in zip(rate, value)]
        dy = [pair(dvs, r) for r in at]
        hk = [jnp.zeros((8, tiles * 128), f32) for r in at]
        hs2 = [jnp.zeros((8, tiles * 128), f32) for r in at]
        for n in range(states):
            ah = h_ref[n]
            later = s_ref[i + 1, 0, n]
            for j in range(GROUP - 1, -1, -1):
                r = at[j]
                kb = kbs[r, n * 128:(n + 1) * 128]
                qb = kbs[r, wide + n * 128:wide + (n + 1) * 128]
                kk = kb * keep[j]
                held = tile(kb * kk)
                h = dy[j] * tile(qb) + ah
                prior = s_ref[i, j, n]
                hs = h * prior
                hk[j] = hk[j] + h * tile(kb)
                hs2[j] = hs2[j] + hs * held
                kbs[r, n * 128:(n + 1) * 128] = fold(h * rv[j]) - 2.0 * kk * fold(hs * rate[j])
                kbs[r, wide + n * 128:wide + (n + 1) * 128] = fold(dy[j] * later)
                later = prior
                ah = (tile(keep[j]) - rate[j] * held) * h
            h_ref[n] = ah
        dskip = carry
        for j, r in enumerate(at):
            drate = value[j] * hk[j] - hs2[j]
            drrs[r, :] = fold(drate * rate[j] * rate[j]) * (-2.0)
            keep_pair(ws, r, drate * pair(ws, r))
            keep_pair(dvs, r, rate[j] * hk[j] + skip * dy[j])
            dskip = dskip + dy[j] * value[j]
        return dskip

    dskip = lax.fori_loop(0, steps // GROUP, backward, jnp.zeros((8, tiles * 128), f32))

    quarter = count // 4
    packed = jnp.zeros((quarter, 128), f32)
    for b in range(4):
        r = slice(b * quarter, (b + 1) * quarter)
        total = jnp.zeros((quarter, 128), f32)
        for part in range(0, 2 * wide, 512):
            total = total + lax.dot_general(kb_ref[r, part:part + 512].astype(bf16), hot_ref[:, part:part + 512], cols, preferred_element_type=f32)
        drr = jnp.sum(drr_ref[r, :], axis=1, keepdims=True)
        k = kq_ref[r, :]
        low = lax.broadcasted_iota(jnp.int32, (quarter, 128), 1)
        total = jnp.where(low < 2 * states, total, 0.0) + jnp.where(low < states, k * drr, 0.0)
        packed = packed + (pltpu.roll(total, 32 * b, 1) if b else total)

    tail = pl.ds(count, quarter)
    part_ref[tail, :] = jnp.where(first, packed, part_ref[tail, :] + packed)

    def after(i, carry):
        r = pl.ds(pl.multiple_of(i * 128, 128), 128)
        live = live_ref[0, r, :]
        sums = list(carry)
        for n in both:
            y = y_ref[n, r, :]
            g = g_ref[n, r, :]
            y_ref[n, r, :] = y * (g * jax.nn.sigmoid(g)) * live
            dm_ref[n, r, :] = y * dm_ref[n, r, :]
            low = w_ref[n, r, :].astype(bf16)
            dpre_ref[r, n * 128:(n + 1) * 128] = low
            sums[n] = sums[n] + jnp.sum(low.astype(f32).reshape(16, 8, 128), axis=0)
        ddl = jnp.dot(dpre_ref[r, :], wdt_ref[...], preferred_element_type=f32)
        part_ref[r, :] = jnp.where(first, ddl, part_ref[r, :] + ddl)
        return tuple(sums)

    sums = lax.fori_loop(0, count // 128, after, (blank,) * tiles)

    def by_row(j, carry):
        r = pl.ds(pl.multiple_of(j * length, length), length)
        for n in both:
            value = y_ref[n, pl.ds(j, length, stride=8), :]
            m_ref[r, n * 128:(n + 1) * 128] = value.astype(bf16)
            mt_ref[n * 128:(n + 1) * 128, r] = value.T.astype(bf16)
            dg_ref[r, n * 128:(n + 1) * 128] = dm_ref[n, pl.ds(j, length, stride=8), :].astype(bf16)
        return carry

    lax.fori_loop(0, 8, by_row, 0)
    gwdt_ref[...] = lax.dot_general(dpre_ref[...], dl_ref[...], (((0,), (0,)), ((), ())), preferred_element_type=f32)
    stat_ref[...] = jnp.zeros_like(stat_ref)
    for n in both:
        lanes = slice(n * 128, (n + 1) * 128)
        stat_ref[0:1, lanes] = jnp.sum(seen[n], axis=0, keepdims=True)
        stat_ref[1:2, lanes] = jnp.max(seen[tiles + n], axis=0, keepdims=True)
        stat_ref[5:6, lanes] = jnp.sum(sums[n], axis=0, keepdims=True)
        stat_ref[6:7, lanes] = jnp.sum(tile_of(dskip, n), axis=0, keepdims=True)


def k2(dl, kq, smalls, vecs, masks, live, v, g, ups, wout, states):
    count, rank = dl.shape
    channels, model = wout.shape
    tiles = 2
    width = tiles * 128
    like = jax.ShapeDtypeStruct
    once = pl.Buffered(buffer_count=1)
    whole = lambda a: pl.BlockSpec(a.shape, lambda h: (0,) * a.ndim, pipeline_mode=once)
    deep = pl.BlockSpec((tiles, count, 128), lambda h: (h, 0, 0))
    flat = pl.BlockSpec((count, width), lambda h: (0, h))
    return pl.pallas_call(
        functools.partial(k2_kernel, states),
        grid=(channels // width,),
        out_shape=(
            like((count, channels), bf16),
            like((channels, count), bf16),
            like((count, channels), bf16),
            like((channels, rank), f32),
            like(v.shape, f32),
            like((count + count // 4, 128), f32),
            like((8, channels), f32),
        ),
        in_specs=[
            whole(dl), whole(kq),
            pl.BlockSpec((width, 128), lambda h: (h, 2)),
            pl.BlockSpec((8, width), lambda h: (0, h)),
            pl.BlockSpec((1, count, 128), lambda h: (0, 0, 0), pipeline_mode=once),
            pl.BlockSpec((1, count, 128), lambda h: (0, 0, 0), pipeline_mode=once),
            deep, deep, whole(ups),
            pl.BlockSpec((width, model), lambda h: (h, 0)),
        ],
        out_specs=(flat, pl.BlockSpec((width, count), lambda h: (h, 0)), flat, pl.BlockSpec((width, rank), lambda h: (h, 0)), deep, pl.BlockSpec((count + count // 4, 128), lambda h: (0, 0)), pl.BlockSpec((8, width), lambda h: (0, h))),
        scratch_shapes=[
            pltpu.VMEM((count, width), bf16),
            pltpu.VMEM((count // 8 // GROUP + 1, GROUP, states, 8, width), f32),
            pltpu.VMEM((states, 8, width), f32),
        ] + [pltpu.VMEM((tiles, count, 128), f32)] * 4
        + [pltpu.VMEM((count, 2 * states * 128), f32), pltpu.VMEM((128, 2 * states * 128), bf16), pltpu.VMEM((count, 128), f32)],
        compiler_params=pltpu.CompilerParams(vmem_limit_bytes=60 * 1024 * 1024),
    )(dl, kq, smalls, vecs, masks, live, v, g, ups, wout)


class Row:
    def __init__(self, part, sib, recv, sems):
        self.part, self.sib, self.recv = part, sib, recv
        self.ss, self.sr, self.gs, self.lr, self.rr = sems
        d, c, z = place()
        self.c = c
        self.other = (d, flip(c, 1), z)
        self.to_left = (d, c, lax.rem(z + 3, 4))
        self.to_right = (d, c, lax.rem(z + 1, 4))

    def start(self):
        for zp in (3, 0, 2, 1):
            put(self.part.at[flip(self.c, 1), zp], self.sib.at[zp], self.ss.at[zp], self.sr.at[zp], self.other)

    def terms(self, zs, zp):
        landed(self.sib.at[zp], self.sr.at[zp], self.other)
        found = [self.sib.at[zp], self.part.at[self.c, zp]]
        if zp >= zs and zs > 0:
            landed(self.recv.at[zp], self.lr.at[zp], self.to_left)
            found.append(self.recv.at[zp])
        if zp <= zs and zs < 3:
            slot = self.recv.at[4 if zp == zs else zp]
            landed(slot, self.rr.at[zp], self.to_right)
            found.append(slot)
        return found

    def step(self, zs, k):
        for zp in range(4):
            if zp > zs and k == 3 - zp + zs:
                add_rows(self.sib.at[zp], self.terms(zs, zp))
                put(self.sib.at[zp], self.recv.at[zp], self.gs.at[zp], self.lr.at[zp], self.to_right)
            if zp < zs and k == zp + 3 - zs:
                add_rows(self.sib.at[zp], self.terms(zs, zp))
                put(self.sib.at[zp], self.recv.at[4 if zp == zs - 1 else zp], self.gs.at[zp], self.rr.at[zp], self.to_left)

    def finish(self, zs):
        add_rows(self.sib.at[zs], self.terms(zs, zs), self.total)

    def close(self, zs):
        for zp in range(4):
            sent(self.sib.at[zp], self.ss.at[zp], self.other)
            if zp != zs:
                sent(self.sib.at[zp], self.gs.at[zp], self.other)

    def along(self, k, total=None):
        self.total = total
        d, c, z = place()
        for zs in range(4):
            @pl.when(z == zs)
            def _():
                if k < 3:
                    self.step(zs, k)
                else:
                    self.finish(zs)
                    self.close(zs)


def row_scratch(rows, columns):
    return [pltpu.VMEM((4, rows, columns), bf16), pltpu.VMEM((5, rows, columns), bf16)] + [pltpu.SemaphoreType.DMA((4,))] * 5


def add_rows(dst, sources, total=None):
    rows = (total if total is not None else dst).shape[0]
    step = 16

    def body(i, carry):
        r = pl.ds(pl.multiple_of(i * step, step), step)
        value = sources[0][r, :].astype(f32)
        for more in sources[1:]:
            value = value + more[r, :].astype(f32)
        if total is not None:
            total[r, :] = value
        else:
            dst[r, :] = value.astype(dst.dtype)
        return carry

    lax.fori_loop(0, rows // step, body, 0)


class Flat:
    def __init__(self, part, xa, yb, rx, ry, ss, rs):
        self.part, self.xa, self.yb, self.rx, self.ry, self.ss, self.rs = part, xa, yb, rx, ry, ss, rs
        d, c, z = place()
        self.d, self.dx, self.dy, self.dd = d, flip(d, 1), flip(d, 2), flip(flip(d, 1), 2)
        self.xn, self.yn = (self.dx, c, z), (self.dy, c, z)
        half = part.shape[1] // 2
        self.a, self.b = pl.ds(0, half), pl.ds(half, half)
        self.sends = []

    def start_far(self):
        p = self.part
        self.sends.append(put(p.at[self.dd, self.a], self.xa, self.ss.at[0], self.rs.at[0], self.xn))
        self.sends.append(put(p.at[self.dd, self.b], self.yb, self.ss.at[1], self.rs.at[1], self.yn))

    def start_near(self):
        p = self.part
        self.sends.append(put(p.at[self.dx, self.a], self.rx.at[self.a], self.ss.at[2], self.rs.at[2], self.xn))
        self.sends.append(put(p.at[self.dy, self.b], self.ry.at[self.b], self.ss.at[3], self.rs.at[3], self.yn))

    def middle(self):
        p = self.part
        landed(self.xa, self.rs.at[0], self.xn)
        add_rows(self.xa, [self.xa, p.at[self.dy, self.a]])
        self.sends.append(put(self.xa, self.ry.at[self.a], self.ss.at[4], self.rs.at[4], self.yn))
        landed(self.yb, self.rs.at[1], self.yn)
        add_rows(self.yb, [self.yb, p.at[self.dx, self.b]])
        self.sends.append(put(self.yb, self.rx.at[self.b], self.ss.at[5], self.rs.at[5], self.xn))

    def finish(self, out):
        landed(self.rx.at[self.a], self.rs.at[2], self.xn)
        landed(self.ry.at[self.b], self.rs.at[3], self.yn)
        landed(self.ry.at[self.a], self.rs.at[4], self.yn)
        landed(self.rx.at[self.b], self.rs.at[5], self.xn)
        add_rows(out, [self.part.at[self.d], self.rx, self.ry])

    def close(self):
        for copy in self.sends:
            copy.wait_send()


def flat_scratch(rows, columns, dtype):
    half = pltpu.VMEM((rows // 2, columns), dtype)
    full = pltpu.VMEM((rows, columns), dtype)
    return [half, half, full, full, pltpu.SemaphoreType.DMA((6,)), pltpu.SemaphoreType.DMA((6,))]


def k3_kernel(part_ref, stat_ref, smalls_ref, vecs_ref, gains_ref, gwdt_ref, masks_ref, tok_ref, up_ref,
              m_any, mt_any, dg_any, dv_any, slope_any, u_any, vt_any, xnt_any, win_any, wout_any, ups_any,
              block_ref, gtok_ref, gwin_ref, gwout_ref, small_ref, tiny_ref, *scratch):
    scratch = list(scratch)

    def take(n):
        found = scratch[:n]
        del scratch[:n]
        return found

    outp, dxnp, gwinp, gwoutp, smallp = take(5)
    m_ref, mt_ref, dz_ref, dc_ref, slope_ref, u_ref, xnt_ref, dp_ref, slots_ref, row_ref = take(10)
    near_ref, pairs_ref, sum_ref, far_ref = take(4)
    loads, as_, ar, ns, nr, fs, fr = take(7)
    totals = take(7)
    total_sems = take(8)
    out_row = Row(outp, *take(2), take(5))
    dxn_row = Row(dxnp, *take(2), take(5))
    gwin_flat = Flat(gwinp, *take(6))
    gwout_flat = Flat(gwoutp, *take(6))
    small_flat = Flat(smallp, *take(6))
    d, c, z = place()
    j = c * 4 + z
    other = flip(c, 1)
    steps = mates()
    planes = [(flip(d, 1), c, z), (flip(d, 2), c, z), (flip(flip(d, 1), 2), c, z)]
    length, model = tok_ref.shape[1:]
    tiles, padded, _ = dc_ref.shape
    count = dz_ref.shape[0]
    width = tiles * 128
    rows_any = [(m_any, m_ref), (wout_any, gwoutp), (ups_any, dxnp), (mt_any, mt_ref), (dv_any, dc_ref.at[:, pl.ds(0, count)]),
                (slope_any, slope_ref), (u_any, u_ref), (dg_any, dz_ref.at[:, pl.ds(width, width)]), (xnt_any, xnt_ref), (win_any, gwinp)]
    copies = [pltpu.make_async_copy(a, b, loads.at[i]) for i, (a, b) in enumerate(rows_any)]
    for copy in copies:
        copy.start()
    greet([mate(s) for s in steps] + planes)
    tile = 256
    nn = (((1,), (0,)), ((), ()))
    nt = (((1,), (1,)), ((), ()))

    def rows_product(half, target, left, right, dims, right_rows):
        def body(i, carry):
            if right_rows:
                group = i // (512 // tile)
                value = right[group, pl.ds(pl.multiple_of((i % (512 // tile)) * tile, tile), tile), :]
            else:
                value = jnp.concatenate([right[g, :, pl.ds(pl.multiple_of(i * tile, tile), tile)] for g in range(4)], axis=0)
            product = lax.dot_general(left[pl.ds(pl.multiple_of(half * 512, 512), 512), :], value, dims, preferred_element_type=f32)
            for zp in range(4):
                target[half, zp, :, pl.ds(pl.multiple_of(i * tile, tile), tile)] = product[zp * length:(zp + 1) * length].astype(bf16)
            return carry

        lax.fori_loop(0, model // tile, body, 0)

    def early():
        copies[0].wait()
        copies[1].wait()
        rows_product(other, outp, m_ref, gwoutp, nn, False)
        out_row.start()
        rows_product(c, outp, m_ref, gwoutp, nn, False)

    def between():
        out_row.along(0)
        copies[2].wait()
        copies[3].wait()

        def body(i, carry):
            lanes = pl.ds(pl.multiple_of(i * tile, tile), tile)
            value = dxnp[:, :, :, lanes].reshape(count, tile)
            product = jnp.dot(mt_ref[...], value, preferred_element_type=f32)
            for g in range(4):
                gwoutp[g, :, lanes] = product[g * 128:(g + 1) * 128].astype(bf16)
            return carry

        lax.fori_loop(0, model // tile, body, 0)
        gwout_flat.start_far()
        gwout_flat.start_near()

    total_ref = totals[0]
    line_total(part_ref, *totals, *total_sems, between, early)
    vt_copy = pltpu.make_async_copy(vt_any, mt_ref, loads.at[10])
    vt_copy.start()
    quarter = count // 4
    lane = lax.broadcasted_iota(jnp.int32, (quarter, 128), 1)
    dp_ref[:, 0:128] = total_ref[0:count, :].astype(bf16)
    for b in range(4):
        packed = total_ref[count:count + quarter, :]
        packed = pltpu.roll(packed, 128 - 32 * b, 1) if b else packed
        dp_ref[b * quarter:(b + 1) * quarter, 128:256] = jnp.where(lane < 32, packed, 0.0).astype(bf16)
    copies[4].wait()
    copies[5].wait()
    dc_ref[:, count:, :] = jnp.zeros((tiles, padded - count, 128), f32)

    def slope_step(i, carry):
        r = pl.ds(pl.multiple_of(i * 256, 256), 256)
        product = lax.dot_general(dp_ref[r, :], smalls_ref[:, 0:256], nt, preferred_element_type=f32)
        for n in range(tiles):
            dc_ref[n, r, :] = (dc_ref[n, r, :] + product[:, n * 128:(n + 1) * 128]) * slope_ref[n, r, :]
        return carry

    lax.fori_loop(0, count // 256, slope_step, 0)
    copies[6].wait()
    taps = [vecs_ref[o:o + 1, :] for o in range(4)]
    lead = u_ref.shape[1] - count

    for n in range(tiles):
        lanes = slice(n * 128, (n + 1) * 128)
        tap = [t[:, lanes] for t in taps]

        def conv_step(i, carry):
            r = pl.ds(pl.multiple_of(i * 32, 32), 32)
            sums = list(carry)
            dc = dc_ref[n, r, :]
            du = tap[3] * dc
            fold8 = lambda x: x[0:8] + x[8:16] + x[16:24] + x[24:32]
            sums[4] = sums[4] + fold8(dc)
            sums[3] = sums[3] + fold8(dc * u_ref[n, pl.ds(pl.multiple_of(lead + i * 32, 8), 32), :])
            for o in range(1, 4):
                sums[3 - o] = sums[3 - o] + fold8(dc * (u_ref[n, pl.ds(pl.multiple_of(lead + i * 32 - 8 * o, 8), 32), :] * masks_ref[o - 1, pl.ds(pl.multiple_of(i * 32, 8), 32), :]))
                du = du + tap[3 - o] * (dc_ref[n, pl.ds(pl.multiple_of(i * 32 + 8 * o, 8), 32), :] * masks_ref[o - 1, pl.ds(pl.multiple_of(i * 32 + 8 * o, 8), 32), :])
            dc_ref[n, r, :] = du
            return tuple(sums)

        sums = lax.fori_loop(0, count // 32, conv_step, (jnp.zeros((8, 128), f32),) * 5)
        smallp[n, 128:160, :] = jnp.zeros((32, 384), f32)
        for k in range(5):
            smallp[n, 128 + k:129 + k, 0:128] = jnp.sum(sums[k], axis=0, keepdims=True)
        smallp[n, 133:134, 0:128] = stat_ref[5:6, lanes]
        smallp[n, 134:135, 0:128] = stat_ref[6:7, lanes]
        smallp[n, 0:128, 256:384] = gwdt_ref[n * 128:(n + 1) * 128, :]

    copies[7].wait()

    def by_row(i, carry):
        r = pl.ds(pl.multiple_of(i * length, length), length)
        for n in range(tiles):
            dz_ref[r, n * 128:(n + 1) * 128] = dc_ref[n, pl.ds(i, length, stride=8), :].astype(bf16)
        return carry

    lax.fori_loop(0, 8, by_row, 0)
    copies[9].wait()
    rows_product(other, dxnp, dz_ref, gwinp, nt, True)
    dxn_row.start()
    rows_product(c, dxnp, dz_ref, gwinp, nt, True)
    out_row.along(1)
    copies[8].wait()

    def weight_rows(group):
        def body(i, carry):
            lanes = pl.ds(pl.multiple_of(i * tile, tile), tile)
            left = xnt_ref[pl.ds(pl.multiple_of(group * 512, 512), 512), :]
            gwinp[group, :, lanes] = jnp.dot(left, dz_ref[:, lanes], preferred_element_type=f32).astype(bf16)
            return carry

        lax.fori_loop(0, 2 * width // tile, body, 0)

    weight_rows(gwin_flat.dd)
    gwin_flat.start_far()
    weight_rows(gwin_flat.dx)
    weight_rows(gwin_flat.dy)
    gwin_flat.start_near()
    out_row.along(2)
    dxn_row.along(0)
    weight_rows(d)
    gwout_flat.middle()
    vt_copy.wait()
    for n in range(tiles):
        smallp[n, 0:128, 0:256] = jnp.dot(mt_ref[n * 128:(n + 1) * 128, :], dp_ref[...], preferred_element_type=f32)
    small_flat.start_far()
    small_flat.start_near()
    out_row.along(3, row_ref)

    def block_step(i, carry):
        r = pl.ds(pl.multiple_of(i * 16, 16), 16)
        block_ref[r, :] = (tok_ref[0, r, :].astype(f32) + row_ref[r, :]).astype(bf16)
        return carry

    lax.fori_loop(0, length // 16, block_step, 0)
    gwin_flat.middle()
    dxn_row.along(1)
    gwout_flat.finish(gwout_ref)
    dxn_row.along(2)
    small_flat.middle()
    block = gwin_ref.shape[0]
    fin = gwinp.at[d]
    gwin_flat.finish(fin)

    def rows_of(rank):
        return gwinp.at[d, pl.ds(pl.multiple_of(rank * block, block), block)]

    pending = []
    for i, s in enumerate(steps):
        to = mate(s)
        pending.append(put(rows_of(rank_of(to)), slots_ref.at[i], as_.at[i], ar.at[i], to))
    dxn_row.along(3, row_ref)

    def norm_step(i, carry):
        r = pl.ds(pl.multiple_of(i * 16, 16), 16)
        x = tok_ref[0, r, :].astype(f32)
        scale = lax.rsqrt(jnp.sum(x * x, axis=1, keepdims=True) * (1.0 / model) + EPS)
        dxn = row_ref[r, :]
        inner = dxn * gains_ref[...]
        dot = jnp.sum(inner * x, axis=1, keepdims=True) * (1.0 / model)
        dxx = scale * inner - x * (scale * scale * scale * dot)
        gtok_ref[r, :] = (up_ref[0, r, :].astype(f32) + dxx).astype(bf16)
        gain = dxn * (x * scale)
        return carry + gain[0:8] + gain[8:16]

    dgain = lax.fori_loop(0, length // 16, norm_step, jnp.zeros((8, model), f32))
    dgain = jnp.sum(dgain, axis=0, keepdims=True)
    seen = jnp.sum(stat_ref[0:1, :], axis=1, keepdims=True)
    peak = jnp.max(stat_ref[1:2, :], axis=1, keepdims=True)
    lane1 = lax.broadcasted_iota(jnp.int32, (1, 128), 1)
    for q in range(4):
        pairs_ref[q] = jnp.zeros((8, 128), f32)
        for g in range(4):
            at = g * 512 + q * 128
            pairs_ref[q, g:g + 1, :] = dgain[:, at:at + 128]
        pairs_ref[q, 4:5, :] = jnp.where(lane1 == 0, seen, jnp.where(lane1 == 1, peak, 0.0))
    for i, s in enumerate(steps):
        to = mate(s)
        put(pairs_ref.at[rank_of(to) // 2], near_ref.at[i], ns.at[i], nr.at[i], to)
    row8 = lax.broadcasted_iota(jnp.int32, (8, 128), 0)
    lane8 = lax.broadcasted_iota(jnp.int32, (8, 128), 1)
    top = (row8 == 4) & (lane8 == 1)

    def join(a, b):
        return jnp.where(top, jnp.maximum(a, b), a + b)

    small_flat.finish(small_ref)
    value = pairs_ref[j // 2]
    for i, s in enumerate(steps):
        landed(near_ref.at[i], nr.at[i], mate(s, -1))
        value = join(value, near_ref[i])
    sum_ref[...] = value
    for i, to in enumerate(planes):
        put(sum_ref, far_ref.at[i], fs.at[i], fr.at[i], to)

    def settle(rank, source):
        for s in range(2):
            for g in range(4):
                at = s * width * 8 + g * 1024
                gwin_ref[:, pl.ds(pl.multiple_of(at + rank * 128, 128), 128)] = source[:, s * width + g * 128:s * width + (g + 1) * 128]

    settle(j, rows_of(j))
    for i, s in enumerate(steps):
        src = mate(s, -1)
        landed(slots_ref.at[i], ar.at[i], src)
        settle(rank_of(src), slots_ref.at[i])
    for i, to in enumerate(planes):
        landed(far_ref.at[i], fr.at[i], to)
        value = join(value, far_ref[i])
    tiny_ref[...] = value
    for i, to in enumerate(planes):
        sent(sum_ref, fs.at[i], to)
    for i, s in enumerate(steps):
        sent(near_ref.at[i], ns.at[i], mate(s))
    for copy in pending:
        copy.wait_send()
    for flat in (gwin_flat, gwout_flat, small_flat):
        flat.close()


def k3(part, stat, smalls, vecs, gains, gwdt, masks, tokens, upstream, m, mt, dg, dv, slope, u, vt, xnt, win, wout, ups):
    like = jax.ShapeDtypeStruct
    length, model = tokens.shape[1:]
    count, channels = m.shape
    tiles = channels // 128
    here = pl.BlockSpec(memory_space=pltpu.VMEM)
    far = pl.BlockSpec(memory_space=pl.ANY)
    dma = lambda n: pltpu.SemaphoreType.DMA((n,))
    own_d = model // 32
    packed = part.shape[0]
    return pl.pallas_call(
        k3_kernel,
        out_shape=(
            like((length, model), bf16),
            like((length, model), bf16),
            like((own_d, 16 * channels), bf16),
            like((128, model), f32),
            like((160, 384), f32),
            like((8, 128), f32),
        ),
        in_specs=[here] * 9 + [far] * 11,
        out_specs=(here,) * 6,
        scratch_shapes=[
            pltpu.VMEM((2, 4, length, model), bf16),
            pltpu.VMEM((2, 4, length, model), bf16),
            pltpu.VMEM((4, 512, 2 * channels), bf16),
            pltpu.VMEM((4, 128, model), bf16),
            pltpu.VMEM((4, 160, 384), f32),
            pltpu.VMEM((count, channels), bf16),
            pltpu.VMEM((channels, count), bf16),
            pltpu.VMEM((count, 2 * channels), bf16),
            pltpu.VMEM((tiles, count + 32, 128), f32),
            pltpu.VMEM((tiles, count, 128), f32),
            pltpu.VMEM(u.shape, f32),
            pltpu.VMEM((model, count), bf16),
            pltpu.VMEM((count, 256), bf16),
            pltpu.VMEM((7, own_d, 2 * channels), bf16),
            pltpu.VMEM((length, model), f32),
            pltpu.VMEM((7, 8, 128), f32),
            pltpu.VMEM((4, 8, 128), f32),
            pltpu.VMEM((8, 128), f32),
            pltpu.VMEM((3, 8, 128), f32),
            dma(11), dma(7), dma(7), dma(7), dma(7), dma(3), dma(3),
            pltpu.VMEM((packed, 128), f32),
        ] + [pltpu.VMEM((packed // 2, 128), f32)] * 6 + [dma(PIECES) for _ in range(8)]
        + row_scratch(length, model) * 2
        + flat_scratch(512, 2 * channels, bf16) + flat_scratch(128, model, bf16) + flat_scratch(160, 384, f32),
        compiler_params=pltpu.CompilerParams(collective_id=1, has_side_effects=True, vmem_limit_bytes=63400000),
    )(part, stat, smalls, vecs, gains, gwdt, masks, tokens, upstream, m, mt, dg, dv, slope, u, vt, xnt, win, wout, ups)

def masks(lengths, count):
    ends = jnp.cumsum(lengths, axis=1)
    places = jnp.arange(count, dtype=jnp.int32)
    segment = jnp.sum((places[:, None, None] >= ends[None, :, :]).astype(jnp.int32), axis=2)
    same = []
    for offset in range(1, 4):
        before = jnp.pad(segment, ((offset, 0), (0, 0)), constant_values=-1)[:count]
        same.append((before == segment).astype(f32))
    return same, (segment < DOCS).astype(f32)


def columns(weights, ways):
    rows, total = weights.shape
    return weights.reshape(rows, 2, total // (2 * ways * 128), ways, 128)


def on_device(tokens, lengths, gain, w_in, conv_w, conv_b, w_x, w_dt, dt_bias, skip, w_out, grad_out):
    ways = lax.axis_size("core") * lax.axis_size("z")
    groups = lax.axis_size("dp")
    length, model = tokens.shape[1:]
    own_d = w_in.shape[0]
    own_e = conv_w.shape[0]
    inner = w_in.shape[1] // 2
    channels = inner // ways
    rank = w_dt.shape[1]
    states = (w_x.shape[1] - rank) // 2
    cols = w_in.reshape(own_d, 2, groups, ways, own_e).transpose(3, 0, 1, 2, 4).reshape(ways, own_d, 2 * channels)
    cols = lax.all_to_all(cols, TP, split_axis=0, concat_axis=0, tiled=True)
    win = lax.all_gather(cols, "dp", axis=0, tiled=True).reshape(model, 2 * channels)
    small = jnp.concatenate([w_x, w_dt, conv_w, conv_b[:, None], dt_bias[:, None], skip[:, None]], axis=1)
    small_width = small.shape[1]
    small = lax.all_gather(small, "dp", axis=0, tiled=True)
    wx = small[:, :rank + 2 * states]
    wdt = small[:, rank + 2 * states:2 * rank + 2 * states]
    rest = small[:, 2 * rank + 2 * states:].astype(f32)
    taps, bias, dtb, skips = rest[:, :4], rest[:, 4], rest[:, 5], rest[:, 6]
    wout = lax.all_gather(w_out, "dp", axis=0, tiled=True)
    gains = lax.all_gather(gain, ALL, axis=0, tiled=True).astype(f32)
    x = tokens[0].astype(f32)
    scale = lax.rsqrt(jnp.mean(x * x, axis=1, keepdims=True) + EPS)
    xn = (x * scale * gains).astype(bf16)
    xns = lax.all_gather(xn, TP, axis=0, tiled=True)
    ups = lax.all_gather(grad_out[0], TP, axis=0, tiled=True)
    lens = lax.all_gather(lengths, TP, axis=0, tiled=True)
    rows = lens.shape[0]
    tall = rows * length

    def time_major(a):
        return a.reshape(rows, length, -1).transpose(1, 0, 2).reshape(tall, -1)

    def row_major(a):
        return a.reshape(length, rows, -1).transpose(1, 0, 2).reshape(tall, -1)

    same, live = masks(lens, length)
    zz = time_major(jnp.dot(xns, win, preferred_element_type=f32))
    u = zz[:, :channels].reshape(length, rows, channels)
    g = zz[:, channels:]
    c = bias + taps[:, 3] * u
    shifted = []
    for offset in range(1, 4):
        earlier = jnp.pad(u, ((offset, 0), (0, 0), (0, 0)))[:length] * same[offset - 1][:, :, None]
        shifted.append(earlier)
        c = c + taps[:, 3 - offset] * earlier
    sig = jax.nn.sigmoid(c)
    v16 = (c * sig).astype(bf16).reshape(tall, channels)
    v = v16.astype(f32)
    p = lax.psum(jnp.dot(v16, wx, preferred_element_type=f32), TP)
    dl = p[:, :rank].astype(bf16)
    kq = p[:, rank:]
    dims_cols = (((1,), (1,)), ((), ()))
    dims_rows = (((0,), (0,)), ((), ()))
    pre = lax.dot_general(dl, wdt, dims_cols, preferred_element_type=f32) + dtb
    dm = time_major(lax.dot_general(ups, wout, dims_cols, preferred_element_type=f32))
    flags = jnp.pad(jnp.stack([same[0].reshape(tall), live.reshape(tall)], axis=1), ((0, 0), (0, 126)))
    hi = kq.astype(bf16)
    mid = (kq - hi.astype(f32)).astype(bf16)
    low = (kq - hi.astype(f32) - mid.astype(f32)).astype(bf16)
    kq3 = jnp.concatenate([hi, mid, low], axis=1)
    keys = kq[:, :states]
    sk = jnp.broadcast_to(jnp.sum(keys * keys, axis=1, keepdims=True), (tall, 8))
    m, dg, dpre, dv, dkq, stats = mixer(flags, kq3, sk, pre, v, g, dm, skips[None], states=states, width=256, unroll=4)
    stats = stats.transpose(1, 2, 0, 3).reshape(3, 8, channels)
    dskip = jnp.sum(stats[0], axis=0)
    total = lax.psum(jnp.sum(stats[1]), ALL)
    peak = lax.pmax(jnp.max(stats[2]), ALL)
    beta_mean = total / float(groups * ways * length * inner)
    m16 = row_major(m).astype(bf16)
    out = jnp.dot(m16, wout, preferred_element_type=f32).astype(bf16)
    out = lax.psum_scatter(out, TP, scatter_dimension=0, tiled=True)
    block_out = (x + out.astype(f32)).astype(bf16)
    grad_wout = lax.dot_general(m16, ups, dims_rows, preferred_element_type=f32).astype(bf16)
    grad_wout = lax.psum_scatter(grad_wout, "dp", scatter_dimension=0, tiled=True)
    dpre16 = dpre.astype(bf16)
    grad_dtb = jnp.sum(dpre16.astype(f32), axis=0)
    grad_wdt = lax.dot_general(dpre16, dl, dims_rows, preferred_element_type=f32)
    ddl = jnp.dot(dpre16, wdt, preferred_element_type=f32)
    dkq = dkq[:, :2 * states] + dkq[:, 2 * states:2 * states + 1] * jnp.pad(keys, ((0, 0), (0, states)))
    dp16 = lax.psum(jnp.concatenate([ddl, dkq], axis=1), TP).astype(bf16)
    grad_wx = lax.dot_general(v16, dp16, dims_rows, preferred_element_type=f32)
    dvt = dv + lax.dot_general(dp16, wx, dims_cols, preferred_element_type=f32)
    dc = (dvt * (sig.reshape(tall, channels) * (1.0 + c.reshape(tall, channels) * (1.0 - sig.reshape(tall, channels))))).reshape(length, rows, channels)
    du = taps[:, 3] * dc
    grad_taps = [jnp.sum(dc * u, axis=(0, 1))]
    for offset in range(1, 4):
        grad_taps.append(jnp.sum(dc * shifted[offset - 1], axis=(0, 1)))
        du = du + taps[:, 3 - offset] * jnp.pad((dc * same[offset - 1][:, :, None])[offset:], ((0, offset), (0, 0), (0, 0)))
    grad_conv = jnp.stack(grad_taps[::-1] + [jnp.sum(dc, axis=(0, 1)), grad_dtb, dskip], axis=1)
    dz = row_major(jnp.concatenate([du.reshape(tall, channels), dg], axis=1)).astype(bf16)
    gwin = lax.dot_general(xns, dz, dims_rows, preferred_element_type=f32).astype(bf16)
    gwin = lax.psum_scatter(gwin, "dp", scatter_dimension=0, tiled=True)
    gwin = lax.all_to_all(gwin.reshape(ways, own_d, 2 * channels), TP, split_axis=0, concat_axis=0, tiled=True)
    grad_win = gwin.reshape(ways, own_d, 2, groups, own_e).transpose(1, 2, 3, 0, 4).reshape(own_d, 2 * inner).astype(f32)
    dxn = lax.dot_general(dz, win, dims_cols, preferred_element_type=f32).astype(bf16)
    dxn = lax.psum_scatter(dxn, TP, scatter_dimension=0, tiled=True).astype(f32)
    small_grad = lax.psum_scatter(jnp.concatenate([grad_wx, grad_wdt, grad_conv], axis=1), "dp", scatter_dimension=0, tiled=True)
    inner_grad = dxn * gains
    dxx = scale * inner_grad - x * (scale * scale * scale) * (jnp.sum(inner_grad * x, axis=1, keepdims=True) / model)
    grad_tokens = (grad_out[0].astype(f32) + dxx).astype(bf16)
    grad_gain = lax.psum_scatter(jnp.sum(dxn * x * scale, axis=0), ALL, scatter_dimension=0, tiled=True)
    at = rank + 2 * states
    return (
        block_out[None],
        grad_tokens[None],
        grad_gain,
        grad_win,
        small_grad[:, at + rank:at + rank + 4],
        small_grad[:, at + rank + 4],
        small_grad[:, :at],
        small_grad[:, at:at + rank],
        small_grad[:, at + rank + 5],
        small_grad[:, at + rank + 6],
        grad_wout.astype(f32),
        beta_mean,
        peak,
    )


def prepare(gain, lengths, w_in, conv_w, conv_b, w_x, w_dt, dt_bias, skip, ways, groups):
    own_d, own_e = w_in.shape[0], conv_w.shape[0]
    channels = own_e * groups
    cols = w_in.reshape(own_d, 2, groups, ways, own_e).transpose(3, 0, 1, 2, 4).reshape(ways, own_d, 2 * channels)
    small = jnp.concatenate([jnp.pad(w_x, ((0, 0), (0, 256 - w_x.shape[1]))), w_dt], axis=1)
    top = jnp.concatenate([jnp.tile(gain.astype(f32), 2)[None], jnp.pad(lengths.astype(f32), ((0, 0), (0, 123))), jnp.zeros((6, 128), f32)])
    low = jnp.concatenate([conv_w.astype(f32).T, conv_b.astype(f32)[None], dt_bias.astype(f32)[None], skip.astype(f32)[None], jnp.zeros((1, own_e), f32)])
    return cols, small, jnp.concatenate([top, low])


def on_device_direct(tokens, lengths, gain, w_in, conv_w, conv_b, w_x, w_dt, dt_bias, skip, w_out, grad_out):
    groups, ways = 4, 8
    length, model = tokens.shape[1:]
    own_d = w_in.shape[0]
    own_e = conv_w.shape[0]
    inner = w_in.shape[1] // 2
    channels = inner // ways
    rank = w_dt.shape[1]
    states = (w_x.shape[1] - rank) // 2
    cols, small, meta = prepare(gain, lengths, w_in, conv_w, conv_b, w_x, w_dt, dt_bias, skip, ways, groups)
    xnt, ups, win, wout, smalls, vecs, gains, masks, live, u, g, v, vt, slope, dl, kq = k1(tokens, grad_out, cols, w_out, small, meta)
    m, mt, dg, gwdt, dv, part, stat = k2(dl, kq, smalls, vecs, masks, live, v, g, ups, wout, states)
    block_out, grad_tokens, grad_win, grad_wout, small_grad, tiny = k3(
        part, stat, smalls, vecs, gains, gwdt, masks, tokens, grad_out, m, mt, dg, dv, slope, u, vt, xnt,
        win.reshape(groups, ways * own_d, 2 * channels), wout.reshape(groups, own_e, model), ups.reshape(2, 4, length, model))
    d, c, z = place()
    grad_gain = lax.dynamic_slice(tiny, (d, lax.rem(z, 2) * own_d), (1, own_d))[0]
    vectors = small_grad[own_e:own_e + 8, :own_e]
    return (
        block_out[None],
        grad_tokens[None],
        grad_gain,
        grad_win.astype(f32),
        vectors[:4].T,
        vectors[4],
        small_grad[:own_e, :rank + 2 * states],
        small_grad[:own_e, 256:],
        vectors[5],
        vectors[6],
        grad_wout,
        tiny[4, 0] / float(groups * ways * length * inner),
        tiny[4, 1],
    )


def on_device_any(*args):
    if lax.axis_size("dp") == 4 and lax.axis_size("z") == 4:
        return on_device_direct(*args)
    return on_device(*args)


def solution(mesh):
    wide, narrow = mesh.devices.shape
    fine = Mesh(mesh.devices.reshape(wide // 2, 2, narrow), ALL)
    cut = (P(ALL, None), P(ALL))
    in_specs = (P(ALL, None, None), cut[0], cut[1], cut[0], cut[0], cut[1], cut[0], cut[0], cut[1], cut[1], cut[0], P(ALL, None, None))
    out_specs = (P(ALL, None, None), P(ALL, None, None), cut[1], cut[0], cut[0], cut[1], cut[0], cut[0], cut[1], cut[1], cut[0], P(), P())
    return jax.shard_map(on_device_any, mesh=fine, in_specs=in_specs, out_specs=out_specs, check_vma=False)
```

```python
import functools
import jax, jax.numpy as jnp
from jax import lax
from jax.experimental import pallas as pl
from jax.experimental.pallas import tpu as pltpu
from jax.sharding import Mesh, PartitionSpec as P

DOCS = 4
EPS = 1e-05
ALL = ("dp", "core", "z")
TP = ("core", "z")

f32 = jnp.float32
bf16 = jnp.bfloat16

def fold(x):
    total = x[:, :128]
    for at in range(128, x.shape[1], 128):
        total = total + x[:, at:at+128]
    return total

def mixer_kernel(states, unroll, chunk, flags_ref, kq3_ref, sk_ref, pre_ref, v_ref, g_ref, dm_ref, skip_ref,
                 m_ref, dg_ref, dpre_ref, dv_ref, dkq_ref, stat_ref, s_ref, h_ref, rate_ref, rv_ref, kb_ref, drr_ref):
    rows = pre_ref.shape[0]
    width = pre_ref.shape[1]
    steps = rows // 8
    wide = states * 128
    spread_rows = kq3_ref.shape[1]
    def spread(i, c):
        r = pl.ds(pl.multiple_of(i * chunk, chunk), chunk)
        left = kq3_ref[r, :]
        for part in range(0, 2 * wide, 512):
            ids = lax.broadcasted_iota(jnp.int32, (spread_rows, 512), 0) % (2 * states)
            col = lax.broadcasted_iota(jnp.int32, (spread_rows, 512), 1) // 128 + part // 128
            hot = jnp.where(ids == col, 1.0, 0.0).astype(bf16)
            kb_ref[r, part:part+512] = jnp.dot(left, hot, preferred_element_type=f32)
        return c
    lax.fori_loop(0, rows // chunk, spread, 0)

    def before(i, c):
        r = pl.ds(pl.multiple_of(i * 64, 64), 64)
        live = flags_ref[r, 1:2]
        beta = jax.nn.sigmoid(pre_ref[r, :])
        part = 1.0 / (1.0 + beta * sk_ref[r, 0:1])
        rate = beta * part
        rate_ref[r, :] = rate
        v = v_ref[r, :]
        rv_ref[r, :] = rate * v
        dpre_ref[r, :] = part * part * beta * (1.0 - beta)
        g = g_ref[r, :]
        sg = jax.nn.sigmoid(g)
        dm = dm_ref[r, :] * live
        dv_ref[r, :] = dm * (g * sg)
        dg_ref[r, :] = dm * (sg * (1.0 + g * (1.0 - sg)))
        return c
    lax.fori_loop(0, rows // 64, before, 0)

    s_ref[0, 0] = jnp.zeros(s_ref.shape[2:], f32)

    group = unroll
    tile = lambda x: jnp.concatenate([x] * (width // 128), axis=1)
    span = group * 8
    at = [slice(j * 8, j * 8 + 8) for j in range(group)]
    def view(ref, i):
        return ref.at[pl.ds(pl.multiple_of(i * span, span), span)]

    def forward(i, carry):
        flags, rates, rvs, vs, kbs, ms = [view(x, i) for x in (flags_ref, rate_ref, rv_ref, v_ref, kb_ref, m_ref)]
        keep = [jnp.broadcast_to(flags[r, 0:1], (8, 128)) for r in at]
        rate = [rates[r, :] for r in at]
        rv = [rvs[r, :] for r in at]
        y = [skip_ref[...] * vs[r, :] for r in at]
        for n in range(states):
            state = s_ref[i, 0, n]
            for j, r in enumerate(at):
                kb = kbs[r, n*128:(n+1)*128]
                qb = kbs[r, wide+n*128:wide+(n+1)*128]
                state = (tile(keep[j]) - rate[j] * tile(kb * kb * keep[j])) * state + rv[j] * tile(kb)
                if j < group - 1:
                    s_ref[i, j + 1, n] = state
                else:
                    s_ref[i + 1, 0, n] = state
                y[j] = y[j] + state * tile(qb)
        for j, r in enumerate(at):
            ms[r, :] = y[j]
        return carry

    lax.fori_loop(0, steps // group, forward, 0)
    h_ref[...] = jnp.zeros_like(h_ref)

    def backward(step, carry):
        i = steps // group - 1 - step
        flags, rates, rvs, vs, kbs, dvs, dpres, drrs = [view(x, i) for x in (flags_ref, rate_ref, rv_ref, v_ref, kb_ref, dv_ref, dpre_ref, drr_ref)]
        keep = [jnp.broadcast_to(flags[r, 0:1], (8, 128)) for r in at]
        rate = [rates[r, :] for r in at]
        rv = [rvs[r, :] for r in at]
        dy = [dvs[r, :] for r in at]
        hk = [jnp.zeros((8, width), f32) for r in at]
        hs2 = [jnp.zeros((8, width), f32) for r in at]
        for n in range(states):
            ah = h_ref[n]
            after_ = s_ref[i + 1, 0, n]
            for j in range(group - 1, -1, -1):
                r = at[j]
                kb = kbs[r, n*128:(n+1)*128]
                qb = kbs[r, wide+n*128:wide+(n+1)*128]
                kk = kb * keep[j]
                held = tile(kb * kk)
                h = dy[j] * tile(qb) + ah
                prior = s_ref[i, j, n]
                hs = h * prior
                hk[j] = hk[j] + h * tile(kb)
                hs2[j] = hs2[j] + hs * held
                kbs[r, n*128:(n+1)*128] = fold(h * rv[j]) - 2.0 * kk * fold(hs * rate[j])
                kbs[r, wide+n*128:wide+(n+1)*128] = fold(dy[j] * after_)
                after_ = prior
                ah = (tile(keep[j]) - rate[j] * held) * h
            h_ref[n] = ah
        for j, r in enumerate(at):
            v = vs[r, :]
            drate = v * hk[j] - hs2[j]
            drrs[r, :] = fold(drate * rate[j] * rate[j]) * (-2.0)
            dpres[r, :] = drate * dpres[r, :]
            dvs[r, :] = rate[j] * hk[j] + skip_ref[...] * dy[j]
            stat_ref[0, 0] += dy[j] * v
        return carry

    stat_ref[...] = jnp.zeros_like(stat_ref)
    lax.fori_loop(0, steps // group, backward, 0)

    first = pl.program_id(0) == 0
    def gather(i, c):
        r = pl.ds(pl.multiple_of(i * chunk, chunk), chunk)
        total = jnp.zeros((chunk, 128), f32)
        for part in range(0, 2 * wide, 512):
            row = lax.broadcasted_iota(jnp.int32, (512, 128), 0) // 128 + part // 128
            col = lax.broadcasted_iota(jnp.int32, (512, 128), 1)
            hot = jnp.where(row == col, 1.0, 0.0).astype(bf16)
            total += jnp.dot(kb_ref[r, part:part+512].astype(bf16), hot, preferred_element_type=f32)
        col = lax.broadcasted_iota(jnp.int32, (128, 128), 1)
        hot = jnp.where(col == 2 * states, 1.0, 0.0).astype(bf16)
        total += jnp.dot(drr_ref[r, :].astype(bf16), hot, preferred_element_type=f32)
        dkq_ref[r, :] = jnp.where(first, total, dkq_ref[r, :] + total)
        return c
    lax.fori_loop(0, rows // chunk, gather, 0)

    def after(i, c):
        r = pl.ds(pl.multiple_of(i * 64, 64), 64)
        live = flags_ref[r, 1:2]
        y = m_ref[r, :]
        g = g_ref[r, :]
        m_ref[r, :] = y * (g * jax.nn.sigmoid(g)) * live
        dg_ref[r, :] = y * dg_ref[r, :]
        shown = (jax.nn.sigmoid(pre_ref[r, :]) * live).reshape(8, 8, width)
        stat_ref[0, 1] += jnp.sum(shown, axis=0)
        stat_ref[0, 2] = jnp.maximum(stat_ref[0, 2], jnp.max(shown, axis=0))
        return c
    lax.fori_loop(0, rows // 64, after, 0)

def mixer(flags, kq3, sk, pre, v, g, dm, skip, states=16, width=256, unroll=1):
    rows, total = pre.shape
    steps = rows // 8
    tiles = total // width
    big = jax.ShapeDtypeStruct((rows, total), f32)
    cut = pl.BlockSpec((rows, width), lambda h: (0, h))
    whole = lambda a: pl.BlockSpec(a.shape, lambda h: (0,) * a.ndim)
    return pl.pallas_call(
        functools.partial(mixer_kernel, states, unroll, min(256, rows)),
        grid=(tiles,),
        out_shape=(big, big, big, big, jax.ShapeDtypeStruct((rows, 128), f32), jax.ShapeDtypeStruct((tiles, 3, 8, width), f32)),
        in_specs=[whole(flags), whole(kq3), whole(sk), cut, cut, cut, cut, pl.BlockSpec((1, width), lambda h: (0, h))],
        out_specs=(cut, cut, cut, cut, pl.BlockSpec((rows, 128), lambda h: (0, 0)), pl.BlockSpec((1, 3, 8, width), lambda h: (h, 0, 0, 0))),
        scratch_shapes=[pltpu.VMEM((steps//unroll+1, unroll, states, 8, width), f32), pltpu.VMEM((states, 8, width), f32)] + [pltpu.VMEM((rows, width), f32)]*2
          + [pltpu.VMEM((rows, 2*states*128), f32), pltpu.VMEM((rows, 128), f32)],
        compiler_params=pltpu.CompilerParams(vmem_limit_bytes=60*1024*1024),
    )(flags, kq3, sk, pre, v, g, dm, skip)


MESH = pl.DeviceIdType.MESH


def flip(value, bit):
    return value + bit * (1 - 2 * ((value // bit) % 2))


def place():
    d, c, z = lax.axis_index("dp"), lax.axis_index("core"), lax.axis_index("z")
    return d, c, z


def put(src, dst, send, recv, device):
    copy = pltpu.make_async_remote_copy(src_ref=src, dst_ref=dst, send_sem=send, recv_sem=recv, device_id=device, device_id_type=MESH)
    copy.start()
    return copy


def landed(slot, sem, device):
    pltpu.make_async_remote_copy(src_ref=slot, dst_ref=slot, send_sem=sem, recv_sem=sem, device_id=device, device_id_type=MESH).wait_recv()


def sent(slot, sem, device):
    pltpu.make_async_remote_copy(src_ref=slot, dst_ref=slot, send_sem=sem, recv_sem=sem, device_id=device, device_id_type=MESH).wait_send()


def greet(devices):
    barrier = pltpu.get_barrier_semaphore()
    for device in devices:
        pl.semaphore_signal(barrier, inc=1, device_id=device, device_id_type=MESH)
    pl.semaphore_wait(barrier, len(devices))


def mates():
    return [(a, k) for k in (0, 1, 3, 2) for a in (1, 0) if (a, k) != (0, 0)]


def mate(step, sign=1):
    d, c, z = place()
    a, k = step
    return d, (flip(c, 1) if a else c), lax.rem(z + sign * k + 4, 4)


def rank_of(device):
    return device[1] * 4 + device[2]


PIECES = 4


def k1_kernel(tok_ref, up_ref, w_ref, wout_ref, small_ref, gain_ref, lens_ref, convw_ref, vec_ref,
              xnt_out, ups_ref, win_out, wouts_ref, smalls_ref, vecs_ref, gains_ref, masks_out, live_out,
              u_out, g_out, v_out, vt_out, slope_out, dl_ref, kq_ref,
              masks_ref, live_ref, u_ref, g_ref, v_ref, vt_ref, slope_ref, save_sem, cols_ref, meta_ref,
              xs_ref, xn_ref, xnt_ref, win_ref, metas_ref, part_ref, out_ref, sib_ref, base_ref, left_ref, right_ref, tor_ref, tol_ref,
              own_sem, ms, mr, qs, qr, xls, xlr, xrs, xrr, xcs, xcr, as_, ar, ps, pr, rs, rr, ws, wr, ts, tr, tls, tlr, trs, trr, tos, tor):
    d, c, z = place()
    j = c * 4 + z
    dx, dy, dd = flip(d, 1), flip(d, 2), flip(flip(d, 1), 2)
    xn, yn, dn = (dx, c, z), (dy, c, z), (dd, c, z)
    sib = (d, flip(c, 1), z)
    left = (d, c, lax.rem(z + 3, 4))
    right = (d, c, lax.rem(z + 1, 4))
    steps = mates()
    length = tok_ref.shape[1]
    model = tok_ref.shape[2]
    depth = cols_ref.shape[1]
    for rank in range(8):
        for n in range(8):
            cols_ref[rank, :, n * 128:(n + 1) * 128] = w_ref[:, (n * 8 + rank) * 128:(n * 8 + rank + 1) * 128]
    meta_ref[...] = jnp.zeros_like(meta_ref)
    meta_ref[0:1, 0:depth] = gain_ref[...].astype(f32)
    meta_ref[0:1, depth:2 * depth] = gain_ref[...].astype(f32)
    meta_ref[1:2, 0:5] = lens_ref[...].astype(f32)
    meta_ref[8:12, :] = convw_ref[...].astype(f32)
    meta_ref[12:15, :] = vec_ref[...].astype(f32)
    greet([mate(s) for s in steps] + [xn, yn, dn])
    tiles = u_ref.shape[0]
    width = tiles * 128
    count = g_ref.shape[1]

    def rows(rank):
        return pl.ds(pl.multiple_of(rank * length, length), length)

    def block(group, rank):
        return pl.ds(pl.multiple_of((group * 8 + rank) * depth, depth), depth)

    own_e = wout_ref.shape[0]

    def part_e(group, start=0, size=own_e):
        return pl.ds(pl.multiple_of(group * own_e + start, 16), size)

    own = [
        pltpu.make_async_copy(tok_ref.at[0], xs_ref.at[rows(j)], own_sem.at[0]),
        pltpu.make_async_copy(up_ref.at[0], ups_ref.at[rows(j)], own_sem.at[1]),
        pltpu.make_async_copy(cols_ref.at[j], win_ref.at[block(d, j)], own_sem.at[2]),
        pltpu.make_async_copy(wout_ref, wouts_ref.at[part_e(d)], own_sem.at[3]),
        pltpu.make_async_copy(small_ref, smalls_ref.at[part_e(d)], own_sem.at[4]),
        pltpu.make_async_copy(meta_ref, metas_ref.at[d, j], own_sem.at[5]),
    ]
    for copy in own:
        copy.start()
    pending = []
    for i, s in enumerate(steps):
        to = mate(s)
        pending.append(put(meta_ref, metas_ref.at[d, j], ms.at[i], mr.at[i], to))
    for i, s in enumerate(steps):
        to = mate(s)
        pending.append(put(cols_ref.at[rank_of(to)], win_ref.at[block(d, j)], as_.at[i], ar.at[i], to))
    for i, to in enumerate((xn, yn, dn)):
        pending.append(put(small_ref, smalls_ref.at[part_e(d)], ps.at[16 + i], pr.at[16 + i], to))
    halves = own_e // 2
    pending.append(put(wout_ref, wouts_ref.at[part_e(d)], ws.at[0], wr.at[0], xn))
    pending.append(put(wout_ref, wouts_ref.at[part_e(d)], ws.at[1], wr.at[1], yn))
    own[2].wait()
    slot = win_ref.at[block(d, j)]
    pending.append(put(slot, slot, ps.at[7], pr.at[7], xn))
    pending.append(put(slot, slot, ps.at[15], pr.at[15], yn))

    def row_start(ref, out, base):
        pending.append(put(ref.at[0], out.at[rows(j)], xcs.at[base + z], xcr.at[base + z], sib))

        @pl.when(z < 3)
        def _():
            put(ref.at[0], out.at[rows(j)], xls.at[base], xlr.at[base], right)

        @pl.when(z > 0)
        def _():
            put(ref.at[0], out.at[rows(j)], xrs.at[base], xrr.at[base], left)

    def row_hop(out, base, i, then=None):
        @pl.when(z > i)
        def _():
            at = z - 1 - i
            slot = out.at[rows(c * 4 + at)]
            landed(slot, xlr.at[base + i], left)
            if i < 2:
                @pl.when(z < 3)
                def _():
                    put(slot, slot, xls.at[base + i + 1], xlr.at[base + i + 1], right)
            put(slot, slot, xcs.at[base + at], xcr.at[base + at], sib)
            if then is not None:
                then(c * 4 + at)

        @pl.when(z < 3 - i)
        def _():
            at = z + 1 + i
            slot = out.at[rows(c * 4 + at)]
            landed(slot, xrr.at[base + i], right)
            if i < 2:
                @pl.when(z > 0)
                def _():
                    put(slot, slot, xrs.at[base + i + 1], xrr.at[base + i + 1], left)
            put(slot, slot, xcs.at[base + at], xcr.at[base + at], sib)
            if then is not None:
                then(c * 4 + at)

    def row_end(out, base):
        for i in range(3):
            @pl.when((z < 3) & (z >= i))
            def _():
                sent(out.at[rows(j)], xls.at[base + i], right)

            @pl.when((z > 0) & (z <= 3 - i))
            def _():
                sent(out.at[rows(j)], xrs.at[base + i], left)
        for at in range(4):
            @pl.when(z != at)
            def _():
                sent(out.at[rows(j)], xcs.at[base + at], sib)

    own[5].wait()
    for i, s in enumerate(steps):
        landed(metas_ref.at[d, rank_of(mate(s, -1))], mr.at[i], xn)
    for i, to in enumerate((xn, yn, dn)):
        pending.append(put(metas_ref.at[d], metas_ref.at[d], qs.at[i], qr.at[i], to))
    slots = {7: j}
    for i, s in enumerate(steps):
        slots[i] = rank_of(mate(s, -1))
    order = [7] + list(range(7))

    def pass_on(i):
        src = mate(steps[i], -1)
        slot = win_ref.at[block(d, slots[i])]
        landed(slot, ar.at[i], src)
        pending.append(put(slot, slot, ps.at[i], pr.at[i], xn))
        pending.append(put(slot, slot, ps.at[8 + i], pr.at[8 + i], yn))

    def relay(k):
        i = order[k]
        slot = win_ref.at[block(dx, slots[i])]
        landed(slot, pr.at[i], xn)
        if k % 2 == 0:
            pending.append(put(slot, slot, rs.at[k // 2], rr.at[k // 2], yn))
        slot = win_ref.at[block(dy, slots[i])]
        landed(slot, pr.at[8 + i], yn)
        if k % 2 == 1:
            pending.append(put(slot, slot, rs.at[4 + k // 2], rr.at[4 + k // 2], xn))

    pass_on(0)
    for i, (to, at) in enumerate(((xn, dx), (yn, dy), (dn, dd))):
        landed(metas_ref.at[at], qr.at[i], to)
    lens = jnp.concatenate([metas_ref[d, r, 1:2, :] for r in range(8)], axis=0)
    ends = []
    last = jnp.zeros((8, 1), f32)
    for i in range(5):
        last = last + lens[:, i:i + 1]
        ends.append(jnp.broadcast_to(last, (8, 128)))

    def mask_step(t, carry):
        here = t.astype(f32)

        def segment(at):
            total = jnp.zeros((8, 128), f32)
            for end in ends:
                total = total + jnp.where(end <= at, 1.0, 0.0)
            return total

        now = segment(here)
        r = pl.ds(pl.multiple_of(t * 8, 8), 8)
        for o in range(1, 4):
            same = jnp.where(segment(here - o) == now, 1.0, 0.0)
            masks_ref[o - 1, r, :] = jnp.where(here >= o, same, 0.0)
        live_ref[0, r, :] = jnp.where(now < DOCS, 1.0, 0.0)
        return carry

    lax.fori_loop(0, length, mask_step, 0)
    masks_ref[:, count:, :] = jnp.zeros((3, masks_ref.shape[1] - count, 128), f32)
    lane = lax.broadcasted_iota(jnp.int32, (1, 128), 1)
    for group in range(4):
        for pair in range(4):
            at = group * 512 + pair * 128
            gains_ref[:, at:at + 128] = jnp.where(lane < depth, metas_ref[group, 2 * pair, 0:1, :], metas_ref[group, 2 * pair + 1, 0:1, :])
        vecs_ref[:, group * own_e:(group + 1) * own_e] = metas_ref[group, j, 8:16, :]

    def normalize(rank):
        def body(i, carry):
            r = pl.ds(pl.multiple_of(rank * length + i * 16, 16), 16)
            x = xs_ref[r, :].astype(f32)
            scale = lax.rsqrt(jnp.sum(x * x, axis=1, keepdims=True) * (1.0 / model) + EPS)
            xn_ref[r, :] = (x * scale * gains_ref[...]).astype(bf16)
            return carry

        lax.fori_loop(0, length // 16, body, 0, unroll=4)

    for i in range(1, 4):
        pass_on(i)
    slot = wouts_ref.at[part_e(dx)]
    landed(slot, wr.at[0], xn)
    slot = wouts_ref.at[part_e(dx, 0, halves)]
    pending.append(put(slot, slot, ws.at[2], wr.at[2], yn))
    slot = wouts_ref.at[part_e(dy)]
    landed(slot, wr.at[1], yn)
    slot = wouts_ref.at[part_e(dy, halves, halves)]
    pending.append(put(slot, slot, ws.at[3], wr.at[3], xn))

    row_start(tok_ref, xs_ref, 0)
    for i in range(4, 7):
        pass_on(i)
    own[0].wait()
    normalize(j)
    row_hop(xs_ref, 0, 0, normalize)
    for k in range(4):
        relay(k)
    row_hop(xs_ref, 0, 1, normalize)
    for k in range(4, 8):
        relay(k)
    row_hop(xs_ref, 0, 2, normalize)
    row_start(up_ref, ups_ref, 4)
    for at in range(4):
        rank = flip(c, 1) * 4 + at
        landed(xs_ref.at[rows(rank)], xcr.at[at], sib)
        normalize(rank)
    for k, i in enumerate(order):
        slot = win_ref.at[block(dd, slots[i])]
        if k % 2 == 0:
            landed(slot, rr.at[k // 2], yn)
        else:
            landed(slot, rr.at[4 + k // 2], xn)
    own += [pltpu.make_async_copy(xnt_ref, xnt_out, own_sem.at[6]), pltpu.make_async_copy(win_ref, win_out, own_sem.at[7])]
    own[7].start()
    lead = u_ref.shape[1] - count
    u_ref[:, 0:lead, :] = jnp.zeros((tiles, lead, 128), f32)

    tile = 256

    def spread(out, first, start):
        def body(i, carry):
            product = jnp.dot(xn_ref[...], win_ref[:, pl.ds(pl.multiple_of(start + i * tile, tile), tile)], preferred_element_type=f32)
            for r in range(8):
                for part in range(0, tile, 128):
                    out[i * (tile // 128) + part // 128, pl.ds(first + r, length, stride=8), :] = product[r * length:(r + 1) * length, part:part + 128]
            return carry

        lax.fori_loop(0, width // tile, body, 0)

    spread(u_ref, lead, 0)
    taps = [vecs_ref[o:o + 1, :] for o in range(4)]
    bias = vecs_ref[4:5, :]

    def conv_step(i, carry):
        r = pl.ds(pl.multiple_of(i * 32, 32), 32)
        for n in range(tiles):
            lanes = slice(n * 128, n * 128 + 128)
            total = bias[:, lanes] + taps[3][:, lanes] * u_ref[n, pl.ds(pl.multiple_of(lead + i * 32, 8), 32), :]
            for o in range(1, 4):
                total = total + taps[3 - o][:, lanes] * (u_ref[n, pl.ds(pl.multiple_of(lead + i * 32 - 8 * o, 8), 32), :] * masks_ref[o - 1, r, :])
            sig = jax.nn.sigmoid(total)
            v_ref[n, r, :] = (total * sig).astype(bf16).astype(f32)
            slope_ref[n, r, :] = sig * (1.0 + total * (1.0 - sig))
        return carry

    lax.fori_loop(0, count // 32, conv_step, 0, unroll=2)
    for copy in own[3:5]:
        copy.wait()
    for i, (to, at) in enumerate(((xn, dx), (yn, dy), (dn, dd))):
        landed(smalls_ref.at[part_e(at)], pr.at[16 + i], to)
    quarter = count // 4
    narrow = smalls_ref[:, 128:256].astype(f32)
    packed = jnp.zeros((quarter, 128), f32)
    for b in range(4):
        r = slice(b * quarter, (b + 1) * quarter)
        values = jnp.concatenate([v_ref[n, r, :].astype(bf16) for n in range(tiles)], axis=1)
        part_ref[r, :] = jnp.dot(values, smalls_ref[:, 0:128], preferred_element_type=f32)
        turned = pltpu.roll(narrow, 32 * b, 1) if b else narrow
        packed = packed + jnp.dot(values, turned.astype(bf16), preferred_element_type=f32)
    part_ref[count:count + quarter, :] = packed
    saves = [(u_ref, u_out), (v_ref, v_out), (slope_ref, slope_out), (masks_ref, masks_out), (live_ref, live_out), (g_ref, g_out), (vt_ref, vt_out)]
    saves = [pltpu.make_async_copy(a, b, save_sem.at[i]) for i, (a, b) in enumerate(saves)]
    for copy in saves[:5]:
        copy.start()

    def early():
        row_hop(ups_ref, 4, 0)

    def between():
        spread(g_ref, 0, width)
        saves[5].start()

    def late():
        def turn_x(i, carry):
            part = pl.ds(pl.multiple_of(i * 128, 128), 128)
            for rank in range(8):
                r = slice(rank * length, (rank + 1) * length)
                xnt_ref[part, r] = xn_ref[r, part].T
            return carry

        lax.fori_loop(0, model // 128, turn_x, 0)
        own[6].start()
        row_hop(ups_ref, 4, 1)

        def turn_v(i, carry):
            r = pl.ds(pl.multiple_of(i * 128, 128), 128)
            for n in range(tiles):
                vt_ref[n * 128:(n + 1) * 128, r] = v_ref[n, r, :].T.astype(bf16)
            return carry

        lax.fori_loop(0, count // 128, turn_v, 0)
        saves[6].start()

    line_total(part_ref, out_ref, sib_ref, base_ref, left_ref, right_ref, tor_ref, tol_ref, ts, tr, tls, tlr, trs, trr, tos, tor, early, between, late)
    dl_ref[...] = out_ref[0:count, :].astype(bf16)
    for b in range(4):
        packed = out_ref[count:count + quarter, :]
        kq_ref[b * quarter:(b + 1) * quarter, :] = pltpu.roll(packed, 128 - 32 * b, 1) if b else packed
    row_hop(ups_ref, 4, 2)
    for at in range(4):
        landed(ups_ref.at[rows(flip(c, 1) * 4 + at)], xcr.at[4 + at], sib)
    landed(wouts_ref.at[part_e(dd, 0, halves)], wr.at[2], yn)
    landed(wouts_ref.at[part_e(dd, halves, halves)], wr.at[3], xn)
    row_end(xs_ref, 0)
    row_end(ups_ref, 4)
    own[1].wait()
    for copy in saves:
        copy.wait()
    own[6].wait()
    own[7].wait()
    for copy in pending:
        copy.wait_send()


def line_total(part_ref, out_ref, sib_ref, base_ref, left_ref, right_ref, tor_ref, tol_ref, ss, sr, ls, lr, rs, rr, os_, or_, early, between, late):
    d, c, z = place()
    sib = (d, flip(c, 1), z)
    left = (d, c, lax.rem(z + 3, 4))
    right = (d, c, lax.rem(z + 1, 4))
    rows = part_ref.shape[0] // 2
    piece = rows // PIECES
    mine, theirs = c * rows, flip(c, 1) * rows

    def cut(p):
        return pl.ds(p * piece, piece)

    def far(base, p):
        return pl.ds(pl.multiple_of(base + p * piece, 8), piece)

    for p in range(PIECES):
        put(part_ref.at[far(theirs, p)], sib_ref.at[cut(p)], ss.at[p], sr.at[p], sib)
    for p in range(PIECES):
        landed(sib_ref.at[cut(p)], sr.at[p], sib)
        base_ref[cut(p), :] = part_ref[far(mine, p), :] + sib_ref[cut(p), :]

        @pl.when(z == 0)
        def _():
            put(base_ref.at[cut(p)], left_ref.at[cut(p)], rs.at[p], lr.at[p], right)

        @pl.when(z == 3)
        def _():
            put(base_ref.at[cut(p)], right_ref.at[cut(p)], ls.at[p], rr.at[p], left)

    early()

    def from_left(p):
        landed(left_ref.at[cut(p)], lr.at[p], left)

        @pl.when(z < 3)
        def _():
            tor_ref[cut(p), :] = base_ref[cut(p), :] + left_ref[cut(p), :]
            put(tor_ref.at[cut(p)], left_ref.at[cut(p)], rs.at[p], lr.at[p], right)

    def from_right(p):
        landed(right_ref.at[cut(p)], rr.at[p], right)

        @pl.when(z > 0)
        def _():
            tol_ref[cut(p), :] = base_ref[cut(p), :] + right_ref[cut(p), :]
            put(tol_ref.at[cut(p)], right_ref.at[cut(p)], ls.at[p], rr.at[p], left)

    @pl.when(z == 1)
    def _():
        for p in range(PIECES):
            from_left(p)

    @pl.when(z == 2)
    def _():
        for p in range(PIECES):
            from_right(p)

    between()

    @pl.when(z < 2)
    def _():
        for p in range(PIECES):
            from_right(p)

    @pl.when(z >= 2)
    def _():
        for p in range(PIECES):
            from_left(p)

    for p in range(PIECES):
        out_ref[far(mine, p), :] = base_ref[cut(p), :]

        @pl.when(z > 0)
        def _():
            out_ref[far(mine, p), :] += left_ref[cut(p), :]

        @pl.when(z < 3)
        def _():
            out_ref[far(mine, p), :] += right_ref[cut(p), :]

        put(out_ref.at[far(mine, p)], out_ref.at[far(mine, p)], os_.at[p], or_.at[p], sib)
    late()
    for p in range(PIECES):
        landed(out_ref.at[far(theirs, p)], or_.at[p], sib)
        sent(out_ref.at[far(mine, p)], os_.at[p], sib)
        sent(part_ref.at[far(theirs, p)], ss.at[p], sib)

        @pl.when(z < 3)
        def _():
            sent(base_ref.at[cut(p)], rs.at[p], right)

        @pl.when(z > 0)
        def _():
            sent(base_ref.at[cut(p)], ls.at[p], left)


def k1(tokens, upstream, w_in, w_out, small, gain, lengths, conv_w, vec):
    groups, ways = 4, 8
    cols = jax.ShapeDtypeStruct((ways, w_in.shape[0], w_in.shape[1] // ways), bf16)
    meta = jax.ShapeDtypeStruct((16, 128), f32)
    like = jax.ShapeDtypeStruct
    length, model = tokens.shape[1:]
    count = ways * length
    channels = groups * w_out.shape[0]
    dma = lambda n: pltpu.SemaphoreType.DMA((n,))
    some = pl.BlockSpec(memory_space=pl.ANY)
    far = pl.BlockSpec(memory_space=pltpu.HBM)
    here = pl.BlockSpec(memory_space=pltpu.VMEM)
    packed = count + count // 4
    return pl.pallas_call(
        k1_kernel,
        out_shape=(
            like((model, count), bf16),
            like((count, model), bf16),
            like((groups * ways * cols.shape[1], cols.shape[2]), bf16),
            like((channels, model), bf16),
            like((channels, small.shape[1]), bf16),
            like((8, channels), f32),
            like((1, model), f32),
            like((3, count + 32, 128), f32),
            like((1, count, 128), f32),
            like((channels // 128, count + 24, 128), f32),
            like((channels // 128, count, 128), f32),
            like((channels // 128, count, 128), f32),
            like((channels, count), bf16),
            like((channels // 128, count, 128), f32),
            like((count, 128), bf16),
            like((count, 128), f32),
        ),
        in_specs=[some] * 2 + [here, some, some] + [here] * 4,
        out_specs=(far,) * 4 + (here,) * 3 + (far,) * 7 + (here,) * 2,
        scratch_shapes=[
            pltpu.VMEM((3, count + 32, 128), f32),
            pltpu.VMEM((1, count, 128), f32),
            pltpu.VMEM((channels // 128, count + 24, 128), f32),
            pltpu.VMEM((channels // 128, count, 128), f32),
            pltpu.VMEM((channels // 128, count, 128), f32),
            pltpu.VMEM((channels, count), bf16),
            pltpu.VMEM((channels // 128, count, 128), f32),
            dma(7),
            pltpu.VMEM(cols.shape, bf16),
            pltpu.VMEM(meta.shape, f32),
            pltpu.VMEM((count, model), bf16),
            pltpu.VMEM((count, model), bf16),
            pltpu.VMEM((model, count), bf16),
            pltpu.VMEM((groups * ways * cols.shape[1], cols.shape[2]), bf16),
            pltpu.VMEM((groups, ways) + meta.shape, f32),
            pltpu.VMEM((packed, 128), f32),
            pltpu.VMEM((packed, 128), f32),
        ] + [pltpu.VMEM((packed // 2, 128), f32)] * 6
        + [dma(8), dma(7), dma(7), dma(3), dma(3), dma(8), dma(8), dma(8), dma(8), dma(8), dma(8), dma(7), dma(7), dma(19), dma(19), dma(8), dma(8), dma(4), dma(4)]
        + [dma(PIECES) for _ in range(8)],
        compiler_params=pltpu.CompilerParams(collective_id=0, has_side_effects=True, vmem_limit_bytes=56 * 1024 * 1024),
    )(tokens, upstream, w_in, w_out, small, gain, lengths, conv_w, vec)


GROUP = 4


def k2_kernel(states, dl_ref, kq_ref, wdt_ref, vecs_ref, keep_ref, live_ref, v_ref, g_ref, ups_ref, wout_ref,
              m_ref, mt_ref, dg_ref, gwdt_ref, dv_ref, part_ref, stat_ref,
              dpre_ref, s_ref, h_ref, rate_ref, w_ref, y_ref, dm_ref, kb_ref, hot_ref, drr_ref):
    tiles, count = v_ref.shape[:2]
    steps = count // 8
    wide = states * 128
    chunk = 256
    first = pl.program_id(0) == 0
    half = pl.program_id(0)
    both = range(tiles)
    rank = wdt_ref.shape[1]

    @pl.when(first)
    def _():
        row = lax.broadcasted_iota(jnp.int32, (128, 512), 0)
        col = lax.broadcasted_iota(jnp.int32, (128, 512), 1) // 128
        for part in range(0, 2 * wide, 512):
            hot_ref[:, part:part + 512] = jnp.where((row % 32 == col + part // 128) & (row < 96), 1.0, 0.0).astype(bf16)

    lane = lax.broadcasted_iota(jnp.int32, (chunk, 128), 1)

    def spread(i, carry):
        r = pl.ds(pl.multiple_of(i * chunk, chunk), chunk)
        value = jnp.where(lane < 2 * states, kq_ref[r, :], 0.0)
        hi = value.astype(bf16).astype(f32)
        mid = (value - hi).astype(bf16).astype(f32)
        low = value - hi - mid
        left = (hi + pltpu.roll(mid, 32, 1) + pltpu.roll(low, 64, 1)).astype(bf16)
        for part in range(0, 2 * wide, 512):
            kb_ref[r, part:part + 512] = jnp.dot(left, hot_ref[:, part:part + 512], preferred_element_type=f32)
        return carry

    lax.fori_loop(0, count // chunk, spread, 0)
    cols = (((1,), (1,)), ((), ()))
    length = count // 8

    def gate_step(i, carry):
        r = pl.ds(pl.multiple_of(i * chunk, chunk), chunk)
        product = lax.dot_general(ups_ref[r, :], wout_ref[...], cols, preferred_element_type=f32)
        for j in range(chunk // length):
            for n in both:
                dm_ref[n, pl.ds(i * (chunk // length) + j, length, stride=8), :] = product[j * length:(j + 1) * length, n * 128:(n + 1) * 128]
        return carry

    lax.fori_loop(0, count // chunk, gate_step, 0)
    bias = vecs_ref[5:6, :]
    skip = vecs_ref[6:7, :]
    tile_of = lambda x, n: x[:, n * 128:(n + 1) * 128]
    ks = lax.broadcasted_iota(jnp.int32, (128, 128), 1)

    def before(i, carry):
        seen = list(carry)
        r = pl.ds(pl.multiple_of(i * 128, 128), 128)
        live = live_ref[0, r, :]
        k = jnp.where(ks < states, kq_ref[r, :], 0.0)
        sk = jnp.sum(k * k, axis=1, keepdims=True)
        pre = lax.dot_general(dl_ref[r, :], wdt_ref[...], cols, preferred_element_type=f32) + bias
        for n in both:
            beta = jax.nn.sigmoid(tile_of(pre, n))
            part = 1.0 / (1.0 + beta * sk)
            rate_ref[n, r, :] = beta * part
            w_ref[n, r, :] = part * part * beta * (1.0 - beta)
            g = g_ref[n, r, :]
            sg = jax.nn.sigmoid(g)
            dm = dm_ref[n, r, :] * live
            dv_ref[n, r, :] = dm * (g * sg)
            dm_ref[n, r, :] = dm * (sg * (1.0 + g * (1.0 - sg)))
            shown = (beta * live).reshape(16, 8, 128)
            seen[n] = seen[n] + jnp.sum(shown, axis=0)
            seen[tiles + n] = jnp.maximum(seen[tiles + n], jnp.max(shown, axis=0))
        return tuple(seen)

    blank = jnp.zeros((8, 128), f32)
    seen = lax.fori_loop(0, count // 128, before, (blank,) * (2 * tiles))
    s_ref[0, 0] = jnp.zeros(s_ref.shape[2:], f32)
    span = GROUP * 8
    at = [slice(j * 8, j * 8 + 8) for j in range(GROUP)]

    def view(ref, i):
        r = pl.ds(pl.multiple_of(i * span, span), span)
        return ref.at[:, r] if len(ref.shape) == 3 else ref.at[r]

    def pair(ref, r):
        return jnp.concatenate([ref[n, r, :] for n in both], axis=1)

    def keep_pair(ref, r, value):
        for n in both:
            ref[n, r, :] = tile_of(value, n)

    tile = lambda x: jnp.concatenate([x] * tiles, axis=1)

    def fold(x):
        total = tile_of(x, 0)
        for n in range(1, tiles):
            total = total + tile_of(x, n)
        return total

    def forward(i, carry):
        keeps, rates, vs, kbs, ys = [view(x, i) for x in (keep_ref, rate_ref, v_ref, kb_ref, y_ref)]
        keep = [keeps[0, r, :] for r in at]
        rate = [pair(rates, r) for r in at]
        value = [pair(vs, r) for r in at]
        rv = [a * b for a, b in zip(rate, value)]
        y = [skip * b for b in value]
        for n in range(states):
            state = s_ref[i, 0, n]
            for j, r in enumerate(at):
                kb = kbs[r, n * 128:(n + 1) * 128]
                qb = kbs[r, wide + n * 128:wide + (n + 1) * 128]
                state = (tile(keep[j]) - rate[j] * tile(kb * kb * keep[j])) * state + rv[j] * tile(kb)
                if j < GROUP - 1:
                    s_ref[i, j + 1, n] = state
                else:
                    s_ref[i + 1, 0, n] = state
                y[j] = y[j] + state * tile(qb)
        for j, r in enumerate(at):
            keep_pair(ys, r, y[j])
        return carry

    lax.fori_loop(0, steps // GROUP, forward, 0)
    h_ref[...] = jnp.zeros_like(h_ref)

    def backward(step, carry):
        i = steps // GROUP - 1 - step
        keeps, rates, vs, kbs, dvs, ws, drrs = [view(x, i) for x in (keep_ref, rate_ref, v_ref, kb_ref, dv_ref, w_ref, drr_ref)]
        keep = [keeps[0, r, :] for r in at]
        rate = [pair(rates, r) for r in at]
        value = [pair(vs, r) for r in at]
        rv = [a * b for a, b in zip(rate, value)]
        dy = [pair(dvs, r) for r in at]
        hk = [jnp.zeros((8, tiles * 128), f32) for r in at]
        hs2 = [jnp.zeros((8, tiles * 128), f32) for r in at]
        for n in range(states):
            ah = h_ref[n]
            later = s_ref[i + 1, 0, n]
            for j in range(GROUP - 1, -1, -1):
                r = at[j]
                kb = kbs[r, n * 128:(n + 1) * 128]
                qb = kbs[r, wide + n * 128:wide + (n + 1) * 128]
                kk = kb * keep[j]
                held = tile(kb * kk)
                h = dy[j] * tile(qb) + ah
                prior = s_ref[i, j, n]
                hs = h * prior
                hk[j] = hk[j] + h * tile(kb)
                hs2[j] = hs2[j] + hs * held
                kbs[r, n * 128:(n + 1) * 128] = fold(h * rv[j]) - 2.0 * kk * fold(hs * rate[j])
                kbs[r, wide + n * 128:wide + (n + 1) * 128] = fold(dy[j] * later)
                later = prior
                ah = (tile(keep[j]) - rate[j] * held) * h
            h_ref[n] = ah
        dskip = carry
        for j, r in enumerate(at):
            drate = value[j] * hk[j] - hs2[j]
            drrs[r, :] = fold(drate * rate[j] * rate[j]) * (-2.0)
            keep_pair(ws, r, drate * pair(ws, r))
            keep_pair(dvs, r, rate[j] * hk[j] + skip * dy[j])
            dskip = dskip + dy[j] * value[j]
        return dskip

    dskip = lax.fori_loop(0, steps // GROUP, backward, jnp.zeros((8, tiles * 128), f32))

    quarter = count // 4
    packed = jnp.zeros((quarter, 128), f32)
    for b in range(4):
        r = slice(b * quarter, (b + 1) * quarter)
        total = jnp.zeros((quarter, 128), f32)
        for part in range(0, 2 * wide, 512):
            total = total + lax.dot_general(kb_ref[r, part:part + 512].astype(bf16), hot_ref[:, part:part + 512], cols, preferred_element_type=f32)
        drr = jnp.sum(drr_ref[r, :], axis=1, keepdims=True)
        k = kq_ref[r, :]
        low = lax.broadcasted_iota(jnp.int32, (quarter, 128), 1)
        total = jnp.where(low < 2 * states, total, 0.0) + jnp.where(low < states, k * drr, 0.0)
        packed = packed + (pltpu.roll(total, 32 * b, 1) if b else total)

    tail = pl.ds(count, quarter)
    part_ref[tail, :] = jnp.where(first, packed, part_ref[tail, :] + packed)

    def after(i, carry):
        r = pl.ds(pl.multiple_of(i * 128, 128), 128)
        live = live_ref[0, r, :]
        sums = list(carry)
        for n in both:
            y = y_ref[n, r, :]
            g = g_ref[n, r, :]
            y_ref[n, r, :] = y * (g * jax.nn.sigmoid(g)) * live
            dm_ref[n, r, :] = y * dm_ref[n, r, :]
            low = w_ref[n, r, :].astype(bf16)
            dpre_ref[r, n * 128:(n + 1) * 128] = low
            sums[n] = sums[n] + jnp.sum(low.astype(f32).reshape(16, 8, 128), axis=0)
        ddl = jnp.dot(dpre_ref[r, :], wdt_ref[...], preferred_element_type=f32)
        part_ref[r, :] = jnp.where(first, ddl, part_ref[r, :] + ddl)
        return tuple(sums)

    sums = lax.fori_loop(0, count // 128, after, (blank,) * tiles)

    def by_row(j, carry):
        r = pl.ds(pl.multiple_of(j * length, length), length)
        for n in both:
            value = y_ref[n, pl.ds(j, length, stride=8), :]
            m_ref[r, n * 128:(n + 1) * 128] = value.astype(bf16)
            mt_ref[n * 128:(n + 1) * 128, r] = value.T.astype(bf16)
            dg_ref[r, n * 128:(n + 1) * 128] = dm_ref[n, pl.ds(j, length, stride=8), :].astype(bf16)
        return carry

    lax.fori_loop(0, 8, by_row, 0)
    gwdt_ref[...] = lax.dot_general(dpre_ref[...], dl_ref[...], (((0,), (0,)), ((), ())), preferred_element_type=f32)
    stat_ref[...] = jnp.zeros_like(stat_ref)
    for n in both:
        lanes = slice(n * 128, (n + 1) * 128)
        stat_ref[0:1, lanes] = jnp.sum(seen[n], axis=0, keepdims=True)
        stat_ref[1:2, lanes] = jnp.max(seen[tiles + n], axis=0, keepdims=True)
        stat_ref[5:6, lanes] = jnp.sum(sums[n], axis=0, keepdims=True)
        stat_ref[6:7, lanes] = jnp.sum(tile_of(dskip, n), axis=0, keepdims=True)


def k2(dl, kq, smalls, vecs, masks, live, v, g, ups, wout, states):
    count, rank = dl.shape
    channels, model = wout.shape
    tiles = 2
    width = tiles * 128
    like = jax.ShapeDtypeStruct
    once = pl.Buffered(buffer_count=1)
    whole = lambda a: pl.BlockSpec(a.shape, lambda h: (0,) * a.ndim, pipeline_mode=once)
    deep = pl.BlockSpec((tiles, count, 128), lambda h: (h, 0, 0))
    flat = pl.BlockSpec((count, width), lambda h: (0, h))
    return pl.pallas_call(
        functools.partial(k2_kernel, states),
        grid=(channels // width,),
        out_shape=(
            like((count, channels), bf16),
            like((channels, count), bf16),
            like((count, channels), bf16),
            like((channels, rank), f32),
            like(v.shape, f32),
            like((count + count // 4, 128), f32),
            like((8, channels), f32),
        ),
        in_specs=[
            whole(dl), whole(kq),
            pl.BlockSpec((width, 128), lambda h: (h, 2)),
            pl.BlockSpec((8, width), lambda h: (0, h)),
            pl.BlockSpec((1, count, 128), lambda h: (0, 0, 0), pipeline_mode=once),
            pl.BlockSpec((1, count, 128), lambda h: (0, 0, 0), pipeline_mode=once),
            deep, deep, whole(ups),
            pl.BlockSpec((width, model), lambda h: (h, 0)),
        ],
        out_specs=(flat, pl.BlockSpec((width, count), lambda h: (h, 0)), flat, pl.BlockSpec((width, rank), lambda h: (h, 0)), deep, pl.BlockSpec((count + count // 4, 128), lambda h: (0, 0)), pl.BlockSpec((8, width), lambda h: (0, h))),
        scratch_shapes=[
            pltpu.VMEM((count, width), bf16),
            pltpu.VMEM((count // 8 // GROUP + 1, GROUP, states, 8, width), f32),
            pltpu.VMEM((states, 8, width), f32),
        ] + [pltpu.VMEM((tiles, count, 128), f32)] * 4
        + [pltpu.VMEM((count, 2 * states * 128), f32), pltpu.VMEM((128, 2 * states * 128), bf16), pltpu.VMEM((count, 128), f32)],
        compiler_params=pltpu.CompilerParams(vmem_limit_bytes=60 * 1024 * 1024),
    )(dl, kq, smalls, vecs, masks, live, v, g, ups, wout)


class Row:
    def __init__(self, part, sib, recv, sems):
        self.part, self.sib, self.recv = part, sib, recv
        self.ss, self.sr, self.gs, self.lr, self.rr = sems
        d, c, z = place()
        self.c = c
        self.other = (d, flip(c, 1), z)
        self.to_left = (d, c, lax.rem(z + 3, 4))
        self.to_right = (d, c, lax.rem(z + 1, 4))

    def start(self):
        for zp in (3, 0, 2, 1):
            put(self.part.at[flip(self.c, 1), zp], self.sib.at[zp], self.ss.at[zp], self.sr.at[zp], self.other)

    def gather(self):
        for zp in (3, 0, 2, 1):
            landed(self.sib.at[zp], self.sr.at[zp], self.other)
            add_rows(self.sib.at[zp], [self.sib.at[zp], self.part.at[self.c, zp]])

    def release(self):
        for zp in range(4):
            sent(self.part.at[flip(self.c, 1), zp], self.ss.at[zp], self.other)

    def terms(self, zs, zp):
        found = [self.sib.at[zp]]
        if zp >= zs and zs > 0:
            landed(self.recv.at[zp], self.lr.at[zp], self.to_left)
            found.append(self.recv.at[zp])
        if zp <= zs and zs < 3:
            slot = self.recv.at[4 if zp == zs else zp]
            landed(slot, self.rr.at[zp], self.to_right)
            found.append(slot)
        return found

    def join(self, zs, zp):
        found = self.terms(zs, zp)
        if len(found) > 1:
            add_rows(self.sib.at[zp], found)

    def step(self, zs, k):
        for zp in ((3, 2, 1, 0) if zs == 0 else (0, 1, 2, 3)):
            if zp > zs and k == (0 if zs == 0 else 3 - zp + zs):
                self.join(zs, zp)
                put(self.sib.at[zp], self.recv.at[zp], self.gs.at[zp], self.lr.at[zp], self.to_right)
            if zp < zs and k == (0 if zs == 3 else zp + 3 - zs):
                self.join(zs, zp)
                put(self.sib.at[zp], self.recv.at[4 if zp == zs - 1 else zp], self.gs.at[zp], self.rr.at[zp], self.to_left)

    def finish(self, zs):
        add_rows(self.sib.at[zs], self.terms(zs, zs), self.total)

    def close(self, zs):
        for zp in range(4):
            if zp != zs:
                sent(self.sib.at[zp], self.gs.at[zp], self.other)

    def along(self, k, total=None):
        self.total = total
        d, c, z = place()
        for zs in range(4):
            @pl.when(z == zs)
            def _():
                if k < 3:
                    self.step(zs, k)
                else:
                    self.finish(zs)
                    self.close(zs)


def row_scratch(rows, columns):
    return [pltpu.VMEM((4, rows, columns), bf16), pltpu.VMEM((5, rows, columns), bf16)] + [pltpu.SemaphoreType.DMA((4,))] * 5


def add_rows(dst, sources, total=None):
    rows = (total if total is not None else dst).shape[0]
    step = 16

    def body(i, carry):
        r = pl.ds(pl.multiple_of(i * step, step), step)
        value = sources[0][r, :].astype(f32)
        for more in sources[1:]:
            value = value + more[r, :].astype(f32)
        if total is not None:
            total[r, :] = value
        else:
            dst[r, :] = value.astype(dst.dtype)
        return carry

    lax.fori_loop(0, rows // step, body, 0)


class Flat:
    def __init__(self, part, xa, yb, rx, ry, ss, rs):
        self.part, self.xa, self.yb, self.rx, self.ry, self.ss, self.rs = part, xa, yb, rx, ry, ss, rs
        d, c, z = place()
        self.d, self.dx, self.dy, self.dd = d, flip(d, 1), flip(d, 2), flip(flip(d, 1), 2)
        self.xn, self.yn = (self.dx, c, z), (self.dy, c, z)
        half = part.shape[1] // 2
        self.a, self.b = pl.ds(0, half), pl.ds(half, half)
        self.sends = []

    def start_far(self):
        p = self.part
        self.sends.append(put(p.at[self.dd, self.a], self.xa, self.ss.at[0], self.rs.at[0], self.xn))
        self.sends.append(put(p.at[self.dd, self.b], self.yb, self.ss.at[1], self.rs.at[1], self.yn))

    def start_near(self):
        p = self.part
        self.sends.append(put(p.at[self.dx, self.a], self.rx.at[self.a], self.ss.at[2], self.rs.at[2], self.xn))
        self.sends.append(put(p.at[self.dy, self.b], self.ry.at[self.b], self.ss.at[3], self.rs.at[3], self.yn))

    def middle(self):
        p = self.part
        landed(self.xa, self.rs.at[0], self.xn)
        add_rows(self.xa, [self.xa, p.at[self.dy, self.a]])
        self.sends.append(put(self.xa, self.ry.at[self.a], self.ss.at[4], self.rs.at[4], self.yn))
        landed(self.yb, self.rs.at[1], self.yn)
        add_rows(self.yb, [self.yb, p.at[self.dx, self.b]])
        self.sends.append(put(self.yb, self.rx.at[self.b], self.ss.at[5], self.rs.at[5], self.xn))

    def finish(self, out):
        landed(self.rx.at[self.a], self.rs.at[2], self.xn)
        landed(self.ry.at[self.b], self.rs.at[3], self.yn)
        landed(self.ry.at[self.a], self.rs.at[4], self.yn)
        landed(self.rx.at[self.b], self.rs.at[5], self.xn)
        add_rows(out, [self.part.at[self.d], self.rx, self.ry])

    def close(self):
        for copy in self.sends:
            copy.wait_send()


def flat_scratch(rows, columns, dtype):
    half = pltpu.VMEM((rows // 2, columns), dtype)
    full = pltpu.VMEM((rows, columns), dtype)
    return [half, half, full, full, pltpu.SemaphoreType.DMA((6,)), pltpu.SemaphoreType.DMA((6,))]


def k3_kernel(part_ref, stat_ref, smalls_ref, vecs_ref, gains_ref, gwdt_ref, masks_ref, tok_ref, up_ref,
              m_any, mt_any, dg_any, dv_any, slope_any, u_any, vt_any, xnt_any, win_any, wout_any, ups_any,
              block_out, gtok_out, gwin_out, gwout_out, small_out, tiny_out, *scratch):
    scratch = list(scratch)

    def take(n):
        found = scratch[:n]
        del scratch[:n]
        return found

    block_ref, gtok_ref, gwin_ref, gwout_ref, small_ref, tiny_ref, stores = take(7)
    outp, win_ref, up, gp, gwoutp, smallp = take(6)
    m_ref, mt_ref, dz_ref, dc_ref, slope_ref, u_ref, xnt_ref, dp_ref, slots_ref, row_ref = take(10)
    near_ref, pairs_ref, sum_ref, far_ref = take(4)
    loads, as_, ar, ns, nr, fs, fr = take(7)
    totals = take(7)
    total_sems = take(8)
    out_row = Row(outp, *take(2), take(5))
    dxn_row = Row(outp, *take(2), take(5))
    flats = [Flat(up, *take(6)), Flat(gp, *take(6))]
    gwout_flat = Flat(gwoutp, *take(6))
    small_flat = Flat(smallp, *take(6))
    d, c, z = place()
    j = c * 4 + z
    other = flip(c, 1)
    steps = mates()
    planes = [(flip(d, 1), c, z), (flip(d, 2), c, z), (flip(flip(d, 1), 2), c, z)]
    length, model = tok_ref.shape[1:]
    tiles, padded, _ = dc_ref.shape
    count = dz_ref.shape[0]
    width = tiles * 128
    rows_any = [(m_any, m_ref), (wout_any, gwoutp), (mt_any, mt_ref)]
    for at, holder in ((0, gp), (1024, up)):
        for h in range(2):
            for q in range(2):
                rows_any.append((ups_any.at[pl.ds(q * 512, 512), pl.ds(at + h * 512, 512)], holder.at[2 * h + q]))
    rows_any += [(dg_any, dz_ref.at[:, pl.ds(width, width)]), (xnt_any, xnt_ref), (dv_any, dc_ref.at[:, pl.ds(0, count)]),
                 (slope_any, slope_ref), (u_any, u_ref), (win_any, win_ref)]
    copies = [pltpu.make_async_copy(a, b, loads.at[i]) for i, (a, b) in enumerate(rows_any)]
    for copy in copies:
        copy.start()
    greet([mate(s) for s in steps] + planes)
    outs = [(block_ref, block_out), (gtok_ref, gtok_out), (gwin_ref, gwin_out), (gwout_ref, gwout_out), (small_ref, small_out), (tiny_ref, tiny_out)]
    outs = [pltpu.make_async_copy(a, b, stores.at[i]) for i, (a, b) in enumerate(outs)]
    tile = 256
    nn = (((1,), (0,)), ((), ()))
    nt = (((1,), (1,)), ((), ()))

    def rows_product(half, target, left, right, dims, right_rows):
        def body(i, carry):
            if right_rows:
                group = i // (512 // tile)
                value = right[group, pl.ds(pl.multiple_of((i % (512 // tile)) * tile, tile), tile), :]
            else:
                value = jnp.concatenate([right[g, :, pl.ds(pl.multiple_of(i * tile, tile), tile)] for g in range(4)], axis=0)
            product = lax.dot_general(left[pl.ds(pl.multiple_of(half * 512, 512), 512), :], value, dims, preferred_element_type=f32)
            for zp in range(4):
                target[half, zp, :, pl.ds(pl.multiple_of(i * tile, tile), tile)] = product[zp * length:(zp + 1) * length].astype(bf16)
            return carry

        lax.fori_loop(0, model // tile, body, 0)

    def weight_rows(holder, first, group):
        def body(i, carry):
            lanes = pl.ds(pl.multiple_of(i * tile, tile), tile)
            left = xnt_ref[pl.ds(pl.multiple_of(group * 512, 512), 512), :]
            value = dz_ref[:, pl.ds(pl.multiple_of(first + i * tile, tile), tile)]
            holder[group, :, lanes] = jnp.dot(left, value, preferred_element_type=f32).astype(bf16)
            return carry

        lax.fori_loop(0, width // tile, body, 0)

    def weight_part(k):
        flat = flats[k]
        holder, first = (up, 0) if k == 0 else (gp, width)
        weight_rows(holder, first, flat.dd)
        flat.start_far()
        weight_rows(holder, first, flat.dx)
        weight_rows(holder, first, flat.dy)
        flat.start_near()
        weight_rows(holder, first, d)

    def early():
        copies[0].wait()
        copies[1].wait()
        rows_product(other, outp, m_ref, gwoutp, nn, False)
        out_row.start()
        rows_product(c, outp, m_ref, gwoutp, nn, False)

    def between():
        out_row.gather()
        out_row.along(0)
        for copy in copies[2:11]:
            copy.wait()
        for holder, at in ((gp, 0), (up, 1024)):
            def body(i, carry):
                h = i // 2
                off = pl.ds(pl.multiple_of((i % 2) * tile, tile), tile)
                value = jnp.concatenate([holder[2 * h, :, off], holder[2 * h + 1, :, off]], axis=0)
                product = jnp.dot(mt_ref[...], value, preferred_element_type=f32)
                for g in range(4):
                    gwoutp[g, :, pl.ds(pl.multiple_of(at + i * tile, tile), tile)] = product[g * 128:(g + 1) * 128].astype(bf16)
                return carry

            lax.fori_loop(0, 4, body, 0)

    def late():
        for copy in copies[11:13]:
            copy.wait()
        weight_part(1)

    seen = jnp.sum(stat_ref[0:1, :], axis=1, keepdims=True)
    peak = jnp.max(stat_ref[1:2, :], axis=1, keepdims=True)
    row8 = lax.broadcasted_iota(jnp.int32, (8, 128), 0)
    lane8 = lax.broadcasted_iota(jnp.int32, (8, 128), 1)
    pairs_ref[...] = jnp.where(lane8 == 0, seen, jnp.where(lane8 == 1, peak, 0.0))
    for i, s in enumerate(steps):
        put(pairs_ref, near_ref.at[i], ns.at[i], nr.at[i], mate(s))

    def join(a, b):
        return jnp.where(lane8 == 1, jnp.maximum(a, b), a + b)

    total_ref = totals[0]
    line_total(part_ref, *totals, *total_sems, early, between, late)
    vt_copy = pltpu.make_async_copy(vt_any, mt_ref, loads.at[17])
    vt_copy.start()
    out_row.along(1)
    value = pairs_ref[...]
    for i, s in enumerate(steps):
        landed(near_ref.at[i], nr.at[i], mate(s, -1))
        value = join(value, near_ref[i])
    sum_ref[...] = value
    for i, to in enumerate(planes):
        put(sum_ref, far_ref.at[i], fs.at[i], fr.at[i], to)
    quarter = count // 4
    lane = lax.broadcasted_iota(jnp.int32, (quarter, 128), 1)
    dp_ref[:, 0:128] = total_ref[0:count, :].astype(bf16)
    for b in range(4):
        packed = total_ref[count:count + quarter, :]
        packed = pltpu.roll(packed, 128 - 32 * b, 1) if b else packed
        dp_ref[b * quarter:(b + 1) * quarter, 128:256] = jnp.where(lane < 32, packed, 0.0).astype(bf16)
    for copy in copies[13:16]:
        copy.wait()
    dc_ref[:, count:, :] = jnp.zeros((tiles, padded - count, 128), f32)

    def slope_step(i, carry):
        r = pl.ds(pl.multiple_of(i * 256, 256), 256)
        product = lax.dot_general(dp_ref[r, :], smalls_ref[:, 0:256], nt, preferred_element_type=f32)
        for n in range(tiles):
            dc_ref[n, r, :] = (dc_ref[n, r, :] + product[:, n * 128:(n + 1) * 128]) * slope_ref[n, r, :]
        return carry

    lax.fori_loop(0, count // 256, slope_step, 0)
    flats[1].middle()
    taps = [vecs_ref[o:o + 1, :] for o in range(4)]
    lead = u_ref.shape[1] - count

    for n in range(tiles):
        lanes = slice(n * 128, (n + 1) * 128)
        tap = [t[:, lanes] for t in taps]

        def conv_step(i, carry):
            r = pl.ds(pl.multiple_of(i * 32, 32), 32)
            sums = list(carry)
            dc = dc_ref[n, r, :]
            du = tap[3] * dc
            fold8 = lambda x: x[0:8] + x[8:16] + x[16:24] + x[24:32]
            sums[4] = sums[4] + fold8(dc)
            sums[3] = sums[3] + fold8(dc * u_ref[n, pl.ds(pl.multiple_of(lead + i * 32, 8), 32), :])
            for o in range(1, 4):
                sums[3 - o] = sums[3 - o] + fold8(dc * (u_ref[n, pl.ds(pl.multiple_of(lead + i * 32 - 8 * o, 8), 32), :] * masks_ref[o - 1, pl.ds(pl.multiple_of(i * 32, 8), 32), :]))
                du = du + tap[3 - o] * (dc_ref[n, pl.ds(pl.multiple_of(i * 32 + 8 * o, 8), 32), :] * masks_ref[o - 1, pl.ds(pl.multiple_of(i * 32 + 8 * o, 8), 32), :])
            dc_ref[n, r, :] = du
            return tuple(sums)

        sums = lax.fori_loop(0, count // 32, conv_step, (jnp.zeros((8, 128), f32),) * 5)
        smallp[n, 128:160, :] = jnp.zeros((32, 384), f32)
        for k in range(5):
            smallp[n, 128 + k:129 + k, 0:128] = jnp.sum(sums[k], axis=0, keepdims=True)
        smallp[n, 133:134, 0:128] = stat_ref[5:6, lanes]
        smallp[n, 134:135, 0:128] = stat_ref[6:7, lanes]
        smallp[n, 0:128, 256:384] = gwdt_ref[n * 128:(n + 1) * 128, :]

    def by_row(i, carry):
        r = pl.ds(pl.multiple_of(i * length, length), length)
        for n in range(tiles):
            dz_ref[r, n * 128:(n + 1) * 128] = dc_ref[n, pl.ds(i, length, stride=8), :].astype(bf16)
        return carry

    lax.fori_loop(0, 8, by_row, 0)
    copies[16].wait()
    out_row.release()
    rows_product(other, outp, dz_ref, win_ref, nt, True)
    dxn_row.start()
    rows_product(c, outp, dz_ref, win_ref, nt, True)
    out_row.along(2)
    dxn_row.gather()
    dxn_row.along(0)
    weight_part(0)
    block = gwin_ref.shape[0]
    pending = []

    def rows_of(k, rank):
        return flats[k].part.at[d, pl.ds(pl.multiple_of(rank * block, block), block)]

    def give(k):
        flats[k].finish(flats[k].part.at[d])
        for i, s in enumerate(steps):
            to = mate(s)
            pending.append(put(rows_of(k, rank_of(to)), slots_ref.at[k, i], as_.at[7 * k + i], ar.at[7 * k + i], to))

    give(1)
    gwout_flat.start_far()
    gwout_flat.start_near()
    vt_copy.wait()
    for n in range(tiles):
        smallp[n, 0:128, 0:256] = jnp.dot(mt_ref[n * 128:(n + 1) * 128, :], dp_ref[...], preferred_element_type=f32)
    small_flat.start_far()
    small_flat.start_near()
    flats[0].middle()
    out_row.along(3, row_ref)

    def block_step(i, carry):
        r = pl.ds(pl.multiple_of(i * 16, 16), 16)
        block_ref[r, :] = (tok_ref[0, r, :].astype(f32) + row_ref[r, :]).astype(bf16)
        return carry

    lax.fori_loop(0, length // 16, block_step, 0)
    outs[0].start()
    dxn_row.along(1)
    give(0)
    gwout_flat.middle()
    small_flat.middle()
    dxn_row.along(2)
    gwout_flat.finish(gwout_ref)
    outs[3].start()
    dxn_row.along(3, row_ref)
    dxn_row.release()
    def norm_step(i, carry):
        r = pl.ds(pl.multiple_of(i * 16, 16), 16)
        x = tok_ref[0, r, :].astype(f32)
        scale = lax.rsqrt(jnp.sum(x * x, axis=1, keepdims=True) * (1.0 / model) + EPS)
        dxn = row_ref[r, :]
        inner = dxn * gains_ref[...]
        dot = jnp.sum(inner * x, axis=1, keepdims=True) * (1.0 / model)
        dxx = scale * inner - x * (scale * scale * scale * dot)
        gtok_ref[r, :] = (up_ref[0, r, :].astype(f32) + dxx).astype(bf16)
        return carry

    lax.fori_loop(0, length // 16, norm_step, 0)
    outs[1].start()
    small_flat.finish(small_ref)
    outs[4].start()

    def settle(k, rank, source):
        for g in range(4):
            at = k * width * 8 + g * 1024
            gwin_ref[:, pl.ds(pl.multiple_of(at + rank * 128, 128), 128)] = source[:, g * 128:(g + 1) * 128]

    for k in (1, 0):
        settle(k, j, rows_of(k, j))
        for i, s in enumerate(steps):
            src = mate(s, -1)
            landed(slots_ref.at[k, i], ar.at[7 * k + i], src)
            settle(k, rank_of(src), slots_ref.at[k, i])
    outs[2].start()
    value = sum_ref[...]
    for i, to in enumerate(planes):
        landed(far_ref.at[i], fr.at[i], to)
        value = join(value, far_ref[i])
    tiny_ref[...] = value
    outs[5].start()
    for i, to in enumerate(planes):
        sent(sum_ref, fs.at[i], to)
    for i, s in enumerate(steps):
        sent(near_ref.at[i], ns.at[i], mate(s))
    for copy in pending:
        copy.wait_send()
    for flat in (*flats, gwout_flat, small_flat):
        flat.close()
    for copy in outs:
        copy.wait()


def k3(part, stat, smalls, vecs, gains, gwdt, masks, tokens, upstream, m, mt, dg, dv, slope, u, vt, xnt, win, wout, ups):
    like = jax.ShapeDtypeStruct
    length, model = tokens.shape[1:]
    count, channels = m.shape
    tiles = channels // 128
    here = pl.BlockSpec(memory_space=pltpu.VMEM)
    far = pl.BlockSpec(memory_space=pl.ANY)
    dma = lambda n: pltpu.SemaphoreType.DMA((n,))
    own_d = model // 32
    packed = part.shape[0]
    return pl.pallas_call(
        k3_kernel,
        out_shape=(
            like((length, model), bf16),
            like((length, model), bf16),
            like((own_d, 16 * channels), bf16),
            like((128, model), f32),
            like((160, 384), f32),
            like((8, 128), f32),
        ),
        in_specs=[here] * 9 + [far] * 11,
        out_specs=(pl.BlockSpec(memory_space=pltpu.HBM),) * 6,
        scratch_shapes=[
            pltpu.VMEM((length, model), bf16),
            pltpu.VMEM((length, model), bf16),
            pltpu.VMEM((own_d, 16 * channels), bf16),
            pltpu.VMEM((128, model), f32),
            pltpu.VMEM((160, 384), f32),
            pltpu.VMEM((8, 128), f32),
            dma(6),
            pltpu.VMEM((2, 4, length, model), bf16),
            pltpu.VMEM((4, 512, 2 * channels), bf16),
            pltpu.VMEM((4, 512, channels), bf16),
            pltpu.VMEM((4, 512, channels), bf16),
            pltpu.VMEM((4, 128, model), bf16),
            pltpu.VMEM((4, 160, 384), f32),
            pltpu.VMEM((count, channels), bf16),
            pltpu.VMEM((channels, count), bf16),
            pltpu.VMEM((count, 2 * channels), bf16),
            pltpu.VMEM((tiles, count + 32, 128), f32),
            pltpu.VMEM((tiles, count, 128), f32),
            pltpu.VMEM(u.shape, f32),
            pltpu.VMEM((model, count), bf16),
            pltpu.VMEM((count, 256), bf16),
            pltpu.VMEM((2, 7, own_d, channels), bf16),
            pltpu.VMEM((length, model), f32),
            pltpu.VMEM((7, 8, 128), f32),
            pltpu.VMEM((8, 128), f32),
            pltpu.VMEM((8, 128), f32),
            pltpu.VMEM((3, 8, 128), f32),
            dma(18), dma(14), dma(14), dma(7), dma(7), dma(3), dma(3),
            pltpu.VMEM((packed, 128), f32),
        ] + [pltpu.VMEM((packed // 2, 128), f32)] * 6 + [dma(PIECES) for _ in range(8)]
        + row_scratch(length, model) * 2
        + flat_scratch(512, channels, bf16) * 2 + flat_scratch(128, model, bf16) + flat_scratch(160, 384, f32),
        compiler_params=pltpu.CompilerParams(collective_id=1, has_side_effects=True, vmem_limit_bytes=63400000),
    )(part, stat, smalls, vecs, gains, gwdt, masks, tokens, upstream, m, mt, dg, dv, slope, u, vt, xnt, win, wout, ups)


def k4_kernel(slots, block_in, gtok_in, gwin_in, gwout_in, small_in, tiny_in, win_ref, gain_ref,
              block_ref, gtok_ref, gain_out, gwin_ref, convw_ref, convb_ref, gwx_ref, gwdt_ref, dtb_ref, skip_ref, gwout_ref, mean_ref, peak_ref):
    block_ref[0] = block_in[...]
    gtok_ref[0] = gtok_in[...]
    gwout_ref[...] = gwout_in[...]
    depth, total = gwin_in.shape
    dot = jnp.zeros((depth, 128), f32)
    for at in range(0, total, 128):
        value = gwin_in[:, at:at + 128].astype(f32)
        gwin_ref[:, at:at + 128] = value
        dot = dot + value * win_ref[:, at:at + 128].astype(f32)
    column = jnp.broadcast_to(jnp.sum(dot, axis=1, keepdims=True), (depth, 128))
    gain_out[...] = column.T[0:1, :] / gain_ref[...].astype(f32)
    gwx_ref[...] = small_in[0:128, 0:256].T[0:gwx_ref.shape[0], :]
    gwdt_ref[...] = small_in[0:128, 256:384]
    convw_ref[...] = small_in[128:132, 0:128]
    convb_ref[...] = small_in[132:133, 0:128]
    dtb_ref[...] = small_in[133:134, 0:128]
    skip_ref[...] = small_in[134:135, 0:128]
    mean_ref[...] = tiny_in[0:1, 0:1] * (1.0 / slots)
    peak_ref[...] = tiny_in[0:1, 1:2]


def k4(slots, block, gtok, gwin, gwout, small, tiny, w_in, gain, columns):
    like = jax.ShapeDtypeStruct
    here = pl.BlockSpec(memory_space=pltpu.VMEM)
    row = like((1, 128), f32)
    return pl.pallas_call(
        functools.partial(k4_kernel, slots),
        out_shape=(
            like((1,) + block.shape, bf16), like((1,) + gtok.shape, bf16), like(gain.shape, f32), like(gwin.shape, f32),
            like((4, 128), f32), row, like((columns, 128), f32), like((128, 128), f32), row, row, like(gwout.shape, f32),
            like((1, 1), f32), like((1, 1), f32),
        ),
        in_specs=[here] * 8,
        out_specs=(here,) * 13,
        compiler_params=pltpu.CompilerParams(vmem_limit_bytes=63400000),
    )(block, gtok, gwin, gwout, small, tiny, w_in, gain)

def masks(lengths, count):
    ends = jnp.cumsum(lengths, axis=1)
    places = jnp.arange(count, dtype=jnp.int32)
    segment = jnp.sum((places[:, None, None] >= ends[None, :, :]).astype(jnp.int32), axis=2)
    same = []
    for offset in range(1, 4):
        before = jnp.pad(segment, ((offset, 0), (0, 0)), constant_values=-1)[:count]
        same.append((before == segment).astype(f32))
    return same, (segment < DOCS).astype(f32)


def columns(weights, ways):
    rows, total = weights.shape
    return weights.reshape(rows, 2, total // (2 * ways * 128), ways, 128)


def on_device(tokens, lengths, gain, w_in, conv_w, conv_b, w_x, w_dt, dt_bias, skip, w_out, grad_out):
    ways = lax.axis_size("core") * lax.axis_size("z")
    groups = lax.axis_size("dp")
    length, model = tokens.shape[1:]
    own_d = w_in.shape[0]
    own_e = conv_w.shape[0]
    inner = w_in.shape[1] // 2
    channels = inner // ways
    rank = w_dt.shape[1]
    states = (w_x.shape[1] - rank) // 2
    cols = w_in.reshape(own_d, 2, groups, ways, own_e).transpose(3, 0, 1, 2, 4).reshape(ways, own_d, 2 * channels)
    cols = lax.all_to_all(cols, TP, split_axis=0, concat_axis=0, tiled=True)
    win = lax.all_gather(cols, "dp", axis=0, tiled=True).reshape(model, 2 * channels)
    small = jnp.concatenate([w_x, w_dt, conv_w, conv_b[:, None], dt_bias[:, None], skip[:, None]], axis=1)
    small_width = small.shape[1]
    small = lax.all_gather(small, "dp", axis=0, tiled=True)
    wx = small[:, :rank + 2 * states]
    wdt = small[:, rank + 2 * states:2 * rank + 2 * states]
    rest = small[:, 2 * rank + 2 * states:].astype(f32)
    taps, bias, dtb, skips = rest[:, :4], rest[:, 4], rest[:, 5], rest[:, 6]
    wout = lax.all_gather(w_out, "dp", axis=0, tiled=True)
    gains = lax.all_gather(gain, ALL, axis=0, tiled=True).astype(f32)
    x = tokens[0].astype(f32)
    scale = lax.rsqrt(jnp.mean(x * x, axis=1, keepdims=True) + EPS)
    xn = (x * scale * gains).astype(bf16)
    xns = lax.all_gather(xn, TP, axis=0, tiled=True)
    ups = lax.all_gather(grad_out[0], TP, axis=0, tiled=True)
    lens = lax.all_gather(lengths, TP, axis=0, tiled=True)
    rows = lens.shape[0]
    tall = rows * length

    def time_major(a):
        return a.reshape(rows, length, -1).transpose(1, 0, 2).reshape(tall, -1)

    def row_major(a):
        return a.reshape(length, rows, -1).transpose(1, 0, 2).reshape(tall, -1)

    same, live = masks(lens, length)
    zz = time_major(jnp.dot(xns, win, preferred_element_type=f32))
    u = zz[:, :channels].reshape(length, rows, channels)
    g = zz[:, channels:]
    c = bias + taps[:, 3] * u
    shifted = []
    for offset in range(1, 4):
        earlier = jnp.pad(u, ((offset, 0), (0, 0), (0, 0)))[:length] * same[offset - 1][:, :, None]
        shifted.append(earlier)
        c = c + taps[:, 3 - offset] * earlier
    sig = jax.nn.sigmoid(c)
    v16 = (c * sig).astype(bf16).reshape(tall, channels)
    v = v16.astype(f32)
    p = lax.psum(jnp.dot(v16, wx, preferred_element_type=f32), TP)
    dl = p[:, :rank].astype(bf16)
    kq = p[:, rank:]
    dims_cols = (((1,), (1,)), ((), ()))
    dims_rows = (((0,), (0,)), ((), ()))
    pre = lax.dot_general(dl, wdt, dims_cols, preferred_element_type=f32) + dtb
    dm = time_major(lax.dot_general(ups, wout, dims_cols, preferred_element_type=f32))
    flags = jnp.pad(jnp.stack([same[0].reshape(tall), live.reshape(tall)], axis=1), ((0, 0), (0, 126)))
    hi = kq.astype(bf16)
    mid = (kq - hi.astype(f32)).astype(bf16)
    low = (kq - hi.astype(f32) - mid.astype(f32)).astype(bf16)
    kq3 = jnp.concatenate([hi, mid, low], axis=1)
    keys = kq[:, :states]
    sk = jnp.broadcast_to(jnp.sum(keys * keys, axis=1, keepdims=True), (tall, 8))
    m, dg, dpre, dv, dkq, stats = mixer(flags, kq3, sk, pre, v, g, dm, skips[None], states=states, width=256, unroll=4)
    stats = stats.transpose(1, 2, 0, 3).reshape(3, 8, channels)
    dskip = jnp.sum(stats[0], axis=0)
    total = lax.psum(jnp.sum(stats[1]), ALL)
    peak = lax.pmax(jnp.max(stats[2]), ALL)
    beta_mean = total / float(groups * ways * length * inner)
    m16 = row_major(m).astype(bf16)
    out = jnp.dot(m16, wout, preferred_element_type=f32).astype(bf16)
    out = lax.psum_scatter(out, TP, scatter_dimension=0, tiled=True)
    block_out = (x + out.astype(f32)).astype(bf16)
    grad_wout = lax.dot_general(m16, ups, dims_rows, preferred_element_type=f32).astype(bf16)
    grad_wout = lax.psum_scatter(grad_wout, "dp", scatter_dimension=0, tiled=True)
    dpre16 = dpre.astype(bf16)
    grad_dtb = jnp.sum(dpre16.astype(f32), axis=0)
    grad_wdt = lax.dot_general(dpre16, dl, dims_rows, preferred_element_type=f32)
    ddl = jnp.dot(dpre16, wdt, preferred_element_type=f32)
    dkq = dkq[:, :2 * states] + dkq[:, 2 * states:2 * states + 1] * jnp.pad(keys, ((0, 0), (0, states)))
    dp16 = lax.psum(jnp.concatenate([ddl, dkq], axis=1), TP).astype(bf16)
    grad_wx = lax.dot_general(v16, dp16, dims_rows, preferred_element_type=f32)
    dvt = dv + lax.dot_general(dp16, wx, dims_cols, preferred_element_type=f32)
    dc = (dvt * (sig.reshape(tall, channels) * (1.0 + c.reshape(tall, channels) * (1.0 - sig.reshape(tall, channels))))).reshape(length, rows, channels)
    du = taps[:, 3] * dc
    grad_taps = [jnp.sum(dc * u, axis=(0, 1))]
    for offset in range(1, 4):
        grad_taps.append(jnp.sum(dc * shifted[offset - 1], axis=(0, 1)))
        du = du + taps[:, 3 - offset] * jnp.pad((dc * same[offset - 1][:, :, None])[offset:], ((0, offset), (0, 0), (0, 0)))
    grad_conv = jnp.stack(grad_taps[::-1] + [jnp.sum(dc, axis=(0, 1)), grad_dtb, dskip], axis=1)
    dz = row_major(jnp.concatenate([du.reshape(tall, channels), dg], axis=1)).astype(bf16)
    gwin = lax.dot_general(xns, dz, dims_rows, preferred_element_type=f32).astype(bf16)
    gwin = lax.psum_scatter(gwin, "dp", scatter_dimension=0, tiled=True)
    gwin = lax.all_to_all(gwin.reshape(ways, own_d, 2 * channels), TP, split_axis=0, concat_axis=0, tiled=True)
    grad_win = gwin.reshape(ways, own_d, 2, groups, own_e).transpose(1, 2, 3, 0, 4).reshape(own_d, 2 * inner).astype(f32)
    dxn = lax.dot_general(dz, win, dims_cols, preferred_element_type=f32).astype(bf16)
    dxn = lax.psum_scatter(dxn, TP, scatter_dimension=0, tiled=True).astype(f32)
    small_grad = lax.psum_scatter(jnp.concatenate([grad_wx, grad_wdt, grad_conv], axis=1), "dp", scatter_dimension=0, tiled=True)
    inner_grad = dxn * gains
    dxx = scale * inner_grad - x * (scale * scale * scale) * (jnp.sum(inner_grad * x, axis=1, keepdims=True) / model)
    grad_tokens = (grad_out[0].astype(f32) + dxx).astype(bf16)
    grad_gain = lax.psum_scatter(jnp.sum(dxn * x * scale, axis=0), ALL, scatter_dimension=0, tiled=True)
    at = rank + 2 * states
    return (
        block_out[None],
        grad_tokens[None],
        grad_gain,
        grad_win,
        small_grad[:, at + rank:at + rank + 4],
        small_grad[:, at + rank + 4],
        small_grad[:, :at],
        small_grad[:, at:at + rank],
        small_grad[:, at + rank + 5],
        small_grad[:, at + rank + 6],
        grad_wout.astype(f32),
        beta_mean,
        peak,
    )


def on_device_direct(tokens, lengths, gain, w_in, conv_w, conv_b, w_x, w_dt, dt_bias, skip, w_out, grad_out):
    groups, ways = 4, 8
    length, model = tokens.shape[1:]
    own_d = w_in.shape[0]
    own_e = conv_w.shape[0]
    inner = w_in.shape[1] // 2
    channels = inner // ways
    rank = w_dt.shape[1]
    states = (w_x.shape[1] - rank) // 2
    small = jnp.concatenate([jnp.pad(w_x, ((0, 0), (0, 256 - w_x.shape[1]))), w_dt], axis=1)
    vec = jnp.stack([conv_b, dt_bias, skip])
    gain = gain[None]
    xnt, ups, win, wout, smalls, vecs, gains, masks, live, u, g, v, vt, slope, dl, kq = k1(tokens, grad_out, w_in, w_out, small, gain, lengths, conv_w.T, vec)
    m, mt, dg, gwdt, dv, part, stat = k2(dl, kq, smalls, vecs, masks, live, v, g, ups, wout, states)
    sums = k3(
        part, stat, smalls, vecs, gains, gwdt, masks, tokens, grad_out, m, mt, dg, dv, slope, u, vt, xnt,
        win.reshape(groups, ways * own_d, 2 * channels), wout.reshape(groups, own_e, model), ups)
    block_out, grad_tokens, grad_gain, grad_win, convw, convb, gwx, gwdt, dtb, dskip, grad_wout, mean, peak = k4(
        float(groups * ways * length * inner), *sums, w_in, gain, rank + 2 * states)
    return (
        block_out, grad_tokens, grad_gain[0], grad_win, convw.T, convb[0], gwx.T, gwdt, dtb[0], dskip[0], grad_wout, mean[0, 0], peak[0, 0],
    )


def on_device_any(*args):
    if lax.axis_size("dp") == 4 and lax.axis_size("z") == 4:
        return on_device_direct(*args)
    return on_device(*args)


def solution(mesh):
    wide, narrow = mesh.devices.shape
    fine = Mesh(mesh.devices.reshape(wide // 2, 2, narrow), ALL)
    cut = (P(ALL, None), P(ALL))
    in_specs = (P(ALL, None, None), cut[0], cut[1], cut[0], cut[0], cut[1], cut[0], cut[0], cut[1], cut[1], cut[0], P(ALL, None, None))
    out_specs = (P(ALL, None, None), P(ALL, None, None), cut[1], cut[0], cut[0], cut[1], cut[0], cut[0], cut[1], cut[1], cut[0], P(), P())
    return jax.shard_map(on_device_any, mesh=fine, in_specs=in_specs, out_specs=out_specs, check_vma=False)
```

```python
import functools
import jax, jax.numpy as jnp
from jax import lax
from jax.experimental import pallas as pl
from jax.experimental.pallas import tpu as pltpu
from jax.sharding import Mesh, PartitionSpec as P

DOCS = 4
EPS = 1e-05
ALL = ("dp", "core", "z")
TP = ("core", "z")

f32 = jnp.float32
bf16 = jnp.bfloat16

def fold(x):
    total = x[:, :128]
    for at in range(128, x.shape[1], 128):
        total = total + x[:, at:at+128]
    return total

def mixer_kernel(states, unroll, chunk, flags_ref, kq3_ref, sk_ref, pre_ref, v_ref, g_ref, dm_ref, skip_ref,
                 m_ref, dg_ref, dpre_ref, dv_ref, dkq_ref, stat_ref, s_ref, h_ref, rate_ref, rv_ref, kb_ref, drr_ref):
    rows = pre_ref.shape[0]
    width = pre_ref.shape[1]
    steps = rows // 8
    wide = states * 128
    spread_rows = kq3_ref.shape[1]
    def spread(i, c):
        r = pl.ds(pl.multiple_of(i * chunk, chunk), chunk)
        left = kq3_ref[r, :]
        for part in range(0, 2 * wide, 512):
            ids = lax.broadcasted_iota(jnp.int32, (spread_rows, 512), 0) % (2 * states)
            col = lax.broadcasted_iota(jnp.int32, (spread_rows, 512), 1) // 128 + part // 128
            hot = jnp.where(ids == col, 1.0, 0.0).astype(bf16)
            kb_ref[r, part:part+512] = jnp.dot(left, hot, preferred_element_type=f32)
        return c
    lax.fori_loop(0, rows // chunk, spread, 0)

    def before(i, c):
        r = pl.ds(pl.multiple_of(i * 64, 64), 64)
        live = flags_ref[r, 1:2]
        beta = jax.nn.sigmoid(pre_ref[r, :])
        part = 1.0 / (1.0 + beta * sk_ref[r, 0:1])
        rate = beta * part
        rate_ref[r, :] = rate
        v = v_ref[r, :]
        rv_ref[r, :] = rate * v
        dpre_ref[r, :] = part * part * beta * (1.0 - beta)
        g = g_ref[r, :]
        sg = jax.nn.sigmoid(g)
        dm = dm_ref[r, :] * live
        dv_ref[r, :] = dm * (g * sg)
        dg_ref[r, :] = dm * (sg * (1.0 + g * (1.0 - sg)))
        return c
    lax.fori_loop(0, rows // 64, before, 0)

    s_ref[0, 0] = jnp.zeros(s_ref.shape[2:], f32)

    group = unroll
    tile = lambda x: jnp.concatenate([x] * (width // 128), axis=1)
    span = group * 8
    at = [slice(j * 8, j * 8 + 8) for j in range(group)]
    def view(ref, i):
        return ref.at[pl.ds(pl.multiple_of(i * span, span), span)]

    def forward(i, carry):
        flags, rates, rvs, vs, kbs, ms = [view(x, i) for x in (flags_ref, rate_ref, rv_ref, v_ref, kb_ref, m_ref)]
        keep = [jnp.broadcast_to(flags[r, 0:1], (8, 128)) for r in at]
        rate = [rates[r, :] for r in at]
        rv = [rvs[r, :] for r in at]
        y = [skip_ref[...] * vs[r, :] for r in at]
        for n in range(states):
            state = s_ref[i, 0, n]
            for j, r in enumerate(at):
                kb = kbs[r, n*128:(n+1)*128]
                qb = kbs[r, wide+n*128:wide+(n+1)*128]
                state = (tile(keep[j]) - rate[j] * tile(kb * kb * keep[j])) * state + rv[j] * tile(kb)
                if j < group - 1:
                    s_ref[i, j + 1, n] = state
                else:
                    s_ref[i + 1, 0, n] = state
                y[j] = y[j] + state * tile(qb)
        for j, r in enumerate(at):
            ms[r, :] = y[j]
        return carry

    lax.fori_loop(0, steps // group, forward, 0)
    h_ref[...] = jnp.zeros_like(h_ref)

    def backward(step, carry):
        i = steps // group - 1 - step
        flags, rates, rvs, vs, kbs, dvs, dpres, drrs = [view(x, i) for x in (flags_ref, rate_ref, rv_ref, v_ref, kb_ref, dv_ref, dpre_ref, drr_ref)]
        keep = [jnp.broadcast_to(flags[r, 0:1], (8, 128)) for r in at]
        rate = [rates[r, :] for r in at]
        rv = [rvs[r, :] for r in at]
        dy = [dvs[r, :] for r in at]
        hk = [jnp.zeros((8, width), f32) for r in at]
        hs2 = [jnp.zeros((8, width), f32) for r in at]
        for n in range(states):
            ah = h_ref[n]
            after_ = s_ref[i + 1, 0, n]
            for j in range(group - 1, -1, -1):
                r = at[j]
                kb = kbs[r, n*128:(n+1)*128]
                qb = kbs[r, wide+n*128:wide+(n+1)*128]
                kk = kb * keep[j]
                held = tile(kb * kk)
                h = dy[j] * tile(qb) + ah
                prior = s_ref[i, j, n]
                hs = h * prior
                hk[j] = hk[j] + h * tile(kb)
                hs2[j] = hs2[j] + hs * held
                kbs[r, n*128:(n+1)*128] = fold(h * rv[j]) - 2.0 * kk * fold(hs * rate[j])
                kbs[r, wide+n*128:wide+(n+1)*128] = fold(dy[j] * after_)
                after_ = prior
                ah = (tile(keep[j]) - rate[j] * held) * h
            h_ref[n] = ah
        for j, r in enumerate(at):
            v = vs[r, :]
            drate = v * hk[j] - hs2[j]
            drrs[r, :] = fold(drate * rate[j] * rate[j]) * (-2.0)
            dpres[r, :] = drate * dpres[r, :]
            dvs[r, :] = rate[j] * hk[j] + skip_ref[...] * dy[j]
            stat_ref[0, 0] += dy[j] * v
        return carry

    stat_ref[...] = jnp.zeros_like(stat_ref)
    lax.fori_loop(0, steps // group, backward, 0)

    first = pl.program_id(0) == 0
    def gather(i, c):
        r = pl.ds(pl.multiple_of(i * chunk, chunk), chunk)
        total = jnp.zeros((chunk, 128), f32)
        for part in range(0, 2 * wide, 512):
            row = lax.broadcasted_iota(jnp.int32, (512, 128), 0) // 128 + part // 128
            col = lax.broadcasted_iota(jnp.int32, (512, 128), 1)
            hot = jnp.where(row == col, 1.0, 0.0).astype(bf16)
            total += jnp.dot(kb_ref[r, part:part+512].astype(bf16), hot, preferred_element_type=f32)
        col = lax.broadcasted_iota(jnp.int32, (128, 128), 1)
        hot = jnp.where(col == 2 * states, 1.0, 0.0).astype(bf16)
        total += jnp.dot(drr_ref[r, :].astype(bf16), hot, preferred_element_type=f32)
        dkq_ref[r, :] = jnp.where(first, total, dkq_ref[r, :] + total)
        return c
    lax.fori_loop(0, rows // chunk, gather, 0)

    def after(i, c):
        r = pl.ds(pl.multiple_of(i * 64, 64), 64)
        live = flags_ref[r, 1:2]
        y = m_ref[r, :]
        g = g_ref[r, :]
        m_ref[r, :] = y * (g * jax.nn.sigmoid(g)) * live
        dg_ref[r, :] = y * dg_ref[r, :]
        shown = (jax.nn.sigmoid(pre_ref[r, :]) * live).reshape(8, 8, width)
        stat_ref[0, 1] += jnp.sum(shown, axis=0)
        stat_ref[0, 2] = jnp.maximum(stat_ref[0, 2], jnp.max(shown, axis=0))
        return c
    lax.fori_loop(0, rows // 64, after, 0)

def mixer(flags, kq3, sk, pre, v, g, dm, skip, states=16, width=256, unroll=1):
    rows, total = pre.shape
    steps = rows // 8
    tiles = total // width
    big = jax.ShapeDtypeStruct((rows, total), f32)
    cut = pl.BlockSpec((rows, width), lambda h: (0, h))
    whole = lambda a: pl.BlockSpec(a.shape, lambda h: (0,) * a.ndim)
    return pl.pallas_call(
        functools.partial(mixer_kernel, states, unroll, min(256, rows)),
        grid=(tiles,),
        out_shape=(big, big, big, big, jax.ShapeDtypeStruct((rows, 128), f32), jax.ShapeDtypeStruct((tiles, 3, 8, width), f32)),
        in_specs=[whole(flags), whole(kq3), whole(sk), cut, cut, cut, cut, pl.BlockSpec((1, width), lambda h: (0, h))],
        out_specs=(cut, cut, cut, cut, pl.BlockSpec((rows, 128), lambda h: (0, 0)), pl.BlockSpec((1, 3, 8, width), lambda h: (h, 0, 0, 0))),
        scratch_shapes=[pltpu.VMEM((steps//unroll+1, unroll, states, 8, width), f32), pltpu.VMEM((states, 8, width), f32)] + [pltpu.VMEM((rows, width), f32)]*2
          + [pltpu.VMEM((rows, 2*states*128), f32), pltpu.VMEM((rows, 128), f32)],
        compiler_params=pltpu.CompilerParams(vmem_limit_bytes=60*1024*1024),
    )(flags, kq3, sk, pre, v, g, dm, skip)


MESH = pl.DeviceIdType.MESH


def flip(value, bit):
    return value + bit * (1 - 2 * ((value // bit) % 2))


def place():
    d, c, z = lax.axis_index("dp"), lax.axis_index("core"), lax.axis_index("z")
    return d, c, z


def put(src, dst, send, recv, device):
    copy = pltpu.make_async_remote_copy(src_ref=src, dst_ref=dst, send_sem=send, recv_sem=recv, device_id=device, device_id_type=MESH)
    copy.start()
    return copy


def landed(slot, sem, device):
    pltpu.make_async_remote_copy(src_ref=slot, dst_ref=slot, send_sem=sem, recv_sem=sem, device_id=device, device_id_type=MESH).wait_recv()


def sent(slot, sem, device):
    pltpu.make_async_remote_copy(src_ref=slot, dst_ref=slot, send_sem=sem, recv_sem=sem, device_id=device, device_id_type=MESH).wait_send()


def greet(devices):
    barrier = pltpu.get_barrier_semaphore()
    for device in devices:
        pl.semaphore_signal(barrier, inc=1, device_id=device, device_id_type=MESH)
    pl.semaphore_wait(barrier, len(devices))


def mates():
    return [(a, k) for k in (0, 1, 3, 2) for a in (1, 0) if (a, k) != (0, 0)]


def mate(step, sign=1):
    d, c, z = place()
    a, k = step
    return d, (flip(c, 1) if a else c), lax.rem(z + sign * k + 4, 4)


def rank_of(device):
    return device[1] * 4 + device[2]


PIECES = 4


UP_HOPS = 2


def k1_kernel(tok_ref, up_ref, w_ref, wout_ref, wx_ref, wdt_ref, gain_ref, lens_ref, convw_ref, convb_ref, dtb_ref, skip_ref,
              xnt_out, ups_ref, win_out, wouts_ref, smalls_ref, vecs_ref, gains_ref, masks_out, live_out,
              u_out, g_out, v_out, vt_out, slope_out, dl_ref, kq_ref,
              masks_ref, live_ref, u_ref, g_ref, v_ref, vt_ref, slope_ref, save_sem, cols_ref, meta_ref, small_ref,
              xs_ref, xn_ref, xnt_ref, win_ref, metas_ref, part_ref, out_ref, sib_ref, base_ref, left_ref, right_ref, tor_ref, tol_ref,
              own_sem, ms, mr, qs, qr, xls, xlr, xrs, xrr, xcs, xcr, as_, ar, ps, pr, rs, rr, ws, wr, ts, tr, tls, tlr, trs, trr, tos, tor):
    d, c, z = place()
    j = c * 4 + z
    dx, dy, dd = flip(d, 1), flip(d, 2), flip(flip(d, 1), 2)
    xn, yn, dn = (dx, c, z), (dy, c, z), (dd, c, z)
    sib = (d, flip(c, 1), z)
    left = (d, c, lax.rem(z + 3, 4))
    right = (d, c, lax.rem(z + 1, 4))
    steps = mates()
    length = tok_ref.shape[1]
    model = tok_ref.shape[2]
    depth = cols_ref.shape[1]
    for rank in range(8):
        for n in range(8):
            cols_ref[rank, :, n * 128:(n + 1) * 128] = w_ref[:, (n * 8 + rank) * 128:(n * 8 + rank + 1) * 128]
    meta_ref[...] = jnp.zeros_like(meta_ref)
    meta_ref[0:1, 0:depth] = gain_ref[...].astype(f32)
    meta_ref[0:1, depth:2 * depth] = gain_ref[...].astype(f32)
    meta_ref[1:2, 0:5] = lens_ref[...].astype(f32)
    meta_ref[8:12, :] = convw_ref[...].astype(f32)
    meta_ref[12:13, :] = convb_ref[...].astype(f32)
    meta_ref[13:14, :] = dtb_ref[...].astype(f32)
    meta_ref[14:15, :] = skip_ref[...].astype(f32)
    narrow_rows = wx_ref.shape[0]
    small_ref[:, 0:128] = wx_ref[0:128, :].astype(f32).T.astype(bf16)
    tail = jnp.concatenate([wx_ref[128:narrow_rows, :].astype(f32), jnp.zeros((256 - narrow_rows, 128), f32)], axis=0)
    small_ref[:, 128:256] = tail.T.astype(bf16)
    small_ref[:, 256:384] = wdt_ref[...]
    greet([mate(s) for s in steps] + [xn, yn, dn])
    tiles = u_ref.shape[0]
    width = tiles * 128
    count = g_ref.shape[1]

    def rows(rank):
        return pl.ds(pl.multiple_of(rank * length, length), length)

    def block(group, rank):
        return pl.ds(pl.multiple_of((group * 8 + rank) * depth, depth), depth)

    own_e = wout_ref.shape[0]

    def part_e(group, start=0, size=own_e):
        return pl.ds(pl.multiple_of(group * own_e + start, 16), size)

    own = [
        pltpu.make_async_copy(tok_ref.at[0], xs_ref.at[rows(j)], own_sem.at[0]),
        pltpu.make_async_copy(up_ref.at[0], ups_ref.at[rows(j)], own_sem.at[1]),
        pltpu.make_async_copy(cols_ref.at[j], win_ref.at[block(d, j)], own_sem.at[2]),
        pltpu.make_async_copy(wout_ref, wouts_ref.at[part_e(d)], own_sem.at[3]),
        pltpu.make_async_copy(small_ref, smalls_ref.at[part_e(d)], own_sem.at[4]),
        pltpu.make_async_copy(meta_ref, metas_ref.at[d, j], own_sem.at[5]),
    ]
    for copy in own:
        copy.start()
    pending = []
    for i, s in enumerate(steps):
        to = mate(s)
        pending.append(put(meta_ref, metas_ref.at[d, j], ms.at[i], mr.at[i], to))
    for i, s in enumerate(steps):
        to = mate(s)
        pending.append(put(cols_ref.at[rank_of(to)], win_ref.at[block(d, j)], as_.at[i], ar.at[i], to))
    for i, to in enumerate((xn, yn, dn)):
        pending.append(put(small_ref, smalls_ref.at[part_e(d)], ps.at[16 + i], pr.at[16 + i], to))
    halves = own_e // 2
    pending.append(put(wout_ref, wouts_ref.at[part_e(d)], ws.at[0], wr.at[0], xn))
    pending.append(put(wout_ref, wouts_ref.at[part_e(d)], ws.at[1], wr.at[1], yn))
    own[2].wait()
    slot = win_ref.at[block(d, j)]
    pending.append(put(slot, slot, ps.at[7], pr.at[7], xn))
    pending.append(put(slot, slot, ps.at[15], pr.at[15], yn))

    def row_start(ref, out, base):
        pending.append(put(ref.at[0], out.at[rows(j)], xcs.at[base + z], xcr.at[base + z], sib))

        @pl.when(z < 3)
        def _():
            put(ref.at[0], out.at[rows(j)], xls.at[base], xlr.at[base], right)

        @pl.when(z > 0)
        def _():
            put(ref.at[0], out.at[rows(j)], xrs.at[base], xrr.at[base], left)

    def row_hop(out, base, i, then=None, hops=3):
        if i >= hops:
            return

        @pl.when(z > i)
        def _():
            at = z - 1 - i
            slot = out.at[rows(c * 4 + at)]
            landed(slot, xlr.at[base + i], left)
            if i < hops - 1:
                @pl.when(z < 3)
                def _():
                    put(slot, slot, xls.at[base + i + 1], xlr.at[base + i + 1], right)
            put(slot, slot, xcs.at[base + at], xcr.at[base + at], sib)
            if then is not None:
                then(c * 4 + at)

        @pl.when(z < 3 - i)
        def _():
            at = z + 1 + i
            slot = out.at[rows(c * 4 + at)]
            landed(slot, xrr.at[base + i], right)
            if i < hops - 1:
                @pl.when(z > 0)
                def _():
                    put(slot, slot, xrs.at[base + i + 1], xrr.at[base + i + 1], left)
            put(slot, slot, xcs.at[base + at], xcr.at[base + at], sib)
            if then is not None:
                then(c * 4 + at)

    def row_end(out, base, hops=3):
        for i in range(hops):
            @pl.when((z < 3) & (z >= i))
            def _():
                sent(out.at[rows(j)], xls.at[base + i], right)

            @pl.when((z > 0) & (z <= 3 - i))
            def _():
                sent(out.at[rows(j)], xrs.at[base + i], left)
        for at in range(4):
            @pl.when((z != at) & (z <= at + hops) & (at <= z + hops))
            def _():
                sent(out.at[rows(j)], xcs.at[base + at], sib)

    own[5].wait()
    for i, s in enumerate(steps):
        landed(metas_ref.at[d, rank_of(mate(s, -1))], mr.at[i], xn)
    for i, to in enumerate((xn, yn, dn)):
        pending.append(put(metas_ref.at[d], metas_ref.at[d], qs.at[i], qr.at[i], to))
    slots = {7: j}
    for i, s in enumerate(steps):
        slots[i] = rank_of(mate(s, -1))
    order = [7] + list(range(7))

    def pass_on(i):
        src = mate(steps[i], -1)
        slot = win_ref.at[block(d, slots[i])]
        landed(slot, ar.at[i], src)
        pending.append(put(slot, slot, ps.at[i], pr.at[i], xn))
        pending.append(put(slot, slot, ps.at[8 + i], pr.at[8 + i], yn))

    def relay(k):
        i = order[k]
        slot = win_ref.at[block(dx, slots[i])]
        landed(slot, pr.at[i], xn)
        if k % 2 == 0:
            pending.append(put(slot, slot, rs.at[k // 2], rr.at[k // 2], yn))
        slot = win_ref.at[block(dy, slots[i])]
        landed(slot, pr.at[8 + i], yn)
        if k % 2 == 1:
            pending.append(put(slot, slot, rs.at[4 + k // 2], rr.at[4 + k // 2], xn))

    pass_on(0)
    for i, (to, at) in enumerate(((xn, dx), (yn, dy), (dn, dd))):
        landed(metas_ref.at[at], qr.at[i], to)
    lens = jnp.concatenate([metas_ref[d, r, 1:2, :] for r in range(8)], axis=0)
    ends = []
    last = jnp.zeros((8, 1), f32)
    for i in range(5):
        last = last + lens[:, i:i + 1]
        ends.append(jnp.broadcast_to(last, (8, 128)))

    def mask_step(t, carry):
        here = t.astype(f32)

        def segment(at):
            total = jnp.zeros((8, 128), f32)
            for end in ends:
                total = total + jnp.where(end <= at, 1.0, 0.0)
            return total

        now = segment(here)
        r = pl.ds(pl.multiple_of(t * 8, 8), 8)
        for o in range(1, 4):
            same = jnp.where(segment(here - o) == now, 1.0, 0.0)
            masks_ref[o - 1, r, :] = jnp.where(here >= o, same, 0.0)
        live_ref[0, r, :] = jnp.where(now < DOCS, 1.0, 0.0)
        return carry

    lax.fori_loop(0, length, mask_step, 0)
    masks_ref[:, count:, :] = jnp.zeros((3, masks_ref.shape[1] - count, 128), f32)
    lane = lax.broadcasted_iota(jnp.int32, (1, 128), 1)
    for group in range(4):
        for pair in range(4):
            at = group * 512 + pair * 128
            gains_ref[:, at:at + 128] = jnp.where(lane < depth, metas_ref[group, 2 * pair, 0:1, :], metas_ref[group, 2 * pair + 1, 0:1, :])
        vecs_ref[:, group * own_e:(group + 1) * own_e] = metas_ref[group, j, 8:16, :]

    def normalize(rank):
        def body(i, carry):
            r = pl.ds(pl.multiple_of(rank * length + i * 16, 16), 16)
            x = xs_ref[r, :].astype(f32)
            scale = lax.rsqrt(jnp.sum(x * x, axis=1, keepdims=True) * (1.0 / model) + EPS)
            xn_ref[r, :] = (x * scale * gains_ref[...]).astype(bf16)
            return carry

        lax.fori_loop(0, length // 16, body, 0, unroll=4)

    for i in range(1, 4):
        pass_on(i)
    slot = wouts_ref.at[part_e(dx)]
    landed(slot, wr.at[0], xn)
    slot = wouts_ref.at[part_e(dx, 0, halves)]
    pending.append(put(slot, slot, ws.at[2], wr.at[2], yn))
    slot = wouts_ref.at[part_e(dy)]
    landed(slot, wr.at[1], yn)
    slot = wouts_ref.at[part_e(dy, halves, halves)]
    pending.append(put(slot, slot, ws.at[3], wr.at[3], xn))

    row_start(tok_ref, xs_ref, 0)
    for i in range(4, 7):
        pass_on(i)
    own[0].wait()
    normalize(j)
    row_hop(xs_ref, 0, 0, normalize)
    for k in range(4):
        relay(k)
    row_hop(xs_ref, 0, 1, normalize)
    for k in range(4, 8):
        relay(k)
    row_hop(xs_ref, 0, 2, normalize)
    row_start(up_ref, ups_ref, 4)
    for at in range(4):
        rank = flip(c, 1) * 4 + at
        landed(xs_ref.at[rows(rank)], xcr.at[at], sib)
        normalize(rank)
    for k, i in enumerate(order):
        slot = win_ref.at[block(dd, slots[i])]
        if k % 2 == 0:
            landed(slot, rr.at[k // 2], yn)
        else:
            landed(slot, rr.at[4 + k // 2], xn)
    own += [pltpu.make_async_copy(xnt_ref, xnt_out, own_sem.at[6]), pltpu.make_async_copy(win_ref, win_out, own_sem.at[7])]
    own[7].start()
    lead = u_ref.shape[1] - count
    u_ref[:, 0:lead, :] = jnp.zeros((tiles, lead, 128), f32)

    tile = 256

    def spread(out, first, start):
        def body(i, carry):
            product = jnp.dot(xn_ref[...], win_ref[:, pl.ds(pl.multiple_of(start + i * tile, tile), tile)], preferred_element_type=f32)
            for r in range(8):
                for part in range(0, tile, 128):
                    out[i * (tile // 128) + part // 128, pl.ds(first + r, length, stride=8), :] = product[r * length:(r + 1) * length, part:part + 128]
            return carry

        lax.fori_loop(0, width // tile, body, 0)

    spread(u_ref, lead, 0)
    taps = [vecs_ref[o:o + 1, :] for o in range(4)]
    bias = vecs_ref[4:5, :]

    def conv_step(i, carry):
        r = pl.ds(pl.multiple_of(i * 32, 32), 32)
        for n in range(tiles):
            lanes = slice(n * 128, n * 128 + 128)
            total = bias[:, lanes] + taps[3][:, lanes] * u_ref[n, pl.ds(pl.multiple_of(lead + i * 32, 8), 32), :]
            for o in range(1, 4):
                total = total + taps[3 - o][:, lanes] * (u_ref[n, pl.ds(pl.multiple_of(lead + i * 32 - 8 * o, 8), 32), :] * masks_ref[o - 1, r, :])
            sig = jax.nn.sigmoid(total)
            v_ref[n, r, :] = (total * sig).astype(bf16).astype(f32)
            slope_ref[n, r, :] = sig * (1.0 + total * (1.0 - sig))
        return carry

    lax.fori_loop(0, count // 32, conv_step, 0, unroll=2)
    for copy in own[3:5]:
        copy.wait()
    for i, (to, at) in enumerate(((xn, dx), (yn, dy), (dn, dd))):
        landed(smalls_ref.at[part_e(at)], pr.at[16 + i], to)
    quarter = count // 4
    narrow = smalls_ref[:, 128:256].astype(f32)
    packed = jnp.zeros((quarter, 128), f32)
    for b in range(4):
        r = slice(b * quarter, (b + 1) * quarter)
        values = jnp.concatenate([v_ref[n, r, :].astype(bf16) for n in range(tiles)], axis=1)
        part_ref[r, :] = jnp.dot(values, smalls_ref[:, 0:128], preferred_element_type=f32)
        turned = pltpu.roll(narrow, 32 * b, 1) if b else narrow
        packed = packed + jnp.dot(values, turned.astype(bf16), preferred_element_type=f32)
    part_ref[count:count + quarter, :] = packed
    saves = [(u_ref, u_out), (v_ref, v_out), (slope_ref, slope_out), (masks_ref, masks_out), (live_ref, live_out), (g_ref, g_out), (vt_ref, vt_out)]
    saves = [pltpu.make_async_copy(a, b, save_sem.at[i]) for i, (a, b) in enumerate(saves)]
    for copy in saves[:5]:
        copy.start()

    def early():
        row_hop(ups_ref, 4, 0, None, UP_HOPS)

    def between():
        spread(g_ref, 0, width)
        saves[5].start()

    def late():
        def turn_x(i, carry):
            part = pl.ds(pl.multiple_of(i * 128, 128), 128)
            for rank in range(8):
                r = slice(rank * length, (rank + 1) * length)
                xnt_ref[part, r] = xn_ref[r, part].T
            return carry

        lax.fori_loop(0, model // 128, turn_x, 0)
        own[6].start()
        row_hop(ups_ref, 4, 1, None, UP_HOPS)

        def turn_v(i, carry):
            r = pl.ds(pl.multiple_of(i * 128, 128), 128)
            for n in range(tiles):
                vt_ref[n * 128:(n + 1) * 128, r] = v_ref[n, r, :].T.astype(bf16)
            return carry

        lax.fori_loop(0, count // 128, turn_v, 0)
        saves[6].start()

    line_total(part_ref, out_ref, sib_ref, base_ref, left_ref, right_ref, tor_ref, tol_ref, ts, tr, tls, tlr, trs, trr, tos, tor, early, between, late)
    dl_ref[...] = out_ref[0:count, :].astype(bf16)
    for b in range(4):
        packed = out_ref[count:count + quarter, :]
        kq_ref[b * quarter:(b + 1) * quarter, :] = pltpu.roll(packed, 128 - 32 * b, 1) if b else packed
    row_hop(ups_ref, 4, 2, None, UP_HOPS)
    for at in range(4):
        @pl.when((z <= at + UP_HOPS) & (at <= z + UP_HOPS))
        def _():
            landed(ups_ref.at[rows(flip(c, 1) * 4 + at)], xcr.at[4 + at], sib)

    landed(wouts_ref.at[part_e(dd, 0, halves)], wr.at[2], yn)
    landed(wouts_ref.at[part_e(dd, halves, halves)], wr.at[3], xn)
    row_end(xs_ref, 0)
    row_end(ups_ref, 4, UP_HOPS)
    own[1].wait()
    for copy in saves:
        copy.wait()
    own[6].wait()
    own[7].wait()
    for copy in pending:
        copy.wait_send()


def line_total(part_ref, out_ref, sib_ref, base_ref, left_ref, right_ref, tor_ref, tol_ref, ss, sr, ls, lr, rs, rr, os_, or_, early, between, late):
    d, c, z = place()
    sib = (d, flip(c, 1), z)
    left = (d, c, lax.rem(z + 3, 4))
    right = (d, c, lax.rem(z + 1, 4))
    rows = part_ref.shape[0] // 2
    piece = rows // PIECES
    mine, theirs = c * rows, flip(c, 1) * rows

    def cut(p):
        return pl.ds(p * piece, piece)

    def far(base, p):
        return pl.ds(pl.multiple_of(base + p * piece, 8), piece)

    for p in range(PIECES):
        put(part_ref.at[far(theirs, p)], sib_ref.at[cut(p)], ss.at[p], sr.at[p], sib)
    for p in range(PIECES):
        landed(sib_ref.at[cut(p)], sr.at[p], sib)
        base_ref[cut(p), :] = part_ref[far(mine, p), :] + sib_ref[cut(p), :]

        @pl.when(z == 0)
        def _():
            put(base_ref.at[cut(p)], left_ref.at[cut(p)], rs.at[p], lr.at[p], right)

        @pl.when(z == 3)
        def _():
            put(base_ref.at[cut(p)], right_ref.at[cut(p)], ls.at[p], rr.at[p], left)

    early()

    def from_left(p):
        landed(left_ref.at[cut(p)], lr.at[p], left)

        @pl.when(z < 3)
        def _():
            tor_ref[cut(p), :] = base_ref[cut(p), :] + left_ref[cut(p), :]
            put(tor_ref.at[cut(p)], left_ref.at[cut(p)], rs.at[p], lr.at[p], right)

    def from_right(p):
        landed(right_ref.at[cut(p)], rr.at[p], right)

        @pl.when(z > 0)
        def _():
            tol_ref[cut(p), :] = base_ref[cut(p), :] + right_ref[cut(p), :]
            put(tol_ref.at[cut(p)], right_ref.at[cut(p)], ls.at[p], rr.at[p], left)

    @pl.when(z == 1)
    def _():
        for p in range(PIECES):
            from_left(p)

    @pl.when(z == 2)
    def _():
        for p in range(PIECES):
            from_right(p)

    between()

    @pl.when(z < 2)
    def _():
        for p in range(PIECES):
            from_right(p)

    @pl.when(z >= 2)
    def _():
        for p in range(PIECES):
            from_left(p)

    for p in range(PIECES):
        out_ref[far(mine, p), :] = base_ref[cut(p), :]

        @pl.when(z > 0)
        def _():
            out_ref[far(mine, p), :] += left_ref[cut(p), :]

        @pl.when(z < 3)
        def _():
            out_ref[far(mine, p), :] += right_ref[cut(p), :]

        put(out_ref.at[far(mine, p)], out_ref.at[far(mine, p)], os_.at[p], or_.at[p], sib)
    late()
    for p in range(PIECES):
        landed(out_ref.at[far(theirs, p)], or_.at[p], sib)
        sent(out_ref.at[far(mine, p)], os_.at[p], sib)
        sent(part_ref.at[far(theirs, p)], ss.at[p], sib)

        @pl.when(z < 3)
        def _():
            sent(base_ref.at[cut(p)], rs.at[p], right)

        @pl.when(z > 0)
        def _():
            sent(base_ref.at[cut(p)], ls.at[p], left)


def k1(tokens, upstream, w_in, w_out, w_x, w_dt, gain, lengths, conv_w, conv_b, dt_bias, skip):
    groups, ways = 4, 8
    small = jax.ShapeDtypeStruct((128, 384), bf16)
    cols = jax.ShapeDtypeStruct((ways, w_in.shape[0], w_in.shape[1] // ways), bf16)
    meta = jax.ShapeDtypeStruct((16, 128), f32)
    like = jax.ShapeDtypeStruct
    length, model = tokens.shape[1:]
    count = ways * length
    channels = groups * w_out.shape[0]
    dma = lambda n: pltpu.SemaphoreType.DMA((n,))
    some = pl.BlockSpec(memory_space=pl.ANY)
    far = pl.BlockSpec(memory_space=pltpu.HBM)
    here = pl.BlockSpec(memory_space=pltpu.VMEM)
    packed = count + count // 4
    return pl.pallas_call(
        k1_kernel,
        out_shape=(
            like((model, count), bf16),
            like((count, model), bf16),
            like((groups * ways * cols.shape[1], cols.shape[2]), bf16),
            like((channels, model), bf16),
            like((channels, small.shape[1]), bf16),
            like((8, channels), f32),
            like((1, model), f32),
            like((3, count + 32, 128), f32),
            like((1, count, 128), f32),
            like((channels // 128, count + 24, 128), f32),
            like((channels // 128, count, 128), f32),
            like((channels // 128, count, 128), f32),
            like((channels, count), bf16),
            like((channels // 128, count, 128), f32),
            like((count, 128), bf16),
            like((count, 128), f32),
        ),
        in_specs=[some] * 2 + [here, some] + [here] * 8,
        out_specs=(far,) * 4 + (here,) * 3 + (far,) * 7 + (here,) * 2,
        scratch_shapes=[
            pltpu.VMEM((3, count + 32, 128), f32),
            pltpu.VMEM((1, count, 128), f32),
            pltpu.VMEM((channels // 128, count + 24, 128), f32),
            pltpu.VMEM((channels // 128, count, 128), f32),
            pltpu.VMEM((channels // 128, count, 128), f32),
            pltpu.VMEM((channels, count), bf16),
            pltpu.VMEM((channels // 128, count, 128), f32),
            dma(7),
            pltpu.VMEM(cols.shape, bf16),
            pltpu.VMEM(meta.shape, f32),
            pltpu.VMEM(small.shape, bf16),
            pltpu.VMEM((count, model), bf16),
            pltpu.VMEM((count, model), bf16),
            pltpu.VMEM((model, count), bf16),
            pltpu.VMEM((groups * ways * cols.shape[1], cols.shape[2]), bf16),
            pltpu.VMEM((groups, ways) + meta.shape, f32),
            pltpu.VMEM((packed, 128), f32),
            pltpu.VMEM((packed, 128), f32),
        ] + [pltpu.VMEM((packed // 2, 128), f32)] * 6
        + [dma(8), dma(7), dma(7), dma(3), dma(3), dma(8), dma(8), dma(8), dma(8), dma(8), dma(8), dma(7), dma(7), dma(19), dma(19), dma(8), dma(8), dma(4), dma(4)]
        + [dma(PIECES) for _ in range(8)],
        compiler_params=pltpu.CompilerParams(collective_id=0, has_side_effects=True, vmem_limit_bytes=56 * 1024 * 1024),
    )(tokens, upstream, w_in, w_out, w_x, w_dt, gain, lengths, conv_w, conv_b, dt_bias, skip)


GROUP = 4


def k2_kernel(states, dl_ref, kq_ref, wdt_ref, vecs_ref, keep_ref, live_ref, v_ref, g_ref, ups_any, wout_ref,
              m_ref, mt_ref, dg_ref, gwdt_ref, ups_out, dv_ref, part_ref, stat_ref,
              ups_ref, loads, stores, zs, zr, cs, cr, dpre_ref, s_ref, h_ref, rate_ref, w_ref, y_ref, dm_ref, kb_ref, hot_ref, drr_ref):
    tiles, count = v_ref.shape[:2]
    steps = count // 8
    wide = states * 128
    chunk = 256
    first = pl.program_id(0) == 0
    half = pl.program_id(0)
    both = range(tiles)
    rank = wdt_ref.shape[1]

    length = count // 8
    d, c, z = place()
    sib = (d, flip(c, 1), z)
    left = (d, c, lax.rem(z + 3, 4))
    right = (d, c, lax.rem(z + 1, 4))

    def rows(rank):
        return pl.ds(pl.multiple_of(rank * length, length), length)

    keeps = [pltpu.make_async_copy(ups_ref.at[r // 4, r % 4], ups_out.at[rows(r)], stores.at[r]) for r in range(8)]

    def arrive(act):
        for rank in range(8):
            at = rank % 4
            here = jnp.logical_not(((z == 0) & (at == 3)) | ((z == 3) & (at == 0))) if at in (0, 3) else None
            copy = pltpu.make_async_copy(ups_any.at[rows(rank)], ups_ref.at[rank // 4, at], loads.at[rank])
            if here is None:
                act(copy)
            else:
                @pl.when(here)
                def _():
                    act(copy)

    @pl.when(first)
    def _():
        arrive(lambda copy: copy.start())
        greet([sib, left, right])

        @pl.when(z == 1)
        def _():
            put(ups_any.at[rows(c * 4 + 3)], ups_ref.at[c, 3], zs, zr, left)

        @pl.when(z == 2)
        def _():
            put(ups_any.at[rows(c * 4)], ups_ref.at[c, 0], zs, zr, right)

    def complete():
        for end, source, at in ((0, right, 3), (3, left, 0)):
            @pl.when(z == end)
            def _():
                slot = ups_ref.at[c, at]
                landed(slot, zr, source)
                put(slot, slot, cs, cr, sib)
                landed(ups_ref.at[flip(c, 1), at], cr, sib)
                sent(slot, cs, sib)

        for end, target, at in ((1, left, 3), (2, right, 0)):
            @pl.when(z == end)
            def _():
                sent(ups_any.at[rows(c * 4 + at)], zs, target)

        arrive(lambda copy: copy.wait())
        for copy in keeps:
            copy.start()

    @pl.when(first)
    def _():
        row = lax.broadcasted_iota(jnp.int32, (128, 512), 0)
        col = lax.broadcasted_iota(jnp.int32, (128, 512), 1) // 128
        for part in range(0, 2 * wide, 512):
            hot_ref[:, part:part + 512] = jnp.where((row % 32 == col + part // 128) & (row < 96), 1.0, 0.0).astype(bf16)

    lane = lax.broadcasted_iota(jnp.int32, (chunk, 128), 1)

    def spread(i, carry):
        r = pl.ds(pl.multiple_of(i * chunk, chunk), chunk)
        value = jnp.where(lane < 2 * states, kq_ref[r, :], 0.0)
        hi = value.astype(bf16).astype(f32)
        mid = (value - hi).astype(bf16).astype(f32)
        low = value - hi - mid
        left = (hi + pltpu.roll(mid, 32, 1) + pltpu.roll(low, 64, 1)).astype(bf16)
        for part in range(0, 2 * wide, 512):
            kb_ref[r, part:part + 512] = jnp.dot(left, hot_ref[:, part:part + 512], preferred_element_type=f32)
        return carry

    lax.fori_loop(0, count // chunk, spread, 0)
    cols = (((1,), (1,)), ((), ()))

    def gate_step(i, carry):
        value = ups_ref[i // 2, pl.ds((i % 2) * 2, 2)].reshape(chunk, wout_ref.shape[1])
        product = lax.dot_general(value, wout_ref[...], cols, preferred_element_type=f32)
        for j in range(chunk // length):
            for n in both:
                dm_ref[n, pl.ds(i * (chunk // length) + j, length, stride=8), :] = product[j * length:(j + 1) * length, n * 128:(n + 1) * 128]
        return carry

    bias = vecs_ref[5:6, :]
    skip = vecs_ref[6:7, :]
    tile_of = lambda x, n: x[:, n * 128:(n + 1) * 128]
    ks = lax.broadcasted_iota(jnp.int32, (128, 128), 1)

    def before(i, carry):
        seen = list(carry)
        r = pl.ds(pl.multiple_of(i * 128, 128), 128)
        live = live_ref[0, r, :]
        k = jnp.where(ks < states, kq_ref[r, :], 0.0)
        sk = jnp.sum(k * k, axis=1, keepdims=True)
        pre = lax.dot_general(dl_ref[r, :], wdt_ref[...], cols, preferred_element_type=f32) + bias
        for n in both:
            beta = jax.nn.sigmoid(tile_of(pre, n))
            part = 1.0 / (1.0 + beta * sk)
            rate_ref[n, r, :] = beta * part
            w_ref[n, r, :] = part * part * beta * (1.0 - beta)
            shown = (beta * live).reshape(16, 8, 128)
            seen[n] = seen[n] + jnp.sum(shown, axis=0)
            seen[tiles + n] = jnp.maximum(seen[tiles + n], jnp.max(shown, axis=0))
        return tuple(seen)

    blank = jnp.zeros((8, 128), f32)
    seen = lax.fori_loop(0, count // 128, before, (blank,) * (2 * tiles))
    s_ref[0, 0] = jnp.zeros(s_ref.shape[2:], f32)
    span = GROUP * 8
    at = [slice(j * 8, j * 8 + 8) for j in range(GROUP)]

    def view(ref, i):
        r = pl.ds(pl.multiple_of(i * span, span), span)
        return ref.at[:, r] if len(ref.shape) == 3 else ref.at[r]

    def pair(ref, r):
        return jnp.concatenate([ref[n, r, :] for n in both], axis=1)

    def keep_pair(ref, r, value):
        for n in both:
            ref[n, r, :] = tile_of(value, n)

    tile = lambda x: jnp.concatenate([x] * tiles, axis=1)

    def fold(x):
        total = tile_of(x, 0)
        for n in range(1, tiles):
            total = total + tile_of(x, n)
        return total

    def forward(i, carry):
        keeps, rates, vs, kbs, ys = [view(x, i) for x in (keep_ref, rate_ref, v_ref, kb_ref, y_ref)]
        keep = [keeps[0, r, :] for r in at]
        rate = [pair(rates, r) for r in at]
        value = [pair(vs, r) for r in at]
        rv = [a * b for a, b in zip(rate, value)]
        y = [skip * b for b in value]
        for n in range(states):
            state = s_ref[i, 0, n]
            for j, r in enumerate(at):
                kb = kbs[r, n * 128:(n + 1) * 128]
                qb = kbs[r, wide + n * 128:wide + (n + 1) * 128]
                state = (tile(keep[j]) - rate[j] * tile(kb * kb * keep[j])) * state + rv[j] * tile(kb)
                if j < GROUP - 1:
                    s_ref[i, j + 1, n] = state
                else:
                    s_ref[i + 1, 0, n] = state
                y[j] = y[j] + state * tile(qb)
        for j, r in enumerate(at):
            keep_pair(ys, r, y[j])
        return carry

    lax.fori_loop(0, steps // GROUP, forward, 0)
    h_ref[...] = jnp.zeros_like(h_ref)

    @pl.when(first)
    def _():
        complete()

    lax.fori_loop(0, count // chunk, gate_step, 0)

    def gates(i, carry):
        r = pl.ds(pl.multiple_of(i * 32, 32), 32)
        live = live_ref[0, r, :]
        for n in both:
            g = g_ref[n, r, :]
            sg = jax.nn.sigmoid(g)
            silu = g * sg
            y = y_ref[n, r, :]
            dm = dm_ref[n, r, :] * live
            dv_ref[n, r, :] = dm * silu
            dm_ref[n, r, :] = dm * y * (sg * (1.0 + g * (1.0 - sg)))
            y_ref[n, r, :] = y * silu * live
        return carry

    lax.fori_loop(0, count // 32, gates, 0, unroll=2)

    def backward(step, carry):
        i = steps // GROUP - 1 - step
        keeps, rates, vs, kbs, dvs, ws, drrs = [view(x, i) for x in (keep_ref, rate_ref, v_ref, kb_ref, dv_ref, w_ref, drr_ref)]
        keep = [keeps[0, r, :] for r in at]
        rate = [pair(rates, r) for r in at]
        value = [pair(vs, r) for r in at]
        rv = [a * b for a, b in zip(rate, value)]
        dy = [pair(dvs, r) for r in at]
        hk = [jnp.zeros((8, tiles * 128), f32) for r in at]
        hs2 = [jnp.zeros((8, tiles * 128), f32) for r in at]
        for n in range(states):
            ah = h_ref[n]
            later = s_ref[i + 1, 0, n]
            for j in range(GROUP - 1, -1, -1):
                r = at[j]
                kb = kbs[r, n * 128:(n + 1) * 128]
                qb = kbs[r, wide + n * 128:wide + (n + 1) * 128]
                kk = kb * keep[j]
                held = tile(kb * kk)
                h = dy[j] * tile(qb) + ah
                prior = s_ref[i, j, n]
                hs = h * prior
                hk[j] = hk[j] + h * tile(kb)
                hs2[j] = hs2[j] + hs * held
                kbs[r, n * 128:(n + 1) * 128] = fold(h * rv[j]) - 2.0 * kk * fold(hs * rate[j])
                kbs[r, wide + n * 128:wide + (n + 1) * 128] = fold(dy[j] * later)
                later = prior
                ah = (tile(keep[j]) - rate[j] * held) * h
            h_ref[n] = ah
        dskip = carry
        for j, r in enumerate(at):
            drate = value[j] * hk[j] - hs2[j]
            drrs[r, :] = fold(drate * rate[j] * rate[j]) * (-2.0)
            keep_pair(ws, r, drate * pair(ws, r))
            keep_pair(dvs, r, rate[j] * hk[j] + skip * dy[j])
            dskip = dskip + dy[j] * value[j]
        return dskip

    dskip = lax.fori_loop(0, steps // GROUP, backward, jnp.zeros((8, tiles * 128), f32))

    quarter = count // 4
    packed = jnp.zeros((quarter, 128), f32)
    for b in range(4):
        r = slice(b * quarter, (b + 1) * quarter)
        total = jnp.zeros((quarter, 128), f32)
        for part in range(0, 2 * wide, 512):
            total = total + lax.dot_general(kb_ref[r, part:part + 512].astype(bf16), hot_ref[:, part:part + 512], cols, preferred_element_type=f32)
        drr = jnp.sum(drr_ref[r, :], axis=1, keepdims=True)
        k = kq_ref[r, :]
        low = lax.broadcasted_iota(jnp.int32, (quarter, 128), 1)
        total = jnp.where(low < 2 * states, total, 0.0) + jnp.where(low < states, k * drr, 0.0)
        packed = packed + (pltpu.roll(total, 32 * b, 1) if b else total)

    tail = pl.ds(count, quarter)
    part_ref[tail, :] = jnp.where(first, packed, part_ref[tail, :] + packed)

    def after(i, carry):
        r = pl.ds(pl.multiple_of(i * 128, 128), 128)
        sums = list(carry)
        for n in both:
            low = w_ref[n, r, :].astype(bf16)
            dpre_ref[r, n * 128:(n + 1) * 128] = low
            sums[n] = sums[n] + jnp.sum(low.astype(f32).reshape(16, 8, 128), axis=0)
        ddl = jnp.dot(dpre_ref[r, :], wdt_ref[...], preferred_element_type=f32)
        part_ref[r, :] = jnp.where(first, ddl, part_ref[r, :] + ddl)
        return tuple(sums)

    sums = lax.fori_loop(0, count // 128, after, (blank,) * tiles)

    def by_row(j, carry):
        r = pl.ds(pl.multiple_of(j * length, length), length)
        for n in both:
            value = y_ref[n, pl.ds(j, length, stride=8), :]
            m_ref[r, n * 128:(n + 1) * 128] = value.astype(bf16)
            mt_ref[n * 128:(n + 1) * 128, r] = value.T.astype(bf16)
            dg_ref[r, n * 128:(n + 1) * 128] = dm_ref[n, pl.ds(j, length, stride=8), :].astype(bf16)
        return carry

    lax.fori_loop(0, 8, by_row, 0)
    gwdt_ref[...] = lax.dot_general(dpre_ref[...], dl_ref[...], (((0,), (0,)), ((), ())), preferred_element_type=f32)
    @pl.when(jnp.logical_not(first))
    def _():
        for copy in keeps:
            copy.wait()

    stat_ref[...] = jnp.zeros_like(stat_ref)
    for n in both:
        lanes = slice(n * 128, (n + 1) * 128)
        stat_ref[0:1, lanes] = jnp.sum(seen[n], axis=0, keepdims=True)
        stat_ref[1:2, lanes] = jnp.max(seen[tiles + n], axis=0, keepdims=True)
        stat_ref[5:6, lanes] = jnp.sum(sums[n], axis=0, keepdims=True)
        stat_ref[6:7, lanes] = jnp.sum(tile_of(dskip, n), axis=0, keepdims=True)


def k2(dl, kq, smalls, vecs, masks, live, v, g, ups, wout, states):
    count, rank = dl.shape
    channels, model = wout.shape
    tiles = 2
    width = tiles * 128
    like = jax.ShapeDtypeStruct
    once = pl.Buffered(buffer_count=1)
    whole = lambda a: pl.BlockSpec(a.shape, lambda h: (0,) * a.ndim, pipeline_mode=once)
    deep = pl.BlockSpec((tiles, count, 128), lambda h: (h, 0, 0))
    flat = pl.BlockSpec((count, width), lambda h: (0, h))
    return pl.pallas_call(
        functools.partial(k2_kernel, states),
        grid=(channels // width,),
        out_shape=(
            like((count, channels), bf16),
            like((channels, count), bf16),
            like((count, channels), bf16),
            like((channels, rank), f32),
            like(ups.shape, bf16),
            like(v.shape, f32),
            like((count + count // 4, 128), f32),
            like((8, channels), f32),
        ),
        in_specs=[
            whole(dl), whole(kq),
            pl.BlockSpec((width, 128), lambda h: (h, 2)),
            pl.BlockSpec((8, width), lambda h: (0, h)),
            pl.BlockSpec((1, count, 128), lambda h: (0, 0, 0), pipeline_mode=once),
            pl.BlockSpec((1, count, 128), lambda h: (0, 0, 0), pipeline_mode=once),
            deep, deep, pl.BlockSpec(memory_space=pl.ANY),
            pl.BlockSpec((width, model), lambda h: (h, 0)),
        ],
        out_specs=(flat, pl.BlockSpec((width, count), lambda h: (h, 0)), flat, pl.BlockSpec((width, rank), lambda h: (h, 0)), pl.BlockSpec(memory_space=pltpu.HBM), deep, pl.BlockSpec((count + count // 4, 128), lambda h: (0, 0)), pl.BlockSpec((8, width), lambda h: (0, h))),
        scratch_shapes=[
            pltpu.VMEM((2, 4, count // 8, model), bf16),
            pltpu.SemaphoreType.DMA((8,)),
            pltpu.SemaphoreType.DMA((8,)),
        ] + [pltpu.SemaphoreType.DMA(())] * 4 + [
            pltpu.VMEM((count, width), bf16),
            pltpu.VMEM((count // 8 // GROUP + 1, GROUP, states, 8, width), f32),
            pltpu.VMEM((states, 8, width), f32),
        ] + [pltpu.VMEM((tiles, count, 128), f32)] * 4
        + [pltpu.VMEM((count, 2 * states * 128), f32), pltpu.VMEM((128, 2 * states * 128), bf16), pltpu.VMEM((count, 128), f32)],
        compiler_params=pltpu.CompilerParams(collective_id=2, has_side_effects=True, vmem_limit_bytes=63400000),
    )(dl, kq, smalls, vecs, masks, live, v, g, ups, wout)


class Row:
    def __init__(self, part, sib, recv, sems):
        self.part, self.sib, self.recv = part, sib, recv
        self.ss, self.sr, self.gs, self.lr, self.rr = sems
        d, c, z = place()
        self.c = c
        self.other = (d, flip(c, 1), z)
        self.to_left = (d, c, lax.rem(z + 3, 4))
        self.to_right = (d, c, lax.rem(z + 1, 4))

    def start(self):
        for zp in (3, 0, 2, 1):
            put(self.part.at[flip(self.c, 1), zp], self.sib.at[zp], self.ss.at[zp], self.sr.at[zp], self.other)

    def gather(self):
        for zp in (3, 0, 2, 1):
            landed(self.sib.at[zp], self.sr.at[zp], self.other)
            add_rows(self.sib.at[zp], [self.sib.at[zp], self.part.at[self.c, zp]])

    def release(self):
        for zp in range(4):
            sent(self.part.at[flip(self.c, 1), zp], self.ss.at[zp], self.other)

    def terms(self, zs, zp):
        found = [self.sib.at[zp]]
        if zp >= zs and zs > 0:
            landed(self.recv.at[zp], self.lr.at[zp], self.to_left)
            found.append(self.recv.at[zp])
        if zp <= zs and zs < 3:
            slot = self.recv.at[4 if zp == zs else zp]
            landed(slot, self.rr.at[zp], self.to_right)
            found.append(slot)
        return found

    def join(self, zs, zp):
        found = self.terms(zs, zp)
        if len(found) > 1:
            add_rows(self.sib.at[zp], found)

    def step(self, zs, k):
        for zp in ((3, 2, 1, 0) if zs == 0 else (0, 1, 2, 3)):
            if zp > zs and k == (0 if zs == 0 else 3 - zp + zs):
                self.join(zs, zp)
                put(self.sib.at[zp], self.recv.at[zp], self.gs.at[zp], self.lr.at[zp], self.to_right)
            if zp < zs and k == (0 if zs == 3 else zp + 3 - zs):
                self.join(zs, zp)
                put(self.sib.at[zp], self.recv.at[4 if zp == zs - 1 else zp], self.gs.at[zp], self.rr.at[zp], self.to_left)

    def finish(self, zs):
        add_rows(self.sib.at[zs], self.terms(zs, zs), self.total)

    def close(self, zs):
        for zp in range(4):
            if zp != zs:
                sent(self.sib.at[zp], self.gs.at[zp], self.other)

    def along(self, k, total=None):
        self.total = total
        d, c, z = place()
        for zs in range(4):
            @pl.when(z == zs)
            def _():
                if k < 3:
                    self.step(zs, k)
                else:
                    self.finish(zs)
                    self.close(zs)


def row_scratch(rows, columns):
    return [pltpu.VMEM((4, rows, columns), bf16), pltpu.VMEM((5, rows, columns), bf16)] + [pltpu.SemaphoreType.DMA((4,))] * 5


def add_rows(dst, sources, total=None):
    rows = (total if total is not None else dst).shape[0]
    step = 16

    def body(i, carry):
        r = pl.ds(pl.multiple_of(i * step, step), step)
        value = sources[0][r, :].astype(f32)
        for more in sources[1:]:
            value = value + more[r, :].astype(f32)
        if total is not None:
            total[r, :] = value
        else:
            dst[r, :] = value.astype(dst.dtype)
        return carry

    lax.fori_loop(0, rows // step, body, 0)


class Flat:
    def __init__(self, part, xa, yb, rx, ry, ss, rs):
        self.part, self.xa, self.yb, self.rx, self.ry, self.ss, self.rs = part, xa, yb, rx, ry, ss, rs
        d, c, z = place()
        self.d, self.dx, self.dy, self.dd = d, flip(d, 1), flip(d, 2), flip(flip(d, 1), 2)
        self.xn, self.yn = (self.dx, c, z), (self.dy, c, z)
        half = part.shape[1] // 2
        self.a, self.b = pl.ds(0, half), pl.ds(half, half)
        self.sends = []

    def start_far(self):
        p = self.part
        self.sends.append(put(p.at[self.dd, self.a], self.xa, self.ss.at[0], self.rs.at[0], self.xn))
        self.sends.append(put(p.at[self.dd, self.b], self.yb, self.ss.at[1], self.rs.at[1], self.yn))

    def start_near(self):
        p = self.part
        self.sends.append(put(p.at[self.dx, self.a], self.rx.at[self.a], self.ss.at[2], self.rs.at[2], self.xn))
        self.sends.append(put(p.at[self.dy, self.b], self.ry.at[self.b], self.ss.at[3], self.rs.at[3], self.yn))

    def middle(self):
        p = self.part
        landed(self.xa, self.rs.at[0], self.xn)
        add_rows(self.xa, [self.xa, p.at[self.dy, self.a]])
        self.sends.append(put(self.xa, self.ry.at[self.a], self.ss.at[4], self.rs.at[4], self.yn))
        landed(self.yb, self.rs.at[1], self.yn)
        add_rows(self.yb, [self.yb, p.at[self.dx, self.b]])
        self.sends.append(put(self.yb, self.rx.at[self.b], self.ss.at[5], self.rs.at[5], self.xn))

    def finish(self, out):
        landed(self.rx.at[self.a], self.rs.at[2], self.xn)
        landed(self.ry.at[self.b], self.rs.at[3], self.yn)
        landed(self.ry.at[self.a], self.rs.at[4], self.yn)
        landed(self.rx.at[self.b], self.rs.at[5], self.xn)
        add_rows(out, [self.part.at[self.d], self.rx, self.ry])

    def close(self):
        for copy in self.sends:
            copy.wait_send()


def flat_scratch(rows, columns, dtype):
    half = pltpu.VMEM((rows // 2, columns), dtype)
    full = pltpu.VMEM((rows, columns), dtype)
    return [half, half, full, full, pltpu.SemaphoreType.DMA((6,)), pltpu.SemaphoreType.DMA((6,))]


def k3_kernel(part_ref, stat_ref, smalls_ref, vecs_ref, gains_ref, gwdt_ref, masks_ref, tok_ref, up_ref,
              m_any, mt_any, dg_any, dv_any, slope_any, u_any, vt_any, xnt_any, win_any, wout_any, ups_any,
              block_out, gtok_out, gwin_out, gwout_out, small_out, tiny_out, *scratch):
    scratch = list(scratch)

    def take(n):
        found = scratch[:n]
        del scratch[:n]
        return found

    block_ref, gtok_ref, gwin_ref, gwout_ref, small_ref, tiny_ref, stores = take(7)
    outp, win_ref, up, gp, gwoutp, smallp = take(6)
    m_ref, mt_ref, dz_ref, dc_ref, slope_ref, u_ref, xnt_ref, dp_ref, slots_ref, row_ref = take(10)
    near_ref, pairs_ref, sum_ref, far_ref = take(4)
    loads, as_, ar, ns, nr, fs, fr = take(7)
    totals = take(7)
    total_sems = take(8)
    out_row = Row(outp, *take(2), take(5))
    dxn_row = Row(outp, *take(2), take(5))
    flats = [Flat(up, *take(6)), Flat(gp, *take(6))]
    gwout_flat = Flat(gwoutp, *take(6))
    small_flat = Flat(smallp, *take(6))
    d, c, z = place()
    j = c * 4 + z
    other = flip(c, 1)
    steps = mates()
    planes = [(flip(d, 1), c, z), (flip(d, 2), c, z), (flip(flip(d, 1), 2), c, z)]
    length, model = tok_ref.shape[1:]
    tiles, padded, _ = dc_ref.shape
    count = dz_ref.shape[0]
    width = tiles * 128
    rows_any = [(m_any, m_ref), (wout_any, gwoutp), (mt_any, mt_ref)]
    for at, holder in ((0, gp), (1024, up)):
        for h in range(2):
            for q in range(2):
                rows_any.append((ups_any.at[pl.ds(q * 512, 512), pl.ds(at + h * 512, 512)], holder.at[2 * h + q]))
    rows_any += [(dg_any, dz_ref.at[:, pl.ds(width, width)]), (xnt_any, xnt_ref), (dv_any, dc_ref.at[:, pl.ds(0, count)]),
                 (slope_any, slope_ref), (u_any, u_ref), (win_any, win_ref)]
    copies = [pltpu.make_async_copy(a, b, loads.at[i]) for i, (a, b) in enumerate(rows_any)]
    for copy in copies:
        copy.start()
    greet([mate(s) for s in steps] + planes)
    outs = [(block_ref, block_out), (gtok_ref, gtok_out), (gwin_ref, gwin_out), (gwout_ref, gwout_out), (small_ref, small_out), (tiny_ref, tiny_out)]
    outs = [pltpu.make_async_copy(a, b, stores.at[i]) for i, (a, b) in enumerate(outs)]
    tile = 256
    nn = (((1,), (0,)), ((), ()))
    nt = (((1,), (1,)), ((), ()))

    def rows_product(half, target, left, right, dims, right_rows):
        def body(i, carry):
            if right_rows:
                group = i // (512 // tile)
                value = right[group, pl.ds(pl.multiple_of((i % (512 // tile)) * tile, tile), tile), :]
            else:
                value = jnp.concatenate([right[g, :, pl.ds(pl.multiple_of(i * tile, tile), tile)] for g in range(4)], axis=0)
            product = lax.dot_general(left[pl.ds(pl.multiple_of(half * 512, 512), 512), :], value, dims, preferred_element_type=f32)
            for zp in range(4):
                target[half, zp, :, pl.ds(pl.multiple_of(i * tile, tile), tile)] = product[zp * length:(zp + 1) * length].astype(bf16)
            return carry

        lax.fori_loop(0, model // tile, body, 0)

    def weight_rows(holder, first, group):
        def body(i, carry):
            lanes = pl.ds(pl.multiple_of(i * tile, tile), tile)
            left = xnt_ref[pl.ds(pl.multiple_of(group * 512, 512), 512), :]
            value = dz_ref[:, pl.ds(pl.multiple_of(first + i * tile, tile), tile)]
            holder[group, :, lanes] = jnp.dot(left, value, preferred_element_type=f32).astype(bf16)
            return carry

        lax.fori_loop(0, width // tile, body, 0)

    def weight_part(k):
        flat = flats[k]
        holder, first = (up, 0) if k == 0 else (gp, width)
        weight_rows(holder, first, flat.dd)
        flat.start_far()
        weight_rows(holder, first, flat.dx)
        weight_rows(holder, first, flat.dy)
        flat.start_near()
        weight_rows(holder, first, d)

    def early():
        copies[0].wait()
        copies[1].wait()
        rows_product(other, outp, m_ref, gwoutp, nn, False)
        out_row.start()
        rows_product(c, outp, m_ref, gwoutp, nn, False)

    def between():
        out_row.gather()
        out_row.along(0)
        for copy in copies[2:11]:
            copy.wait()
        for holder, at in ((gp, 0), (up, 1024)):
            def body(i, carry):
                h = i // 2
                off = pl.ds(pl.multiple_of((i % 2) * tile, tile), tile)
                value = jnp.concatenate([holder[2 * h, :, off], holder[2 * h + 1, :, off]], axis=0)
                product = jnp.dot(mt_ref[...], value, preferred_element_type=f32)
                for g in range(4):
                    gwoutp[g, :, pl.ds(pl.multiple_of(at + i * tile, tile), tile)] = product[g * 128:(g + 1) * 128].astype(bf16)
                return carry

            lax.fori_loop(0, 4, body, 0)

    def late():
        for copy in copies[11:13]:
            copy.wait()
        weight_part(1)

    seen = jnp.sum(stat_ref[0:1, :], axis=1, keepdims=True)
    peak = jnp.max(stat_ref[1:2, :], axis=1, keepdims=True)
    row8 = lax.broadcasted_iota(jnp.int32, (8, 128), 0)
    lane8 = lax.broadcasted_iota(jnp.int32, (8, 128), 1)
    pairs_ref[...] = jnp.where(lane8 == 0, seen, jnp.where(lane8 == 1, peak, 0.0))
    for i, s in enumerate(steps):
        put(pairs_ref, near_ref.at[i], ns.at[i], nr.at[i], mate(s))

    def join(a, b):
        return jnp.where(lane8 == 1, jnp.maximum(a, b), a + b)

    total_ref = totals[0]
    line_total(part_ref, *totals, *total_sems, early, between, late)
    vt_copy = pltpu.make_async_copy(vt_any, mt_ref, loads.at[17])
    vt_copy.start()
    out_row.along(1)
    value = pairs_ref[...]
    for i, s in enumerate(steps):
        landed(near_ref.at[i], nr.at[i], mate(s, -1))
        value = join(value, near_ref[i])
    sum_ref[...] = value
    for i, to in enumerate(planes):
        put(sum_ref, far_ref.at[i], fs.at[i], fr.at[i], to)
    quarter = count // 4
    lane = lax.broadcasted_iota(jnp.int32, (quarter, 128), 1)
    dp_ref[:, 0:128] = total_ref[0:count, :].astype(bf16)
    for b in range(4):
        packed = total_ref[count:count + quarter, :]
        packed = pltpu.roll(packed, 128 - 32 * b, 1) if b else packed
        dp_ref[b * quarter:(b + 1) * quarter, 128:256] = jnp.where(lane < 32, packed, 0.0).astype(bf16)
    for copy in copies[13:16]:
        copy.wait()
    dc_ref[:, count:, :] = jnp.zeros((tiles, padded - count, 128), f32)

    def slope_step(i, carry):
        r = pl.ds(pl.multiple_of(i * 256, 256), 256)
        product = lax.dot_general(dp_ref[r, :], smalls_ref[:, 0:256], nt, preferred_element_type=f32)
        for n in range(tiles):
            dc_ref[n, r, :] = (dc_ref[n, r, :] + product[:, n * 128:(n + 1) * 128]) * slope_ref[n, r, :]
        return carry

    lax.fori_loop(0, count // 256, slope_step, 0)
    flats[1].middle()
    taps = [vecs_ref[o:o + 1, :] for o in range(4)]
    lead = u_ref.shape[1] - count

    for n in range(tiles):
        lanes = slice(n * 128, (n + 1) * 128)
        tap = [t[:, lanes] for t in taps]

        def conv_step(i, carry):
            r = pl.ds(pl.multiple_of(i * 32, 32), 32)
            sums = list(carry)
            dc = dc_ref[n, r, :]
            du = tap[3] * dc
            fold8 = lambda x: x[0:8] + x[8:16] + x[16:24] + x[24:32]
            sums[4] = sums[4] + fold8(dc)
            sums[3] = sums[3] + fold8(dc * u_ref[n, pl.ds(pl.multiple_of(lead + i * 32, 8), 32), :])
            for o in range(1, 4):
                sums[3 - o] = sums[3 - o] + fold8(dc * (u_ref[n, pl.ds(pl.multiple_of(lead + i * 32 - 8 * o, 8), 32), :] * masks_ref[o - 1, pl.ds(pl.multiple_of(i * 32, 8), 32), :]))
                du = du + tap[3 - o] * (dc_ref[n, pl.ds(pl.multiple_of(i * 32 + 8 * o, 8), 32), :] * masks_ref[o - 1, pl.ds(pl.multiple_of(i * 32 + 8 * o, 8), 32), :])
            dc_ref[n, r, :] = du
            return tuple(sums)

        sums = lax.fori_loop(0, count // 32, conv_step, (jnp.zeros((8, 128), f32),) * 5)
        smallp[n, 128:160, :] = jnp.zeros((32, 384), f32)
        for k in range(5):
            smallp[n, 128 + k:129 + k, 0:128] = jnp.sum(sums[k], axis=0, keepdims=True)
        smallp[n, 133:134, 0:128] = stat_ref[5:6, lanes]
        smallp[n, 134:135, 0:128] = stat_ref[6:7, lanes]
        smallp[n, 0:128, 256:384] = gwdt_ref[n * 128:(n + 1) * 128, :]

    def by_row(i, carry):
        r = pl.ds(pl.multiple_of(i * length, length), length)
        for n in range(tiles):
            dz_ref[r, n * 128:(n + 1) * 128] = dc_ref[n, pl.ds(i, length, stride=8), :].astype(bf16)
        return carry

    lax.fori_loop(0, 8, by_row, 0)
    copies[16].wait()
    out_row.release()
    rows_product(other, outp, dz_ref, win_ref, nt, True)
    dxn_row.start()
    rows_product(c, outp, dz_ref, win_ref, nt, True)
    out_row.along(2)
    dxn_row.gather()
    dxn_row.along(0)
    weight_part(0)
    block = gwin_ref.shape[0]
    pending = []

    def rows_of(k, rank):
        return flats[k].part.at[d, pl.ds(pl.multiple_of(rank * block, block), block)]

    def give(k):
        flats[k].finish(flats[k].part.at[d])
        for i, s in enumerate(steps):
            to = mate(s)
            pending.append(put(rows_of(k, rank_of(to)), slots_ref.at[k, i], as_.at[7 * k + i], ar.at[7 * k + i], to))

    give(1)
    gwout_flat.start_far()
    gwout_flat.start_near()
    vt_copy.wait()
    for n in range(tiles):
        smallp[n, 0:128, 0:256] = jnp.dot(mt_ref[n * 128:(n + 1) * 128, :], dp_ref[...], preferred_element_type=f32)
    small_flat.start_far()
    small_flat.start_near()
    flats[0].middle()
    out_row.along(3, row_ref)

    def block_step(i, carry):
        r = pl.ds(pl.multiple_of(i * 16, 16), 16)
        block_ref[r, :] = (tok_ref[0, r, :].astype(f32) + row_ref[r, :]).astype(bf16)
        return carry

    lax.fori_loop(0, length // 16, block_step, 0)
    outs[0].start()
    dxn_row.along(1)
    give(0)
    gwout_flat.middle()
    small_flat.middle()
    dxn_row.along(2)
    gwout_flat.finish(gwout_ref)
    outs[3].start()
    dxn_row.along(3, row_ref)
    dxn_row.release()
    def norm_step(i, carry):
        r = pl.ds(pl.multiple_of(i * 16, 16), 16)
        x = tok_ref[0, r, :].astype(f32)
        scale = lax.rsqrt(jnp.sum(x * x, axis=1, keepdims=True) * (1.0 / model) + EPS)
        dxn = row_ref[r, :]
        inner = dxn * gains_ref[...]
        dot = jnp.sum(inner * x, axis=1, keepdims=True) * (1.0 / model)
        dxx = scale * inner - x * (scale * scale * scale * dot)
        gtok_ref[r, :] = (up_ref[0, r, :].astype(f32) + dxx).astype(bf16)
        return carry

    lax.fori_loop(0, length // 16, norm_step, 0)
    outs[1].start()
    small_flat.finish(small_ref)
    outs[4].start()

    def settle(k, rank, source):
        for g in range(4):
            at = k * width * 8 + g * 1024
            gwin_ref[:, pl.ds(pl.multiple_of(at + rank * 128, 128), 128)] = source[:, g * 128:(g + 1) * 128]

    for k in (1, 0):
        settle(k, j, rows_of(k, j))
        for i, s in enumerate(steps):
            src = mate(s, -1)
            landed(slots_ref.at[k, i], ar.at[7 * k + i], src)
            settle(k, rank_of(src), slots_ref.at[k, i])
    outs[2].start()
    value = sum_ref[...]
    for i, to in enumerate(planes):
        landed(far_ref.at[i], fr.at[i], to)
        value = join(value, far_ref[i])
    tiny_ref[...] = value
    outs[5].start()
    for i, to in enumerate(planes):
        sent(sum_ref, fs.at[i], to)
    for i, s in enumerate(steps):
        sent(near_ref.at[i], ns.at[i], mate(s))
    for copy in pending:
        copy.wait_send()
    for flat in (*flats, gwout_flat, small_flat):
        flat.close()
    for copy in outs:
        copy.wait()


def k3(part, stat, smalls, vecs, gains, gwdt, masks, tokens, upstream, m, mt, dg, dv, slope, u, vt, xnt, win, wout, ups):
    like = jax.ShapeDtypeStruct
    length, model = tokens.shape[1:]
    count, channels = m.shape
    tiles = channels // 128
    here = pl.BlockSpec(memory_space=pltpu.VMEM)
    far = pl.BlockSpec(memory_space=pl.ANY)
    dma = lambda n: pltpu.SemaphoreType.DMA((n,))
    own_d = model // 32
    packed = part.shape[0]
    return pl.pallas_call(
        k3_kernel,
        out_shape=(
            like((length, model), bf16),
            like((length, model), bf16),
            like((own_d, 16 * channels), bf16),
            like((128, model), f32),
            like((160, 384), f32),
            like((8, 128), f32),
        ),
        in_specs=[here] * 9 + [far] * 11,
        out_specs=(pl.BlockSpec(memory_space=pltpu.HBM),) * 6,
        scratch_shapes=[
            pltpu.VMEM((length, model), bf16),
            pltpu.VMEM((length, model), bf16),
            pltpu.VMEM((own_d, 16 * channels), bf16),
            pltpu.VMEM((128, model), f32),
            pltpu.VMEM((160, 384), f32),
            pltpu.VMEM((8, 128), f32),
            dma(6),
            pltpu.VMEM((2, 4, length, model), bf16),
            pltpu.VMEM((4, 512, 2 * channels), bf16),
            pltpu.VMEM((4, 512, channels), bf16),
            pltpu.VMEM((4, 512, channels), bf16),
            pltpu.VMEM((4, 128, model), bf16),
            pltpu.VMEM((4, 160, 384), f32),
            pltpu.VMEM((count, channels), bf16),
            pltpu.VMEM((channels, count), bf16),
            pltpu.VMEM((count, 2 * channels), bf16),
            pltpu.VMEM((tiles, count + 32, 128), f32),
            pltpu.VMEM((tiles, count, 128), f32),
            pltpu.VMEM(u.shape, f32),
            pltpu.VMEM((model, count), bf16),
            pltpu.VMEM((count, 256), bf16),
            pltpu.VMEM((2, 7, own_d, channels), bf16),
            pltpu.VMEM((length, model), f32),
            pltpu.VMEM((7, 8, 128), f32),
            pltpu.VMEM((8, 128), f32),
            pltpu.VMEM((8, 128), f32),
            pltpu.VMEM((3, 8, 128), f32),
            dma(18), dma(14), dma(14), dma(7), dma(7), dma(3), dma(3),
            pltpu.VMEM((packed, 128), f32),
        ] + [pltpu.VMEM((packed // 2, 128), f32)] * 6 + [dma(PIECES) for _ in range(8)]
        + row_scratch(length, model) * 2
        + flat_scratch(512, channels, bf16) * 2 + flat_scratch(128, model, bf16) + flat_scratch(160, 384, f32),
        compiler_params=pltpu.CompilerParams(collective_id=1, has_side_effects=True, vmem_limit_bytes=63400000),
    )(part, stat, smalls, vecs, gains, gwdt, masks, tokens, upstream, m, mt, dg, dv, slope, u, vt, xnt, win, wout, ups)


def k4_kernel(slots, block_in, gtok_in, gwin_in, gwout_in, small_in, tiny_in, win_ref, gain_ref,
              block_ref, gtok_ref, gain_out, gwin_ref, convw_ref, convb_ref, gwx_ref, gwdt_ref, dtb_ref, skip_ref, gwout_ref, mean_ref, peak_ref):
    block_ref[0] = block_in[...]
    gtok_ref[0] = gtok_in[...]
    gwout_ref[...] = gwout_in[...]
    depth, total = gwin_in.shape
    dot = jnp.zeros((depth, 128), f32)
    for at in range(0, total, 128):
        value = gwin_in[:, at:at + 128].astype(f32)
        gwin_ref[:, at:at + 128] = value
        dot = dot + value * win_ref[:, at:at + 128].astype(f32)
    column = jnp.broadcast_to(jnp.sum(dot, axis=1, keepdims=True), (depth, 128))
    gain_out[...] = column.T[0:1, :] / gain_ref[...].astype(f32)
    gwx_ref[...] = small_in[0:128, 0:256].T[0:gwx_ref.shape[0], :]
    gwdt_ref[...] = small_in[0:128, 256:384]
    convw_ref[...] = small_in[128:132, 0:128]
    convb_ref[...] = small_in[132:133, 0:128]
    dtb_ref[...] = small_in[133:134, 0:128]
    skip_ref[...] = small_in[134:135, 0:128]
    mean_ref[...] = tiny_in[0:1, 0:1] * (1.0 / slots)
    peak_ref[...] = tiny_in[0:1, 1:2]


def k4(slots, block, gtok, gwin, gwout, small, tiny, w_in, gain, columns):
    like = jax.ShapeDtypeStruct
    here = pl.BlockSpec(memory_space=pltpu.VMEM)
    row = like((1, 128), f32)
    return pl.pallas_call(
        functools.partial(k4_kernel, slots),
        out_shape=(
            like((1,) + block.shape, bf16), like((1,) + gtok.shape, bf16), like(gain.shape, f32), like(gwin.shape, f32),
            like((4, 128), f32), row, like((columns, 128), f32), like((128, 128), f32), row, row, like(gwout.shape, f32),
            like((1, 1), f32), like((1, 1), f32),
        ),
        in_specs=[here] * 8,
        out_specs=(here,) * 13,
        compiler_params=pltpu.CompilerParams(vmem_limit_bytes=63400000),
    )(block, gtok, gwin, gwout, small, tiny, w_in, gain)

def masks(lengths, count):
    ends = jnp.cumsum(lengths, axis=1)
    places = jnp.arange(count, dtype=jnp.int32)
    segment = jnp.sum((places[:, None, None] >= ends[None, :, :]).astype(jnp.int32), axis=2)
    same = []
    for offset in range(1, 4):
        before = jnp.pad(segment, ((offset, 0), (0, 0)), constant_values=-1)[:count]
        same.append((before == segment).astype(f32))
    return same, (segment < DOCS).astype(f32)


def columns(weights, ways):
    rows, total = weights.shape
    return weights.reshape(rows, 2, total // (2 * ways * 128), ways, 128)


def on_device(tokens, lengths, gain, w_in, conv_w, conv_b, w_x, w_dt, dt_bias, skip, w_out, grad_out):
    ways = lax.axis_size("core") * lax.axis_size("z")
    groups = lax.axis_size("dp")
    length, model = tokens.shape[1:]
    own_d = w_in.shape[0]
    own_e = conv_w.shape[0]
    inner = w_in.shape[1] // 2
    channels = inner // ways
    rank = w_dt.shape[1]
    states = (w_x.shape[1] - rank) // 2
    cols = w_in.reshape(own_d, 2, groups, ways, own_e).transpose(3, 0, 1, 2, 4).reshape(ways, own_d, 2 * channels)
    cols = lax.all_to_all(cols, TP, split_axis=0, concat_axis=0, tiled=True)
    win = lax.all_gather(cols, "dp", axis=0, tiled=True).reshape(model, 2 * channels)
    small = jnp.concatenate([w_x, w_dt, conv_w, conv_b[:, None], dt_bias[:, None], skip[:, None]], axis=1)
    small_width = small.shape[1]
    small = lax.all_gather(small, "dp", axis=0, tiled=True)
    wx = small[:, :rank + 2 * states]
    wdt = small[:, rank + 2 * states:2 * rank + 2 * states]
    rest = small[:, 2 * rank + 2 * states:].astype(f32)
    taps, bias, dtb, skips = rest[:, :4], rest[:, 4], rest[:, 5], rest[:, 6]
    wout = lax.all_gather(w_out, "dp", axis=0, tiled=True)
    gains = lax.all_gather(gain, ALL, axis=0, tiled=True).astype(f32)
    x = tokens[0].astype(f32)
    scale = lax.rsqrt(jnp.mean(x * x, axis=1, keepdims=True) + EPS)
    xn = (x * scale * gains).astype(bf16)
    xns = lax.all_gather(xn, TP, axis=0, tiled=True)
    ups = lax.all_gather(grad_out[0], TP, axis=0, tiled=True)
    lens = lax.all_gather(lengths, TP, axis=0, tiled=True)
    rows = lens.shape[0]
    tall = rows * length

    def time_major(a):
        return a.reshape(rows, length, -1).transpose(1, 0, 2).reshape(tall, -1)

    def row_major(a):
        return a.reshape(length, rows, -1).transpose(1, 0, 2).reshape(tall, -1)

    same, live = masks(lens, length)
    zz = time_major(jnp.dot(xns, win, preferred_element_type=f32))
    u = zz[:, :channels].reshape(length, rows, channels)
    g = zz[:, channels:]
    c = bias + taps[:, 3] * u
    shifted = []
    for offset in range(1, 4):
        earlier = jnp.pad(u, ((offset, 0), (0, 0), (0, 0)))[:length] * same[offset - 1][:, :, None]
        shifted.append(earlier)
        c = c + taps[:, 3 - offset] * earlier
    sig = jax.nn.sigmoid(c)
    v16 = (c * sig).astype(bf16).reshape(tall, channels)
    v = v16.astype(f32)
    p = lax.psum(jnp.dot(v16, wx, preferred_element_type=f32), TP)
    dl = p[:, :rank].astype(bf16)
    kq = p[:, rank:]
    dims_cols = (((1,), (1,)), ((), ()))
    dims_rows = (((0,), (0,)), ((), ()))
    pre = lax.dot_general(dl, wdt, dims_cols, preferred_element_type=f32) + dtb
    dm = time_major(lax.dot_general(ups, wout, dims_cols, preferred_element_type=f32))
    flags = jnp.pad(jnp.stack([same[0].reshape(tall), live.reshape(tall)], axis=1), ((0, 0), (0, 126)))
    hi = kq.astype(bf16)
    mid = (kq - hi.astype(f32)).astype(bf16)
    low = (kq - hi.astype(f32) - mid.astype(f32)).astype(bf16)
    kq3 = jnp.concatenate([hi, mid, low], axis=1)
    keys = kq[:, :states]
    sk = jnp.broadcast_to(jnp.sum(keys * keys, axis=1, keepdims=True), (tall, 8))
    m, dg, dpre, dv, dkq, stats = mixer(flags, kq3, sk, pre, v, g, dm, skips[None], states=states, width=256, unroll=4)
    stats = stats.transpose(1, 2, 0, 3).reshape(3, 8, channels)
    dskip = jnp.sum(stats[0], axis=0)
    total = lax.psum(jnp.sum(stats[1]), ALL)
    peak = lax.pmax(jnp.max(stats[2]), ALL)
    beta_mean = total / float(groups * ways * length * inner)
    m16 = row_major(m).astype(bf16)
    out = jnp.dot(m16, wout, preferred_element_type=f32).astype(bf16)
    out = lax.psum_scatter(out, TP, scatter_dimension=0, tiled=True)
    block_out = (x + out.astype(f32)).astype(bf16)
    grad_wout = lax.dot_general(m16, ups, dims_rows, preferred_element_type=f32).astype(bf16)
    grad_wout = lax.psum_scatter(grad_wout, "dp", scatter_dimension=0, tiled=True)
    dpre16 = dpre.astype(bf16)
    grad_dtb = jnp.sum(dpre16.astype(f32), axis=0)
    grad_wdt = lax.dot_general(dpre16, dl, dims_rows, preferred_element_type=f32)
    ddl = jnp.dot(dpre16, wdt, preferred_element_type=f32)
    dkq = dkq[:, :2 * states] + dkq[:, 2 * states:2 * states + 1] * jnp.pad(keys, ((0, 0), (0, states)))
    dp16 = lax.psum(jnp.concatenate([ddl, dkq], axis=1), TP).astype(bf16)
    grad_wx = lax.dot_general(v16, dp16, dims_rows, preferred_element_type=f32)
    dvt = dv + lax.dot_general(dp16, wx, dims_cols, preferred_element_type=f32)
    dc = (dvt * (sig.reshape(tall, channels) * (1.0 + c.reshape(tall, channels) * (1.0 - sig.reshape(tall, channels))))).reshape(length, rows, channels)
    du = taps[:, 3] * dc
    grad_taps = [jnp.sum(dc * u, axis=(0, 1))]
    for offset in range(1, 4):
        grad_taps.append(jnp.sum(dc * shifted[offset - 1], axis=(0, 1)))
        du = du + taps[:, 3 - offset] * jnp.pad((dc * same[offset - 1][:, :, None])[offset:], ((0, offset), (0, 0), (0, 0)))
    grad_conv = jnp.stack(grad_taps[::-1] + [jnp.sum(dc, axis=(0, 1)), grad_dtb, dskip], axis=1)
    dz = row_major(jnp.concatenate([du.reshape(tall, channels), dg], axis=1)).astype(bf16)
    gwin = lax.dot_general(xns, dz, dims_rows, preferred_element_type=f32).astype(bf16)
    gwin = lax.psum_scatter(gwin, "dp", scatter_dimension=0, tiled=True)
    gwin = lax.all_to_all(gwin.reshape(ways, own_d, 2 * channels), TP, split_axis=0, concat_axis=0, tiled=True)
    grad_win = gwin.reshape(ways, own_d, 2, groups, own_e).transpose(1, 2, 3, 0, 4).reshape(own_d, 2 * inner).astype(f32)
    dxn = lax.dot_general(dz, win, dims_cols, preferred_element_type=f32).astype(bf16)
    dxn = lax.psum_scatter(dxn, TP, scatter_dimension=0, tiled=True).astype(f32)
    small_grad = lax.psum_scatter(jnp.concatenate([grad_wx, grad_wdt, grad_conv], axis=1), "dp", scatter_dimension=0, tiled=True)
    inner_grad = dxn * gains
    dxx = scale * inner_grad - x * (scale * scale * scale) * (jnp.sum(inner_grad * x, axis=1, keepdims=True) / model)
    grad_tokens = (grad_out[0].astype(f32) + dxx).astype(bf16)
    grad_gain = lax.psum_scatter(jnp.sum(dxn * x * scale, axis=0), ALL, scatter_dimension=0, tiled=True)
    at = rank + 2 * states
    return (
        block_out[None],
        grad_tokens[None],
        grad_gain,
        grad_win,
        small_grad[:, at + rank:at + rank + 4],
        small_grad[:, at + rank + 4],
        small_grad[:, :at],
        small_grad[:, at:at + rank],
        small_grad[:, at + rank + 5],
        small_grad[:, at + rank + 6],
        grad_wout.astype(f32),
        beta_mean,
        peak,
    )


def on_device_direct(tokens, lengths, gain, w_in, conv_w, conv_b, w_x, w_dt, dt_bias, skip, w_out, grad_out):
    groups, ways = 4, 8
    length, model = tokens.shape[1:]
    own_d = w_in.shape[0]
    own_e = conv_w.shape[0]
    inner = w_in.shape[1] // 2
    channels = inner // ways
    rank = w_dt.shape[1]
    states = (w_x.shape[1] - rank) // 2
    gain = gain[None]
    xnt, ups, win, wout, smalls, vecs, gains, masks, live, u, g, v, vt, slope, dl, kq = k1(
        tokens, grad_out, w_in, w_out, w_x.T, w_dt, gain, lengths, conv_w.T, conv_b[None], dt_bias[None], skip[None])
    m, mt, dg, gwdt, ups, dv, part, stat = k2(dl, kq, smalls, vecs, masks, live, v, g, ups, wout, states)
    sums = k3(
        part, stat, smalls, vecs, gains, gwdt, masks, tokens, grad_out, m, mt, dg, dv, slope, u, vt, xnt,
        win.reshape(groups, ways * own_d, 2 * channels), wout.reshape(groups, own_e, model), ups)
    block_out, grad_tokens, grad_gain, grad_win, convw, convb, gwx, gwdt, dtb, dskip, grad_wout, mean, peak = k4(
        float(groups * ways * length * inner), *sums, w_in, gain, rank + 2 * states)
    return (
        block_out, grad_tokens, grad_gain[0], grad_win, convw.T, convb[0], gwx.T, gwdt, dtb[0], dskip[0], grad_wout, mean[0, 0], peak[0, 0],
    )


def on_device_any(*args):
    if lax.axis_size("dp") == 4 and lax.axis_size("z") == 4:
        return on_device_direct(*args)
    return on_device(*args)


def solution(mesh):
    wide, narrow = mesh.devices.shape
    fine = Mesh(mesh.devices.reshape(wide // 2, 2, narrow), ALL)
    cut = (P(ALL, None), P(ALL))
    in_specs = (P(ALL, None, None), cut[0], cut[1], cut[0], cut[0], cut[1], cut[0], cut[0], cut[1], cut[1], cut[0], P(ALL, None, None))
    out_specs = (P(ALL, None, None), P(ALL, None, None), cut[1], cut[0], cut[0], cut[1], cut[0], cut[0], cut[1], cut[1], cut[0], P(), P())
    return jax.shard_map(on_device_any, mesh=fine, in_specs=in_specs, out_specs=out_specs, check_vma=False)
```

```python
import functools
import jax, jax.numpy as jnp
from jax import lax
from jax.experimental import pallas as pl
from jax.experimental.pallas import tpu as pltpu
from jax.sharding import Mesh, PartitionSpec as P

DOCS = 4
EPS = 1e-05
ALL = ("dp", "core", "z")
TP = ("core", "z")

f32 = jnp.float32
bf16 = jnp.bfloat16

def fold(x):
    total = x[:, :128]
    for at in range(128, x.shape[1], 128):
        total = total + x[:, at:at+128]
    return total

def mixer_kernel(states, unroll, chunk, flags_ref, kq3_ref, sk_ref, pre_ref, v_ref, g_ref, dm_ref, skip_ref,
                 m_ref, dg_ref, dpre_ref, dv_ref, dkq_ref, stat_ref, s_ref, h_ref, rate_ref, rv_ref, kb_ref, drr_ref):
    rows = pre_ref.shape[0]
    width = pre_ref.shape[1]
    steps = rows // 8
    wide = states * 128
    spread_rows = kq3_ref.shape[1]
    def spread(i, c):
        r = pl.ds(pl.multiple_of(i * chunk, chunk), chunk)
        left = kq3_ref[r, :]
        for part in range(0, 2 * wide, 512):
            ids = lax.broadcasted_iota(jnp.int32, (spread_rows, 512), 0) % (2 * states)
            col = lax.broadcasted_iota(jnp.int32, (spread_rows, 512), 1) // 128 + part // 128
            hot = jnp.where(ids == col, 1.0, 0.0).astype(bf16)
            kb_ref[r, part:part+512] = jnp.dot(left, hot, preferred_element_type=f32)
        return c
    lax.fori_loop(0, rows // chunk, spread, 0)

    def before(i, c):
        r = pl.ds(pl.multiple_of(i * 64, 64), 64)
        live = flags_ref[r, 1:2]
        beta = jax.nn.sigmoid(pre_ref[r, :])
        part = 1.0 / (1.0 + beta * sk_ref[r, 0:1])
        rate = beta * part
        rate_ref[r, :] = rate
        v = v_ref[r, :]
        rv_ref[r, :] = rate * v
        dpre_ref[r, :] = part * part * beta * (1.0 - beta)
        g = g_ref[r, :]
        sg = jax.nn.sigmoid(g)
        dm = dm_ref[r, :] * live
        dv_ref[r, :] = dm * (g * sg)
        dg_ref[r, :] = dm * (sg * (1.0 + g * (1.0 - sg)))
        return c
    lax.fori_loop(0, rows // 64, before, 0)

    s_ref[0, 0] = jnp.zeros(s_ref.shape[2:], f32)

    group = unroll
    tile = lambda x: jnp.concatenate([x] * (width // 128), axis=1)
    span = group * 8
    at = [slice(j * 8, j * 8 + 8) for j in range(group)]
    def view(ref, i):
        return ref.at[pl.ds(pl.multiple_of(i * span, span), span)]

    def forward(i, carry):
        flags, rates, rvs, vs, kbs, ms = [view(x, i) for x in (flags_ref, rate_ref, rv_ref, v_ref, kb_ref, m_ref)]
        keep = [jnp.broadcast_to(flags[r, 0:1], (8, 128)) for r in at]
        rate = [rates[r, :] for r in at]
        rv = [rvs[r, :] for r in at]
        y = [skip_ref[...] * vs[r, :] for r in at]
        for n in range(states):
            state = s_ref[i, 0, n]
            for j, r in enumerate(at):
                kb = kbs[r, n*128:(n+1)*128]
                qb = kbs[r, wide+n*128:wide+(n+1)*128]
                state = (tile(keep[j]) - rate[j] * tile(kb * kb * keep[j])) * state + rv[j] * tile(kb)
                if j < group - 1:
                    s_ref[i, j + 1, n] = state
                else:
                    s_ref[i + 1, 0, n] = state
                y[j] = y[j] + state * tile(qb)
        for j, r in enumerate(at):
            ms[r, :] = y[j]
        return carry

    lax.fori_loop(0, steps // group, forward, 0)
    h_ref[...] = jnp.zeros_like(h_ref)

    def backward(step, carry):
        i = steps // group - 1 - step
        flags, rates, rvs, vs, kbs, dvs, dpres, drrs = [view(x, i) for x in (flags_ref, rate_ref, rv_ref, v_ref, kb_ref, dv_ref, dpre_ref, drr_ref)]
        keep = [jnp.broadcast_to(flags[r, 0:1], (8, 128)) for r in at]
        rate = [rates[r, :] for r in at]
        rv = [rvs[r, :] for r in at]
        dy = [dvs[r, :] for r in at]
        hk = [jnp.zeros((8, width), f32) for r in at]
        hs2 = [jnp.zeros((8, width), f32) for r in at]
        for n in range(states):
            ah = h_ref[n]
            after_ = s_ref[i + 1, 0, n]
            for j in range(group - 1, -1, -1):
                r = at[j]
                kb = kbs[r, n*128:(n+1)*128]
                qb = kbs[r, wide+n*128:wide+(n+1)*128]
                kk = kb * keep[j]
                held = tile(kb * kk)
                h = dy[j] * tile(qb) + ah
                prior = s_ref[i, j, n]
                hs = h * prior
                hk[j] = hk[j] + h * tile(kb)
                hs2[j] = hs2[j] + hs * held
                kbs[r, n*128:(n+1)*128] = fold(h * rv[j]) - 2.0 * kk * fold(hs * rate[j])
                kbs[r, wide+n*128:wide+(n+1)*128] = fold(dy[j] * after_)
                after_ = prior
                ah = (tile(keep[j]) - rate[j] * held) * h
            h_ref[n] = ah
        for j, r in enumerate(at):
            v = vs[r, :]
            drate = v * hk[j] - hs2[j]
            drrs[r, :] = fold(drate * rate[j] * rate[j]) * (-2.0)
            dpres[r, :] = drate * dpres[r, :]
            dvs[r, :] = rate[j] * hk[j] + skip_ref[...] * dy[j]
            stat_ref[0, 0] += dy[j] * v
        return carry

    stat_ref[...] = jnp.zeros_like(stat_ref)
    lax.fori_loop(0, steps // group, backward, 0)

    first = pl.program_id(0) == 0
    def gather(i, c):
        r = pl.ds(pl.multiple_of(i * chunk, chunk), chunk)
        total = jnp.zeros((chunk, 128), f32)
        for part in range(0, 2 * wide, 512):
            row = lax.broadcasted_iota(jnp.int32, (512, 128), 0) // 128 + part // 128
            col = lax.broadcasted_iota(jnp.int32, (512, 128), 1)
            hot = jnp.where(row == col, 1.0, 0.0).astype(bf16)
            total += jnp.dot(kb_ref[r, part:part+512].astype(bf16), hot, preferred_element_type=f32)
        col = lax.broadcasted_iota(jnp.int32, (128, 128), 1)
        hot = jnp.where(col == 2 * states, 1.0, 0.0).astype(bf16)
        total += jnp.dot(drr_ref[r, :].astype(bf16), hot, preferred_element_type=f32)
        dkq_ref[r, :] = jnp.where(first, total, dkq_ref[r, :] + total)
        return c
    lax.fori_loop(0, rows // chunk, gather, 0)

    def after(i, c):
        r = pl.ds(pl.multiple_of(i * 64, 64), 64)
        live = flags_ref[r, 1:2]
        y = m_ref[r, :]
        g = g_ref[r, :]
        m_ref[r, :] = y * (g * jax.nn.sigmoid(g)) * live
        dg_ref[r, :] = y * dg_ref[r, :]
        shown = (jax.nn.sigmoid(pre_ref[r, :]) * live).reshape(8, 8, width)
        stat_ref[0, 1] += jnp.sum(shown, axis=0)
        stat_ref[0, 2] = jnp.maximum(stat_ref[0, 2], jnp.max(shown, axis=0))
        return c
    lax.fori_loop(0, rows // 64, after, 0)

def mixer(flags, kq3, sk, pre, v, g, dm, skip, states=16, width=256, unroll=1):
    rows, total = pre.shape
    steps = rows // 8
    tiles = total // width
    big = jax.ShapeDtypeStruct((rows, total), f32)
    cut = pl.BlockSpec((rows, width), lambda h: (0, h))
    whole = lambda a: pl.BlockSpec(a.shape, lambda h: (0,) * a.ndim)
    return pl.pallas_call(
        functools.partial(mixer_kernel, states, unroll, min(256, rows)),
        grid=(tiles,),
        out_shape=(big, big, big, big, jax.ShapeDtypeStruct((rows, 128), f32), jax.ShapeDtypeStruct((tiles, 3, 8, width), f32)),
        in_specs=[whole(flags), whole(kq3), whole(sk), cut, cut, cut, cut, pl.BlockSpec((1, width), lambda h: (0, h))],
        out_specs=(cut, cut, cut, cut, pl.BlockSpec((rows, 128), lambda h: (0, 0)), pl.BlockSpec((1, 3, 8, width), lambda h: (h, 0, 0, 0))),
        scratch_shapes=[pltpu.VMEM((steps//unroll+1, unroll, states, 8, width), f32), pltpu.VMEM((states, 8, width), f32)] + [pltpu.VMEM((rows, width), f32)]*2
          + [pltpu.VMEM((rows, 2*states*128), f32), pltpu.VMEM((rows, 128), f32)],
        compiler_params=pltpu.CompilerParams(vmem_limit_bytes=60*1024*1024),
    )(flags, kq3, sk, pre, v, g, dm, skip)


MESH = pl.DeviceIdType.MESH


def flip(value, bit):
    return value + bit * (1 - 2 * ((value // bit) % 2))


def place():
    d, c, z = lax.axis_index("dp"), lax.axis_index("core"), lax.axis_index("z")
    return d, c, z


def put(src, dst, send, recv, device):
    copy = pltpu.make_async_remote_copy(src_ref=src, dst_ref=dst, send_sem=send, recv_sem=recv, device_id=device, device_id_type=MESH)
    copy.start()
    return copy


def landed(slot, sem, device):
    pltpu.make_async_remote_copy(src_ref=slot, dst_ref=slot, send_sem=sem, recv_sem=sem, device_id=device, device_id_type=MESH).wait_recv()


def sent(slot, sem, device):
    pltpu.make_async_remote_copy(src_ref=slot, dst_ref=slot, send_sem=sem, recv_sem=sem, device_id=device, device_id_type=MESH).wait_send()


def greet(devices):
    barrier = pltpu.get_barrier_semaphore()
    for device in devices:
        pl.semaphore_signal(barrier, inc=1, device_id=device, device_id_type=MESH)
    pl.semaphore_wait(barrier, len(devices))


def mates():
    return [(a, k) for k in (0, 1, 3, 2) for a in (1, 0) if (a, k) != (0, 0)]


def mate(step, sign=1):
    d, c, z = place()
    a, k = step
    return d, (flip(c, 1) if a else c), lax.rem(z + sign * k + 4, 4)


def rank_of(device):
    return device[1] * 4 + device[2]


PIECES = 4


UP_HOPS = 2


def k1_kernel(tok_ref, up_ref, w_ref, wout_ref, wx_ref, wdt_ref, gain_ref, lens_ref, convw_ref, convb_ref, dtb_ref, skip_ref,
              xnt_out, ups_ref, win_out, wouts_ref, smalls_ref, vecs_ref, gains_ref, masks_out, live_out,
              u_out, g_out, v_out, vt_out, slope_out, dl_ref, kq_ref,
              masks_ref, live_ref, u_ref, g_ref, v_ref, vt_ref, slope_ref, save_sem, cols_ref, meta_ref, small_ref,
              xs_ref, xn_ref, xnt_ref, win_ref, metas_ref, part_ref, out_ref, sib_ref, base_ref, left_ref, right_ref, tor_ref, tol_ref,
              own_sem, ms, mr, qs, qr, xls, xlr, xrs, xrr, xcs, xcr, as_, ar, ps, pr, rs, rr, ws, wr, ts, tr, tls, tlr, trs, trr, tos, tor):
    d, c, z = place()
    j = c * 4 + z
    dx, dy, dd = flip(d, 1), flip(d, 2), flip(flip(d, 1), 2)
    xn, yn, dn = (dx, c, z), (dy, c, z), (dd, c, z)
    sib = (d, flip(c, 1), z)
    left = (d, c, lax.rem(z + 3, 4))
    right = (d, c, lax.rem(z + 1, 4))
    steps = mates()
    length = tok_ref.shape[1]
    model = tok_ref.shape[2]
    depth = cols_ref.shape[1]
    for rank in range(8):
        for n in range(8):
            cols_ref[rank, :, n * 128:(n + 1) * 128] = w_ref[:, (n * 8 + rank) * 128:(n * 8 + rank + 1) * 128]
    meta_ref[...] = jnp.zeros_like(meta_ref)
    meta_ref[0:1, 0:depth] = gain_ref[...].astype(f32)
    meta_ref[0:1, depth:2 * depth] = gain_ref[...].astype(f32)
    meta_ref[1:2, 0:5] = lens_ref[...].astype(f32)
    meta_ref[8:12, :] = convw_ref[...].astype(f32)
    meta_ref[12:13, :] = convb_ref[...].astype(f32)
    meta_ref[13:14, :] = dtb_ref[...].astype(f32)
    meta_ref[14:15, :] = skip_ref[...].astype(f32)
    narrow_rows = wx_ref.shape[0]
    small_ref[:, 0:128] = wx_ref[0:128, :].astype(f32).T.astype(bf16)
    tail = jnp.concatenate([wx_ref[128:narrow_rows, :].astype(f32), jnp.zeros((256 - narrow_rows, 128), f32)], axis=0)
    small_ref[:, 128:256] = tail.T.astype(bf16)
    small_ref[:, 256:384] = wdt_ref[...]
    greet([mate(s) for s in steps] + [xn, yn, dn])
    tiles = u_ref.shape[0]
    width = tiles * 128
    count = g_ref.shape[1]

    def rows(rank):
        return pl.ds(pl.multiple_of(rank * length, length), length)

    def block(group, rank):
        return pl.ds(pl.multiple_of((group * 8 + rank) * depth, depth), depth)

    own_e = wout_ref.shape[0]

    def part_e(group, start=0, size=own_e):
        return pl.ds(pl.multiple_of(group * own_e + start, 16), size)

    own = [
        pltpu.make_async_copy(tok_ref.at[0], xs_ref.at[rows(j)], own_sem.at[0]),
        pltpu.make_async_copy(up_ref.at[0], ups_ref.at[rows(j)], own_sem.at[1]),
        pltpu.make_async_copy(cols_ref.at[j], win_ref.at[block(d, j)], own_sem.at[2]),
        pltpu.make_async_copy(wout_ref, wouts_ref.at[part_e(d)], own_sem.at[3]),
        pltpu.make_async_copy(small_ref, smalls_ref.at[part_e(d)], own_sem.at[4]),
        pltpu.make_async_copy(meta_ref, metas_ref.at[d, j], own_sem.at[5]),
    ]
    for copy in own:
        copy.start()
    pending = []
    for i, s in enumerate(steps):
        to = mate(s)
        pending.append(put(meta_ref, metas_ref.at[d, j], ms.at[i], mr.at[i], to))
    for i, s in enumerate(steps):
        to = mate(s)
        pending.append(put(cols_ref.at[rank_of(to)], win_ref.at[block(d, j)], as_.at[i], ar.at[i], to))
    for i, to in enumerate((xn, yn, dn)):
        pending.append(put(small_ref, smalls_ref.at[part_e(d)], ps.at[16 + i], pr.at[16 + i], to))
    halves = own_e // 2
    pending.append(put(wout_ref, wouts_ref.at[part_e(d)], ws.at[0], wr.at[0], xn))
    pending.append(put(wout_ref, wouts_ref.at[part_e(d)], ws.at[1], wr.at[1], yn))
    own[2].wait()
    slot = win_ref.at[block(d, j)]
    pending.append(put(slot, slot, ps.at[7], pr.at[7], xn))
    pending.append(put(slot, slot, ps.at[15], pr.at[15], yn))

    def row_start(ref, out, base):
        pending.append(put(ref.at[0], out.at[rows(j)], xcs.at[base + z], xcr.at[base + z], sib))

        @pl.when(z < 3)
        def _():
            put(ref.at[0], out.at[rows(j)], xls.at[base], xlr.at[base], right)

        @pl.when(z > 0)
        def _():
            put(ref.at[0], out.at[rows(j)], xrs.at[base], xrr.at[base], left)

    def row_hop(out, base, i, then=None, hops=3):
        if i >= hops:
            return

        @pl.when(z > i)
        def _():
            at = z - 1 - i
            slot = out.at[rows(c * 4 + at)]
            landed(slot, xlr.at[base + i], left)
            if i < hops - 1:
                @pl.when(z < 3)
                def _():
                    put(slot, slot, xls.at[base + i + 1], xlr.at[base + i + 1], right)
            put(slot, slot, xcs.at[base + at], xcr.at[base + at], sib)
            if then is not None:
                then(c * 4 + at)

        @pl.when(z < 3 - i)
        def _():
            at = z + 1 + i
            slot = out.at[rows(c * 4 + at)]
            landed(slot, xrr.at[base + i], right)
            if i < hops - 1:
                @pl.when(z > 0)
                def _():
                    put(slot, slot, xrs.at[base + i + 1], xrr.at[base + i + 1], left)
            put(slot, slot, xcs.at[base + at], xcr.at[base + at], sib)
            if then is not None:
                then(c * 4 + at)

    def row_end(out, base, hops=3):
        for i in range(hops):
            @pl.when((z < 3) & (z >= i))
            def _():
                sent(out.at[rows(j)], xls.at[base + i], right)

            @pl.when((z > 0) & (z <= 3 - i))
            def _():
                sent(out.at[rows(j)], xrs.at[base + i], left)
        for at in range(4):
            @pl.when((z != at) & (z <= at + hops) & (at <= z + hops))
            def _():
                sent(out.at[rows(j)], xcs.at[base + at], sib)

    own[5].wait()
    for i, s in enumerate(steps):
        landed(metas_ref.at[d, rank_of(mate(s, -1))], mr.at[i], xn)
    for i, to in enumerate((xn, yn, dn)):
        pending.append(put(metas_ref.at[d], metas_ref.at[d], qs.at[i], qr.at[i], to))
    slots = {7: j}
    for i, s in enumerate(steps):
        slots[i] = rank_of(mate(s, -1))
    order = [7] + list(range(7))

    def pass_on(i):
        src = mate(steps[i], -1)
        slot = win_ref.at[block(d, slots[i])]
        landed(slot, ar.at[i], src)
        pending.append(put(slot, slot, ps.at[i], pr.at[i], xn))
        pending.append(put(slot, slot, ps.at[8 + i], pr.at[8 + i], yn))

    def relay(k):
        i = order[k]
        slot = win_ref.at[block(dx, slots[i])]
        landed(slot, pr.at[i], xn)
        if k % 2 == 0:
            pending.append(put(slot, slot, rs.at[k // 2], rr.at[k // 2], yn))
        slot = win_ref.at[block(dy, slots[i])]
        landed(slot, pr.at[8 + i], yn)
        if k % 2 == 1:
            pending.append(put(slot, slot, rs.at[4 + k // 2], rr.at[4 + k // 2], xn))

    pass_on(0)
    for i, (to, at) in enumerate(((xn, dx), (yn, dy), (dn, dd))):
        landed(metas_ref.at[at], qr.at[i], to)
    lens = jnp.concatenate([metas_ref[d, r, 1:2, :] for r in range(8)], axis=0)
    ends = []
    last = jnp.zeros((8, 1), f32)
    for i in range(5):
        last = last + lens[:, i:i + 1]
        ends.append(jnp.broadcast_to(last, (8, 128)))

    def mask_step(t, carry):
        here = t.astype(f32)

        def segment(at):
            total = jnp.zeros((8, 128), f32)
            for end in ends:
                total = total + jnp.where(end <= at, 1.0, 0.0)
            return total

        now = segment(here)
        r = pl.ds(pl.multiple_of(t * 8, 8), 8)
        for o in range(1, 4):
            same = jnp.where(segment(here - o) == now, 1.0, 0.0)
            masks_ref[o - 1, r, :] = jnp.where(here >= o, same, 0.0)
        live_ref[0, r, :] = jnp.where(now < DOCS, 1.0, 0.0)
        return carry

    lax.fori_loop(0, length, mask_step, 0)
    masks_ref[:, count:, :] = jnp.zeros((3, masks_ref.shape[1] - count, 128), f32)
    lane = lax.broadcasted_iota(jnp.int32, (1, 128), 1)
    for group in range(4):
        for pair in range(4):
            at = group * 512 + pair * 128
            gains_ref[:, at:at + 128] = jnp.where(lane < depth, metas_ref[group, 2 * pair, 0:1, :], metas_ref[group, 2 * pair + 1, 0:1, :])
        vecs_ref[:, group * own_e:(group + 1) * own_e] = metas_ref[group, j, 8:16, :]

    def normalize(rank):
        def body(i, carry):
            r = pl.ds(pl.multiple_of(rank * length + i * 16, 16), 16)
            x = xs_ref[r, :].astype(f32)
            scale = lax.rsqrt(jnp.sum(x * x, axis=1, keepdims=True) * (1.0 / model) + EPS)
            xn_ref[r, :] = (x * scale * gains_ref[...]).astype(bf16)
            return carry

        lax.fori_loop(0, length // 16, body, 0, unroll=4)

    for i in range(1, 4):
        pass_on(i)
    slot = wouts_ref.at[part_e(dx)]
    landed(slot, wr.at[0], xn)
    slot = wouts_ref.at[part_e(dx, 0, halves)]
    pending.append(put(slot, slot, ws.at[2], wr.at[2], yn))
    slot = wouts_ref.at[part_e(dy)]
    landed(slot, wr.at[1], yn)
    slot = wouts_ref.at[part_e(dy, halves, halves)]
    pending.append(put(slot, slot, ws.at[3], wr.at[3], xn))

    row_start(tok_ref, xs_ref, 0)
    for i in range(4, 7):
        pass_on(i)
    own[0].wait()
    normalize(j)
    row_hop(xs_ref, 0, 0, normalize)
    for k in range(4):
        relay(k)
    row_hop(xs_ref, 0, 1, normalize)
    for k in range(4, 8):
        relay(k)
    row_hop(xs_ref, 0, 2, normalize)
    row_start(up_ref, ups_ref, 4)
    for at in range(4):
        rank = flip(c, 1) * 4 + at
        landed(xs_ref.at[rows(rank)], xcr.at[at], sib)
        normalize(rank)
    for k, i in enumerate(order):
        slot = win_ref.at[block(dd, slots[i])]
        if k % 2 == 0:
            landed(slot, rr.at[k // 2], yn)
        else:
            landed(slot, rr.at[4 + k // 2], xn)
    own += [pltpu.make_async_copy(xnt_ref, xnt_out, own_sem.at[6]), pltpu.make_async_copy(win_ref, win_out, own_sem.at[7])]
    own[7].start()
    lead = u_ref.shape[1] - count
    u_ref[:, 0:lead, :] = jnp.zeros((tiles, lead, 128), f32)

    tile = 256

    def spread(out, first, start):
        def body(i, carry):
            product = jnp.dot(xn_ref[...], win_ref[:, pl.ds(pl.multiple_of(start + i * tile, tile), tile)], preferred_element_type=f32)
            for r in range(8):
                for part in range(0, tile, 128):
                    out[i * (tile // 128) + part // 128, pl.ds(first + r, length, stride=8), :] = product[r * length:(r + 1) * length, part:part + 128]
            return carry

        lax.fori_loop(0, width // tile, body, 0)

    spread(u_ref, lead, 0)
    taps = [vecs_ref[o:o + 1, :] for o in range(4)]
    bias = vecs_ref[4:5, :]

    def conv_step(i, carry):
        r = pl.ds(pl.multiple_of(i * 32, 32), 32)
        for n in range(tiles):
            lanes = slice(n * 128, n * 128 + 128)
            total = bias[:, lanes] + taps[3][:, lanes] * u_ref[n, pl.ds(pl.multiple_of(lead + i * 32, 8), 32), :]
            for o in range(1, 4):
                total = total + taps[3 - o][:, lanes] * (u_ref[n, pl.ds(pl.multiple_of(lead + i * 32 - 8 * o, 8), 32), :] * masks_ref[o - 1, r, :])
            sig = jax.nn.sigmoid(total)
            v_ref[n, r, :] = (total * sig).astype(bf16).astype(f32)
            slope_ref[n, r, :] = sig * (1.0 + total * (1.0 - sig))
        return carry

    lax.fori_loop(0, count // 32, conv_step, 0, unroll=2)
    for copy in own[3:5]:
        copy.wait()
    for i, (to, at) in enumerate(((xn, dx), (yn, dy), (dn, dd))):
        landed(smalls_ref.at[part_e(at)], pr.at[16 + i], to)
    quarter = count // 4
    narrow = smalls_ref[:, 128:256].astype(f32)
    packed = jnp.zeros((quarter, 128), f32)
    for b in range(4):
        r = slice(b * quarter, (b + 1) * quarter)
        values = jnp.concatenate([v_ref[n, r, :].astype(bf16) for n in range(tiles)], axis=1)
        part_ref[r, :] = jnp.dot(values, smalls_ref[:, 0:128], preferred_element_type=f32)
        turned = pltpu.roll(narrow, 32 * b, 1) if b else narrow
        packed = packed + jnp.dot(values, turned.astype(bf16), preferred_element_type=f32)
    part_ref[count:count + quarter, :] = packed
    saves = [(u_ref, u_out), (v_ref, v_out), (slope_ref, slope_out), (masks_ref, masks_out), (live_ref, live_out), (g_ref, g_out), (vt_ref, vt_out)]
    saves = [pltpu.make_async_copy(a, b, save_sem.at[i]) for i, (a, b) in enumerate(saves)]
    for copy in saves[:5]:
        copy.start()

    def early():
        row_hop(ups_ref, 4, 0, None, UP_HOPS)

    def between():
        spread(g_ref, 0, width)
        saves[5].start()

    def late():
        def turn_x(i, carry):
            part = pl.ds(pl.multiple_of(i * 128, 128), 128)
            for rank in range(8):
                r = slice(rank * length, (rank + 1) * length)
                xnt_ref[part, r] = xn_ref[r, part].T
            return carry

        lax.fori_loop(0, model // 128, turn_x, 0)
        own[6].start()
        row_hop(ups_ref, 4, 1, None, UP_HOPS)

        def turn_v(i, carry):
            r = pl.ds(pl.multiple_of(i * 128, 128), 128)
            for n in range(tiles):
                vt_ref[n * 128:(n + 1) * 128, r] = v_ref[n, r, :].T.astype(bf16)
            return carry

        lax.fori_loop(0, count // 128, turn_v, 0)
        saves[6].start()

    line_total(part_ref, out_ref, sib_ref, base_ref, left_ref, right_ref, tor_ref, tol_ref, ts, tr, tls, tlr, trs, trr, tos, tor, early, between, late)
    dl_ref[...] = out_ref[0:count, :].astype(bf16)
    for b in range(4):
        packed = out_ref[count:count + quarter, :]
        kq_ref[b * quarter:(b + 1) * quarter, :] = pltpu.roll(packed, 128 - 32 * b, 1) if b else packed
    row_hop(ups_ref, 4, 2, None, UP_HOPS)
    for at in range(4):
        @pl.when((z <= at + UP_HOPS) & (at <= z + UP_HOPS))
        def _():
            landed(ups_ref.at[rows(flip(c, 1) * 4 + at)], xcr.at[4 + at], sib)

    landed(wouts_ref.at[part_e(dd, 0, halves)], wr.at[2], yn)
    landed(wouts_ref.at[part_e(dd, halves, halves)], wr.at[3], xn)
    row_end(xs_ref, 0)
    row_end(ups_ref, 4, UP_HOPS)
    own[1].wait()
    for copy in saves:
        copy.wait()
    own[6].wait()
    own[7].wait()
    for copy in pending:
        copy.wait_send()


def line_total(part_ref, out_ref, sib_ref, base_ref, left_ref, right_ref, tor_ref, tol_ref, ss, sr, ls, lr, rs, rr, os_, or_, early, between, late):
    d, c, z = place()
    sib = (d, flip(c, 1), z)
    left = (d, c, lax.rem(z + 3, 4))
    right = (d, c, lax.rem(z + 1, 4))
    rows = part_ref.shape[0] // 2
    piece = rows // PIECES
    mine, theirs = c * rows, flip(c, 1) * rows

    def cut(p):
        return pl.ds(p * piece, piece)

    def far(base, p):
        return pl.ds(pl.multiple_of(base + p * piece, 8), piece)

    for p in range(PIECES):
        put(part_ref.at[far(theirs, p)], sib_ref.at[cut(p)], ss.at[p], sr.at[p], sib)
    for p in range(PIECES):
        landed(sib_ref.at[cut(p)], sr.at[p], sib)
        base_ref[cut(p), :] = part_ref[far(mine, p), :] + sib_ref[cut(p), :]

        @pl.when(z == 0)
        def _():
            put(base_ref.at[cut(p)], left_ref.at[cut(p)], rs.at[p], lr.at[p], right)

        @pl.when(z == 3)
        def _():
            put(base_ref.at[cut(p)], right_ref.at[cut(p)], ls.at[p], rr.at[p], left)

    early()

    def from_left(p):
        landed(left_ref.at[cut(p)], lr.at[p], left)

        @pl.when(z < 3)
        def _():
            tor_ref[cut(p), :] = base_ref[cut(p), :] + left_ref[cut(p), :]
            put(tor_ref.at[cut(p)], left_ref.at[cut(p)], rs.at[p], lr.at[p], right)

    def from_right(p):
        landed(right_ref.at[cut(p)], rr.at[p], right)

        @pl.when(z > 0)
        def _():
            tol_ref[cut(p), :] = base_ref[cut(p), :] + right_ref[cut(p), :]
            put(tol_ref.at[cut(p)], right_ref.at[cut(p)], ls.at[p], rr.at[p], left)

    @pl.when(z == 1)
    def _():
        for p in range(PIECES):
            from_left(p)

    @pl.when(z == 2)
    def _():
        for p in range(PIECES):
            from_right(p)

    between()

    @pl.when(z < 2)
    def _():
        for p in range(PIECES):
            from_right(p)

    @pl.when(z >= 2)
    def _():
        for p in range(PIECES):
            from_left(p)

    for p in range(PIECES):
        out_ref[far(mine, p), :] = base_ref[cut(p), :]

        @pl.when(z > 0)
        def _():
            out_ref[far(mine, p), :] += left_ref[cut(p), :]

        @pl.when(z < 3)
        def _():
            out_ref[far(mine, p), :] += right_ref[cut(p), :]

        put(out_ref.at[far(mine, p)], out_ref.at[far(mine, p)], os_.at[p], or_.at[p], sib)
    late()
    for p in range(PIECES):
        landed(out_ref.at[far(theirs, p)], or_.at[p], sib)
        sent(out_ref.at[far(mine, p)], os_.at[p], sib)
        sent(part_ref.at[far(theirs, p)], ss.at[p], sib)

        @pl.when(z < 3)
        def _():
            sent(base_ref.at[cut(p)], rs.at[p], right)

        @pl.when(z > 0)
        def _():
            sent(base_ref.at[cut(p)], ls.at[p], left)


def k1(tokens, upstream, w_in, w_out, w_x, w_dt, gain, lengths, conv_w, conv_b, dt_bias, skip):
    groups, ways = 4, 8
    small = jax.ShapeDtypeStruct((128, 384), bf16)
    cols = jax.ShapeDtypeStruct((ways, w_in.shape[0], w_in.shape[1] // ways), bf16)
    meta = jax.ShapeDtypeStruct((16, 128), f32)
    like = jax.ShapeDtypeStruct
    length, model = tokens.shape[1:]
    count = ways * length
    channels = groups * w_out.shape[0]
    dma = lambda n: pltpu.SemaphoreType.DMA((n,))
    some = pl.BlockSpec(memory_space=pl.ANY)
    far = pl.BlockSpec(memory_space=pltpu.HBM)
    here = pl.BlockSpec(memory_space=pltpu.VMEM)
    packed = count + count // 4
    return pl.pallas_call(
        k1_kernel,
        out_shape=(
            like((model, count), bf16),
            like((count, model), bf16),
            like((groups * ways * cols.shape[1], cols.shape[2]), bf16),
            like((channels, model), bf16),
            like((channels, small.shape[1]), bf16),
            like((8, channels), f32),
            like((1, model), f32),
            like((3, count + 32, 128), f32),
            like((1, count, 128), f32),
            like((channels // 128, count + 24, 128), f32),
            like((channels // 128, count, 128), f32),
            like((channels // 128, count, 128), f32),
            like((channels, count), bf16),
            like((channels // 128, count, 128), f32),
            like((count, 128), bf16),
            like((count, 128), f32),
        ),
        in_specs=[some] * 2 + [here, some] + [here] * 8,
        out_specs=(far,) * 4 + (here,) * 3 + (far,) * 7 + (here,) * 2,
        scratch_shapes=[
            pltpu.VMEM((3, count + 32, 128), f32),
            pltpu.VMEM((1, count, 128), f32),
            pltpu.VMEM((channels // 128, count + 24, 128), f32),
            pltpu.VMEM((channels // 128, count, 128), f32),
            pltpu.VMEM((channels // 128, count, 128), f32),
            pltpu.VMEM((channels, count), bf16),
            pltpu.VMEM((channels // 128, count, 128), f32),
            dma(7),
            pltpu.VMEM(cols.shape, bf16),
            pltpu.VMEM(meta.shape, f32),
            pltpu.VMEM(small.shape, bf16),
            pltpu.VMEM((count, model), bf16),
            pltpu.VMEM((count, model), bf16),
            pltpu.VMEM((model, count), bf16),
            pltpu.VMEM((groups * ways * cols.shape[1], cols.shape[2]), bf16),
            pltpu.VMEM((groups, ways) + meta.shape, f32),
            pltpu.VMEM((packed, 128), f32),
            pltpu.VMEM((packed, 128), f32),
        ] + [pltpu.VMEM((packed // 2, 128), f32)] * 6
        + [dma(8), dma(7), dma(7), dma(3), dma(3), dma(8), dma(8), dma(8), dma(8), dma(8), dma(8), dma(7), dma(7), dma(19), dma(19), dma(8), dma(8), dma(4), dma(4)]
        + [dma(PIECES) for _ in range(8)],
        compiler_params=pltpu.CompilerParams(collective_id=0, has_side_effects=True, vmem_limit_bytes=56 * 1024 * 1024),
    )(tokens, upstream, w_in, w_out, w_x, w_dt, gain, lengths, conv_w, conv_b, dt_bias, skip)


GROUP = 4


def k2_kernel(states, dl_ref, kq_ref, wdt_ref, vecs_ref, keep_ref, live_ref, v_ref, g_ref, ups_any, wout_any,
              acc_out, mt_ref, dg_ref, gwdt_ref, ups_out, dv_ref, part_ref, stat_ref,
              ups_ref, loads, stores, zs, zr, cs, cr, ls, lr, ss, sr, m_ref, wout_ref, acc_ref, recv_ref, dpre_ref, s_ref, h_ref, rate_ref, w_ref, y_ref, dm_ref, kb_ref, hot_ref, drr_ref):
    tiles, count = v_ref.shape[:2]
    steps = count // 8
    wide = states * 128
    chunk = 256
    first = pl.program_id(0) == 0
    half = pl.program_id(0)
    both = range(tiles)
    width = tiles * 128
    rank = wdt_ref.shape[1]

    length = count // 8
    d, c, z = place()
    sib = (d, flip(c, 1), z)
    left = (d, c, lax.rem(z + 3, 4))
    right = (d, c, lax.rem(z + 1, 4))

    def rows(rank):
        return pl.ds(pl.multiple_of(rank * length, length), length)

    keeps = [pltpu.make_async_copy(ups_ref.at[r // 4, r % 4], ups_out.at[r // 4, r % 4], stores.at[r]) for r in range(8)]

    def arrive(act):
        for rank in range(8):
            at = rank % 4
            here = jnp.logical_not(((z == 0) & (at == 3)) | ((z == 3) & (at == 0))) if at in (0, 3) else None
            copy = pltpu.make_async_copy(ups_any.at[rows(rank)], ups_ref.at[rank // 4, at], loads.at[rank])
            if here is None:
                act(copy)
            else:
                @pl.when(here)
                def _():
                    act(copy)

    @pl.when(first)
    def _():
        arrive(lambda copy: copy.start())
        pltpu.make_async_copy(wout_any, wout_ref, loads.at[8]).start()
        greet([sib, left, right])

        @pl.when(z == 1)
        def _():
            put(ups_any.at[rows(c * 4 + 3)], ups_ref.at[c, 3], zs, zr, left)

        @pl.when(z == 2)
        def _():
            put(ups_any.at[rows(c * 4)], ups_ref.at[c, 0], zs, zr, right)

    def complete():
        for end, source, at in ((0, right, 3), (3, left, 0)):
            @pl.when(z == end)
            def _():
                slot = ups_ref.at[c, at]
                landed(slot, zr, source)
                put(slot, slot, cs, cr, sib)
                landed(ups_ref.at[flip(c, 1), at], cr, sib)
                sent(slot, cs, sib)

        for end, target, at in ((1, left, 3), (2, right, 0)):
            @pl.when(z == end)
            def _():
                sent(ups_any.at[rows(c * 4 + at)], zs, target)

        arrive(lambda copy: copy.wait())
        pltpu.make_async_copy(wout_any, wout_ref, loads.at[8]).wait()
        for copy in keeps:
            copy.start()

    @pl.when(first)
    def _():
        row = lax.broadcasted_iota(jnp.int32, (128, 512), 0)
        col = lax.broadcasted_iota(jnp.int32, (128, 512), 1) // 128
        for part in range(0, 2 * wide, 512):
            hot_ref[:, part:part + 512] = jnp.where((row % 32 == col + part // 128) & (row < 96), 1.0, 0.0).astype(bf16)

    lane = lax.broadcasted_iota(jnp.int32, (chunk, 128), 1)

    def spread(i, carry):
        r = pl.ds(pl.multiple_of(i * chunk, chunk), chunk)
        value = jnp.where(lane < 2 * states, kq_ref[r, :], 0.0)
        hi = value.astype(bf16).astype(f32)
        mid = (value - hi).astype(bf16).astype(f32)
        low = value - hi - mid
        left = (hi + pltpu.roll(mid, 32, 1) + pltpu.roll(low, 64, 1)).astype(bf16)
        for part in range(0, 2 * wide, 512):
            kb_ref[r, part:part + 512] = jnp.dot(left, hot_ref[:, part:part + 512], preferred_element_type=f32)
        return carry

    lax.fori_loop(0, count // chunk, spread, 0)
    cols = (((1,), (1,)), ((), ()))

    def gate_step(i, carry):
        value = ups_ref[i // 2, pl.ds((i % 2) * 2, 2)].reshape(chunk, wout_ref.shape[1])
        product = lax.dot_general(value, wout_ref[pl.ds(pl.multiple_of(half * width, width), width), :], cols, preferred_element_type=f32)
        for j in range(chunk // length):
            for n in both:
                dm_ref[n, pl.ds(i * (chunk // length) + j, length, stride=8), :] = product[j * length:(j + 1) * length, n * 128:(n + 1) * 128]
        return carry

    bias = vecs_ref[5:6, :]
    skip = vecs_ref[6:7, :]
    tile_of = lambda x, n: x[:, n * 128:(n + 1) * 128]
    ks = lax.broadcasted_iota(jnp.int32, (128, 128), 1)

    def before(i, carry):
        seen = list(carry)
        r = pl.ds(pl.multiple_of(i * 128, 128), 128)
        live = live_ref[0, r, :]
        k = jnp.where(ks < states, kq_ref[r, :], 0.0)
        sk = jnp.sum(k * k, axis=1, keepdims=True)
        pre = lax.dot_general(dl_ref[r, :], wdt_ref[...], cols, preferred_element_type=f32) + bias
        for n in both:
            beta = jax.nn.sigmoid(tile_of(pre, n))
            part = 1.0 / (1.0 + beta * sk)
            rate_ref[n, r, :] = beta * part
            w_ref[n, r, :] = part * part * beta * (1.0 - beta)
            shown = (beta * live).reshape(16, 8, 128)
            seen[n] = seen[n] + jnp.sum(shown, axis=0)
            seen[tiles + n] = jnp.maximum(seen[tiles + n], jnp.max(shown, axis=0))
        return tuple(seen)

    blank = jnp.zeros((8, 128), f32)
    seen = lax.fori_loop(0, count // 128, before, (blank,) * (2 * tiles))
    s_ref[0, 0] = jnp.zeros(s_ref.shape[2:], f32)
    span = GROUP * 8
    at = [slice(j * 8, j * 8 + 8) for j in range(GROUP)]

    def view(ref, i):
        r = pl.ds(pl.multiple_of(i * span, span), span)
        return ref.at[:, r] if len(ref.shape) == 3 else ref.at[r]

    def pair(ref, r):
        return jnp.concatenate([ref[n, r, :] for n in both], axis=1)

    def keep_pair(ref, r, value):
        for n in both:
            ref[n, r, :] = tile_of(value, n)

    tile = lambda x: jnp.concatenate([x] * tiles, axis=1)

    def fold(x):
        total = tile_of(x, 0)
        for n in range(1, tiles):
            total = total + tile_of(x, n)
        return total

    def forward(i, carry):
        keeps, rates, vs, kbs, ys = [view(x, i) for x in (keep_ref, rate_ref, v_ref, kb_ref, y_ref)]
        keep = [keeps[0, r, :] for r in at]
        rate = [pair(rates, r) for r in at]
        value = [pair(vs, r) for r in at]
        rv = [a * b for a, b in zip(rate, value)]
        y = [skip * b for b in value]
        for n in range(states):
            state = s_ref[i, 0, n]
            for j, r in enumerate(at):
                kb = kbs[r, n * 128:(n + 1) * 128]
                qb = kbs[r, wide + n * 128:wide + (n + 1) * 128]
                state = (tile(keep[j]) - rate[j] * tile(kb * kb * keep[j])) * state + rv[j] * tile(kb)
                if j < GROUP - 1:
                    s_ref[i, j + 1, n] = state
                else:
                    s_ref[i + 1, 0, n] = state
                y[j] = y[j] + state * tile(qb)
        for j, r in enumerate(at):
            keep_pair(ys, r, y[j])
        return carry

    lax.fori_loop(0, steps // GROUP, forward, 0)
    h_ref[...] = jnp.zeros_like(h_ref)

    @pl.when(first)
    def _():
        complete()

    lax.fori_loop(0, count // chunk, gate_step, 0)

    def gates(i, carry):
        r = pl.ds(pl.multiple_of(i * 32, 32), 32)
        live = live_ref[0, r, :]
        for n in both:
            g = g_ref[n, r, :]
            sg = jax.nn.sigmoid(g)
            silu = g * sg
            y = y_ref[n, r, :]
            dm = dm_ref[n, r, :] * live
            dv_ref[n, r, :] = dm * silu
            dm_ref[n, r, :] = dm * y * (sg * (1.0 + g * (1.0 - sg)))
            y_ref[n, r, :] = y * silu * live
        return carry

    lax.fori_loop(0, count // 32, gates, 0, unroll=2)

    def by_row(j, carry):
        r = pl.ds(pl.multiple_of(j * length, length), length)
        for n in both:
            value = y_ref[n, pl.ds(j, length, stride=8), :]
            m_ref[r, pl.ds(pl.multiple_of(half * width + n * 128, 128), 128)] = value.astype(bf16)
            mt_ref[n * 128:(n + 1) * 128, r] = value.T.astype(bf16)
            dg_ref[r, n * 128:(n + 1) * 128] = dm_ref[n, pl.ds(j, length, stride=8), :].astype(bf16)
        return carry

    lax.fori_loop(0, 8, by_row, 0)

    def rows_product(core):
        def body(i, carry):
            lanes = pl.ds(pl.multiple_of(i * chunk, chunk), chunk)
            product = jnp.dot(m_ref[pl.ds(pl.multiple_of(core * 4 * length, 4 * length), 4 * length), :], wout_ref[:, lanes], preferred_element_type=f32)
            for at_z in range(4):
                ups_ref[core, at_z, :, lanes] = product[at_z * length:(at_z + 1) * length].astype(bf16)
            return carry

        lax.fori_loop(0, wout_ref.shape[1] // chunk, body, 0)

    def gather(at_z):
        landed(acc_ref.at[at_z], sr.at[at_z], sib)
        add_rows(acc_ref.at[at_z], [acc_ref.at[at_z], ups_ref.at[c, at_z]])

    @pl.when(jnp.logical_not(first))
    def _():
        for copy in keeps:
            copy.wait()
        rows_product(flip(c, 1))
        for at_z in (3, 0, 2, 1):
            put(ups_ref.at[flip(c, 1), at_z], acc_ref.at[at_z], ss.at[at_z], sr.at[at_z], sib)
        rows_product(c)
        gather(3)
        gather(0)

        @pl.when(z == 0)
        def _():
            put(acc_ref.at[3], recv_ref, ls, lr, right)

        @pl.when(z == 3)
        def _():
            put(acc_ref.at[0], recv_ref, ls, lr, left)


    def backward(step, carry):
        i = steps // GROUP - 1 - step
        keeps, rates, vs, kbs, dvs, ws, drrs = [view(x, i) for x in (keep_ref, rate_ref, v_ref, kb_ref, dv_ref, w_ref, drr_ref)]
        keep = [keeps[0, r, :] for r in at]
        rate = [pair(rates, r) for r in at]
        value = [pair(vs, r) for r in at]
        rv = [a * b for a, b in zip(rate, value)]
        dy = [pair(dvs, r) for r in at]
        hk = [jnp.zeros((8, tiles * 128), f32) for r in at]
        hs2 = [jnp.zeros((8, tiles * 128), f32) for r in at]
        for n in range(states):
            ah = h_ref[n]
            later = s_ref[i + 1, 0, n]
            for j in range(GROUP - 1, -1, -1):
                r = at[j]
                kb = kbs[r, n * 128:(n + 1) * 128]
                qb = kbs[r, wide + n * 128:wide + (n + 1) * 128]
                kk = kb * keep[j]
                held = tile(kb * kk)
                h = dy[j] * tile(qb) + ah
                prior = s_ref[i, j, n]
                hs = h * prior
                hk[j] = hk[j] + h * tile(kb)
                hs2[j] = hs2[j] + hs * held
                kbs[r, n * 128:(n + 1) * 128] = fold(h * rv[j]) - 2.0 * kk * fold(hs * rate[j])
                kbs[r, wide + n * 128:wide + (n + 1) * 128] = fold(dy[j] * later)
                later = prior
                ah = (tile(keep[j]) - rate[j] * held) * h
            h_ref[n] = ah
        dskip = carry
        for j, r in enumerate(at):
            drate = value[j] * hk[j] - hs2[j]
            drrs[r, :] = fold(drate * rate[j] * rate[j]) * (-2.0)
            keep_pair(ws, r, drate * pair(ws, r))
            keep_pair(dvs, r, rate[j] * hk[j] + skip * dy[j])
            dskip = dskip + dy[j] * value[j]
        return dskip

    dskip = lax.fori_loop(0, steps // GROUP, backward, jnp.zeros((8, tiles * 128), f32))

    quarter = count // 4
    packed = jnp.zeros((quarter, 128), f32)
    for b in range(4):
        r = slice(b * quarter, (b + 1) * quarter)
        total = jnp.zeros((quarter, 128), f32)
        for part in range(0, 2 * wide, 512):
            total = total + lax.dot_general(kb_ref[r, part:part + 512].astype(bf16), hot_ref[:, part:part + 512], cols, preferred_element_type=f32)
        drr = jnp.sum(drr_ref[r, :], axis=1, keepdims=True)
        k = kq_ref[r, :]
        low = lax.broadcasted_iota(jnp.int32, (quarter, 128), 1)
        total = jnp.where(low < 2 * states, total, 0.0) + jnp.where(low < states, k * drr, 0.0)
        packed = packed + (pltpu.roll(total, 32 * b, 1) if b else total)

    tail = pl.ds(count, quarter)
    part_ref[tail, :] = jnp.where(first, packed, part_ref[tail, :] + packed)

    def after(i, carry):
        r = pl.ds(pl.multiple_of(i * 128, 128), 128)
        sums = list(carry)
        for n in both:
            low = w_ref[n, r, :].astype(bf16)
            dpre_ref[r, n * 128:(n + 1) * 128] = low
            sums[n] = sums[n] + jnp.sum(low.astype(f32).reshape(16, 8, 128), axis=0)
        ddl = jnp.dot(dpre_ref[r, :], wdt_ref[...], preferred_element_type=f32)
        part_ref[r, :] = jnp.where(first, ddl, part_ref[r, :] + ddl)
        return tuple(sums)

    sums = lax.fori_loop(0, count // 128, after, (blank,) * tiles)

    gwdt_ref[...] = lax.dot_general(dpre_ref[...], dl_ref[...], (((0,), (0,)), ((), ())), preferred_element_type=f32)

    @pl.when(jnp.logical_not(first))
    def _():
        gather(2)
        gather(1)
        for end, source, at_z in ((1, left, 3), (2, right, 0)):
            @pl.when(z == end)
            def _():
                landed(recv_ref, lr, source)
                add_rows(acc_ref.at[at_z], [acc_ref.at[at_z], recv_ref])

        save = pltpu.make_async_copy(acc_ref, acc_out, loads.at[8])
        save.start()
        for at_z in range(4):
            sent(ups_ref.at[flip(c, 1), at_z], ss.at[at_z], sib)
        for end, target, at_z in ((0, right, 3), (3, left, 0)):
            @pl.when(z == end)
            def _():
                sent(acc_ref.at[at_z], ls, target)
        save.wait()

    stat_ref[...] = jnp.zeros_like(stat_ref)
    for n in both:
        lanes = slice(n * 128, (n + 1) * 128)
        stat_ref[0:1, lanes] = jnp.sum(seen[n], axis=0, keepdims=True)
        stat_ref[1:2, lanes] = jnp.max(seen[tiles + n], axis=0, keepdims=True)
        stat_ref[5:6, lanes] = jnp.sum(sums[n], axis=0, keepdims=True)
        stat_ref[6:7, lanes] = jnp.sum(tile_of(dskip, n), axis=0, keepdims=True)


def k2(dl, kq, smalls, vecs, masks, live, v, g, ups, wout, states):
    count, rank = dl.shape
    channels, model = wout.shape
    tiles = 2
    width = tiles * 128
    like = jax.ShapeDtypeStruct
    once = pl.Buffered(buffer_count=1)
    whole = lambda a: pl.BlockSpec(a.shape, lambda h: (0,) * a.ndim, pipeline_mode=once)
    deep = pl.BlockSpec((tiles, count, 128), lambda h: (h, 0, 0))
    flat = pl.BlockSpec((count, width), lambda h: (0, h))
    return pl.pallas_call(
        functools.partial(k2_kernel, states),
        grid=(channels // width,),
        out_shape=(
            like((4, count // 8, model), bf16),
            like((channels, count), bf16),
            like((count, channels), bf16),
            like((channels, rank), f32),
            like((2, 4, count // 8, model), bf16),
            like(v.shape, f32),
            like((count + count // 4, 128), f32),
            like((8, channels), f32),
        ),
        in_specs=[
            whole(dl), whole(kq),
            pl.BlockSpec((width, 128), lambda h: (h, 2)),
            pl.BlockSpec((8, width), lambda h: (0, h)),
            pl.BlockSpec((1, count, 128), lambda h: (0, 0, 0), pipeline_mode=once),
            pl.BlockSpec((1, count, 128), lambda h: (0, 0, 0), pipeline_mode=once),
            deep, deep, pl.BlockSpec(memory_space=pl.ANY),
            pl.BlockSpec(memory_space=pl.ANY),
        ],
        out_specs=(pl.BlockSpec(memory_space=pltpu.HBM), pl.BlockSpec((width, count), lambda h: (h, 0)), flat, pl.BlockSpec((width, rank), lambda h: (h, 0)), pl.BlockSpec(memory_space=pltpu.HBM), deep, pl.BlockSpec((count + count // 4, 128), lambda h: (0, 0)), pl.BlockSpec((8, width), lambda h: (0, h))),
        scratch_shapes=[
            pltpu.VMEM((2, 4, count // 8, model), bf16),
            pltpu.SemaphoreType.DMA((9,)),
            pltpu.SemaphoreType.DMA((8,)),
        ] + [pltpu.SemaphoreType.DMA(())] * 6 + [
            pltpu.SemaphoreType.DMA((4,)),
            pltpu.SemaphoreType.DMA((4,)),
            pltpu.VMEM((count, channels), bf16),
            pltpu.VMEM((channels, model), bf16),
            pltpu.VMEM((4, count // 8, model), bf16),
            pltpu.VMEM((count // 8, model), bf16),
            pltpu.VMEM((count, width), bf16),
            pltpu.VMEM((count // 8 // GROUP + 1, GROUP, states, 8, width), f32),
            pltpu.VMEM((states, 8, width), f32),
        ] + [pltpu.VMEM((tiles, count, 128), f32)] * 4
        + [pltpu.VMEM((count, 2 * states * 128), f32), pltpu.VMEM((128, 2 * states * 128), bf16), pltpu.VMEM((count, 128), f32)],
        compiler_params=pltpu.CompilerParams(collective_id=2, has_side_effects=True, vmem_limit_bytes=63400000),
    )(dl, kq, smalls, vecs, masks, live, v, g, ups, wout)


class Row:
    def __init__(self, part, sib, recv, sems, merged=False):
        self.part, self.sib, self.recv, self.merged = part, sib, recv, merged
        self.ss, self.sr, self.gs, self.lr, self.rr = sems
        d, c, z = place()
        self.c = c
        self.other = (d, flip(c, 1), z)
        self.to_left = (d, c, lax.rem(z + 3, 4))
        self.to_right = (d, c, lax.rem(z + 1, 4))

    def start(self):
        for zp in (3, 0, 2, 1):
            put(self.part.at[flip(self.c, 1), zp], self.sib.at[zp], self.ss.at[zp], self.sr.at[zp], self.other)

    def gather(self):
        for zp in (3, 0, 2, 1):
            landed(self.sib.at[zp], self.sr.at[zp], self.other)
            add_rows(self.sib.at[zp], [self.sib.at[zp], self.part.at[self.c, zp]])

    def release(self):
        for zp in range(4):
            sent(self.part.at[flip(self.c, 1), zp], self.ss.at[zp], self.other)

    def terms(self, zs, zp):
        found = [self.sib.at[zp]]
        if zp >= zs and zs > 0 and not (self.merged and (zs, zp) == (1, 3)):
            landed(self.recv.at[zp], self.lr.at[zp], self.to_left)
            found.append(self.recv.at[zp])
        if zp <= zs and zs < 3 and not (self.merged and (zs, zp) == (2, 0)):
            slot = self.recv.at[4 if zp == zs else zp]
            landed(slot, self.rr.at[zp], self.to_right)
            found.append(slot)
        return found

    def join(self, zs, zp):
        found = self.terms(zs, zp)
        if len(found) > 1:
            add_rows(self.sib.at[zp], found)

    def skips(self, zs, zp):
        return self.merged and (zs, zp) in ((0, 3), (3, 0))

    def step(self, zs, k):
        k = k + 1 if self.merged else k
        ends = 1 if self.merged else 0
        for zp in ((3, 2, 1, 0) if zs == 0 else (0, 1, 2, 3)):
            if zp > zs and not self.skips(zs, zp) and k == (ends if zs == 0 else 3 - zp + zs):
                self.join(zs, zp)
                put(self.sib.at[zp], self.recv.at[zp], self.gs.at[zp], self.lr.at[zp], self.to_right)
            if zp < zs and not self.skips(zs, zp) and k == (ends if zs == 3 else zp + 3 - zs):
                self.join(zs, zp)
                put(self.sib.at[zp], self.recv.at[4 if zp == zs - 1 else zp], self.gs.at[zp], self.rr.at[zp], self.to_left)

    def finish(self, zs):
        add_rows(self.sib.at[zs], self.terms(zs, zs), self.total)

    def close(self, zs):
        for zp in range(4):
            if zp != zs and not self.skips(zs, zp):
                sent(self.sib.at[zp], self.gs.at[zp], self.other)

    def along(self, k, total=None):
        self.total = total
        d, c, z = place()
        for zs in range(4):
            @pl.when(z == zs)
            def _():
                if k < (2 if self.merged else 3):
                    self.step(zs, k)
                else:
                    self.finish(zs)
                    self.close(zs)


def row_scratch(rows, columns):
    return [pltpu.VMEM((4, rows, columns), bf16), pltpu.VMEM((5, rows, columns), bf16)] + [pltpu.SemaphoreType.DMA((4,))] * 5


def add_rows(dst, sources, total=None):
    rows = (total if total is not None else dst).shape[0]
    step = 16

    def body(i, carry):
        r = pl.ds(pl.multiple_of(i * step, step), step)
        value = sources[0][r, :].astype(f32)
        for more in sources[1:]:
            value = value + more[r, :].astype(f32)
        if total is not None:
            total[r, :] = value
        else:
            dst[r, :] = value.astype(dst.dtype)
        return carry

    lax.fori_loop(0, rows // step, body, 0)


class Flat:
    def __init__(self, part, xa, yb, rx, ry, ss, rs):
        self.part, self.xa, self.yb, self.rx, self.ry, self.ss, self.rs = part, xa, yb, rx, ry, ss, rs
        d, c, z = place()
        self.d, self.dx, self.dy, self.dd = d, flip(d, 1), flip(d, 2), flip(flip(d, 1), 2)
        self.xn, self.yn = (self.dx, c, z), (self.dy, c, z)
        half = part.shape[1] // 2
        self.a, self.b = pl.ds(0, half), pl.ds(half, half)
        self.sends = []

    def start_far(self):
        p = self.part
        self.sends.append(put(p.at[self.dd, self.a], self.xa, self.ss.at[0], self.rs.at[0], self.xn))
        self.sends.append(put(p.at[self.dd, self.b], self.yb, self.ss.at[1], self.rs.at[1], self.yn))

    def start_near(self):
        p = self.part
        self.sends.append(put(p.at[self.dx, self.a], self.rx.at[self.a], self.ss.at[2], self.rs.at[2], self.xn))
        self.sends.append(put(p.at[self.dy, self.b], self.ry.at[self.b], self.ss.at[3], self.rs.at[3], self.yn))

    def middle(self):
        p = self.part
        landed(self.xa, self.rs.at[0], self.xn)
        add_rows(self.xa, [self.xa, p.at[self.dy, self.a]])
        self.sends.append(put(self.xa, self.ry.at[self.a], self.ss.at[4], self.rs.at[4], self.yn))
        landed(self.yb, self.rs.at[1], self.yn)
        add_rows(self.yb, [self.yb, p.at[self.dx, self.b]])
        self.sends.append(put(self.yb, self.rx.at[self.b], self.ss.at[5], self.rs.at[5], self.xn))

    def finish(self, out):
        landed(self.rx.at[self.a], self.rs.at[2], self.xn)
        landed(self.ry.at[self.b], self.rs.at[3], self.yn)
        landed(self.ry.at[self.a], self.rs.at[4], self.yn)
        landed(self.rx.at[self.b], self.rs.at[5], self.xn)
        add_rows(out, [self.part.at[self.d], self.rx, self.ry])

    def close(self):
        for copy in self.sends:
            copy.wait_send()


def flat_scratch(rows, columns, dtype):
    half = pltpu.VMEM((rows // 2, columns), dtype)
    full = pltpu.VMEM((rows, columns), dtype)
    return [half, half, full, full, pltpu.SemaphoreType.DMA((6,)), pltpu.SemaphoreType.DMA((6,))]


def k3_kernel(part_ref, stat_ref, smalls_ref, vecs_ref, gains_ref, gwdt_ref, masks_ref, tok_ref, up_ref,
              acc_any, mt_any, dg_any, dv_any, slope_any, u_any, vt_any, xnt_any, win_any, ups_any,
              block_out, gtok_out, gwin_out, gwout_out, small_out, tiny_out, *scratch):
    scratch = list(scratch)

    def take(n):
        found = scratch[:n]
        del scratch[:n]
        return found

    block_ref, gtok_ref, gwin_ref, gwout_ref, small_ref, tiny_ref, stores = take(7)
    outp, win_ref, up, gp, gwoutp, smallp = take(6)
    mt_ref, dz_ref, dc_ref, slope_ref, u_ref, xnt_ref, dp_ref, slots_ref, row_ref = take(9)
    near_ref, pairs_ref, sum_ref, far_ref = take(4)
    loads, as_, ar, ns, nr, fs, fr = take(7)
    totals = take(7)
    total_sems = take(8)
    out_row = Row(None, *take(2), take(5), True)
    dxn_row = Row(outp, *take(2), take(5))
    flats = [Flat(up, *take(6)), Flat(gp, *take(6))]
    gwout_flat = Flat(gwoutp, *take(6))
    small_flat = Flat(smallp, *take(6))
    d, c, z = place()
    j = c * 4 + z
    other = flip(c, 1)
    steps = mates()
    planes = [(flip(d, 1), c, z), (flip(d, 2), c, z), (flip(flip(d, 1), 2), c, z)]
    length, model = tok_ref.shape[1:]
    tiles, padded, _ = dc_ref.shape
    count = dz_ref.shape[0]
    width = tiles * 128
    rows_any = [(dg_any, dz_ref.at[:, pl.ds(width, width)]), (xnt_any, xnt_ref), (acc_any, out_row.sib), (mt_any, mt_ref), (ups_any, outp),
                (dv_any, dc_ref.at[:, pl.ds(0, count)]), (slope_any, slope_ref), (u_any, u_ref), (win_any, win_ref)]
    copies = [pltpu.make_async_copy(a, b, loads.at[i]) for i, (a, b) in enumerate(rows_any)]
    for copy in copies:
        copy.start()
    greet([mate(s) for s in steps] + planes)
    outs = [(block_ref, block_out), (gtok_ref, gtok_out), (gwin_ref, gwin_out), (gwout_ref, gwout_out), (small_ref, small_out), (tiny_ref, tiny_out)]
    outs = [pltpu.make_async_copy(a, b, stores.at[i]) for i, (a, b) in enumerate(outs)]
    tile = 256
    nt = (((1,), (1,)), ((), ()))

    def rows_product(half):
        def body(i, carry):
            value = win_ref[i // (512 // tile), pl.ds(pl.multiple_of((i % (512 // tile)) * tile, tile), tile), :]
            product = lax.dot_general(dz_ref[pl.ds(pl.multiple_of(half * 512, 512), 512), :], value, nt, preferred_element_type=f32)
            for zp in range(4):
                outp[half, zp, :, pl.ds(pl.multiple_of(i * tile, tile), tile)] = product[zp * length:(zp + 1) * length].astype(bf16)
            return carry

        lax.fori_loop(0, model // tile, body, 0)

    def weight_rows(holder, first, group):
        def body(i, carry):
            lanes = pl.ds(pl.multiple_of(i * tile, tile), tile)
            left = xnt_ref[pl.ds(pl.multiple_of(group * 512, 512), 512), :]
            value = dz_ref[:, pl.ds(pl.multiple_of(first + i * tile, tile), tile)]
            holder[group, :, lanes] = jnp.dot(left, value, preferred_element_type=f32).astype(bf16)
            return carry

        lax.fori_loop(0, width // tile, body, 0)

    def weight_part(k):
        flat = flats[k]
        holder, first = (up, 0) if k == 0 else (gp, width)
        weight_rows(holder, first, flat.dd)
        flat.start_far()
        weight_rows(holder, first, flat.dx)
        weight_rows(holder, first, flat.dy)
        flat.start_near()
        weight_rows(holder, first, d)

    def early():
        for copy in copies[0:2]:
            copy.wait()
        weight_part(1)

    def between():
        copies[2].wait()
        out_row.along(0)
        flats[1].middle()

    def late():
        for copy in copies[3:5]:
            copy.wait()

        def body(i, carry):
            lanes = pl.ds(pl.multiple_of(i * tile, tile), tile)
            product = jnp.dot(mt_ref[...], outp[:, :, :, lanes].reshape(count, tile), preferred_element_type=f32)
            for g in range(4):
                gwoutp[g, :, lanes] = product[g * 128:(g + 1) * 128].astype(bf16)
            return carry

        lax.fori_loop(0, model // tile, body, 0)
        gwout_flat.start_far()
        gwout_flat.start_near()

    seen = jnp.sum(stat_ref[0:1, :], axis=1, keepdims=True)
    peak = jnp.max(stat_ref[1:2, :], axis=1, keepdims=True)
    row8 = lax.broadcasted_iota(jnp.int32, (8, 128), 0)
    lane8 = lax.broadcasted_iota(jnp.int32, (8, 128), 1)
    pairs_ref[...] = jnp.where(lane8 == 0, seen, jnp.where(lane8 == 1, peak, 0.0))
    for i, s in enumerate(steps):
        put(pairs_ref, near_ref.at[i], ns.at[i], nr.at[i], mate(s))

    def join(a, b):
        return jnp.where(lane8 == 1, jnp.maximum(a, b), a + b)

    total_ref = totals[0]
    line_total(part_ref, *totals, *total_sems, early, between, late)
    vt_copy = pltpu.make_async_copy(vt_any, mt_ref, loads.at[9])
    vt_copy.start()
    block = gwin_ref.shape[0]
    pending = []

    def rows_of(k, rank):
        return flats[k].part.at[d, pl.ds(pl.multiple_of(rank * block, block), block)]

    def give(k):
        flats[k].finish(flats[k].part.at[d])
        for i, s in enumerate(steps):
            to = mate(s)
            pending.append(put(rows_of(k, rank_of(to)), slots_ref.at[k, i], as_.at[7 * k + i], ar.at[7 * k + i], to))

    value = pairs_ref[...]
    for i, s in enumerate(steps):
        landed(near_ref.at[i], nr.at[i], mate(s, -1))
        value = join(value, near_ref[i])
    sum_ref[...] = value
    for i, to in enumerate(planes):
        put(sum_ref, far_ref.at[i], fs.at[i], fr.at[i], to)
    quarter = count // 4
    lane = lax.broadcasted_iota(jnp.int32, (quarter, 128), 1)
    dp_ref[:, 0:128] = total_ref[0:count, :].astype(bf16)
    for b in range(4):
        packed = total_ref[count:count + quarter, :]
        packed = pltpu.roll(packed, 128 - 32 * b, 1) if b else packed
        dp_ref[b * quarter:(b + 1) * quarter, 128:256] = jnp.where(lane < 32, packed, 0.0).astype(bf16)
    for copy in copies[5:8]:
        copy.wait()
    dc_ref[:, count:, :] = jnp.zeros((tiles, padded - count, 128), f32)

    def slope_step(i, carry):
        r = pl.ds(pl.multiple_of(i * 256, 256), 256)
        product = lax.dot_general(dp_ref[r, :], smalls_ref[:, 0:256], nt, preferred_element_type=f32)
        for n in range(tiles):
            dc_ref[n, r, :] = (dc_ref[n, r, :] + product[:, n * 128:(n + 1) * 128]) * slope_ref[n, r, :]
        return carry

    lax.fori_loop(0, count // 256, slope_step, 0)
    give(1)
    out_row.along(1)
    taps = [vecs_ref[o:o + 1, :] for o in range(4)]
    lead = u_ref.shape[1] - count

    for n in range(tiles):
        lanes = slice(n * 128, (n + 1) * 128)
        tap = [t[:, lanes] for t in taps]

        def conv_step(i, carry):
            r = pl.ds(pl.multiple_of(i * 32, 32), 32)
            sums = list(carry)
            dc = dc_ref[n, r, :]
            du = tap[3] * dc
            fold8 = lambda x: x[0:8] + x[8:16] + x[16:24] + x[24:32]
            sums[4] = sums[4] + fold8(dc)
            sums[3] = sums[3] + fold8(dc * u_ref[n, pl.ds(pl.multiple_of(lead + i * 32, 8), 32), :])
            for o in range(1, 4):
                sums[3 - o] = sums[3 - o] + fold8(dc * (u_ref[n, pl.ds(pl.multiple_of(lead + i * 32 - 8 * o, 8), 32), :] * masks_ref[o - 1, pl.ds(pl.multiple_of(i * 32, 8), 32), :]))
                du = du + tap[3 - o] * (dc_ref[n, pl.ds(pl.multiple_of(i * 32 + 8 * o, 8), 32), :] * masks_ref[o - 1, pl.ds(pl.multiple_of(i * 32 + 8 * o, 8), 32), :])
            dc_ref[n, r, :] = du
            return tuple(sums)

        sums = lax.fori_loop(0, count // 32, conv_step, (jnp.zeros((8, 128), f32),) * 5)
        smallp[n, 128:160, :] = jnp.zeros((32, 384), f32)
        for k in range(5):
            smallp[n, 128 + k:129 + k, 0:128] = jnp.sum(sums[k], axis=0, keepdims=True)
        smallp[n, 133:134, 0:128] = stat_ref[5:6, lanes]
        smallp[n, 134:135, 0:128] = stat_ref[6:7, lanes]
        smallp[n, 0:128, 256:384] = gwdt_ref[n * 128:(n + 1) * 128, :]

    def by_row(i, carry):
        r = pl.ds(pl.multiple_of(i * length, length), length)
        for n in range(tiles):
            dz_ref[r, n * 128:(n + 1) * 128] = dc_ref[n, pl.ds(i, length, stride=8), :].astype(bf16)
        return carry

    lax.fori_loop(0, 8, by_row, 0)
    gwout_flat.middle()
    copies[8].wait()
    rows_product(other)
    dxn_row.start()
    weight_rows(up, 0, flats[0].dd)
    flats[0].start_far()
    rows_product(c)
    dxn_row.gather()
    dxn_row.along(0)
    weight_rows(up, 0, flats[0].dx)
    weight_rows(up, 0, flats[0].dy)
    flats[0].start_near()
    weight_rows(up, 0, d)
    vt_copy.wait()
    for n in range(tiles):
        smallp[n, 0:128, 0:256] = jnp.dot(mt_ref[n * 128:(n + 1) * 128, :], dp_ref[...], preferred_element_type=f32)
    small_flat.start_far()
    small_flat.start_near()
    flats[0].middle()
    out_row.along(2, row_ref)

    def block_step(i, carry):
        r = pl.ds(pl.multiple_of(i * 16, 16), 16)
        block_ref[r, :] = (tok_ref[0, r, :].astype(f32) + row_ref[r, :]).astype(bf16)
        return carry

    lax.fori_loop(0, length // 16, block_step, 0)
    outs[0].start()
    dxn_row.along(1)
    give(0)
    small_flat.middle()
    dxn_row.along(2)
    gwout_flat.finish(gwout_ref)
    outs[3].start()
    dxn_row.along(3, row_ref)
    dxn_row.release()
    def norm_step(i, carry):
        r = pl.ds(pl.multiple_of(i * 16, 16), 16)
        x = tok_ref[0, r, :].astype(f32)
        scale = lax.rsqrt(jnp.sum(x * x, axis=1, keepdims=True) * (1.0 / model) + EPS)
        dxn = row_ref[r, :]
        inner = dxn * gains_ref[...]
        dot = jnp.sum(inner * x, axis=1, keepdims=True) * (1.0 / model)
        dxx = scale * inner - x * (scale * scale * scale * dot)
        gtok_ref[r, :] = (up_ref[0, r, :].astype(f32) + dxx).astype(bf16)
        return carry

    lax.fori_loop(0, length // 16, norm_step, 0)
    outs[1].start()
    small_flat.finish(small_ref)
    outs[4].start()

    def settle(k, rank, source):
        for g in range(4):
            at = k * width * 8 + g * 1024
            gwin_ref[:, pl.ds(pl.multiple_of(at + rank * 128, 128), 128)] = source[:, g * 128:(g + 1) * 128]

    for k in (1, 0):
        settle(k, j, rows_of(k, j))
        for i, s in enumerate(steps):
            src = mate(s, -1)
            landed(slots_ref.at[k, i], ar.at[7 * k + i], src)
            settle(k, rank_of(src), slots_ref.at[k, i])
    outs[2].start()
    value = sum_ref[...]
    for i, to in enumerate(planes):
        landed(far_ref.at[i], fr.at[i], to)
        value = join(value, far_ref[i])
    tiny_ref[...] = value
    outs[5].start()
    for i, to in enumerate(planes):
        sent(sum_ref, fs.at[i], to)
    for i, s in enumerate(steps):
        sent(near_ref.at[i], ns.at[i], mate(s))
    for copy in pending:
        copy.wait_send()
    for flat in (*flats, gwout_flat, small_flat):
        flat.close()
    for copy in outs:
        copy.wait()


def k3(part, stat, smalls, vecs, gains, gwdt, masks, tokens, upstream, acc, mt, dg, dv, slope, u, vt, xnt, win, ups):
    like = jax.ShapeDtypeStruct
    length, model = tokens.shape[1:]
    channels, count = mt.shape
    tiles = channels // 128
    here = pl.BlockSpec(memory_space=pltpu.VMEM)
    far = pl.BlockSpec(memory_space=pl.ANY)
    dma = lambda n: pltpu.SemaphoreType.DMA((n,))
    own_d = model // 32
    packed = part.shape[0]
    return pl.pallas_call(
        k3_kernel,
        out_shape=(
            like((length, model), bf16),
            like((length, model), bf16),
            like((own_d, 16 * channels), bf16),
            like((128, model), f32),
            like((160, 384), f32),
            like((8, 128), f32),
        ),
        in_specs=[here] * 9 + [far] * 10,
        out_specs=(pl.BlockSpec(memory_space=pltpu.HBM),) * 6,
        scratch_shapes=[
            pltpu.VMEM((length, model), bf16),
            pltpu.VMEM((length, model), bf16),
            pltpu.VMEM((own_d, 16 * channels), bf16),
            pltpu.VMEM((128, model), f32),
            pltpu.VMEM((160, 384), f32),
            pltpu.VMEM((8, 128), f32),
            dma(6),
            pltpu.VMEM((2, 4, length, model), bf16),
            pltpu.VMEM((4, 512, 2 * channels), bf16),
            pltpu.VMEM((4, 512, channels), bf16),
            pltpu.VMEM((4, 512, channels), bf16),
            pltpu.VMEM((4, 128, model), bf16),
            pltpu.VMEM((4, 160, 384), f32),
            pltpu.VMEM((channels, count), bf16),
            pltpu.VMEM((count, 2 * channels), bf16),
            pltpu.VMEM((tiles, count + 32, 128), f32),
            pltpu.VMEM((tiles, count, 128), f32),
            pltpu.VMEM(u.shape, f32),
            pltpu.VMEM((model, count), bf16),
            pltpu.VMEM((count, 256), bf16),
            pltpu.VMEM((2, 7, own_d, channels), bf16),
            pltpu.VMEM((length, model), f32),
            pltpu.VMEM((7, 8, 128), f32),
            pltpu.VMEM((8, 128), f32),
            pltpu.VMEM((8, 128), f32),
            pltpu.VMEM((3, 8, 128), f32),
            dma(10), dma(14), dma(14), dma(7), dma(7), dma(3), dma(3),
            pltpu.VMEM((packed, 128), f32),
        ] + [pltpu.VMEM((packed // 2, 128), f32)] * 6 + [dma(PIECES) for _ in range(8)]
        + row_scratch(length, model) * 2
        + flat_scratch(512, channels, bf16) * 2 + flat_scratch(128, model, bf16) + flat_scratch(160, 384, f32),
        compiler_params=pltpu.CompilerParams(collective_id=1, has_side_effects=True, vmem_limit_bytes=63400000),
    )(part, stat, smalls, vecs, gains, gwdt, masks, tokens, upstream, acc, mt, dg, dv, slope, u, vt, xnt, win, ups)


def k4_kernel(slots, block_in, gtok_in, gwin_in, gwout_in, small_in, tiny_in, win_ref, gain_ref,
              block_ref, gtok_ref, gain_out, gwin_ref, convw_ref, convb_ref, gwx_ref, gwdt_ref, dtb_ref, skip_ref, gwout_ref, mean_ref, peak_ref):
    block_ref[0] = block_in[...]
    gtok_ref[0] = gtok_in[...]
    gwout_ref[...] = gwout_in[...]
    depth, total = gwin_in.shape
    dot = jnp.zeros((depth, 128), f32)
    for at in range(0, total, 128):
        value = gwin_in[:, at:at + 128].astype(f32)
        gwin_ref[:, at:at + 128] = value
        dot = dot + value * win_ref[:, at:at + 128].astype(f32)
    column = jnp.broadcast_to(jnp.sum(dot, axis=1, keepdims=True), (depth, 128))
    gain_out[...] = column.T[0:1, :] / gain_ref[...].astype(f32)
    gwx_ref[...] = small_in[0:128, 0:256].T[0:gwx_ref.shape[0], :]
    gwdt_ref[...] = small_in[0:128, 256:384]
    convw_ref[...] = small_in[128:132, 0:128]
    convb_ref[...] = small_in[132:133, 0:128]
    dtb_ref[...] = small_in[133:134, 0:128]
    skip_ref[...] = small_in[134:135, 0:128]
    mean_ref[...] = tiny_in[0:1, 0:1] * (1.0 / slots)
    peak_ref[...] = tiny_in[0:1, 1:2]


def k4(slots, block, gtok, gwin, gwout, small, tiny, w_in, gain, columns):
    like = jax.ShapeDtypeStruct
    here = pl.BlockSpec(memory_space=pltpu.VMEM)
    row = like((1, 128), f32)
    return pl.pallas_call(
        functools.partial(k4_kernel, slots),
        out_shape=(
            like((1,) + block.shape, bf16), like((1,) + gtok.shape, bf16), like(gain.shape, f32), like(gwin.shape, f32),
            like((4, 128), f32), row, like((columns, 128), f32), like((128, 128), f32), row, row, like(gwout.shape, f32),
            like((1, 1), f32), like((1, 1), f32),
        ),
        in_specs=[here] * 8,
        out_specs=(here,) * 13,
        compiler_params=pltpu.CompilerParams(vmem_limit_bytes=63400000),
    )(block, gtok, gwin, gwout, small, tiny, w_in, gain)

def masks(lengths, count):
    ends = jnp.cumsum(lengths, axis=1)
    places = jnp.arange(count, dtype=jnp.int32)
    segment = jnp.sum((places[:, None, None] >= ends[None, :, :]).astype(jnp.int32), axis=2)
    same = []
    for offset in range(1, 4):
        before = jnp.pad(segment, ((offset, 0), (0, 0)), constant_values=-1)[:count]
        same.append((before == segment).astype(f32))
    return same, (segment < DOCS).astype(f32)


def columns(weights, ways):
    rows, total = weights.shape
    return weights.reshape(rows, 2, total // (2 * ways * 128), ways, 128)


def on_device(tokens, lengths, gain, w_in, conv_w, conv_b, w_x, w_dt, dt_bias, skip, w_out, grad_out):
    ways = lax.axis_size("core") * lax.axis_size("z")
    groups = lax.axis_size("dp")
    length, model = tokens.shape[1:]
    own_d = w_in.shape[0]
    own_e = conv_w.shape[0]
    inner = w_in.shape[1] // 2
    channels = inner // ways
    rank = w_dt.shape[1]
    states = (w_x.shape[1] - rank) // 2
    cols = w_in.reshape(own_d, 2, groups, ways, own_e).transpose(3, 0, 1, 2, 4).reshape(ways, own_d, 2 * channels)
    cols = lax.all_to_all(cols, TP, split_axis=0, concat_axis=0, tiled=True)
    win = lax.all_gather(cols, "dp", axis=0, tiled=True).reshape(model, 2 * channels)
    small = jnp.concatenate([w_x, w_dt, conv_w, conv_b[:, None], dt_bias[:, None], skip[:, None]], axis=1)
    small_width = small.shape[1]
    small = lax.all_gather(small, "dp", axis=0, tiled=True)
    wx = small[:, :rank + 2 * states]
    wdt = small[:, rank + 2 * states:2 * rank + 2 * states]
    rest = small[:, 2 * rank + 2 * states:].astype(f32)
    taps, bias, dtb, skips = rest[:, :4], rest[:, 4], rest[:, 5], rest[:, 6]
    wout = lax.all_gather(w_out, "dp", axis=0, tiled=True)
    gains = lax.all_gather(gain, ALL, axis=0, tiled=True).astype(f32)
    x = tokens[0].astype(f32)
    scale = lax.rsqrt(jnp.mean(x * x, axis=1, keepdims=True) + EPS)
    xn = (x * scale * gains).astype(bf16)
    xns = lax.all_gather(xn, TP, axis=0, tiled=True)
    ups = lax.all_gather(grad_out[0], TP, axis=0, tiled=True)
    lens = lax.all_gather(lengths, TP, axis=0, tiled=True)
    rows = lens.shape[0]
    tall = rows * length

    def time_major(a):
        return a.reshape(rows, length, -1).transpose(1, 0, 2).reshape(tall, -1)

    def row_major(a):
        return a.reshape(length, rows, -1).transpose(1, 0, 2).reshape(tall, -1)

    same, live = masks(lens, length)
    zz = time_major(jnp.dot(xns, win, preferred_element_type=f32))
    u = zz[:, :channels].reshape(length, rows, channels)
    g = zz[:, channels:]
    c = bias + taps[:, 3] * u
    shifted = []
    for offset in range(1, 4):
        earlier = jnp.pad(u, ((offset, 0), (0, 0), (0, 0)))[:length] * same[offset - 1][:, :, None]
        shifted.append(earlier)
        c = c + taps[:, 3 - offset] * earlier
    sig = jax.nn.sigmoid(c)
    v16 = (c * sig).astype(bf16).reshape(tall, channels)
    v = v16.astype(f32)
    p = lax.psum(jnp.dot(v16, wx, preferred_element_type=f32), TP)
    dl = p[:, :rank].astype(bf16)
    kq = p[:, rank:]
    dims_cols = (((1,), (1,)), ((), ()))
    dims_rows = (((0,), (0,)), ((), ()))
    pre = lax.dot_general(dl, wdt, dims_cols, preferred_element_type=f32) + dtb
    dm = time_major(lax.dot_general(ups, wout, dims_cols, preferred_element_type=f32))
    flags = jnp.pad(jnp.stack([same[0].reshape(tall), live.reshape(tall)], axis=1), ((0, 0), (0, 126)))
    hi = kq.astype(bf16)
    mid = (kq - hi.astype(f32)).astype(bf16)
    low = (kq - hi.astype(f32) - mid.astype(f32)).astype(bf16)
    kq3 = jnp.concatenate([hi, mid, low], axis=1)
    keys = kq[:, :states]
    sk = jnp.broadcast_to(jnp.sum(keys * keys, axis=1, keepdims=True), (tall, 8))
    m, dg, dpre, dv, dkq, stats = mixer(flags, kq3, sk, pre, v, g, dm, skips[None], states=states, width=256, unroll=4)
    stats = stats.transpose(1, 2, 0, 3).reshape(3, 8, channels)
    dskip = jnp.sum(stats[0], axis=0)
    total = lax.psum(jnp.sum(stats[1]), ALL)
    peak = lax.pmax(jnp.max(stats[2]), ALL)
    beta_mean = total / float(groups * ways * length * inner)
    m16 = row_major(m).astype(bf16)
    out = jnp.dot(m16, wout, preferred_element_type=f32).astype(bf16)
    out = lax.psum_scatter(out, TP, scatter_dimension=0, tiled=True)
    block_out = (x + out.astype(f32)).astype(bf16)
    grad_wout = lax.dot_general(m16, ups, dims_rows, preferred_element_type=f32).astype(bf16)
    grad_wout = lax.psum_scatter(grad_wout, "dp", scatter_dimension=0, tiled=True)
    dpre16 = dpre.astype(bf16)
    grad_dtb = jnp.sum(dpre16.astype(f32), axis=0)
    grad_wdt = lax.dot_general(dpre16, dl, dims_rows, preferred_element_type=f32)
    ddl = jnp.dot(dpre16, wdt, preferred_element_type=f32)
    dkq = dkq[:, :2 * states] + dkq[:, 2 * states:2 * states + 1] * jnp.pad(keys, ((0, 0), (0, states)))
    dp16 = lax.psum(jnp.concatenate([ddl, dkq], axis=1), TP).astype(bf16)
    grad_wx = lax.dot_general(v16, dp16, dims_rows, preferred_element_type=f32)
    dvt = dv + lax.dot_general(dp16, wx, dims_cols, preferred_element_type=f32)
    dc = (dvt * (sig.reshape(tall, channels) * (1.0 + c.reshape(tall, channels) * (1.0 - sig.reshape(tall, channels))))).reshape(length, rows, channels)
    du = taps[:, 3] * dc
    grad_taps = [jnp.sum(dc * u, axis=(0, 1))]
    for offset in range(1, 4):
        grad_taps.append(jnp.sum(dc * shifted[offset - 1], axis=(0, 1)))
        du = du + taps[:, 3 - offset] * jnp.pad((dc * same[offset - 1][:, :, None])[offset:], ((0, offset), (0, 0), (0, 0)))
    grad_conv = jnp.stack(grad_taps[::-1] + [jnp.sum(dc, axis=(0, 1)), grad_dtb, dskip], axis=1)
    dz = row_major(jnp.concatenate([du.reshape(tall, channels), dg], axis=1)).astype(bf16)
    gwin = lax.dot_general(xns, dz, dims_rows, preferred_element_type=f32).astype(bf16)
    gwin = lax.psum_scatter(gwin, "dp", scatter_dimension=0, tiled=True)
    gwin = lax.all_to_all(gwin.reshape(ways, own_d, 2 * channels), TP, split_axis=0, concat_axis=0, tiled=True)
    grad_win = gwin.reshape(ways, own_d, 2, groups, own_e).transpose(1, 2, 3, 0, 4).reshape(own_d, 2 * inner).astype(f32)
    dxn = lax.dot_general(dz, win, dims_cols, preferred_element_type=f32).astype(bf16)
    dxn = lax.psum_scatter(dxn, TP, scatter_dimension=0, tiled=True).astype(f32)
    small_grad = lax.psum_scatter(jnp.concatenate([grad_wx, grad_wdt, grad_conv], axis=1), "dp", scatter_dimension=0, tiled=True)
    inner_grad = dxn * gains
    dxx = scale * inner_grad - x * (scale * scale * scale) * (jnp.sum(inner_grad * x, axis=1, keepdims=True) / model)
    grad_tokens = (grad_out[0].astype(f32) + dxx).astype(bf16)
    grad_gain = lax.psum_scatter(jnp.sum(dxn * x * scale, axis=0), ALL, scatter_dimension=0, tiled=True)
    at = rank + 2 * states
    return (
        block_out[None],
        grad_tokens[None],
        grad_gain,
        grad_win,
        small_grad[:, at + rank:at + rank + 4],
        small_grad[:, at + rank + 4],
        small_grad[:, :at],
        small_grad[:, at:at + rank],
        small_grad[:, at + rank + 5],
        small_grad[:, at + rank + 6],
        grad_wout.astype(f32),
        beta_mean,
        peak,
    )


def on_device_direct(tokens, lengths, gain, w_in, conv_w, conv_b, w_x, w_dt, dt_bias, skip, w_out, grad_out):
    groups, ways = 4, 8
    length, model = tokens.shape[1:]
    own_d = w_in.shape[0]
    own_e = conv_w.shape[0]
    inner = w_in.shape[1] // 2
    channels = inner // ways
    rank = w_dt.shape[1]
    states = (w_x.shape[1] - rank) // 2
    gain = gain[None]
    xnt, ups, win, wout, smalls, vecs, gains, masks, live, u, g, v, vt, slope, dl, kq = k1(
        tokens, grad_out, w_in, w_out, w_x.T, w_dt, gain, lengths, conv_w.T, conv_b[None], dt_bias[None], skip[None])
    acc, mt, dg, gwdt, ups, dv, part, stat = k2(dl, kq, smalls, vecs, masks, live, v, g, ups, wout, states)
    sums = k3(
        part, stat, smalls, vecs, gains, gwdt, masks, tokens, grad_out, acc, mt, dg, dv, slope, u, vt, xnt,
        win.reshape(groups, ways * own_d, 2 * channels), ups)
    block_out, grad_tokens, grad_gain, grad_win, convw, convb, gwx, gwdt, dtb, dskip, grad_wout, mean, peak = k4(
        float(groups * ways * length * inner), *sums, w_in, gain, rank + 2 * states)
    return (
        block_out, grad_tokens, grad_gain[0], grad_win, convw.T, convb[0], gwx.T, gwdt, dtb[0], dskip[0], grad_wout, mean[0, 0], peak[0, 0],
    )


def on_device_any(*args):
    if lax.axis_size("dp") == 4 and lax.axis_size("z") == 4:
        return on_device_direct(*args)
    return on_device(*args)


def solution(mesh):
    wide, narrow = mesh.devices.shape
    fine = Mesh(mesh.devices.reshape(wide // 2, 2, narrow), ALL)
    cut = (P(ALL, None), P(ALL))
    in_specs = (P(ALL, None, None), cut[0], cut[1], cut[0], cut[0], cut[1], cut[0], cut[0], cut[1], cut[1], cut[0], P(ALL, None, None))
    out_specs = (P(ALL, None, None), P(ALL, None, None), cut[1], cut[0], cut[0], cut[1], cut[0], cut[0], cut[1], cut[1], cut[0], P(), P())
    return jax.shard_map(on_device_any, mesh=fine, in_specs=in_specs, out_specs=out_specs, check_vma=False)
```

```python
import functools
import jax, jax.numpy as jnp
from jax import lax
from jax.experimental import pallas as pl
from jax.experimental.pallas import tpu as pltpu
from jax.sharding import Mesh, PartitionSpec as P

DOCS = 4
EPS = 1e-05
ALL = ("dp", "core", "z")
TP = ("core", "z")

f32 = jnp.float32
bf16 = jnp.bfloat16

def fold(x):
    total = x[:, :128]
    for at in range(128, x.shape[1], 128):
        total = total + x[:, at:at+128]
    return total

def mixer_kernel(states, unroll, chunk, flags_ref, kq3_ref, sk_ref, pre_ref, v_ref, g_ref, dm_ref, skip_ref,
                 m_ref, dg_ref, dpre_ref, dv_ref, dkq_ref, stat_ref, s_ref, h_ref, rate_ref, rv_ref, kb_ref, drr_ref):
    rows = pre_ref.shape[0]
    width = pre_ref.shape[1]
    steps = rows // 8
    wide = states * 128
    spread_rows = kq3_ref.shape[1]
    def spread(i, c):
        r = pl.ds(pl.multiple_of(i * chunk, chunk), chunk)
        left = kq3_ref[r, :]
        for part in range(0, 2 * wide, 512):
            ids = lax.broadcasted_iota(jnp.int32, (spread_rows, 512), 0) % (2 * states)
            col = lax.broadcasted_iota(jnp.int32, (spread_rows, 512), 1) // 128 + part // 128
            hot = jnp.where(ids == col, 1.0, 0.0).astype(bf16)
            kb_ref[r, part:part+512] = jnp.dot(left, hot, preferred_element_type=f32)
        return c
    lax.fori_loop(0, rows // chunk, spread, 0)

    def before(i, c):
        r = pl.ds(pl.multiple_of(i * 64, 64), 64)
        live = flags_ref[r, 1:2]
        beta = jax.nn.sigmoid(pre_ref[r, :])
        part = 1.0 / (1.0 + beta * sk_ref[r, 0:1])
        rate = beta * part
        rate_ref[r, :] = rate
        v = v_ref[r, :]
        rv_ref[r, :] = rate * v
        dpre_ref[r, :] = part * part * beta * (1.0 - beta)
        g = g_ref[r, :]
        sg = jax.nn.sigmoid(g)
        dm = dm_ref[r, :] * live
        dv_ref[r, :] = dm * (g * sg)
        dg_ref[r, :] = dm * (sg * (1.0 + g * (1.0 - sg)))
        return c
    lax.fori_loop(0, rows // 64, before, 0)

    s_ref[0, 0] = jnp.zeros(s_ref.shape[2:], f32)

    group = unroll
    tile = lambda x: jnp.concatenate([x] * (width // 128), axis=1)
    span = group * 8
    at = [slice(j * 8, j * 8 + 8) for j in range(group)]
    def view(ref, i):
        return ref.at[pl.ds(pl.multiple_of(i * span, span), span)]

    def forward(i, carry):
        flags, rates, rvs, vs, kbs, ms = [view(x, i) for x in (flags_ref, rate_ref, rv_ref, v_ref, kb_ref, m_ref)]
        keep = [jnp.broadcast_to(flags[r, 0:1], (8, 128)) for r in at]
        rate = [rates[r, :] for r in at]
        rv = [rvs[r, :] for r in at]
        y = [skip_ref[...] * vs[r, :] for r in at]
        for n in range(states):
            state = s_ref[i, 0, n]
            for j, r in enumerate(at):
                kb = kbs[r, n*128:(n+1)*128]
                qb = kbs[r, wide+n*128:wide+(n+1)*128]
                state = (tile(keep[j]) - rate[j] * tile(kb * kb * keep[j])) * state + rv[j] * tile(kb)
                if j < group - 1:
                    s_ref[i, j + 1, n] = state
                else:
                    s_ref[i + 1, 0, n] = state
                y[j] = y[j] + state * tile(qb)
        for j, r in enumerate(at):
            ms[r, :] = y[j]
        return carry

    lax.fori_loop(0, steps // group, forward, 0)
    h_ref[...] = jnp.zeros_like(h_ref)

    def backward(step, carry):
        i = steps // group - 1 - step
        flags, rates, rvs, vs, kbs, dvs, dpres, drrs = [view(x, i) for x in (flags_ref, rate_ref, rv_ref, v_ref, kb_ref, dv_ref, dpre_ref, drr_ref)]
        keep = [jnp.broadcast_to(flags[r, 0:1], (8, 128)) for r in at]
        rate = [rates[r, :] for r in at]
        rv = [rvs[r, :] for r in at]
        dy = [dvs[r, :] for r in at]
        hk = [jnp.zeros((8, width), f32) for r in at]
        hs2 = [jnp.zeros((8, width), f32) for r in at]
        for n in range(states):
            ah = h_ref[n]
            after_ = s_ref[i + 1, 0, n]
            for j in range(group - 1, -1, -1):
                r = at[j]
                kb = kbs[r, n*128:(n+1)*128]
                qb = kbs[r, wide+n*128:wide+(n+1)*128]
                kk = kb * keep[j]
                held = tile(kb * kk)
                h = dy[j] * tile(qb) + ah
                prior = s_ref[i, j, n]
                hs = h * prior
                hk[j] = hk[j] + h * tile(kb)
                hs2[j] = hs2[j] + hs * held
                kbs[r, n*128:(n+1)*128] = fold(h * rv[j]) - 2.0 * kk * fold(hs * rate[j])
                kbs[r, wide+n*128:wide+(n+1)*128] = fold(dy[j] * after_)
                after_ = prior
                ah = (tile(keep[j]) - rate[j] * held) * h
            h_ref[n] = ah
        for j, r in enumerate(at):
            v = vs[r, :]
            drate = v * hk[j] - hs2[j]
            drrs[r, :] = fold(drate * rate[j] * rate[j]) * (-2.0)
            dpres[r, :] = drate * dpres[r, :]
            dvs[r, :] = rate[j] * hk[j] + skip_ref[...] * dy[j]
            stat_ref[0, 0] += dy[j] * v
        return carry

    stat_ref[...] = jnp.zeros_like(stat_ref)
    lax.fori_loop(0, steps // group, backward, 0)

    first = pl.program_id(0) == 0
    def gather(i, c):
        r = pl.ds(pl.multiple_of(i * chunk, chunk), chunk)
        total = jnp.zeros((chunk, 128), f32)
        for part in range(0, 2 * wide, 512):
            row = lax.broadcasted_iota(jnp.int32, (512, 128), 0) // 128 + part // 128
            col = lax.broadcasted_iota(jnp.int32, (512, 128), 1)
            hot = jnp.where(row == col, 1.0, 0.0).astype(bf16)
            total += jnp.dot(kb_ref[r, part:part+512].astype(bf16), hot, preferred_element_type=f32)
        col = lax.broadcasted_iota(jnp.int32, (128, 128), 1)
        hot = jnp.where(col == 2 * states, 1.0, 0.0).astype(bf16)
        total += jnp.dot(drr_ref[r, :].astype(bf16), hot, preferred_element_type=f32)
        dkq_ref[r, :] = jnp.where(first, total, dkq_ref[r, :] + total)
        return c
    lax.fori_loop(0, rows // chunk, gather, 0)

    def after(i, c):
        r = pl.ds(pl.multiple_of(i * 64, 64), 64)
        live = flags_ref[r, 1:2]
        y = m_ref[r, :]
        g = g_ref[r, :]
        m_ref[r, :] = y * (g * jax.nn.sigmoid(g)) * live
        dg_ref[r, :] = y * dg_ref[r, :]
        shown = (jax.nn.sigmoid(pre_ref[r, :]) * live).reshape(8, 8, width)
        stat_ref[0, 1] += jnp.sum(shown, axis=0)
        stat_ref[0, 2] = jnp.maximum(stat_ref[0, 2], jnp.max(shown, axis=0))
        return c
    lax.fori_loop(0, rows // 64, after, 0)

def mixer(flags, kq3, sk, pre, v, g, dm, skip, states=16, width=256, unroll=1):
    rows, total = pre.shape
    steps = rows // 8
    tiles = total // width
    big = jax.ShapeDtypeStruct((rows, total), f32)
    cut = pl.BlockSpec((rows, width), lambda h: (0, h))
    whole = lambda a: pl.BlockSpec(a.shape, lambda h: (0,) * a.ndim)
    return pl.pallas_call(
        functools.partial(mixer_kernel, states, unroll, min(256, rows)),
        grid=(tiles,),
        out_shape=(big, big, big, big, jax.ShapeDtypeStruct((rows, 128), f32), jax.ShapeDtypeStruct((tiles, 3, 8, width), f32)),
        in_specs=[whole(flags), whole(kq3), whole(sk), cut, cut, cut, cut, pl.BlockSpec((1, width), lambda h: (0, h))],
        out_specs=(cut, cut, cut, cut, pl.BlockSpec((rows, 128), lambda h: (0, 0)), pl.BlockSpec((1, 3, 8, width), lambda h: (h, 0, 0, 0))),
        scratch_shapes=[pltpu.VMEM((steps//unroll+1, unroll, states, 8, width), f32), pltpu.VMEM((states, 8, width), f32)] + [pltpu.VMEM((rows, width), f32)]*2
          + [pltpu.VMEM((rows, 2*states*128), f32), pltpu.VMEM((rows, 128), f32)],
        compiler_params=pltpu.CompilerParams(vmem_limit_bytes=60*1024*1024),
    )(flags, kq3, sk, pre, v, g, dm, skip)


MESH = pl.DeviceIdType.MESH


def flip(value, bit):
    return value + bit * (1 - 2 * ((value // bit) % 2))


def place():
    d, c, z = lax.axis_index("dp"), lax.axis_index("core"), lax.axis_index("z")
    return d, c, z


def put(src, dst, send, recv, device):
    copy = pltpu.make_async_remote_copy(src_ref=src, dst_ref=dst, send_sem=send, recv_sem=recv, device_id=device, device_id_type=MESH)
    copy.start()
    return copy


def landed(slot, sem, device):
    pltpu.make_async_remote_copy(src_ref=slot, dst_ref=slot, send_sem=sem, recv_sem=sem, device_id=device, device_id_type=MESH).wait_recv()


def sent(slot, sem, device):
    pltpu.make_async_remote_copy(src_ref=slot, dst_ref=slot, send_sem=sem, recv_sem=sem, device_id=device, device_id_type=MESH).wait_send()


def greet(devices):
    barrier = pltpu.get_barrier_semaphore()
    for device in devices:
        pl.semaphore_signal(barrier, inc=1, device_id=device, device_id_type=MESH)
    pl.semaphore_wait(barrier, len(devices))


def mates():
    return [(a, k) for k in (0, 1, 3, 2) for a in (1, 0) if (a, k) != (0, 0)]


def mate(step, sign=1):
    d, c, z = place()
    a, k = step
    return d, (flip(c, 1) if a else c), lax.rem(z + sign * k + 4, 4)


def rank_of(device):
    return device[1] * 4 + device[2]


PIECES = 4


UP_HOPS = 2
LINE1 = bf16
LINE2 = bf16


def k1_kernel(tok_ref, up_ref, w_ref, wout_ref, wx_ref, wdt_ref, gain_ref, lens_ref, convw_ref, convb_ref, dtb_ref, skip_ref,
              xnt_out, ups_ref, win_out, wouts_ref, smalls_ref, vecs_ref, gains_ref, masks_out, live_out,
              u_out, g_out, v_out, vt_out, slope_out, dl_ref, kq_ref,
              masks_ref, live_ref, u_ref, g_ref, v_ref, vt_ref, slope_ref, save_sem, cols_ref, meta_ref, small_ref,
              xs_ref, xn_ref, xnt_ref, win_ref, metas_ref, part_ref, out_ref, sib_ref, base_ref, left_ref, right_ref, tor_ref, tol_ref,
              own_sem, ms, mr, qs, qr, xls, xlr, xrs, xrr, xcs, xcr, as_, ar, ps, pr, rs, rr, ws, wr, ts, tr, tls, tlr, trs, trr, tos, tor):
    d, c, z = place()
    j = c * 4 + z
    dx, dy, dd = flip(d, 1), flip(d, 2), flip(flip(d, 1), 2)
    xn, yn, dn = (dx, c, z), (dy, c, z), (dd, c, z)
    sib = (d, flip(c, 1), z)
    left = (d, c, lax.rem(z + 3, 4))
    right = (d, c, lax.rem(z + 1, 4))
    steps = mates()
    length = tok_ref.shape[1]
    model = tok_ref.shape[2]
    depth = cols_ref.shape[1]
    for rank in range(8):
        for n in range(8):
            cols_ref[rank, :, n * 128:(n + 1) * 128] = w_ref[:, (n * 8 + rank) * 128:(n * 8 + rank + 1) * 128]
    meta_ref[...] = jnp.zeros_like(meta_ref)
    meta_ref[0:1, 0:depth] = gain_ref[...].astype(f32)
    meta_ref[0:1, depth:2 * depth] = gain_ref[...].astype(f32)
    meta_ref[1:2, 0:5] = lens_ref[...].astype(f32)
    meta_ref[8:12, :] = convw_ref[...].astype(f32)
    meta_ref[12:13, :] = convb_ref[...].astype(f32)
    meta_ref[13:14, :] = dtb_ref[...].astype(f32)
    meta_ref[14:15, :] = skip_ref[...].astype(f32)
    narrow_rows = wx_ref.shape[0]
    small_ref[:, 0:128] = wx_ref[0:128, :].astype(f32).T.astype(bf16)
    tail = jnp.concatenate([wx_ref[128:narrow_rows, :].astype(f32), jnp.zeros((256 - narrow_rows, 128), f32)], axis=0)
    small_ref[:, 128:256] = tail.T.astype(bf16)
    small_ref[:, 256:384] = wdt_ref[...]
    greet([mate(s) for s in steps] + [xn, yn, dn])
    tiles = u_ref.shape[0]
    width = tiles * 128
    count = g_ref.shape[1]

    def rows(rank):
        return pl.ds(pl.multiple_of(rank * length, length), length)

    def block(group, rank):
        return pl.ds(pl.multiple_of((group * 8 + rank) * depth, depth), depth)

    own_e = wout_ref.shape[0]

    def part_e(group, start=0, size=own_e):
        return pl.ds(pl.multiple_of(group * own_e + start, 16), size)

    own = [
        pltpu.make_async_copy(tok_ref.at[0], xs_ref.at[rows(j)], own_sem.at[0]),
        pltpu.make_async_copy(up_ref.at[0], ups_ref.at[rows(j)], own_sem.at[1]),
        pltpu.make_async_copy(cols_ref.at[j], win_ref.at[block(d, j)], own_sem.at[2]),
        pltpu.make_async_copy(wout_ref, wouts_ref.at[part_e(d)], own_sem.at[3]),
        pltpu.make_async_copy(small_ref, smalls_ref.at[part_e(d)], own_sem.at[4]),
        pltpu.make_async_copy(meta_ref, metas_ref.at[d, j], own_sem.at[5]),
    ]
    for copy in own:
        copy.start()
    pending = []
    for i, s in enumerate(steps):
        to = mate(s)
        pending.append(put(meta_ref, metas_ref.at[d, j], ms.at[i], mr.at[i], to))
    for i, s in enumerate(steps):
        to = mate(s)
        pending.append(put(cols_ref.at[rank_of(to)], win_ref.at[block(d, j)], as_.at[i], ar.at[i], to))
    for i, to in enumerate((xn, yn, dn)):
        pending.append(put(small_ref, smalls_ref.at[part_e(d)], ps.at[16 + i], pr.at[16 + i], to))
    halves = own_e // 2
    pending.append(put(wout_ref, wouts_ref.at[part_e(d)], ws.at[0], wr.at[0], xn))
    pending.append(put(wout_ref, wouts_ref.at[part_e(d)], ws.at[1], wr.at[1], yn))
    own[2].wait()
    slot = win_ref.at[block(d, j)]
    pending.append(put(slot, slot, ps.at[7], pr.at[7], xn))
    pending.append(put(slot, slot, ps.at[15], pr.at[15], yn))

    def row_start(ref, out, base):
        pending.append(put(ref.at[0], out.at[rows(j)], xcs.at[base + z], xcr.at[base + z], sib))

        @pl.when(z < 3)
        def _():
            put(ref.at[0], out.at[rows(j)], xls.at[base], xlr.at[base], right)

        @pl.when(z > 0)
        def _():
            put(ref.at[0], out.at[rows(j)], xrs.at[base], xrr.at[base], left)

    def row_hop(out, base, i, then=None, hops=3):
        if i >= hops:
            return

        @pl.when(z > i)
        def _():
            at = z - 1 - i
            slot = out.at[rows(c * 4 + at)]
            landed(slot, xlr.at[base + i], left)
            if i < hops - 1:
                @pl.when(z < 3)
                def _():
                    put(slot, slot, xls.at[base + i + 1], xlr.at[base + i + 1], right)
            put(slot, slot, xcs.at[base + at], xcr.at[base + at], sib)
            if then is not None:
                then(c * 4 + at)

        @pl.when(z < 3 - i)
        def _():
            at = z + 1 + i
            slot = out.at[rows(c * 4 + at)]
            landed(slot, xrr.at[base + i], right)
            if i < hops - 1:
                @pl.when(z > 0)
                def _():
                    put(slot, slot, xrs.at[base + i + 1], xrr.at[base + i + 1], left)
            put(slot, slot, xcs.at[base + at], xcr.at[base + at], sib)
            if then is not None:
                then(c * 4 + at)

    def row_end(out, base, hops=3):
        for i in range(hops):
            @pl.when((z < 3) & (z >= i))
            def _():
                sent(out.at[rows(j)], xls.at[base + i], right)

            @pl.when((z > 0) & (z <= 3 - i))
            def _():
                sent(out.at[rows(j)], xrs.at[base + i], left)
        for at in range(4):
            @pl.when((z != at) & (z <= at + hops) & (at <= z + hops))
            def _():
                sent(out.at[rows(j)], xcs.at[base + at], sib)

    own[5].wait()
    for i, s in enumerate(steps):
        landed(metas_ref.at[d, rank_of(mate(s, -1))], mr.at[i], xn)
    for i, to in enumerate((xn, yn, dn)):
        pending.append(put(metas_ref.at[d], metas_ref.at[d], qs.at[i], qr.at[i], to))
    slots = {7: j}
    for i, s in enumerate(steps):
        slots[i] = rank_of(mate(s, -1))
    order = [7] + list(range(7))

    def pass_on(i):
        src = mate(steps[i], -1)
        slot = win_ref.at[block(d, slots[i])]
        landed(slot, ar.at[i], src)
        pending.append(put(slot, slot, ps.at[i], pr.at[i], xn))
        pending.append(put(slot, slot, ps.at[8 + i], pr.at[8 + i], yn))

    def relay(k):
        i = order[k]
        slot = win_ref.at[block(dx, slots[i])]
        landed(slot, pr.at[i], xn)
        if k % 2 == 0:
            pending.append(put(slot, slot, rs.at[k // 2], rr.at[k // 2], yn))
        slot = win_ref.at[block(dy, slots[i])]
        landed(slot, pr.at[8 + i], yn)
        if k % 2 == 1:
            pending.append(put(slot, slot, rs.at[4 + k // 2], rr.at[4 + k // 2], xn))

    pass_on(0)
    for i, (to, at) in enumerate(((xn, dx), (yn, dy), (dn, dd))):
        landed(metas_ref.at[at], qr.at[i], to)
    lens = jnp.concatenate([metas_ref[d, r, 1:2, :] for r in range(8)], axis=0)
    ends = []
    last = jnp.zeros((8, 1), f32)
    for i in range(5):
        last = last + lens[:, i:i + 1]
        ends.append(jnp.broadcast_to(last, (8, 128)))

    def mask_step(t, carry):
        here = t.astype(f32)

        def segment(at):
            total = jnp.zeros((8, 128), f32)
            for end in ends:
                total = total + jnp.where(end <= at, 1.0, 0.0)
            return total

        now = segment(here)
        r = pl.ds(pl.multiple_of(t * 8, 8), 8)
        for o in range(1, 4):
            same = jnp.where(segment(here - o) == now, 1.0, 0.0)
            masks_ref[o - 1, r, :] = jnp.where(here >= o, same, 0.0)
        live_ref[0, r, :] = jnp.where(now < DOCS, 1.0, 0.0)
        return carry

    lax.fori_loop(0, length, mask_step, 0)
    masks_ref[:, count:, :] = jnp.zeros((3, masks_ref.shape[1] - count, 128), f32)
    lane = lax.broadcasted_iota(jnp.int32, (1, 128), 1)
    for group in range(4):
        for pair in range(4):
            at = group * 512 + pair * 128
            gains_ref[:, at:at + 128] = jnp.where(lane < depth, metas_ref[group, 2 * pair, 0:1, :], metas_ref[group, 2 * pair + 1, 0:1, :])
        vecs_ref[:, group * own_e:(group + 1) * own_e] = metas_ref[group, j, 8:16, :]

    def normalize(rank):
        def body(i, carry):
            r = pl.ds(pl.multiple_of(rank * length + i * 16, 16), 16)
            x = xs_ref[r, :].astype(f32)
            scale = lax.rsqrt(jnp.sum(x * x, axis=1, keepdims=True) * (1.0 / model) + EPS)
            xn_ref[r, :] = (x * scale * gains_ref[...]).astype(bf16)
            return carry

        lax.fori_loop(0, length // 16, body, 0, unroll=4)

    for i in range(1, 4):
        pass_on(i)
    slot = wouts_ref.at[part_e(dx)]
    landed(slot, wr.at[0], xn)
    slot = wouts_ref.at[part_e(dx, 0, halves)]
    pending.append(put(slot, slot, ws.at[2], wr.at[2], yn))
    slot = wouts_ref.at[part_e(dy)]
    landed(slot, wr.at[1], yn)
    slot = wouts_ref.at[part_e(dy, halves, halves)]
    pending.append(put(slot, slot, ws.at[3], wr.at[3], xn))

    row_start(tok_ref, xs_ref, 0)
    for i in range(4, 7):
        pass_on(i)
    own[0].wait()
    normalize(j)
    row_hop(xs_ref, 0, 0, normalize)
    for k in range(4):
        relay(k)
    row_hop(xs_ref, 0, 1, normalize)
    for k in range(4, 8):
        relay(k)
    row_start(up_ref, ups_ref, 4)
    row_hop(xs_ref, 0, 2, normalize)
    for at in range(4):
        rank = flip(c, 1) * 4 + at
        landed(xs_ref.at[rows(rank)], xcr.at[at], sib)
        normalize(rank)
    for k, i in enumerate(order):
        slot = win_ref.at[block(dd, slots[i])]
        if k % 2 == 0:
            landed(slot, rr.at[k // 2], yn)
        else:
            landed(slot, rr.at[4 + k // 2], xn)
    own += [pltpu.make_async_copy(xnt_ref, xnt_out, own_sem.at[6]), pltpu.make_async_copy(win_ref, win_out, own_sem.at[7])]
    own[7].start()
    lead = u_ref.shape[1] - count
    u_ref[:, 0:lead, :] = jnp.zeros((tiles, lead, 128), f32)

    tile = 256

    def spread(out, first, start):
        def body(i, carry):
            product = jnp.dot(xn_ref[...], win_ref[:, pl.ds(pl.multiple_of(start + i * tile, tile), tile)], preferred_element_type=f32)
            for r in range(8):
                for part in range(0, tile, 128):
                    out[i * (tile // 128) + part // 128, pl.ds(first + r, length, stride=8), :] = product[r * length:(r + 1) * length, part:part + 128]
            return carry

        lax.fori_loop(0, width // tile, body, 0)

    spread(u_ref, lead, 0)
    taps = [vecs_ref[o:o + 1, :] for o in range(4)]
    bias = vecs_ref[4:5, :]

    def conv_step(i, carry):
        r = pl.ds(pl.multiple_of(i * 32, 32), 32)
        for n in range(tiles):
            lanes = slice(n * 128, n * 128 + 128)
            total = bias[:, lanes] + taps[3][:, lanes] * u_ref[n, pl.ds(pl.multiple_of(lead + i * 32, 8), 32), :]
            for o in range(1, 4):
                total = total + taps[3 - o][:, lanes] * (u_ref[n, pl.ds(pl.multiple_of(lead + i * 32 - 8 * o, 8), 32), :] * masks_ref[o - 1, r, :])
            sig = jax.nn.sigmoid(total)
            v_ref[n, r, :] = (total * sig).astype(bf16).astype(f32)
            slope_ref[n, r, :] = sig * (1.0 + total * (1.0 - sig))
        return carry

    lax.fori_loop(0, count // 32, conv_step, 0, unroll=2)
    for copy in own[3:5]:
        copy.wait()
    for i, (to, at) in enumerate(((xn, dx), (yn, dy), (dn, dd))):
        landed(smalls_ref.at[part_e(at)], pr.at[16 + i], to)
    quarter = count // 4
    narrow = smalls_ref[:, 128:256].astype(f32)
    packed = jnp.zeros((quarter, 128), f32)
    for b in range(4):
        r = slice(b * quarter, (b + 1) * quarter)
        values = jnp.concatenate([v_ref[n, r, :].astype(bf16) for n in range(tiles)], axis=1)
        part_ref[r, :] = jnp.dot(values, smalls_ref[:, 0:128], preferred_element_type=f32)
        turned = pltpu.roll(narrow, 32 * b, 1) if b else narrow
        packed = packed + jnp.dot(values, turned.astype(bf16), preferred_element_type=f32)
    part_ref[count:count + quarter, :] = packed
    saves = [(u_ref, u_out), (v_ref, v_out), (slope_ref, slope_out), (masks_ref, masks_out), (live_ref, live_out), (g_ref, g_out), (vt_ref, vt_out)]
    saves = [pltpu.make_async_copy(a, b, save_sem.at[i]) for i, (a, b) in enumerate(saves)]
    for copy in saves[:5]:
        copy.start()

    def early():
        row_hop(ups_ref, 4, 0, None, UP_HOPS)

    def between():
        spread(g_ref, 0, width)
        saves[5].start()

    def late():
        def turn_x(i, carry):
            part = pl.ds(pl.multiple_of(i * 128, 128), 128)
            for rank in range(8):
                r = slice(rank * length, (rank + 1) * length)
                xnt_ref[part, r] = xn_ref[r, part].T
            return carry

        lax.fori_loop(0, model // 128, turn_x, 0)
        own[6].start()
        row_hop(ups_ref, 4, 1, None, UP_HOPS)

        def turn_v(i, carry):
            r = pl.ds(pl.multiple_of(i * 128, 128), 128)
            for n in range(tiles):
                vt_ref[n * 128:(n + 1) * 128, r] = v_ref[n, r, :].T.astype(bf16)
            return carry

        lax.fori_loop(0, count // 128, turn_v, 0)
        saves[6].start()

    line_total(part_ref, out_ref, sib_ref, base_ref, left_ref, right_ref, tor_ref, tol_ref, ts, tr, tls, tlr, trs, trr, tos, tor, early, between, late)
    dl_ref[...] = out_ref[0:count, :].astype(bf16)
    for b in range(4):
        packed = out_ref[count:count + quarter, :]
        kq_ref[b * quarter:(b + 1) * quarter, :] = pltpu.roll(packed, 128 - 32 * b, 1) if b else packed
    row_hop(ups_ref, 4, 2, None, UP_HOPS)
    for at in range(4):
        @pl.when((z <= at + UP_HOPS) & (at <= z + UP_HOPS))
        def _():
            landed(ups_ref.at[rows(flip(c, 1) * 4 + at)], xcr.at[4 + at], sib)

    landed(wouts_ref.at[part_e(dd, 0, halves)], wr.at[2], yn)
    landed(wouts_ref.at[part_e(dd, halves, halves)], wr.at[3], xn)
    row_end(xs_ref, 0)
    row_end(ups_ref, 4, UP_HOPS)
    own[1].wait()
    for copy in saves:
        copy.wait()
    own[6].wait()
    own[7].wait()
    for copy in pending:
        copy.wait_send()


def line_total(part_ref, out_ref, sib_ref, base_ref, left_ref, right_ref, tor_ref, tol_ref, ss, sr, ls, lr, rs, rr, os_, or_, early, between, late):
    d, c, z = place()
    sib = (d, flip(c, 1), z)
    left = (d, c, lax.rem(z + 3, 4))
    right = (d, c, lax.rem(z + 1, 4))
    rows = part_ref.shape[0] // 2
    piece = rows // PIECES
    mine, theirs = c * rows, flip(c, 1) * rows

    def cut(p):
        return pl.ds(p * piece, piece)

    def far(base, p):
        return pl.ds(pl.multiple_of(base + p * piece, 8), piece)

    for p in range(PIECES):
        put(part_ref.at[far(theirs, p)], sib_ref.at[cut(p)], ss.at[p], sr.at[p], sib)
    for p in range(PIECES):
        landed(sib_ref.at[cut(p)], sr.at[p], sib)
        value = part_ref[far(mine, p), :] + sib_ref[cut(p), :]
        out_ref[far(mine, p), :] = value
        base_ref[cut(p), :] = value.astype(base_ref.dtype)

        @pl.when(z == 0)
        def _():
            put(base_ref.at[cut(p)], left_ref.at[cut(p)], rs.at[p], lr.at[p], right)

        @pl.when(z == 3)
        def _():
            put(base_ref.at[cut(p)], right_ref.at[cut(p)], ls.at[p], rr.at[p], left)

    early()

    def from_left(p):
        landed(left_ref.at[cut(p)], lr.at[p], left)

        @pl.when(z < 3)
        def _():
            tor_ref[cut(p), :] = (out_ref[far(mine, p), :] + left_ref[cut(p), :].astype(f32)).astype(tor_ref.dtype)
            put(tor_ref.at[cut(p)], left_ref.at[cut(p)], rs.at[p], lr.at[p], right)

    def from_right(p):
        landed(right_ref.at[cut(p)], rr.at[p], right)

        @pl.when(z > 0)
        def _():
            tol_ref[cut(p), :] = (out_ref[far(mine, p), :] + right_ref[cut(p), :].astype(f32)).astype(tol_ref.dtype)
            put(tol_ref.at[cut(p)], right_ref.at[cut(p)], ls.at[p], rr.at[p], left)

    @pl.when(z == 1)
    def _():
        for p in range(PIECES):
            from_left(p)

    @pl.when(z == 2)
    def _():
        for p in range(PIECES):
            from_right(p)

    between()

    @pl.when(z < 2)
    def _():
        for p in range(PIECES):
            from_right(p)

    @pl.when(z >= 2)
    def _():
        for p in range(PIECES):
            from_left(p)

    for p in range(PIECES):
        @pl.when(z > 0)
        def _():
            out_ref[far(mine, p), :] += left_ref[cut(p), :].astype(f32)

        @pl.when(z < 3)
        def _():
            out_ref[far(mine, p), :] += right_ref[cut(p), :].astype(f32)

        put(out_ref.at[far(mine, p)], out_ref.at[far(mine, p)], os_.at[p], or_.at[p], sib)
    late()
    for p in range(PIECES):
        landed(out_ref.at[far(theirs, p)], or_.at[p], sib)
        sent(out_ref.at[far(mine, p)], os_.at[p], sib)
        sent(part_ref.at[far(theirs, p)], ss.at[p], sib)

        @pl.when(z < 3)
        def _():
            sent(base_ref.at[cut(p)], rs.at[p], right)

        @pl.when(z > 0)
        def _():
            sent(base_ref.at[cut(p)], ls.at[p], left)


def k1(tokens, upstream, w_in, w_out, w_x, w_dt, gain, lengths, conv_w, conv_b, dt_bias, skip):
    groups, ways = 4, 8
    small = jax.ShapeDtypeStruct((128, 384), bf16)
    cols = jax.ShapeDtypeStruct((ways, w_in.shape[0], w_in.shape[1] // ways), bf16)
    meta = jax.ShapeDtypeStruct((16, 128), f32)
    like = jax.ShapeDtypeStruct
    length, model = tokens.shape[1:]
    count = ways * length
    channels = groups * w_out.shape[0]
    dma = lambda n: pltpu.SemaphoreType.DMA((n,))
    some = pl.BlockSpec(memory_space=pl.ANY)
    far = pl.BlockSpec(memory_space=pltpu.HBM)
    here = pl.BlockSpec(memory_space=pltpu.VMEM)
    packed = count + count // 4
    return pl.pallas_call(
        k1_kernel,
        out_shape=(
            like((model, count), bf16),
            like((count, model), bf16),
            like((groups * ways * cols.shape[1], cols.shape[2]), bf16),
            like((channels, model), bf16),
            like((channels, small.shape[1]), bf16),
            like((8, channels), f32),
            like((1, model), f32),
            like((3, count + 32, 128), f32),
            like((1, count, 128), f32),
            like((channels // 128, count + 24, 128), f32),
            like((channels // 128, count, 128), f32),
            like((channels // 128, count, 128), f32),
            like((channels, count), bf16),
            like((channels // 128, count, 128), f32),
            like((count, 128), bf16),
            like((count, 128), f32),
        ),
        in_specs=[some] * 2 + [here, some] + [here] * 8,
        out_specs=(far,) * 4 + (here,) * 3 + (far,) * 7 + (here,) * 2,
        scratch_shapes=[
            pltpu.VMEM((3, count + 32, 128), f32),
            pltpu.VMEM((1, count, 128), f32),
            pltpu.VMEM((channels // 128, count + 24, 128), f32),
            pltpu.VMEM((channels // 128, count, 128), f32),
            pltpu.VMEM((channels // 128, count, 128), f32),
            pltpu.VMEM((channels, count), bf16),
            pltpu.VMEM((channels // 128, count, 128), f32),
            dma(7),
            pltpu.VMEM(cols.shape, bf16),
            pltpu.VMEM(meta.shape, f32),
            pltpu.VMEM(small.shape, bf16),
            pltpu.VMEM((count, model), bf16),
            pltpu.VMEM((count, model), bf16),
            pltpu.VMEM((model, count), bf16),
            pltpu.VMEM((groups * ways * cols.shape[1], cols.shape[2]), bf16),
            pltpu.VMEM((groups, ways) + meta.shape, f32),
            pltpu.VMEM((packed, 128), f32),
            pltpu.VMEM((packed, 128), f32),
        ] + [pltpu.VMEM((packed // 2, 128), f32)] + [pltpu.VMEM((packed // 2, 128), LINE1)] * 5
        + [dma(8), dma(7), dma(7), dma(3), dma(3), dma(8), dma(8), dma(8), dma(8), dma(8), dma(8), dma(7), dma(7), dma(19), dma(19), dma(8), dma(8), dma(4), dma(4)]
        + [dma(PIECES) for _ in range(8)],
        compiler_params=pltpu.CompilerParams(collective_id=0, has_side_effects=True, vmem_limit_bytes=56 * 1024 * 1024),
    )(tokens, upstream, w_in, w_out, w_x, w_dt, gain, lengths, conv_w, conv_b, dt_bias, skip)


GROUP = 4


def k2_kernel(states, dl_ref, kq_ref, wdt_ref, vecs_ref, keep_ref, live_ref, v_ref, g_ref, ups_any, wout_any,
              acc_out, mt_ref, dg_ref, gwdt_ref, ups_out, dv_ref, part_ref, stat_ref,
              ups_ref, loads, stores, zs, zr, cs, cr, ls, lr, ss, sr, m_ref, wout_ref, acc_ref, recv_ref, dpre_ref, s_ref, h_ref, rate_ref, w_ref, y_ref, dm_ref, kb_ref, hot_ref, drr_ref):
    tiles, count = v_ref.shape[:2]
    steps = count // 8
    wide = states * 128
    chunk = 256
    first = pl.program_id(0) == 0
    half = pl.program_id(0)
    both = range(tiles)
    width = tiles * 128
    rank = wdt_ref.shape[1]

    length = count // 8
    d, c, z = place()
    sib = (d, flip(c, 1), z)
    left = (d, c, lax.rem(z + 3, 4))
    right = (d, c, lax.rem(z + 1, 4))

    def rows(rank):
        return pl.ds(pl.multiple_of(rank * length, length), length)

    keeps = [pltpu.make_async_copy(ups_ref.at[r // 4, r % 4], ups_out.at[r // 4, r % 4], stores.at[r]) for r in range(8)]

    def arrive(act):
        for rank in range(8):
            at = rank % 4
            here = jnp.logical_not(((z == 0) & (at == 3)) | ((z == 3) & (at == 0))) if at in (0, 3) else None
            copy = pltpu.make_async_copy(ups_any.at[rows(rank)], ups_ref.at[rank // 4, at], loads.at[rank])
            if here is None:
                act(copy)
            else:
                @pl.when(here)
                def _():
                    act(copy)

    @pl.when(first)
    def _():
        arrive(lambda copy: copy.start())
        pltpu.make_async_copy(wout_any, wout_ref, loads.at[8]).start()
        greet([sib, left, right])

        @pl.when(z == 1)
        def _():
            put(ups_any.at[rows(c * 4 + 3)], ups_ref.at[c, 3], zs, zr, left)

        @pl.when(z == 2)
        def _():
            put(ups_any.at[rows(c * 4)], ups_ref.at[c, 0], zs, zr, right)

    def complete():
        for end, source, at in ((0, right, 3), (3, left, 0)):
            @pl.when(z == end)
            def _():
                slot = ups_ref.at[c, at]
                landed(slot, zr, source)
                put(slot, slot, cs, cr, sib)
                landed(ups_ref.at[flip(c, 1), at], cr, sib)
                sent(slot, cs, sib)

        for end, target, at in ((1, left, 3), (2, right, 0)):
            @pl.when(z == end)
            def _():
                sent(ups_any.at[rows(c * 4 + at)], zs, target)

        arrive(lambda copy: copy.wait())
        pltpu.make_async_copy(wout_any, wout_ref, loads.at[8]).wait()
        for copy in keeps:
            copy.start()

    @pl.when(first)
    def _():
        row = lax.broadcasted_iota(jnp.int32, (128, 512), 0)
        col = lax.broadcasted_iota(jnp.int32, (128, 512), 1) // 128
        for part in range(0, 2 * wide, 512):
            hot_ref[:, part:part + 512] = jnp.where((row % 32 == col + part // 128) & (row < 96), 1.0, 0.0).astype(bf16)

    lane = lax.broadcasted_iota(jnp.int32, (512, 128), 1)

    def spread(i, carry):
        r = pl.ds(pl.multiple_of(i * 512, 512), 512)
        value = jnp.where(lane < 2 * states, kq_ref[r, :], 0.0)
        hi = value.astype(bf16).astype(f32)
        mid = (value - hi).astype(bf16).astype(f32)
        low = value - hi - mid
        left = (hi + pltpu.roll(mid, 32, 1) + pltpu.roll(low, 64, 1)).astype(bf16)
        for part in range(0, 2 * wide, 256):
            kb_ref[r, part:part + 256] = jnp.dot(left, hot_ref[:, part:part + 256], preferred_element_type=f32)
        return carry

    lax.fori_loop(0, count // 512, spread, 0)
    cols = (((1,), (1,)), ((), ()))

    def gate_step(i, carry):
        product = lax.dot_general(ups_ref[i].reshape(4 * length, wout_ref.shape[1]), wout_ref[pl.ds(pl.multiple_of(half * width, width), width), :], cols, preferred_element_type=f32)
        for j in range(4):
            for n in both:
                dm_ref[n, pl.ds(i * 4 + j, length, stride=8), :] = product[j * length:(j + 1) * length, n * 128:(n + 1) * 128]
        return carry

    bias = vecs_ref[5:6, :]
    skip = vecs_ref[6:7, :]
    tile_of = lambda x, n: x[:, n * 128:(n + 1) * 128]
    ks = lax.broadcasted_iota(jnp.int32, (128, 128), 1)

    def before(i, carry):
        seen = list(carry)
        r = pl.ds(pl.multiple_of(i * 128, 128), 128)
        live = live_ref[0, r, :]
        k = jnp.where(ks < states, kq_ref[r, :], 0.0)
        sk = jnp.sum(k * k, axis=1, keepdims=True)
        pre = lax.dot_general(dl_ref[r, :], wdt_ref[...], cols, preferred_element_type=f32) + bias
        for n in both:
            beta = jax.nn.sigmoid(tile_of(pre, n))
            part = 1.0 / (1.0 + beta * sk)
            rate_ref[n, r, :] = beta * part
            w_ref[n, r, :] = part * part * beta * (1.0 - beta)
            shown = (beta * live).reshape(16, 8, 128)
            seen[n] = seen[n] + jnp.sum(shown, axis=0)
            seen[tiles + n] = jnp.maximum(seen[tiles + n], jnp.max(shown, axis=0))
        return tuple(seen)

    blank = jnp.zeros((8, 128), f32)
    seen = lax.fori_loop(0, count // 128, before, (blank,) * (2 * tiles))
    s_ref[0, 0] = jnp.zeros(s_ref.shape[2:], f32)
    span = GROUP * 8
    at = [slice(j * 8, j * 8 + 8) for j in range(GROUP)]

    def view(ref, i):
        r = pl.ds(pl.multiple_of(i * span, span), span)
        return ref.at[:, r] if len(ref.shape) == 3 else ref.at[r]

    def pair(ref, r):
        return jnp.concatenate([ref[n, r, :] for n in both], axis=1)

    def keep_pair(ref, r, value):
        for n in both:
            ref[n, r, :] = tile_of(value, n)

    tile = lambda x: jnp.concatenate([x] * tiles, axis=1)

    def fold(x):
        total = tile_of(x, 0)
        for n in range(1, tiles):
            total = total + tile_of(x, n)
        return total

    def forward(i, carry):
        keeps, rates, vs, kbs, ys = [view(x, i) for x in (keep_ref, rate_ref, v_ref, kb_ref, y_ref)]
        keep = [keeps[0, r, :] for r in at]
        rate = [pair(rates, r) for r in at]
        value = [pair(vs, r) for r in at]
        rv = [a * b for a, b in zip(rate, value)]
        y = [skip * b for b in value]
        for n in range(states):
            state = s_ref[i, 0, n]
            for j, r in enumerate(at):
                kb = kbs[r, n * 128:(n + 1) * 128]
                qb = kbs[r, wide + n * 128:wide + (n + 1) * 128]
                state = (tile(keep[j]) - rate[j] * tile(kb * kb * keep[j])) * state + rv[j] * tile(kb)
                if j < GROUP - 1:
                    s_ref[i, j + 1, n] = state
                else:
                    s_ref[i + 1, 0, n] = state
                y[j] = y[j] + state * tile(qb)
        for j, r in enumerate(at):
            keep_pair(ys, r, y[j])
        return carry

    lax.fori_loop(0, steps // GROUP, forward, 0)
    h_ref[...] = jnp.zeros_like(h_ref)

    @pl.when(first)
    def _():
        complete()

    lax.fori_loop(0, 2, gate_step, 0)

    def gates(i, carry):
        r = pl.ds(pl.multiple_of(i * 32, 32), 32)
        live = live_ref[0, r, :]
        for n in both:
            g = g_ref[n, r, :]
            sg = jax.nn.sigmoid(g)
            silu = g * sg
            y = y_ref[n, r, :]
            dm = dm_ref[n, r, :] * live
            dv_ref[n, r, :] = dm * silu
            dm_ref[n, r, :] = dm * y * (sg * (1.0 + g * (1.0 - sg)))
            y_ref[n, r, :] = y * silu * live
        return carry

    lax.fori_loop(0, count // 32, gates, 0, unroll=2)

    def by_row(j, carry):
        r = pl.ds(pl.multiple_of(j * length, length), length)
        for n in both:
            value = y_ref[n, pl.ds(j, length, stride=8), :]
            m_ref[r, pl.ds(pl.multiple_of(half * width + n * 128, 128), 128)] = value.astype(bf16)
            mt_ref[n * 128:(n + 1) * 128, r] = value.T.astype(bf16)
            dg_ref[r, n * 128:(n + 1) * 128] = dm_ref[n, pl.ds(j, length, stride=8), :].astype(bf16)
        return carry

    lax.fori_loop(0, 8, by_row, 0)

    def rows_product(core):
        def body(i, carry):
            lanes = pl.ds(pl.multiple_of(i * chunk, chunk), chunk)
            product = jnp.dot(m_ref[pl.ds(pl.multiple_of(core * 4 * length, 4 * length), 4 * length), :], wout_ref[:, lanes], preferred_element_type=f32)
            for at_z in range(4):
                ups_ref[core, at_z, :, lanes] = product[at_z * length:(at_z + 1) * length].astype(bf16)
            return carry

        lax.fori_loop(0, wout_ref.shape[1] // chunk, body, 0)

    def gather(at_z):
        landed(acc_ref.at[at_z], sr.at[at_z], sib)
        add_rows(acc_ref.at[at_z], [acc_ref.at[at_z], ups_ref.at[c, at_z]])

    @pl.when(jnp.logical_not(first))
    def _():
        for copy in keeps:
            copy.wait()
        rows_product(flip(c, 1))
        for at_z in (3, 0, 2, 1):
            put(ups_ref.at[flip(c, 1), at_z], acc_ref.at[at_z], ss.at[at_z], sr.at[at_z], sib)
        rows_product(c)
        gather(3)
        gather(0)

        @pl.when(z == 0)
        def _():
            put(acc_ref.at[3], recv_ref, ls, lr, right)

        @pl.when(z == 3)
        def _():
            put(acc_ref.at[0], recv_ref, ls, lr, left)


    def backward(step, carry):
        i = steps // GROUP - 1 - step
        keeps, rates, vs, kbs, dvs, ws, drrs = [view(x, i) for x in (keep_ref, rate_ref, v_ref, kb_ref, dv_ref, w_ref, drr_ref)]
        keep = [keeps[0, r, :] for r in at]
        rate = [pair(rates, r) for r in at]
        value = [pair(vs, r) for r in at]
        rv = [a * b for a, b in zip(rate, value)]
        dy = [pair(dvs, r) for r in at]
        hk = [jnp.zeros((8, tiles * 128), f32) for r in at]
        hs2 = [jnp.zeros((8, tiles * 128), f32) for r in at]
        for n in range(states):
            ah = h_ref[n]
            later = s_ref[i + 1, 0, n]
            for j in range(GROUP - 1, -1, -1):
                r = at[j]
                kb = kbs[r, n * 128:(n + 1) * 128]
                qb = kbs[r, wide + n * 128:wide + (n + 1) * 128]
                kk = kb * keep[j]
                held = tile(kb * kk)
                h = dy[j] * tile(qb) + ah
                prior = s_ref[i, j, n]
                hs = h * prior
                hk[j] = hk[j] + h * tile(kb)
                hs2[j] = hs2[j] + hs * held
                kbs[r, n * 128:(n + 1) * 128] = fold(h * rv[j]) - 2.0 * kk * fold(hs * rate[j])
                kbs[r, wide + n * 128:wide + (n + 1) * 128] = fold(dy[j] * later)
                later = prior
                ah = (tile(keep[j]) - rate[j] * held) * h
            h_ref[n] = ah
        dskip = carry
        for j, r in enumerate(at):
            drate = value[j] * hk[j] - hs2[j]
            drrs[r, :] = fold(drate * rate[j] * rate[j]) * (-2.0)
            keep_pair(ws, r, drate * pair(ws, r))
            keep_pair(dvs, r, rate[j] * hk[j] + skip * dy[j])
            dskip = dskip + dy[j] * value[j]
        return dskip

    dskip = lax.fori_loop(0, steps // GROUP, backward, jnp.zeros((8, tiles * 128), f32))

    quarter = count // 4
    packed = jnp.zeros((quarter, 128), f32)
    for b in range(4):
        r = slice(b * quarter, (b + 1) * quarter)
        total = jnp.zeros((quarter, 128), f32)
        for part in range(0, 2 * wide, 512):
            total = total + lax.dot_general(kb_ref[r, part:part + 512].astype(bf16), hot_ref[:, part:part + 512], cols, preferred_element_type=f32)
        drr = jnp.sum(drr_ref[r, :], axis=1, keepdims=True)
        k = kq_ref[r, :]
        low = lax.broadcasted_iota(jnp.int32, (quarter, 128), 1)
        total = jnp.where(low < 2 * states, total, 0.0) + jnp.where(low < states, k * drr, 0.0)
        packed = packed + (pltpu.roll(total, 32 * b, 1) if b else total)

    tail = pl.ds(count, quarter)
    part_ref[tail, :] = jnp.where(first, packed, part_ref[tail, :] + packed)

    def after(i, carry):
        r = pl.ds(pl.multiple_of(i * 128, 128), 128)
        sums = list(carry)
        for n in both:
            low = w_ref[n, r, :].astype(bf16)
            dpre_ref[r, n * 128:(n + 1) * 128] = low
            sums[n] = sums[n] + jnp.sum(low.astype(f32).reshape(16, 8, 128), axis=0)
        ddl = jnp.dot(dpre_ref[r, :], wdt_ref[...], preferred_element_type=f32)
        part_ref[r, :] = jnp.where(first, ddl, part_ref[r, :] + ddl)
        return tuple(sums)

    sums = lax.fori_loop(0, count // 128, after, (blank,) * tiles)

    gwdt_ref[...] = lax.dot_general(dpre_ref[...], dl_ref[...], (((0,), (0,)), ((), ())), preferred_element_type=f32)

    @pl.when(jnp.logical_not(first))
    def _():
        gather(2)
        gather(1)
        for end, source, at_z in ((1, left, 3), (2, right, 0)):
            @pl.when(z == end)
            def _():
                landed(recv_ref, lr, source)
                add_rows(acc_ref.at[at_z], [acc_ref.at[at_z], recv_ref])

        save = pltpu.make_async_copy(acc_ref, acc_out, loads.at[8])
        save.start()
        for at_z in range(4):
            sent(ups_ref.at[flip(c, 1), at_z], ss.at[at_z], sib)
        for end, target, at_z in ((0, right, 3), (3, left, 0)):
            @pl.when(z == end)
            def _():
                sent(acc_ref.at[at_z], ls, target)
        save.wait()

    stat_ref[...] = jnp.zeros_like(stat_ref)
    for n in both:
        lanes = slice(n * 128, (n + 1) * 128)
        stat_ref[0:1, lanes] = jnp.sum(seen[n], axis=0, keepdims=True)
        stat_ref[1:2, lanes] = jnp.max(seen[tiles + n], axis=0, keepdims=True)
        stat_ref[5:6, lanes] = jnp.sum(sums[n], axis=0, keepdims=True)
        stat_ref[6:7, lanes] = jnp.sum(tile_of(dskip, n), axis=0, keepdims=True)


def k2(dl, kq, smalls, vecs, masks, live, v, g, ups, wout, states):
    count, rank = dl.shape
    channels, model = wout.shape
    tiles = 2
    width = tiles * 128
    like = jax.ShapeDtypeStruct
    once = pl.Buffered(buffer_count=1)
    whole = lambda a: pl.BlockSpec(a.shape, lambda h: (0,) * a.ndim, pipeline_mode=once)
    deep = pl.BlockSpec((tiles, count, 128), lambda h: (h, 0, 0))
    flat = pl.BlockSpec((count, width), lambda h: (0, h))
    return pl.pallas_call(
        functools.partial(k2_kernel, states),
        grid=(channels // width,),
        out_shape=(
            like((4, count // 8, model), bf16),
            like((channels, count), bf16),
            like((count, channels), bf16),
            like((channels, rank), f32),
            like((2, 4, count // 8, model), bf16),
            like(v.shape, f32),
            like((count + count // 4, 128), f32),
            like((8, channels), f32),
        ),
        in_specs=[
            whole(dl), whole(kq),
            pl.BlockSpec((width, 128), lambda h: (h, 2)),
            pl.BlockSpec((8, width), lambda h: (0, h)),
            pl.BlockSpec((1, count, 128), lambda h: (0, 0, 0), pipeline_mode=once),
            pl.BlockSpec((1, count, 128), lambda h: (0, 0, 0), pipeline_mode=once),
            deep, deep, pl.BlockSpec(memory_space=pl.ANY),
            pl.BlockSpec(memory_space=pl.ANY),
        ],
        out_specs=(pl.BlockSpec(memory_space=pltpu.HBM), pl.BlockSpec((width, count), lambda h: (h, 0)), flat, pl.BlockSpec((width, rank), lambda h: (h, 0)), pl.BlockSpec(memory_space=pltpu.HBM), deep, pl.BlockSpec((count + count // 4, 128), lambda h: (0, 0)), pl.BlockSpec((8, width), lambda h: (0, h))),
        scratch_shapes=[
            pltpu.VMEM((2, 4, count // 8, model), bf16),
            pltpu.SemaphoreType.DMA((9,)),
            pltpu.SemaphoreType.DMA((8,)),
        ] + [pltpu.SemaphoreType.DMA(())] * 6 + [
            pltpu.SemaphoreType.DMA((4,)),
            pltpu.SemaphoreType.DMA((4,)),
            pltpu.VMEM((count, channels), bf16),
            pltpu.VMEM((channels, model), bf16),
            pltpu.VMEM((4, count // 8, model), bf16),
            pltpu.VMEM((count // 8, model), bf16),
            pltpu.VMEM((count, width), bf16),
            pltpu.VMEM((count // 8 // GROUP + 1, GROUP, states, 8, width), f32),
            pltpu.VMEM((states, 8, width), f32),
        ] + [pltpu.VMEM((tiles, count, 128), f32)] * 4
        + [pltpu.VMEM((count, 2 * states * 128), f32), pltpu.VMEM((128, 2 * states * 128), bf16), pltpu.VMEM((count, 128), f32)],
        compiler_params=pltpu.CompilerParams(collective_id=2, has_side_effects=True, vmem_limit_bytes=63400000),
    )(dl, kq, smalls, vecs, masks, live, v, g, ups, wout)


class Row:
    def __init__(self, part, sib, recv, sems, merged=False):
        self.part, self.sib, self.recv, self.merged = part, sib, recv, merged
        self.ss, self.sr, self.gs, self.lr, self.rr = sems
        d, c, z = place()
        self.c = c
        self.other = (d, flip(c, 1), z)
        self.to_left = (d, c, lax.rem(z + 3, 4))
        self.to_right = (d, c, lax.rem(z + 1, 4))

    def start(self):
        for zp in (3, 0, 2, 1):
            put(self.part.at[flip(self.c, 1), zp], self.sib.at[zp], self.ss.at[zp], self.sr.at[zp], self.other)

    def gather(self):
        for zp in (3, 0, 2, 1):
            landed(self.sib.at[zp], self.sr.at[zp], self.other)
            add_rows(self.sib.at[zp], [self.sib.at[zp], self.part.at[self.c, zp]])

    def release(self):
        for zp in range(4):
            sent(self.part.at[flip(self.c, 1), zp], self.ss.at[zp], self.other)

    def terms(self, zs, zp):
        found = [self.sib.at[zp]]
        if zp >= zs and zs > 0 and not (self.merged and (zs, zp) == (1, 3)):
            landed(self.recv.at[zp], self.lr.at[zp], self.to_left)
            found.append(self.recv.at[zp])
        if zp <= zs and zs < 3 and not (self.merged and (zs, zp) == (2, 0)):
            slot = self.recv.at[4 if zp == zs else zp]
            landed(slot, self.rr.at[zp], self.to_right)
            found.append(slot)
        return found

    def join(self, zs, zp):
        found = self.terms(zs, zp)
        if len(found) > 1:
            add_rows(self.sib.at[zp], found)

    def skips(self, zs, zp):
        return self.merged and (zs, zp) in ((0, 3), (3, 0))

    def step(self, zs, k):
        k = k + 1 if self.merged else k
        ends = 1 if self.merged else 0
        for zp in ((3, 2, 1, 0) if zs == 0 else (0, 1, 2, 3)):
            if zp > zs and not self.skips(zs, zp) and k == (ends if zs == 0 else 3 - zp + zs):
                self.join(zs, zp)
                put(self.sib.at[zp], self.recv.at[zp], self.gs.at[zp], self.lr.at[zp], self.to_right)
            if zp < zs and not self.skips(zs, zp) and k == (ends if zs == 3 else zp + 3 - zs):
                self.join(zs, zp)
                put(self.sib.at[zp], self.recv.at[4 if zp == zs - 1 else zp], self.gs.at[zp], self.rr.at[zp], self.to_left)

    def finish(self, zs):
        add_rows(self.sib.at[zs], self.terms(zs, zs), self.total)

    def close(self, zs):
        for zp in range(4):
            if zp != zs and not self.skips(zs, zp):
                sent(self.sib.at[zp], self.gs.at[zp], self.other)

    def along(self, k, total=None):
        self.total = total
        d, c, z = place()
        for zs in range(4):
            @pl.when(z == zs)
            def _():
                if k < (2 if self.merged else 3):
                    self.step(zs, k)
                else:
                    self.finish(zs)
                    self.close(zs)


def row_scratch(rows, columns):
    return [pltpu.VMEM((4, rows, columns), bf16), pltpu.VMEM((5, rows, columns), bf16)] + [pltpu.SemaphoreType.DMA((4,))] * 5


def add_rows(dst, sources, total=None):
    rows = (total if total is not None else dst).shape[0]
    step = 16

    def body(i, carry):
        r = pl.ds(pl.multiple_of(i * step, step), step)
        value = sources[0][r, :].astype(f32)
        for more in sources[1:]:
            value = value + more[r, :].astype(f32)
        if total is not None:
            total[r, :] = value
        else:
            dst[r, :] = value.astype(dst.dtype)
        return carry

    lax.fori_loop(0, rows // step, body, 0)


class Flat:
    def __init__(self, part, xa, yb, rx, ry, ss, rs):
        self.part, self.xa, self.yb, self.rx, self.ry, self.ss, self.rs = part, xa, yb, rx, ry, ss, rs
        d, c, z = place()
        self.d, self.dx, self.dy, self.dd = d, flip(d, 1), flip(d, 2), flip(flip(d, 1), 2)
        self.xn, self.yn = (self.dx, c, z), (self.dy, c, z)
        half = part.shape[1] // 2
        self.a, self.b = pl.ds(0, half), pl.ds(half, half)
        self.sends = []

    def start_far(self):
        p = self.part
        self.sends.append(put(p.at[self.dd, self.a], self.xa, self.ss.at[0], self.rs.at[0], self.xn))
        self.sends.append(put(p.at[self.dd, self.b], self.yb, self.ss.at[1], self.rs.at[1], self.yn))

    def start_near(self):
        p = self.part
        self.sends.append(put(p.at[self.dx, self.a], self.rx.at[self.a], self.ss.at[2], self.rs.at[2], self.xn))
        self.sends.append(put(p.at[self.dy, self.b], self.ry.at[self.b], self.ss.at[3], self.rs.at[3], self.yn))

    def middle(self):
        p = self.part
        landed(self.xa, self.rs.at[0], self.xn)
        add_rows(self.xa, [self.xa, p.at[self.dy, self.a]])
        self.sends.append(put(self.xa, self.ry.at[self.a], self.ss.at[4], self.rs.at[4], self.yn))
        landed(self.yb, self.rs.at[1], self.yn)
        add_rows(self.yb, [self.yb, p.at[self.dx, self.b]])
        self.sends.append(put(self.yb, self.rx.at[self.b], self.ss.at[5], self.rs.at[5], self.xn))

    def finish(self, out):
        landed(self.rx.at[self.a], self.rs.at[2], self.xn)
        landed(self.ry.at[self.b], self.rs.at[3], self.yn)
        landed(self.ry.at[self.a], self.rs.at[4], self.yn)
        landed(self.rx.at[self.b], self.rs.at[5], self.xn)
        add_rows(out, [self.part.at[self.d], self.rx, self.ry])

    def close(self):
        for copy in self.sends:
            copy.wait_send()


def flat_scratch(rows, columns, dtype):
    half = pltpu.VMEM((rows // 2, columns), dtype)
    full = pltpu.VMEM((rows, columns), dtype)
    return [half, half, full, full, pltpu.SemaphoreType.DMA((6,)), pltpu.SemaphoreType.DMA((6,))]


def k3_kernel(part_ref, stat_ref, smalls_ref, vecs_ref, gains_ref, gwdt_ref, masks_ref, tok_ref, up_ref,
              acc_any, mt_any, dg_any, dv_any, slope_any, u_any, vt_any, xnt_any, win_any, ups_any,
              block_out, gtok_out, gwin_out, gwout_out, small_out, tiny_out, *scratch):
    scratch = list(scratch)

    def take(n):
        found = scratch[:n]
        del scratch[:n]
        return found

    block_ref, gtok_ref, gwin_ref, gwout_ref, small_ref, tiny_ref, stores = take(7)
    outp, win_ref, up, gp, gwoutp, smallp = take(6)
    mt_ref, dz_ref, dc_ref, slope_ref, u_ref, xnt_ref, dp_ref, slots_ref, row_ref = take(9)
    near_ref, pairs_ref, sum_ref, far_ref = take(4)
    loads, as_, ar, ns, nr, fs, fr = take(7)
    totals = take(7)
    total_sems = take(8)
    out_row = Row(None, *take(2), take(5), True)
    dxn_row = Row(outp, *take(2), take(5))
    flats = [Flat(up, *take(6)), Flat(gp, *take(6))]
    gwout_flat = Flat(gwoutp, *take(6))
    small_flat = Flat(smallp, *take(6))
    d, c, z = place()
    j = c * 4 + z
    other = flip(c, 1)
    steps = mates()
    planes = [(flip(d, 1), c, z), (flip(d, 2), c, z), (flip(flip(d, 1), 2), c, z)]
    length, model = tok_ref.shape[1:]
    tiles, padded, _ = dc_ref.shape
    count = dz_ref.shape[0]
    width = tiles * 128
    rows_any = [(dg_any, dz_ref.at[:, pl.ds(width, width)]), (xnt_any, xnt_ref), (acc_any, out_row.sib), (mt_any, mt_ref), (ups_any, outp),
                (dv_any, dc_ref.at[:, pl.ds(0, count)]), (slope_any, slope_ref), (u_any, u_ref), (win_any, win_ref)]
    copies = [pltpu.make_async_copy(a, b, loads.at[i]) for i, (a, b) in enumerate(rows_any)]
    for copy in copies:
        copy.start()
    greet([mate(s) for s in steps] + planes)
    outs = [(block_ref, block_out), (gtok_ref, gtok_out), (gwin_ref, gwin_out), (gwout_ref, gwout_out), (small_ref, small_out), (tiny_ref, tiny_out)]
    outs = [pltpu.make_async_copy(a, b, stores.at[i]) for i, (a, b) in enumerate(outs)]
    tile = 256
    nt = (((1,), (1,)), ((), ()))

    def rows_product(half):
        def body(i, carry):
            value = win_ref[i // (512 // tile), pl.ds(pl.multiple_of((i % (512 // tile)) * tile, tile), tile), :]
            product = lax.dot_general(dz_ref[pl.ds(pl.multiple_of(half * 512, 512), 512), :], value, nt, preferred_element_type=f32)
            for zp in range(4):
                outp[half, zp, :, pl.ds(pl.multiple_of(i * tile, tile), tile)] = product[zp * length:(zp + 1) * length].astype(bf16)
            return carry

        lax.fori_loop(0, model // tile, body, 0)

    def weight_rows(holder, first, group):
        def body(i, carry):
            lanes = pl.ds(pl.multiple_of(i * tile, tile), tile)
            left = xnt_ref[pl.ds(pl.multiple_of(group * 512, 512), 512), :]
            value = dz_ref[:, pl.ds(pl.multiple_of(first + i * tile, tile), tile)]
            holder[group, :, lanes] = jnp.dot(left, value, preferred_element_type=f32).astype(bf16)
            return carry

        lax.fori_loop(0, width // tile, body, 0)

    def weight_part(k):
        flat = flats[k]
        holder, first = (up, 0) if k == 0 else (gp, width)
        weight_rows(holder, first, flat.dd)
        flat.start_far()
        weight_rows(holder, first, flat.dx)
        weight_rows(holder, first, flat.dy)
        flat.start_near()
        weight_rows(holder, first, d)

    def early():
        for copy in copies[0:2]:
            copy.wait()
        weight_part(1)

    def between():
        copies[2].wait()
        out_row.along(0)
        flats[1].middle()

    def late():
        for copy in copies[3:5]:
            copy.wait()

        def body(i, carry):
            lanes = pl.ds(pl.multiple_of(i * tile, tile), tile)
            product = jnp.dot(mt_ref[...], outp[:, :, :, lanes].reshape(count, tile), preferred_element_type=f32)
            for g in range(4):
                gwoutp[g, :, lanes] = product[g * 128:(g + 1) * 128].astype(bf16)
            return carry

        lax.fori_loop(0, model // tile, body, 0)
        gwout_flat.start_far()
        gwout_flat.start_near()

    seen = jnp.sum(stat_ref[0:1, :], axis=1, keepdims=True)
    peak = jnp.max(stat_ref[1:2, :], axis=1, keepdims=True)
    row8 = lax.broadcasted_iota(jnp.int32, (8, 128), 0)
    lane8 = lax.broadcasted_iota(jnp.int32, (8, 128), 1)
    pairs_ref[...] = jnp.where(lane8 == 0, seen, jnp.where(lane8 == 1, peak, 0.0))
    for i, s in enumerate(steps):
        put(pairs_ref, near_ref.at[i], ns.at[i], nr.at[i], mate(s))

    def join(a, b):
        return jnp.where(lane8 == 1, jnp.maximum(a, b), a + b)

    total_ref = totals[0]
    line_total(part_ref, *totals, *total_sems, early, between, late)
    vt_copy = pltpu.make_async_copy(vt_any, mt_ref, loads.at[9])
    vt_copy.start()
    block = gwin_ref.shape[0]
    pending = []

    def rows_of(k, rank):
        return flats[k].part.at[d, pl.ds(pl.multiple_of(rank * block, block), block)]

    def give(k):
        flats[k].finish(flats[k].part.at[d])
        for i, s in enumerate(steps):
            to = mate(s)
            pending.append(put(rows_of(k, rank_of(to)), slots_ref.at[k, i], as_.at[7 * k + i], ar.at[7 * k + i], to))

    value = pairs_ref[...]
    for i, s in enumerate(steps):
        landed(near_ref.at[i], nr.at[i], mate(s, -1))
        value = join(value, near_ref[i])
    sum_ref[...] = value
    for i, to in enumerate(planes):
        put(sum_ref, far_ref.at[i], fs.at[i], fr.at[i], to)
    quarter = count // 4
    lane = lax.broadcasted_iota(jnp.int32, (quarter, 128), 1)
    dp_ref[:, 0:128] = total_ref[0:count, :].astype(bf16)
    for b in range(4):
        packed = total_ref[count:count + quarter, :]
        packed = pltpu.roll(packed, 128 - 32 * b, 1) if b else packed
        dp_ref[b * quarter:(b + 1) * quarter, 128:256] = jnp.where(lane < 32, packed, 0.0).astype(bf16)
    for copy in copies[5:8]:
        copy.wait()
    dc_ref[:, count:, :] = jnp.zeros((tiles, padded - count, 128), f32)

    def slope_step(i, carry):
        r = pl.ds(pl.multiple_of(i * 256, 256), 256)
        product = lax.dot_general(dp_ref[r, :], smalls_ref[:, 0:256], nt, preferred_element_type=f32)
        for n in range(tiles):
            dc_ref[n, r, :] = (dc_ref[n, r, :] + product[:, n * 128:(n + 1) * 128]) * slope_ref[n, r, :]
        return carry

    lax.fori_loop(0, count // 256, slope_step, 0)
    give(1)
    out_row.along(1)
    taps = [vecs_ref[o:o + 1, :] for o in range(4)]
    lead = u_ref.shape[1] - count

    for n in range(tiles):
        lanes = slice(n * 128, (n + 1) * 128)
        tap = [t[:, lanes] for t in taps]

        def conv_step(i, carry):
            r = pl.ds(pl.multiple_of(i * 32, 32), 32)
            sums = list(carry)
            dc = dc_ref[n, r, :]
            du = tap[3] * dc
            fold8 = lambda x: x[0:8] + x[8:16] + x[16:24] + x[24:32]
            sums[4] = sums[4] + fold8(dc)
            sums[3] = sums[3] + fold8(dc * u_ref[n, pl.ds(pl.multiple_of(lead + i * 32, 8), 32), :])
            for o in range(1, 4):
                sums[3 - o] = sums[3 - o] + fold8(dc * (u_ref[n, pl.ds(pl.multiple_of(lead + i * 32 - 8 * o, 8), 32), :] * masks_ref[o - 1, pl.ds(pl.multiple_of(i * 32, 8), 32), :]))
                du = du + tap[3 - o] * (dc_ref[n, pl.ds(pl.multiple_of(i * 32 + 8 * o, 8), 32), :] * masks_ref[o - 1, pl.ds(pl.multiple_of(i * 32 + 8 * o, 8), 32), :])
            dc_ref[n, r, :] = du
            return tuple(sums)

        sums = lax.fori_loop(0, count // 32, conv_step, (jnp.zeros((8, 128), f32),) * 5)
        smallp[n, 128:160, :] = jnp.zeros((32, 384), f32)
        for k in range(5):
            smallp[n, 128 + k:129 + k, 0:128] = jnp.sum(sums[k], axis=0, keepdims=True)
        smallp[n, 133:134, 0:128] = stat_ref[5:6, lanes]
        smallp[n, 134:135, 0:128] = stat_ref[6:7, lanes]
        smallp[n, 0:128, 256:384] = gwdt_ref[n * 128:(n + 1) * 128, :]

    def by_row(i, carry):
        r = pl.ds(pl.multiple_of(i * length, length), length)
        for n in range(tiles):
            dz_ref[r, n * 128:(n + 1) * 128] = dc_ref[n, pl.ds(i, length, stride=8), :].astype(bf16)
        return carry

    lax.fori_loop(0, 8, by_row, 0)
    gwout_flat.middle()
    copies[8].wait()
    rows_product(other)
    dxn_row.start()
    weight_rows(up, 0, flats[0].dd)
    flats[0].start_far()
    rows_product(c)
    dxn_row.gather()
    dxn_row.along(0)
    weight_rows(up, 0, flats[0].dx)
    weight_rows(up, 0, flats[0].dy)
    flats[0].start_near()
    weight_rows(up, 0, d)
    vt_copy.wait()
    for n in range(tiles):
        smallp[n, 0:128, 0:256] = jnp.dot(mt_ref[n * 128:(n + 1) * 128, :], dp_ref[...], preferred_element_type=f32)
    small_flat.start_far()
    small_flat.start_near()
    flats[0].middle()
    out_row.along(2, row_ref)

    def block_step(i, carry):
        r = pl.ds(pl.multiple_of(i * 16, 16), 16)
        block_ref[r, :] = (tok_ref[0, r, :].astype(f32) + row_ref[r, :]).astype(bf16)
        return carry

    lax.fori_loop(0, length // 16, block_step, 0)
    outs[0].start()
    dxn_row.along(1)
    give(0)
    small_flat.middle()
    dxn_row.along(2)
    gwout_flat.finish(gwout_ref)
    outs[3].start()
    dxn_row.along(3, row_ref)
    dxn_row.release()
    def norm_step(i, carry):
        r = pl.ds(pl.multiple_of(i * 16, 16), 16)
        x = tok_ref[0, r, :].astype(f32)
        scale = lax.rsqrt(jnp.sum(x * x, axis=1, keepdims=True) * (1.0 / model) + EPS)
        dxn = row_ref[r, :]
        inner = dxn * gains_ref[...]
        dot = jnp.sum(inner * x, axis=1, keepdims=True) * (1.0 / model)
        dxx = scale * inner - x * (scale * scale * scale * dot)
        gtok_ref[r, :] = (up_ref[0, r, :].astype(f32) + dxx).astype(bf16)
        return carry

    lax.fori_loop(0, length // 16, norm_step, 0)
    outs[1].start()
    small_flat.finish(small_ref)
    outs[4].start()

    def settle(k, rank, source):
        for g in range(4):
            at = k * width * 8 + g * 1024
            gwin_ref[:, pl.ds(pl.multiple_of(at + rank * 128, 128), 128)] = source[:, g * 128:(g + 1) * 128]

    for k in (1, 0):
        settle(k, j, rows_of(k, j))
        for i, s in enumerate(steps):
            src = mate(s, -1)
            landed(slots_ref.at[k, i], ar.at[7 * k + i], src)
            settle(k, rank_of(src), slots_ref.at[k, i])
    outs[2].start()
    value = sum_ref[...]
    for i, to in enumerate(planes):
        landed(far_ref.at[i], fr.at[i], to)
        value = join(value, far_ref[i])
    tiny_ref[...] = value
    outs[5].start()
    for i, to in enumerate(planes):
        sent(sum_ref, fs.at[i], to)
    for i, s in enumerate(steps):
        sent(near_ref.at[i], ns.at[i], mate(s))
    for copy in pending:
        copy.wait_send()
    for flat in (*flats, gwout_flat, small_flat):
        flat.close()
    for copy in outs:
        copy.wait()


def k3(part, stat, smalls, vecs, gains, gwdt, masks, tokens, upstream, acc, mt, dg, dv, slope, u, vt, xnt, win, ups):
    like = jax.ShapeDtypeStruct
    length, model = tokens.shape[1:]
    channels, count = mt.shape
    tiles = channels // 128
    here = pl.BlockSpec(memory_space=pltpu.VMEM)
    far = pl.BlockSpec(memory_space=pl.ANY)
    dma = lambda n: pltpu.SemaphoreType.DMA((n,))
    own_d = model // 32
    packed = part.shape[0]
    return pl.pallas_call(
        k3_kernel,
        out_shape=(
            like((length, model), bf16),
            like((length, model), bf16),
            like((own_d, 16 * channels), bf16),
            like((128, model), f32),
            like((160, 384), f32),
            like((8, 128), f32),
        ),
        in_specs=[here] * 9 + [far] * 10,
        out_specs=(pl.BlockSpec(memory_space=pltpu.HBM),) * 6,
        scratch_shapes=[
            pltpu.VMEM((length, model), bf16),
            pltpu.VMEM((length, model), bf16),
            pltpu.VMEM((own_d, 16 * channels), bf16),
            pltpu.VMEM((128, model), f32),
            pltpu.VMEM((160, 384), f32),
            pltpu.VMEM((8, 128), f32),
            dma(6),
            pltpu.VMEM((2, 4, length, model), bf16),
            pltpu.VMEM((4, 512, 2 * channels), bf16),
            pltpu.VMEM((4, 512, channels), bf16),
            pltpu.VMEM((4, 512, channels), bf16),
            pltpu.VMEM((4, 128, model), bf16),
            pltpu.VMEM((4, 160, 384), f32),
            pltpu.VMEM((channels, count), bf16),
            pltpu.VMEM((count, 2 * channels), bf16),
            pltpu.VMEM((tiles, count + 32, 128), f32),
            pltpu.VMEM((tiles, count, 128), f32),
            pltpu.VMEM(u.shape, f32),
            pltpu.VMEM((model, count), bf16),
            pltpu.VMEM((count, 256), bf16),
            pltpu.VMEM((2, 7, own_d, channels), bf16),
            pltpu.VMEM((length, model), f32),
            pltpu.VMEM((7, 8, 128), f32),
            pltpu.VMEM((8, 128), f32),
            pltpu.VMEM((8, 128), f32),
            pltpu.VMEM((3, 8, 128), f32),
            dma(10), dma(14), dma(14), dma(7), dma(7), dma(3), dma(3),
            pltpu.VMEM((packed, 128), f32),
        ] + [pltpu.VMEM((packed // 2, 128), f32)] + [pltpu.VMEM((packed // 2, 128), LINE2)] * 5 + [dma(PIECES) for _ in range(8)]
        + row_scratch(length, model) * 2
        + flat_scratch(512, channels, bf16) * 2 + flat_scratch(128, model, bf16) + flat_scratch(160, 384, f32),
        compiler_params=pltpu.CompilerParams(collective_id=1, has_side_effects=True, vmem_limit_bytes=63400000),
    )(part, stat, smalls, vecs, gains, gwdt, masks, tokens, upstream, acc, mt, dg, dv, slope, u, vt, xnt, win, ups)


def k4_kernel(slots, block_in, gtok_in, gwin_in, gwout_in, small_in, tiny_in, win_ref, gain_ref,
              block_ref, gtok_ref, gain_out, gwin_ref, convw_ref, convb_ref, gwx_ref, gwdt_ref, dtb_ref, skip_ref, gwout_ref, mean_ref, peak_ref):
    block_ref[0] = block_in[...]
    gtok_ref[0] = gtok_in[...]
    gwout_ref[...] = gwout_in[...]
    depth, total = gwin_in.shape
    dot = jnp.zeros((depth, 128), f32)
    for at in range(0, total, 128):
        value = gwin_in[:, at:at + 128].astype(f32)
        gwin_ref[:, at:at + 128] = value
        dot = dot + value * win_ref[:, at:at + 128].astype(f32)
    column = jnp.broadcast_to(jnp.sum(dot, axis=1, keepdims=True), (depth, 128))
    gain_out[...] = column.T[0:1, :] / gain_ref[...].astype(f32)
    gwx_ref[...] = small_in[0:128, 0:256].T[0:gwx_ref.shape[0], :]
    gwdt_ref[...] = small_in[0:128, 256:384]
    convw_ref[...] = small_in[128:132, 0:128]
    convb_ref[...] = small_in[132:133, 0:128]
    dtb_ref[...] = small_in[133:134, 0:128]
    skip_ref[...] = small_in[134:135, 0:128]
    mean_ref[...] = tiny_in[0:1, 0:1] * (1.0 / slots)
    peak_ref[...] = tiny_in[0:1, 1:2]


def k4(slots, block, gtok, gwin, gwout, small, tiny, w_in, gain, columns):
    like = jax.ShapeDtypeStruct
    here = pl.BlockSpec(memory_space=pltpu.VMEM)
    row = like((1, 128), f32)
    return pl.pallas_call(
        functools.partial(k4_kernel, slots),
        out_shape=(
            like((1,) + block.shape, bf16), like((1,) + gtok.shape, bf16), like(gain.shape, f32), like(gwin.shape, f32),
            like((4, 128), f32), row, like((columns, 128), f32), like((128, 128), f32), row, row, like(gwout.shape, f32),
            like((1, 1), f32), like((1, 1), f32),
        ),
        in_specs=[here] * 8,
        out_specs=(here,) * 13,
        compiler_params=pltpu.CompilerParams(vmem_limit_bytes=63400000),
    )(block, gtok, gwin, gwout, small, tiny, w_in, gain)

def masks(lengths, count):
    ends = jnp.cumsum(lengths, axis=1)
    places = jnp.arange(count, dtype=jnp.int32)
    segment = jnp.sum((places[:, None, None] >= ends[None, :, :]).astype(jnp.int32), axis=2)
    same = []
    for offset in range(1, 4):
        before = jnp.pad(segment, ((offset, 0), (0, 0)), constant_values=-1)[:count]
        same.append((before == segment).astype(f32))
    return same, (segment < DOCS).astype(f32)


def columns(weights, ways):
    rows, total = weights.shape
    return weights.reshape(rows, 2, total // (2 * ways * 128), ways, 128)


def on_device(tokens, lengths, gain, w_in, conv_w, conv_b, w_x, w_dt, dt_bias, skip, w_out, grad_out):
    ways = lax.axis_size("core") * lax.axis_size("z")
    groups = lax.axis_size("dp")
    length, model = tokens.shape[1:]
    own_d = w_in.shape[0]
    own_e = conv_w.shape[0]
    inner = w_in.shape[1] // 2
    channels = inner // ways
    rank = w_dt.shape[1]
    states = (w_x.shape[1] - rank) // 2
    cols = w_in.reshape(own_d, 2, groups, ways, own_e).transpose(3, 0, 1, 2, 4).reshape(ways, own_d, 2 * channels)
    cols = lax.all_to_all(cols, TP, split_axis=0, concat_axis=0, tiled=True)
    win = lax.all_gather(cols, "dp", axis=0, tiled=True).reshape(model, 2 * channels)
    small = jnp.concatenate([w_x, w_dt, conv_w, conv_b[:, None], dt_bias[:, None], skip[:, None]], axis=1)
    small_width = small.shape[1]
    small = lax.all_gather(small, "dp", axis=0, tiled=True)
    wx = small[:, :rank + 2 * states]
    wdt = small[:, rank + 2 * states:2 * rank + 2 * states]
    rest = small[:, 2 * rank + 2 * states:].astype(f32)
    taps, bias, dtb, skips = rest[:, :4], rest[:, 4], rest[:, 5], rest[:, 6]
    wout = lax.all_gather(w_out, "dp", axis=0, tiled=True)
    gains = lax.all_gather(gain, ALL, axis=0, tiled=True).astype(f32)
    x = tokens[0].astype(f32)
    scale = lax.rsqrt(jnp.mean(x * x, axis=1, keepdims=True) + EPS)
    xn = (x * scale * gains).astype(bf16)
    xns = lax.all_gather(xn, TP, axis=0, tiled=True)
    ups = lax.all_gather(grad_out[0], TP, axis=0, tiled=True)
    lens = lax.all_gather(lengths, TP, axis=0, tiled=True)
    rows = lens.shape[0]
    tall = rows * length

    def time_major(a):
        return a.reshape(rows, length, -1).transpose(1, 0, 2).reshape(tall, -1)

    def row_major(a):
        return a.reshape(length, rows, -1).transpose(1, 0, 2).reshape(tall, -1)

    same, live = masks(lens, length)
    zz = time_major(jnp.dot(xns, win, preferred_element_type=f32))
    u = zz[:, :channels].reshape(length, rows, channels)
    g = zz[:, channels:]
    c = bias + taps[:, 3] * u
    shifted = []
    for offset in range(1, 4):
        earlier = jnp.pad(u, ((offset, 0), (0, 0), (0, 0)))[:length] * same[offset - 1][:, :, None]
        shifted.append(earlier)
        c = c + taps[:, 3 - offset] * earlier
    sig = jax.nn.sigmoid(c)
    v16 = (c * sig).astype(bf16).reshape(tall, channels)
    v = v16.astype(f32)
    p = lax.psum(jnp.dot(v16, wx, preferred_element_type=f32), TP)
    dl = p[:, :rank].astype(bf16)
    kq = p[:, rank:]
    dims_cols = (((1,), (1,)), ((), ()))
    dims_rows = (((0,), (0,)), ((), ()))
    pre = lax.dot_general(dl, wdt, dims_cols, preferred_element_type=f32) + dtb
    dm = time_major(lax.dot_general(ups, wout, dims_cols, preferred_element_type=f32))
    flags = jnp.pad(jnp.stack([same[0].reshape(tall), live.reshape(tall)], axis=1), ((0, 0), (0, 126)))
    hi = kq.astype(bf16)
    mid = (kq - hi.astype(f32)).astype(bf16)
    low = (kq - hi.astype(f32) - mid.astype(f32)).astype(bf16)
    kq3 = jnp.concatenate([hi, mid, low], axis=1)
    keys = kq[:, :states]
    sk = jnp.broadcast_to(jnp.sum(keys * keys, axis=1, keepdims=True), (tall, 8))
    m, dg, dpre, dv, dkq, stats = mixer(flags, kq3, sk, pre, v, g, dm, skips[None], states=states, width=256, unroll=4)
    stats = stats.transpose(1, 2, 0, 3).reshape(3, 8, channels)
    dskip = jnp.sum(stats[0], axis=0)
    total = lax.psum(jnp.sum(stats[1]), ALL)
    peak = lax.pmax(jnp.max(stats[2]), ALL)
    beta_mean = total / float(groups * ways * length * inner)
    m16 = row_major(m).astype(bf16)
    out = jnp.dot(m16, wout, preferred_element_type=f32).astype(bf16)
    out = lax.psum_scatter(out, TP, scatter_dimension=0, tiled=True)
    block_out = (x + out.astype(f32)).astype(bf16)
    grad_wout = lax.dot_general(m16, ups, dims_rows, preferred_element_type=f32).astype(bf16)
    grad_wout = lax.psum_scatter(grad_wout, "dp", scatter_dimension=0, tiled=True)
    dpre16 = dpre.astype(bf16)
    grad_dtb = jnp.sum(dpre16.astype(f32), axis=0)
    grad_wdt = lax.dot_general(dpre16, dl, dims_rows, preferred_element_type=f32)
    ddl = jnp.dot(dpre16, wdt, preferred_element_type=f32)
    dkq = dkq[:, :2 * states] + dkq[:, 2 * states:2 * states + 1] * jnp.pad(keys, ((0, 0), (0, states)))
    dp16 = lax.psum(jnp.concatenate([ddl, dkq], axis=1), TP).astype(bf16)
    grad_wx = lax.dot_general(v16, dp16, dims_rows, preferred_element_type=f32)
    dvt = dv + lax.dot_general(dp16, wx, dims_cols, preferred_element_type=f32)
    dc = (dvt * (sig.reshape(tall, channels) * (1.0 + c.reshape(tall, channels) * (1.0 - sig.reshape(tall, channels))))).reshape(length, rows, channels)
    du = taps[:, 3] * dc
    grad_taps = [jnp.sum(dc * u, axis=(0, 1))]
    for offset in range(1, 4):
        grad_taps.append(jnp.sum(dc * shifted[offset - 1], axis=(0, 1)))
        du = du + taps[:, 3 - offset] * jnp.pad((dc * same[offset - 1][:, :, None])[offset:], ((0, offset), (0, 0), (0, 0)))
    grad_conv = jnp.stack(grad_taps[::-1] + [jnp.sum(dc, axis=(0, 1)), grad_dtb, dskip], axis=1)
    dz = row_major(jnp.concatenate([du.reshape(tall, channels), dg], axis=1)).astype(bf16)
    gwin = lax.dot_general(xns, dz, dims_rows, preferred_element_type=f32).astype(bf16)
    gwin = lax.psum_scatter(gwin, "dp", scatter_dimension=0, tiled=True)
    gwin = lax.all_to_all(gwin.reshape(ways, own_d, 2 * channels), TP, split_axis=0, concat_axis=0, tiled=True)
    grad_win = gwin.reshape(ways, own_d, 2, groups, own_e).transpose(1, 2, 3, 0, 4).reshape(own_d, 2 * inner).astype(f32)
    dxn = lax.dot_general(dz, win, dims_cols, preferred_element_type=f32).astype(bf16)
    dxn = lax.psum_scatter(dxn, TP, scatter_dimension=0, tiled=True).astype(f32)
    small_grad = lax.psum_scatter(jnp.concatenate([grad_wx, grad_wdt, grad_conv], axis=1), "dp", scatter_dimension=0, tiled=True)
    inner_grad = dxn * gains
    dxx = scale * inner_grad - x * (scale * scale * scale) * (jnp.sum(inner_grad * x, axis=1, keepdims=True) / model)
    grad_tokens = (grad_out[0].astype(f32) + dxx).astype(bf16)
    grad_gain = lax.psum_scatter(jnp.sum(dxn * x * scale, axis=0), ALL, scatter_dimension=0, tiled=True)
    at = rank + 2 * states
    return (
        block_out[None],
        grad_tokens[None],
        grad_gain,
        grad_win,
        small_grad[:, at + rank:at + rank + 4],
        small_grad[:, at + rank + 4],
        small_grad[:, :at],
        small_grad[:, at:at + rank],
        small_grad[:, at + rank + 5],
        small_grad[:, at + rank + 6],
        grad_wout.astype(f32),
        beta_mean,
        peak,
    )


def on_device_direct(tokens, lengths, gain, w_in, conv_w, conv_b, w_x, w_dt, dt_bias, skip, w_out, grad_out):
    groups, ways = 4, 8
    length, model = tokens.shape[1:]
    own_d = w_in.shape[0]
    own_e = conv_w.shape[0]
    inner = w_in.shape[1] // 2
    channels = inner // ways
    rank = w_dt.shape[1]
    states = (w_x.shape[1] - rank) // 2
    gain = gain[None]
    xnt, ups, win, wout, smalls, vecs, gains, masks, live, u, g, v, vt, slope, dl, kq = k1(
        tokens, grad_out, w_in, w_out, w_x.T, w_dt, gain, lengths, conv_w.T, conv_b[None], dt_bias[None], skip[None])
    acc, mt, dg, gwdt, ups, dv, part, stat = k2(dl, kq, smalls, vecs, masks, live, v, g, ups, wout, states)
    sums = k3(
        part, stat, smalls, vecs, gains, gwdt, masks, tokens, grad_out, acc, mt, dg, dv, slope, u, vt, xnt,
        win.reshape(groups, ways * own_d, 2 * channels), ups)
    block_out, grad_tokens, grad_gain, grad_win, convw, convb, gwx, gwdt, dtb, dskip, grad_wout, mean, peak = k4(
        float(groups * ways * length * inner), *sums, w_in, gain, rank + 2 * states)
    return (
        block_out, grad_tokens, grad_gain[0], grad_win, convw.T, convb[0], gwx.T, gwdt, dtb[0], dskip[0], grad_wout, mean[0, 0], peak[0, 0],
    )


def on_device_any(*args):
    if lax.axis_size("dp") == 4 and lax.axis_size("z") == 4:
        return on_device_direct(*args)
    return on_device(*args)


def solution(mesh):
    wide, narrow = mesh.devices.shape
    fine = Mesh(mesh.devices.reshape(wide // 2, 2, narrow), ALL)
    cut = (P(ALL, None), P(ALL))
    in_specs = (P(ALL, None, None), cut[0], cut[1], cut[0], cut[0], cut[1], cut[0], cut[0], cut[1], cut[1], cut[0], P(ALL, None, None))
    out_specs = (P(ALL, None, None), P(ALL, None, None), cut[1], cut[0], cut[0], cut[1], cut[0], cut[0], cut[1], cut[1], cut[0], P(), P())
    return jax.shard_map(on_device_any, mesh=fine, in_specs=in_specs, out_specs=out_specs, check_vma=False)
```

```python
import functools
import jax, jax.numpy as jnp
from jax import lax
from jax.experimental import pallas as pl
from jax.experimental.pallas import tpu as pltpu
from jax.sharding import Mesh, PartitionSpec as P

DOCS = 4
EPS = 1e-05
ALL = ("dp", "core", "z")
TP = ("core", "z")

f32 = jnp.float32
bf16 = jnp.bfloat16

def fold(x):
    total = x[:, :128]
    for at in range(128, x.shape[1], 128):
        total = total + x[:, at:at+128]
    return total

def mixer_kernel(states, unroll, chunk, flags_ref, kq3_ref, sk_ref, pre_ref, v_ref, g_ref, dm_ref, skip_ref,
                 m_ref, dg_ref, dpre_ref, dv_ref, dkq_ref, stat_ref, s_ref, h_ref, rate_ref, rv_ref, kb_ref, drr_ref):
    rows = pre_ref.shape[0]
    width = pre_ref.shape[1]
    steps = rows // 8
    wide = states * 128
    spread_rows = kq3_ref.shape[1]
    def spread(i, c):
        r = pl.ds(pl.multiple_of(i * chunk, chunk), chunk)
        left = kq3_ref[r, :]
        for part in range(0, 2 * wide, 512):
            ids = lax.broadcasted_iota(jnp.int32, (spread_rows, 512), 0) % (2 * states)
            col = lax.broadcasted_iota(jnp.int32, (spread_rows, 512), 1) // 128 + part // 128
            hot = jnp.where(ids == col, 1.0, 0.0).astype(bf16)
            kb_ref[r, part:part+512] = jnp.dot(left, hot, preferred_element_type=f32)
        return c
    lax.fori_loop(0, rows // chunk, spread, 0)

    def before(i, c):
        r = pl.ds(pl.multiple_of(i * 64, 64), 64)
        live = flags_ref[r, 1:2]
        beta = jax.nn.sigmoid(pre_ref[r, :])
        part = 1.0 / (1.0 + beta * sk_ref[r, 0:1])
        rate = beta * part
        rate_ref[r, :] = rate
        v = v_ref[r, :]
        rv_ref[r, :] = rate * v
        dpre_ref[r, :] = part * part * beta * (1.0 - beta)
        g = g_ref[r, :]
        sg = jax.nn.sigmoid(g)
        dm = dm_ref[r, :] * live
        dv_ref[r, :] = dm * (g * sg)
        dg_ref[r, :] = dm * (sg * (1.0 + g * (1.0 - sg)))
        return c
    lax.fori_loop(0, rows // 64, before, 0)

    s_ref[0, 0] = jnp.zeros(s_ref.shape[2:], f32)

    group = unroll
    tile = lambda x: jnp.concatenate([x] * (width // 128), axis=1)
    span = group * 8
    at = [slice(j * 8, j * 8 + 8) for j in range(group)]
    def view(ref, i):
        return ref.at[pl.ds(pl.multiple_of(i * span, span), span)]

    def forward(i, carry):
        flags, rates, rvs, vs, kbs, ms = [view(x, i) for x in (flags_ref, rate_ref, rv_ref, v_ref, kb_ref, m_ref)]
        keep = [jnp.broadcast_to(flags[r, 0:1], (8, 128)) for r in at]
        rate = [rates[r, :] for r in at]
        rv = [rvs[r, :] for r in at]
        y = [skip_ref[...] * vs[r, :] for r in at]
        for n in range(states):
            state = s_ref[i, 0, n]
            for j, r in enumerate(at):
                kb = kbs[r, n*128:(n+1)*128]
                qb = kbs[r, wide+n*128:wide+(n+1)*128]
                state = (tile(keep[j]) - rate[j] * tile(kb * kb * keep[j])) * state + rv[j] * tile(kb)
                if j < group - 1:
                    s_ref[i, j + 1, n] = state
                else:
                    s_ref[i + 1, 0, n] = state
                y[j] = y[j] + state * tile(qb)
        for j, r in enumerate(at):
            ms[r, :] = y[j]
        return carry

    lax.fori_loop(0, steps // group, forward, 0)
    h_ref[...] = jnp.zeros_like(h_ref)

    def backward(step, carry):
        i = steps // group - 1 - step
        flags, rates, rvs, vs, kbs, dvs, dpres, drrs = [view(x, i) for x in (flags_ref, rate_ref, rv_ref, v_ref, kb_ref, dv_ref, dpre_ref, drr_ref)]
        keep = [jnp.broadcast_to(flags[r, 0:1], (8, 128)) for r in at]
        rate = [rates[r, :] for r in at]
        rv = [rvs[r, :] for r in at]
        dy = [dvs[r, :] for r in at]
        hk = [jnp.zeros((8, width), f32) for r in at]
        hs2 = [jnp.zeros((8, width), f32) for r in at]
        for n in range(states):
            ah = h_ref[n]
            after_ = s_ref[i + 1, 0, n]
            for j in range(group - 1, -1, -1):
                r = at[j]
                kb = kbs[r, n*128:(n+1)*128]
                qb = kbs[r, wide+n*128:wide+(n+1)*128]
                kk = kb * keep[j]
                held = tile(kb * kk)
                h = dy[j] * tile(qb) + ah
                prior = s_ref[i, j, n]
                hs = h * prior
                hk[j] = hk[j] + h * tile(kb)
                hs2[j] = hs2[j] + hs * held
                kbs[r, n*128:(n+1)*128] = fold(h * rv[j]) - 2.0 * kk * fold(hs * rate[j])
                kbs[r, wide+n*128:wide+(n+1)*128] = fold(dy[j] * after_)
                after_ = prior
                ah = (tile(keep[j]) - rate[j] * held) * h
            h_ref[n] = ah
        for j, r in enumerate(at):
            v = vs[r, :]
            drate = v * hk[j] - hs2[j]
            drrs[r, :] = fold(drate * rate[j] * rate[j]) * (-2.0)
            dpres[r, :] = drate * dpres[r, :]
            dvs[r, :] = rate[j] * hk[j] + skip_ref[...] * dy[j]
            stat_ref[0, 0] += dy[j] * v
        return carry

    stat_ref[...] = jnp.zeros_like(stat_ref)
    lax.fori_loop(0, steps // group, backward, 0)

    first = pl.program_id(0) == 0
    def gather(i, c):
        r = pl.ds(pl.multiple_of(i * chunk, chunk), chunk)
        total = jnp.zeros((chunk, 128), f32)
        for part in range(0, 2 * wide, 512):
            row = lax.broadcasted_iota(jnp.int32, (512, 128), 0) // 128 + part // 128
            col = lax.broadcasted_iota(jnp.int32, (512, 128), 1)
            hot = jnp.where(row == col, 1.0, 0.0).astype(bf16)
            total += jnp.dot(kb_ref[r, part:part+512].astype(bf16), hot, preferred_element_type=f32)
        col = lax.broadcasted_iota(jnp.int32, (128, 128), 1)
        hot = jnp.where(col == 2 * states, 1.0, 0.0).astype(bf16)
        total += jnp.dot(drr_ref[r, :].astype(bf16), hot, preferred_element_type=f32)
        dkq_ref[r, :] = jnp.where(first, total, dkq_ref[r, :] + total)
        return c
    lax.fori_loop(0, rows // chunk, gather, 0)

    def after(i, c):
        r = pl.ds(pl.multiple_of(i * 64, 64), 64)
        live = flags_ref[r, 1:2]
        y = m_ref[r, :]
        g = g_ref[r, :]
        m_ref[r, :] = y * (g * jax.nn.sigmoid(g)) * live
        dg_ref[r, :] = y * dg_ref[r, :]
        shown = (jax.nn.sigmoid(pre_ref[r, :]) * live).reshape(8, 8, width)
        stat_ref[0, 1] += jnp.sum(shown, axis=0)
        stat_ref[0, 2] = jnp.maximum(stat_ref[0, 2], jnp.max(shown, axis=0))
        return c
    lax.fori_loop(0, rows // 64, after, 0)

def mixer(flags, kq3, sk, pre, v, g, dm, skip, states=16, width=256, unroll=1):
    rows, total = pre.shape
    steps = rows // 8
    tiles = total // width
    big = jax.ShapeDtypeStruct((rows, total), f32)
    cut = pl.BlockSpec((rows, width), lambda h: (0, h))
    whole = lambda a: pl.BlockSpec(a.shape, lambda h: (0,) * a.ndim)
    return pl.pallas_call(
        functools.partial(mixer_kernel, states, unroll, min(256, rows)),
        grid=(tiles,),
        out_shape=(big, big, big, big, jax.ShapeDtypeStruct((rows, 128), f32), jax.ShapeDtypeStruct((tiles, 3, 8, width), f32)),
        in_specs=[whole(flags), whole(kq3), whole(sk), cut, cut, cut, cut, pl.BlockSpec((1, width), lambda h: (0, h))],
        out_specs=(cut, cut, cut, cut, pl.BlockSpec((rows, 128), lambda h: (0, 0)), pl.BlockSpec((1, 3, 8, width), lambda h: (h, 0, 0, 0))),
        scratch_shapes=[pltpu.VMEM((steps//unroll+1, unroll, states, 8, width), f32), pltpu.VMEM((states, 8, width), f32)] + [pltpu.VMEM((rows, width), f32)]*2
          + [pltpu.VMEM((rows, 2*states*128), f32), pltpu.VMEM((rows, 128), f32)],
        compiler_params=pltpu.CompilerParams(vmem_limit_bytes=60*1024*1024),
    )(flags, kq3, sk, pre, v, g, dm, skip)


MESH = pl.DeviceIdType.MESH


def flip(value, bit):
    return value + bit * (1 - 2 * ((value // bit) % 2))


def place():
    d, c, z = lax.axis_index("dp"), lax.axis_index("core"), lax.axis_index("z")
    return d, c, z


def put(src, dst, send, recv, device):
    copy = pltpu.make_async_remote_copy(src_ref=src, dst_ref=dst, send_sem=send, recv_sem=recv, device_id=device, device_id_type=MESH)
    copy.start()
    return copy


def landed(slot, sem, device):
    pltpu.make_async_remote_copy(src_ref=slot, dst_ref=slot, send_sem=sem, recv_sem=sem, device_id=device, device_id_type=MESH).wait_recv()


def sent(slot, sem, device):
    pltpu.make_async_remote_copy(src_ref=slot, dst_ref=slot, send_sem=sem, recv_sem=sem, device_id=device, device_id_type=MESH).wait_send()


def greet(devices):
    barrier = pltpu.get_barrier_semaphore()
    for device in devices:
        pl.semaphore_signal(barrier, inc=1, device_id=device, device_id_type=MESH)
    pl.semaphore_wait(barrier, len(devices))


def mates():
    return [(a, k) for k in (0, 1, 3, 2) for a in (1, 0) if (a, k) != (0, 0)]


def mate(step, sign=1):
    d, c, z = place()
    a, k = step
    return d, (flip(c, 1) if a else c), lax.rem(z + sign * k + 4, 4)


def rank_of(device):
    return device[1] * 4 + device[2]


PIECES = 4


UP_HOPS = 2
LINE1 = bf16
LINE2 = bf16


def k1_kernel(tok_ref, up_ref, w_ref, wout_ref, wx_ref, wdt_ref, gain_ref, lens_ref, convw_ref, convb_ref, dtb_ref, skip_ref,
              xnt_out, ups_ref, win_out, wouts_ref, smalls_ref, vecs_ref, gains_ref, masks_out, live_out,
              u_out, g_out, v_out, vt_out, slope_out, dl_ref, kq_ref,
              masks_ref, live_ref, u_ref, g_ref, v_ref, vt_ref, slope_ref, save_sem, cols_ref, meta_ref, small_ref,
              xs_ref, xn_ref, xnt_ref, win_ref, metas_ref, part_ref, out_ref, sib_ref, base_ref, left_ref, right_ref, tor_ref, tol_ref,
              own_sem, ms, mr, qs, qr, xls, xlr, xrs, xrr, xcs, xcr, as_, ar, ps, pr, rs, rr, ws, wr, ts, tr, tls, tlr, trs, trr, tos, tor):
    d, c, z = place()
    j = c * 4 + z
    dx, dy, dd = flip(d, 1), flip(d, 2), flip(flip(d, 1), 2)
    xn, yn, dn = (dx, c, z), (dy, c, z), (dd, c, z)
    sib = (d, flip(c, 1), z)
    left = (d, c, lax.rem(z + 3, 4))
    right = (d, c, lax.rem(z + 1, 4))
    steps = mates()
    length = tok_ref.shape[1]
    model = tok_ref.shape[2]
    depth = cols_ref.shape[1]
    for rank in range(8):
        for n in range(8):
            cols_ref[rank, :, n * 128:(n + 1) * 128] = w_ref[:, (n * 8 + rank) * 128:(n * 8 + rank + 1) * 128]
    meta_ref[...] = jnp.zeros_like(meta_ref)
    meta_ref[0:1, 0:depth] = gain_ref[...].astype(f32)
    meta_ref[0:1, depth:2 * depth] = gain_ref[...].astype(f32)
    meta_ref[1:2, 0:5] = lens_ref[...].astype(f32)
    meta_ref[8:12, :] = convw_ref[...].astype(f32)
    meta_ref[12:13, :] = convb_ref[...].astype(f32)
    meta_ref[13:14, :] = dtb_ref[...].astype(f32)
    meta_ref[14:15, :] = skip_ref[...].astype(f32)
    narrow_rows = wx_ref.shape[0]
    small_ref[:, 0:128] = wx_ref[0:128, :].astype(f32).T.astype(bf16)
    tail = jnp.concatenate([wx_ref[128:narrow_rows, :].astype(f32), jnp.zeros((256 - narrow_rows, 128), f32)], axis=0)
    small_ref[:, 128:256] = tail.T.astype(bf16)
    small_ref[:, 256:384] = wdt_ref[...]
    greet([mate(s) for s in steps] + [xn, yn, dn])
    tiles = u_ref.shape[0]
    width = tiles * 128
    count = g_ref.shape[1]

    def rows(rank):
        return pl.ds(pl.multiple_of(rank * length, length), length)

    def block(group, rank):
        return pl.ds(pl.multiple_of((group * 8 + rank) * depth, depth), depth)

    own_e = wout_ref.shape[0]
    half_w = cols_ref.shape[2] // 2

    def part_w(q):
        return pl.ds(q * half_w, half_w)

    def part_e(group, start=0, size=own_e):
        return pl.ds(pl.multiple_of(group * own_e + start, 16), size)

    own = [
        pltpu.make_async_copy(tok_ref.at[0], xs_ref.at[rows(j)], own_sem.at[0]),
        pltpu.make_async_copy(up_ref.at[0], ups_ref.at[rows(j)], own_sem.at[1]),
        pltpu.make_async_copy(cols_ref.at[j], win_ref.at[block(d, j)], own_sem.at[2]),
        pltpu.make_async_copy(wout_ref, wouts_ref.at[part_e(d)], own_sem.at[3]),
        pltpu.make_async_copy(small_ref, smalls_ref.at[part_e(d)], own_sem.at[4]),
        pltpu.make_async_copy(meta_ref, metas_ref.at[d, j], own_sem.at[5]),
    ]
    for copy in own:
        copy.start()
    pending = []
    for i, s in enumerate(steps):
        to = mate(s)
        pending.append(put(meta_ref, metas_ref.at[d, j], ms.at[i], mr.at[i], to))
    for i, s in enumerate(steps):
        to = mate(s)
        pending.append(put(cols_ref.at[rank_of(to), :, part_w(0)], win_ref.at[block(d, j), part_w(0)], as_.at[i], ar.at[i], to))
    for i, to in enumerate((xn, yn, dn)):
        pending.append(put(small_ref, smalls_ref.at[part_e(d)], ps.at[32 + i], pr.at[32 + i], to))
    halves = own_e // 2
    pending.append(put(wout_ref, wouts_ref.at[part_e(d)], ws.at[0], wr.at[0], xn))
    pending.append(put(wout_ref, wouts_ref.at[part_e(d)], ws.at[1], wr.at[1], yn))
    own[2].wait()

    def own_part(q):
        slot = win_ref.at[block(d, j), part_w(q)]
        pending.append(put(slot, slot, ps.at[16 * q + 7], pr.at[16 * q + 7], xn))
        pending.append(put(slot, slot, ps.at[16 * q + 15], pr.at[16 * q + 15], yn))

    own_part(0)

    def row_start(ref, out, base):
        pending.append(put(ref.at[0], out.at[rows(j)], xcs.at[base + z], xcr.at[base + z], sib))

        @pl.when(z < 3)
        def _():
            put(ref.at[0], out.at[rows(j)], xls.at[base], xlr.at[base], right)

        @pl.when(z > 0)
        def _():
            put(ref.at[0], out.at[rows(j)], xrs.at[base], xrr.at[base], left)

    def row_hop(out, base, i, then=None, hops=3):
        if i >= hops:
            return

        @pl.when(z > i)
        def _():
            at = z - 1 - i
            slot = out.at[rows(c * 4 + at)]
            landed(slot, xlr.at[base + i], left)
            if i < hops - 1:
                @pl.when(z < 3)
                def _():
                    put(slot, slot, xls.at[base + i + 1], xlr.at[base + i + 1], right)
            put(slot, slot, xcs.at[base + at], xcr.at[base + at], sib)
            if then is not None:
                then(c * 4 + at)

        @pl.when(z < 3 - i)
        def _():
            at = z + 1 + i
            slot = out.at[rows(c * 4 + at)]
            landed(slot, xrr.at[base + i], right)
            if i < hops - 1:
                @pl.when(z > 0)
                def _():
                    put(slot, slot, xrs.at[base + i + 1], xrr.at[base + i + 1], left)
            put(slot, slot, xcs.at[base + at], xcr.at[base + at], sib)
            if then is not None:
                then(c * 4 + at)

    def row_end(out, base, hops=3):
        for i in range(hops):
            @pl.when((z < 3) & (z >= i))
            def _():
                sent(out.at[rows(j)], xls.at[base + i], right)

            @pl.when((z > 0) & (z <= 3 - i))
            def _():
                sent(out.at[rows(j)], xrs.at[base + i], left)
        for at in range(4):
            @pl.when((z != at) & (z <= at + hops) & (at <= z + hops))
            def _():
                sent(out.at[rows(j)], xcs.at[base + at], sib)

    row_start(tok_ref, xs_ref, 0)
    own[5].wait()
    for i, s in enumerate(steps):
        landed(metas_ref.at[d, rank_of(mate(s, -1))], mr.at[i], xn)
    for i, to in enumerate((xn, yn, dn)):
        pending.append(put(metas_ref.at[d], metas_ref.at[d], qs.at[i], qr.at[i], to))
    slots = {7: j}
    for i, s in enumerate(steps):
        slots[i] = rank_of(mate(s, -1))
    order = [7] + list(range(7))

    def pass_on(i, q):
        src = mate(steps[i], -1)
        slot = win_ref.at[block(d, slots[i]), part_w(q)]
        landed(slot, ar.at[7 * q + i], src)
        pending.append(put(slot, slot, ps.at[16 * q + i], pr.at[16 * q + i], xn))
        pending.append(put(slot, slot, ps.at[16 * q + 8 + i], pr.at[16 * q + 8 + i], yn))

    def relay(k, q):
        i = order[k]
        slot = win_ref.at[block(dx, slots[i]), part_w(q)]
        landed(slot, pr.at[16 * q + i], xn)
        if k % 2 == 0:
            pending.append(put(slot, slot, rs.at[8 * q + k // 2], rr.at[8 * q + k // 2], yn))
        slot = win_ref.at[block(dy, slots[i]), part_w(q)]
        landed(slot, pr.at[16 * q + 8 + i], yn)
        if k % 2 == 1:
            pending.append(put(slot, slot, rs.at[8 * q + 4 + k // 2], rr.at[8 * q + 4 + k // 2], xn))

    def relayed(q):
        for k, i in enumerate(order):
            slot = win_ref.at[block(dd, slots[i]), part_w(q)]
            if k % 2 == 0:
                landed(slot, rr.at[8 * q + k // 2], yn)
            else:
                landed(slot, rr.at[8 * q + 4 + k // 2], xn)

    pass_on(0, 0)
    for i, (to, at) in enumerate(((xn, dx), (yn, dy), (dn, dd))):
        landed(metas_ref.at[at], qr.at[i], to)
    lens = jnp.concatenate([metas_ref[d, r, 1:2, :] for r in range(8)], axis=0)
    ends = []
    last = jnp.zeros((8, 1), f32)
    for i in range(5):
        last = last + lens[:, i:i + 1]
        ends.append(jnp.broadcast_to(last, (8, 128)))

    def mask_step(t, carry):
        here = t.astype(f32)

        def segment(at):
            total = jnp.zeros((8, 128), f32)
            for end in ends:
                total = total + jnp.where(end <= at, 1.0, 0.0)
            return total

        now = segment(here)
        r = pl.ds(pl.multiple_of(t * 8, 8), 8)
        for o in range(1, 4):
            same = jnp.where(segment(here - o) == now, 1.0, 0.0)
            masks_ref[o - 1, r, :] = jnp.where(here >= o, same, 0.0)
        live_ref[0, r, :] = jnp.where(now < DOCS, 1.0, 0.0)
        return carry

    lax.fori_loop(0, length, mask_step, 0)
    masks_ref[:, count:, :] = jnp.zeros((3, masks_ref.shape[1] - count, 128), f32)
    lane = lax.broadcasted_iota(jnp.int32, (1, 128), 1)
    for group in range(4):
        for pair in range(4):
            at = group * 512 + pair * 128
            gains_ref[:, at:at + 128] = jnp.where(lane < depth, metas_ref[group, 2 * pair, 0:1, :], metas_ref[group, 2 * pair + 1, 0:1, :])
        vecs_ref[:, group * own_e:(group + 1) * own_e] = metas_ref[group, j, 8:16, :]

    def normalize(rank):
        def body(i, carry):
            r = pl.ds(pl.multiple_of(rank * length + i * 16, 16), 16)
            x = xs_ref[r, :].astype(f32)
            scale = lax.rsqrt(jnp.sum(x * x, axis=1, keepdims=True) * (1.0 / model) + EPS)
            xn_ref[r, :] = (x * scale * gains_ref[...]).astype(bf16)
            return carry

        lax.fori_loop(0, length // 16, body, 0, unroll=4)

    for i in range(1, 4):
        pass_on(i, 0)
    slot = wouts_ref.at[part_e(dx)]
    landed(slot, wr.at[0], xn)
    slot = wouts_ref.at[part_e(dx, 0, halves)]
    pending.append(put(slot, slot, ws.at[2], wr.at[2], yn))
    slot = wouts_ref.at[part_e(dy)]
    landed(slot, wr.at[1], yn)
    slot = wouts_ref.at[part_e(dy, halves, halves)]
    pending.append(put(slot, slot, ws.at[3], wr.at[3], xn))

    for i in range(4, 7):
        pass_on(i, 0)
    own[0].wait()
    normalize(j)
    row_hop(xs_ref, 0, 0, normalize)
    for i, s in enumerate(steps):
        to = mate(s)
        pending.append(put(cols_ref.at[rank_of(to), :, part_w(1)], win_ref.at[block(d, j), part_w(1)], as_.at[7 + i], ar.at[7 + i], to))
    own_part(1)
    for k in range(8):
        relay(k, 0)
    row_hop(xs_ref, 0, 1, normalize)
    for i in range(7):
        pass_on(i, 1)
    row_start(up_ref, ups_ref, 4)
    row_hop(xs_ref, 0, 2, normalize)
    for at in range(4):
        rank = flip(c, 1) * 4 + at
        landed(xs_ref.at[rows(rank)], xcr.at[at], sib)
        normalize(rank)
    relayed(0)
    own += [pltpu.make_async_copy(xnt_ref, xnt_out, own_sem.at[6]), pltpu.make_async_copy(win_ref, win_out, own_sem.at[7])]
    lead = u_ref.shape[1] - count
    u_ref[:, 0:lead, :] = jnp.zeros((tiles, lead, 128), f32)

    tile = 256

    def spread(out, first, start):
        def body(i, carry):
            product = jnp.dot(xn_ref[...], win_ref[:, pl.ds(pl.multiple_of(start + i * tile, tile), tile)], preferred_element_type=f32)
            for r in range(8):
                for part in range(0, tile, 128):
                    out[i * (tile // 128) + part // 128, pl.ds(first + r, length, stride=8), :] = product[r * length:(r + 1) * length, part:part + 128]
            return carry

        lax.fori_loop(0, width // tile, body, 0)

    spread(u_ref, lead, 0)
    taps = [vecs_ref[o:o + 1, :] for o in range(4)]
    bias = vecs_ref[4:5, :]

    def conv_step(i, carry):
        r = pl.ds(pl.multiple_of(i * 32, 32), 32)
        for n in range(tiles):
            lanes = slice(n * 128, n * 128 + 128)
            total = bias[:, lanes] + taps[3][:, lanes] * u_ref[n, pl.ds(pl.multiple_of(lead + i * 32, 8), 32), :]
            for o in range(1, 4):
                total = total + taps[3 - o][:, lanes] * (u_ref[n, pl.ds(pl.multiple_of(lead + i * 32 - 8 * o, 8), 32), :] * masks_ref[o - 1, r, :])
            sig = jax.nn.sigmoid(total)
            v_ref[n, r, :] = (total * sig).astype(bf16).astype(f32)
            slope_ref[n, r, :] = sig * (1.0 + total * (1.0 - sig))
        return carry

    lax.fori_loop(0, count // 32, conv_step, 0, unroll=2)
    for k in range(8):
        relay(k, 1)
    for copy in own[3:5]:
        copy.wait()
    for i, (to, at) in enumerate(((xn, dx), (yn, dy), (dn, dd))):
        landed(smalls_ref.at[part_e(at)], pr.at[32 + i], to)
    quarter = count // 4
    narrow = smalls_ref[:, 128:256].astype(f32)
    packed = jnp.zeros((quarter, 128), f32)
    for b in range(4):
        r = slice(b * quarter, (b + 1) * quarter)
        values = jnp.concatenate([v_ref[n, r, :].astype(bf16) for n in range(tiles)], axis=1)
        part_ref[r, :] = jnp.dot(values, smalls_ref[:, 0:128], preferred_element_type=f32)
        turned = pltpu.roll(narrow, 32 * b, 1) if b else narrow
        packed = packed + jnp.dot(values, turned.astype(bf16), preferred_element_type=f32)
    part_ref[count:count + quarter, :] = packed
    saves = [(u_ref, u_out), (v_ref, v_out), (slope_ref, slope_out), (masks_ref, masks_out), (live_ref, live_out), (g_ref, g_out), (vt_ref, vt_out)]
    saves = [pltpu.make_async_copy(a, b, save_sem.at[i]) for i, (a, b) in enumerate(saves)]
    for copy in saves[:5]:
        copy.start()

    def early():
        row_hop(ups_ref, 4, 0, None, UP_HOPS)

    def between():
        relayed(1)
        own[7].start()
        spread(g_ref, 0, width)
        saves[5].start()

    def late():
        def turn_x(i, carry):
            part = pl.ds(pl.multiple_of(i * 128, 128), 128)
            for rank in range(8):
                r = slice(rank * length, (rank + 1) * length)
                xnt_ref[part, r] = xn_ref[r, part].T
            return carry

        lax.fori_loop(0, model // 128, turn_x, 0)
        own[6].start()
        row_hop(ups_ref, 4, 1, None, UP_HOPS)

        def turn_v(i, carry):
            r = pl.ds(pl.multiple_of(i * 128, 128), 128)
            for n in range(tiles):
                vt_ref[n * 128:(n + 1) * 128, r] = v_ref[n, r, :].T.astype(bf16)
            return carry

        lax.fori_loop(0, count // 128, turn_v, 0)
        saves[6].start()

    line_total(part_ref, out_ref, sib_ref, base_ref, left_ref, right_ref, tor_ref, tol_ref, ts, tr, tls, tlr, trs, trr, tos, tor, early, between, late)
    dl_ref[...] = out_ref[0:count, :].astype(bf16)
    for b in range(4):
        packed = out_ref[count:count + quarter, :]
        kq_ref[b * quarter:(b + 1) * quarter, :] = pltpu.roll(packed, 128 - 32 * b, 1) if b else packed
    row_hop(ups_ref, 4, 2, None, UP_HOPS)
    for at in range(4):
        @pl.when((z <= at + UP_HOPS) & (at <= z + UP_HOPS))
        def _():
            landed(ups_ref.at[rows(flip(c, 1) * 4 + at)], xcr.at[4 + at], sib)

    landed(wouts_ref.at[part_e(dd, 0, halves)], wr.at[2], yn)
    landed(wouts_ref.at[part_e(dd, halves, halves)], wr.at[3], xn)
    row_end(xs_ref, 0)
    row_end(ups_ref, 4, UP_HOPS)
    own[1].wait()
    for copy in saves:
        copy.wait()
    own[6].wait()
    own[7].wait()
    for copy in pending:
        copy.wait_send()


def line_total(part_ref, out_ref, sib_ref, base_ref, left_ref, right_ref, tor_ref, tol_ref, ss, sr, ls, lr, rs, rr, os_, or_, early, between, late):
    d, c, z = place()
    sib = (d, flip(c, 1), z)
    left = (d, c, lax.rem(z + 3, 4))
    right = (d, c, lax.rem(z + 1, 4))
    rows = part_ref.shape[0] // 2
    piece = rows // PIECES
    mine, theirs = c * rows, flip(c, 1) * rows

    def cut(p):
        return pl.ds(p * piece, piece)

    def far(base, p):
        return pl.ds(pl.multiple_of(base + p * piece, 8), piece)

    for p in range(PIECES):
        put(part_ref.at[far(theirs, p)], sib_ref.at[cut(p)], ss.at[p], sr.at[p], sib)
    for p in range(PIECES):
        landed(sib_ref.at[cut(p)], sr.at[p], sib)
        value = part_ref[far(mine, p), :] + sib_ref[cut(p), :]
        out_ref[far(mine, p), :] = value
        base_ref[cut(p), :] = value.astype(base_ref.dtype)

        @pl.when(z == 0)
        def _():
            put(base_ref.at[cut(p)], left_ref.at[cut(p)], rs.at[p], lr.at[p], right)

        @pl.when(z == 3)
        def _():
            put(base_ref.at[cut(p)], right_ref.at[cut(p)], ls.at[p], rr.at[p], left)

    early()

    def from_left(p):
        landed(left_ref.at[cut(p)], lr.at[p], left)

        @pl.when(z < 3)
        def _():
            tor_ref[cut(p), :] = (out_ref[far(mine, p), :] + left_ref[cut(p), :].astype(f32)).astype(tor_ref.dtype)
            put(tor_ref.at[cut(p)], left_ref.at[cut(p)], rs.at[p], lr.at[p], right)

    def from_right(p):
        landed(right_ref.at[cut(p)], rr.at[p], right)

        @pl.when(z > 0)
        def _():
            tol_ref[cut(p), :] = (out_ref[far(mine, p), :] + right_ref[cut(p), :].astype(f32)).astype(tol_ref.dtype)
            put(tol_ref.at[cut(p)], right_ref.at[cut(p)], ls.at[p], rr.at[p], left)

    @pl.when(z == 1)
    def _():
        for p in range(PIECES):
            from_left(p)

    @pl.when(z == 2)
    def _():
        for p in range(PIECES):
            from_right(p)

    between()

    @pl.when(z < 2)
    def _():
        for p in range(PIECES):
            from_right(p)

    @pl.when(z >= 2)
    def _():
        for p in range(PIECES):
            from_left(p)

    for p in range(PIECES):
        @pl.when(z > 0)
        def _():
            out_ref[far(mine, p), :] += left_ref[cut(p), :].astype(f32)

        @pl.when(z < 3)
        def _():
            out_ref[far(mine, p), :] += right_ref[cut(p), :].astype(f32)

        put(out_ref.at[far(mine, p)], out_ref.at[far(mine, p)], os_.at[p], or_.at[p], sib)
    late()
    for p in range(PIECES):
        landed(out_ref.at[far(theirs, p)], or_.at[p], sib)
        sent(out_ref.at[far(mine, p)], os_.at[p], sib)
        sent(part_ref.at[far(theirs, p)], ss.at[p], sib)

        @pl.when(z < 3)
        def _():
            sent(base_ref.at[cut(p)], rs.at[p], right)

        @pl.when(z > 0)
        def _():
            sent(base_ref.at[cut(p)], ls.at[p], left)


def k1(tokens, upstream, w_in, w_out, w_x, w_dt, gain, lengths, conv_w, conv_b, dt_bias, skip):
    groups, ways = 4, 8
    small = jax.ShapeDtypeStruct((128, 384), bf16)
    cols = jax.ShapeDtypeStruct((ways, w_in.shape[0], w_in.shape[1] // ways), bf16)
    meta = jax.ShapeDtypeStruct((16, 128), f32)
    like = jax.ShapeDtypeStruct
    length, model = tokens.shape[1:]
    count = ways * length
    channels = groups * w_out.shape[0]
    dma = lambda n: pltpu.SemaphoreType.DMA((n,))
    some = pl.BlockSpec(memory_space=pl.ANY)
    far = pl.BlockSpec(memory_space=pltpu.HBM)
    here = pl.BlockSpec(memory_space=pltpu.VMEM)
    packed = count + count // 4
    return pl.pallas_call(
        k1_kernel,
        out_shape=(
            like((model, count), bf16),
            like((count, model), bf16),
            like((groups * ways * cols.shape[1], cols.shape[2]), bf16),
            like((channels, model), bf16),
            like((channels, small.shape[1]), bf16),
            like((8, channels), f32),
            like((1, model), f32),
            like((3, count + 32, 128), f32),
            like((1, count, 128), f32),
            like((channels // 128, count + 24, 128), f32),
            like((channels // 128, count, 128), f32),
            like((channels // 128, count, 128), f32),
            like((channels, count), bf16),
            like((channels // 128, count, 128), f32),
            like((count, 128), bf16),
            like((count, 128), f32),
        ),
        in_specs=[some] * 2 + [here, some] + [here] * 8,
        out_specs=(far,) * 4 + (here,) * 3 + (far,) * 7 + (here,) * 2,
        scratch_shapes=[
            pltpu.VMEM((3, count + 32, 128), f32),
            pltpu.VMEM((1, count, 128), f32),
            pltpu.VMEM((channels // 128, count + 24, 128), f32),
            pltpu.VMEM((channels // 128, count, 128), f32),
            pltpu.VMEM((channels // 128, count, 128), f32),
            pltpu.VMEM((channels, count), bf16),
            pltpu.VMEM((channels // 128, count, 128), f32),
            dma(7),
            pltpu.VMEM(cols.shape, bf16),
            pltpu.VMEM(meta.shape, f32),
            pltpu.VMEM(small.shape, bf16),
            pltpu.VMEM((count, model), bf16),
            pltpu.VMEM((count, model), bf16),
            pltpu.VMEM((model, count), bf16),
            pltpu.VMEM((groups * ways * cols.shape[1], cols.shape[2]), bf16),
            pltpu.VMEM((groups, ways) + meta.shape, f32),
            pltpu.VMEM((packed, 128), f32),
            pltpu.VMEM((packed, 128), f32),
        ] + [pltpu.VMEM((packed // 2, 128), f32)] + [pltpu.VMEM((packed // 2, 128), LINE1)] * 5
        + [dma(8), dma(7), dma(7), dma(3), dma(3), dma(8), dma(8), dma(8), dma(8), dma(8), dma(8), dma(14), dma(14), dma(35), dma(35), dma(16), dma(16), dma(4), dma(4)]
        + [dma(PIECES) for _ in range(8)],
        compiler_params=pltpu.CompilerParams(collective_id=0, has_side_effects=True, vmem_limit_bytes=56 * 1024 * 1024),
    )(tokens, upstream, w_in, w_out, w_x, w_dt, gain, lengths, conv_w, conv_b, dt_bias, skip)


GROUP = 4


def k2_kernel(states, dl_ref, kq_ref, wdt_ref, vecs_ref, keep_ref, live_ref, v_ref, g_ref, ups_any, wout_any,
              acc_out, mt_ref, dg_ref, gwdt_ref, ups_out, dv_ref, part_ref, stat_ref,
              ups_ref, loads, stores, zs, zr, cs, cr, ls, lr, ss, sr, m_ref, wout_ref, acc_ref, recv_ref, dpre_ref, s_ref, h_ref, rate_ref, w_ref, y_ref, dm_ref, kb_ref, hot_ref, drr_ref):
    tiles, count = v_ref.shape[:2]
    steps = count // 8
    wide = states * 128
    chunk = 256
    first = pl.program_id(0) == 0
    half = pl.program_id(0)
    both = range(tiles)
    width = tiles * 128
    rank = wdt_ref.shape[1]

    length = count // 8
    d, c, z = place()
    sib = (d, flip(c, 1), z)
    left = (d, c, lax.rem(z + 3, 4))
    right = (d, c, lax.rem(z + 1, 4))

    def rows(rank):
        return pl.ds(pl.multiple_of(rank * length, length), length)

    keeps = [pltpu.make_async_copy(ups_ref.at[r // 4, r % 4], ups_out.at[r // 4, r % 4], stores.at[r]) for r in range(8)]

    def arrive(act):
        for rank in range(8):
            at = rank % 4
            here = jnp.logical_not(((z == 0) & (at == 3)) | ((z == 3) & (at == 0))) if at in (0, 3) else None
            copy = pltpu.make_async_copy(ups_any.at[rows(rank)], ups_ref.at[rank // 4, at], loads.at[rank])
            if here is None:
                act(copy)
            else:
                @pl.when(here)
                def _():
                    act(copy)

    @pl.when(first)
    def _():
        arrive(lambda copy: copy.start())
        pltpu.make_async_copy(wout_any, wout_ref, loads.at[8]).start()
        greet([sib, left, right])

        @pl.when(z == 1)
        def _():
            put(ups_any.at[rows(c * 4 + 3)], ups_ref.at[c, 3], zs, zr, left)

        @pl.when(z == 2)
        def _():
            put(ups_any.at[rows(c * 4)], ups_ref.at[c, 0], zs, zr, right)

    def complete():
        for end, source, at in ((0, right, 3), (3, left, 0)):
            @pl.when(z == end)
            def _():
                slot = ups_ref.at[c, at]
                landed(slot, zr, source)
                put(slot, slot, cs, cr, sib)
                landed(ups_ref.at[flip(c, 1), at], cr, sib)
                sent(slot, cs, sib)

        for end, target, at in ((1, left, 3), (2, right, 0)):
            @pl.when(z == end)
            def _():
                sent(ups_any.at[rows(c * 4 + at)], zs, target)

        arrive(lambda copy: copy.wait())
        pltpu.make_async_copy(wout_any, wout_ref, loads.at[8]).wait()
        for copy in keeps:
            copy.start()

    @pl.when(first)
    def _():
        row = lax.broadcasted_iota(jnp.int32, (128, 512), 0)
        col = lax.broadcasted_iota(jnp.int32, (128, 512), 1) // 128
        for part in range(0, 2 * wide, 512):
            hot_ref[:, part:part + 512] = jnp.where((row % 32 == col + part // 128) & (row < 96), 1.0, 0.0).astype(bf16)

    lane = lax.broadcasted_iota(jnp.int32, (512, 128), 1)

    def spread(i, carry):
        r = pl.ds(pl.multiple_of(i * 512, 512), 512)
        value = jnp.where(lane < 2 * states, kq_ref[r, :], 0.0)
        hi = value.astype(bf16).astype(f32)
        mid = (value - hi).astype(bf16).astype(f32)
        low = value - hi - mid
        left = (hi + pltpu.roll(mid, 32, 1) + pltpu.roll(low, 64, 1)).astype(bf16)
        for part in range(0, 2 * wide, 256):
            kb_ref[r, part:part + 256] = jnp.dot(left, hot_ref[:, part:part + 256], preferred_element_type=f32)
        return carry

    lax.fori_loop(0, count // 512, spread, 0)
    cols = (((1,), (1,)), ((), ()))

    def gate_step(i, carry):
        product = lax.dot_general(ups_ref[i].reshape(4 * length, wout_ref.shape[1]), wout_ref[pl.ds(pl.multiple_of(half * width, width), width), :], cols, preferred_element_type=f32)
        for j in range(4):
            for n in both:
                dm_ref[n, pl.ds(i * 4 + j, length, stride=8), :] = product[j * length:(j + 1) * length, n * 128:(n + 1) * 128]
        return carry

    bias = vecs_ref[5:6, :]
    skip = vecs_ref[6:7, :]
    tile_of = lambda x, n: x[:, n * 128:(n + 1) * 128]
    ks = lax.broadcasted_iota(jnp.int32, (128, 128), 1)

    def before(i, carry):
        seen = list(carry)
        r = pl.ds(pl.multiple_of(i * 128, 128), 128)
        live = live_ref[0, r, :]
        k = jnp.where(ks < states, kq_ref[r, :], 0.0)
        sk = jnp.sum(k * k, axis=1, keepdims=True)
        pre = lax.dot_general(dl_ref[r, :], wdt_ref[...], cols, preferred_element_type=f32) + bias
        for n in both:
            beta = jax.nn.sigmoid(tile_of(pre, n))
            part = 1.0 / (1.0 + beta * sk)
            rate_ref[n, r, :] = beta * part
            w_ref[n, r, :] = part * part * beta * (1.0 - beta)
            shown = (beta * live).reshape(16, 8, 128)
            seen[n] = seen[n] + jnp.sum(shown, axis=0)
            seen[tiles + n] = jnp.maximum(seen[tiles + n], jnp.max(shown, axis=0))
        return tuple(seen)

    blank = jnp.zeros((8, 128), f32)
    seen = lax.fori_loop(0, count // 128, before, (blank,) * (2 * tiles))
    s_ref[0, 0] = jnp.zeros(s_ref.shape[2:], f32)
    span = GROUP * 8
    at = [slice(j * 8, j * 8 + 8) for j in range(GROUP)]

    def view(ref, i):
        r = pl.ds(pl.multiple_of(i * span, span), span)
        return ref.at[:, r] if len(ref.shape) == 3 else ref.at[r]

    def pair(ref, r):
        return jnp.concatenate([ref[n, r, :] for n in both], axis=1)

    def keep_pair(ref, r, value):
        for n in both:
            ref[n, r, :] = tile_of(value, n)

    tile = lambda x: jnp.concatenate([x] * tiles, axis=1)

    def fold(x):
        total = tile_of(x, 0)
        for n in range(1, tiles):
            total = total + tile_of(x, n)
        return total

    def forward(i, carry):
        keeps, rates, vs, kbs, ys = [view(x, i) for x in (keep_ref, rate_ref, v_ref, kb_ref, y_ref)]
        keep = [keeps[0, r, :] for r in at]
        rate = [pair(rates, r) for r in at]
        value = [pair(vs, r) for r in at]
        rv = [a * b for a, b in zip(rate, value)]
        y = [skip * b for b in value]
        for n in range(states):
            state = s_ref[i, 0, n]
            for j, r in enumerate(at):
                kb = kbs[r, n * 128:(n + 1) * 128]
                qb = kbs[r, wide + n * 128:wide + (n + 1) * 128]
                state = (tile(keep[j]) - rate[j] * tile(kb * kb * keep[j])) * state + rv[j] * tile(kb)
                if j < GROUP - 1:
                    s_ref[i, j + 1, n] = state
                else:
                    s_ref[i + 1, 0, n] = state
                y[j] = y[j] + state * tile(qb)
        for j, r in enumerate(at):
            keep_pair(ys, r, y[j])
        return carry

    lax.fori_loop(0, steps // GROUP, forward, 0)
    h_ref[...] = jnp.zeros_like(h_ref)

    @pl.when(first)
    def _():
        complete()

    lax.fori_loop(0, 2, gate_step, 0)

    def gates(i, carry):
        r = pl.ds(pl.multiple_of(i * 32, 32), 32)
        live = live_ref[0, r, :]
        for n in both:
            g = g_ref[n, r, :]
            sg = jax.nn.sigmoid(g)
            silu = g * sg
            y = y_ref[n, r, :]
            dm = dm_ref[n, r, :] * live
            dv_ref[n, r, :] = dm * silu
            dm_ref[n, r, :] = dm * y * (sg * (1.0 + g * (1.0 - sg)))
            y_ref[n, r, :] = y * silu * live
        return carry

    lax.fori_loop(0, count // 32, gates, 0, unroll=2)

    def by_row(j, carry):
        r = pl.ds(pl.multiple_of(j * length, length), length)
        for n in both:
            value = y_ref[n, pl.ds(j, length, stride=8), :]
            m_ref[r, pl.ds(pl.multiple_of(half * width + n * 128, 128), 128)] = value.astype(bf16)
            mt_ref[n * 128:(n + 1) * 128, r] = value.T.astype(bf16)
            dg_ref[r, n * 128:(n + 1) * 128] = dm_ref[n, pl.ds(j, length, stride=8), :].astype(bf16)
        return carry

    lax.fori_loop(0, 8, by_row, 0)

    def rows_product(core):
        def body(i, carry):
            lanes = pl.ds(pl.multiple_of(i * chunk, chunk), chunk)
            product = jnp.dot(m_ref[pl.ds(pl.multiple_of(core * 4 * length, 4 * length), 4 * length), :], wout_ref[:, lanes], preferred_element_type=f32)
            for at_z in range(4):
                ups_ref[core, at_z, :, lanes] = product[at_z * length:(at_z + 1) * length].astype(bf16)
            return carry

        lax.fori_loop(0, wout_ref.shape[1] // chunk, body, 0)

    def gather(at_z):
        landed(acc_ref.at[at_z], sr.at[at_z], sib)
        add_rows(acc_ref.at[at_z], [acc_ref.at[at_z], ups_ref.at[c, at_z]])

    @pl.when(jnp.logical_not(first))
    def _():
        for copy in keeps:
            copy.wait()
        rows_product(flip(c, 1))
        for at_z in (3, 0, 2, 1):
            put(ups_ref.at[flip(c, 1), at_z], acc_ref.at[at_z], ss.at[at_z], sr.at[at_z], sib)
        rows_product(c)
        gather(3)
        gather(0)

        @pl.when(z == 0)
        def _():
            put(acc_ref.at[3], recv_ref, ls, lr, right)

        @pl.when(z == 3)
        def _():
            put(acc_ref.at[0], recv_ref, ls, lr, left)


    def backward(step, carry):
        i = steps // GROUP - 1 - step
        keeps, rates, vs, kbs, dvs, ws, drrs = [view(x, i) for x in (keep_ref, rate_ref, v_ref, kb_ref, dv_ref, w_ref, drr_ref)]
        keep = [keeps[0, r, :] for r in at]
        rate = [pair(rates, r) for r in at]
        value = [pair(vs, r) for r in at]
        rv = [a * b for a, b in zip(rate, value)]
        dy = [pair(dvs, r) for r in at]
        hk = [jnp.zeros((8, tiles * 128), f32) for r in at]
        hs2 = [jnp.zeros((8, tiles * 128), f32) for r in at]
        for n in range(states):
            ah = h_ref[n]
            later = s_ref[i + 1, 0, n]
            for j in range(GROUP - 1, -1, -1):
                r = at[j]
                kb = kbs[r, n * 128:(n + 1) * 128]
                qb = kbs[r, wide + n * 128:wide + (n + 1) * 128]
                kk = kb * keep[j]
                held = tile(kb * kk)
                h = dy[j] * tile(qb) + ah
                prior = s_ref[i, j, n]
                hs = h * prior
                hk[j] = hk[j] + h * tile(kb)
                hs2[j] = hs2[j] + hs * held
                kbs[r, n * 128:(n + 1) * 128] = fold(h * rv[j]) - 2.0 * kk * fold(hs * rate[j])
                kbs[r, wide + n * 128:wide + (n + 1) * 128] = fold(dy[j] * later)
                later = prior
                ah = (tile(keep[j]) - rate[j] * held) * h
            h_ref[n] = ah
        dskip = carry
        for j, r in enumerate(at):
            drate = value[j] * hk[j] - hs2[j]
            drrs[r, :] = fold(drate * rate[j] * rate[j]) * (-2.0)
            keep_pair(ws, r, drate * pair(ws, r))
            keep_pair(dvs, r, rate[j] * hk[j] + skip * dy[j])
            dskip = dskip + dy[j] * value[j]
        return dskip

    dskip = lax.fori_loop(0, steps // GROUP, backward, jnp.zeros((8, tiles * 128), f32))

    quarter = count // 4
    packed = jnp.zeros((quarter, 128), f32)
    for b in range(4):
        r = slice(b * quarter, (b + 1) * quarter)
        total = jnp.zeros((quarter, 128), f32)
        for part in range(0, 2 * wide, 512):
            total = total + lax.dot_general(kb_ref[r, part:part + 512].astype(bf16), hot_ref[:, part:part + 512], cols, preferred_element_type=f32)
        drr = jnp.sum(drr_ref[r, :], axis=1, keepdims=True)
        k = kq_ref[r, :]
        low = lax.broadcasted_iota(jnp.int32, (quarter, 128), 1)
        total = jnp.where(low < 2 * states, total, 0.0) + jnp.where(low < states, k * drr, 0.0)
        packed = packed + (pltpu.roll(total, 32 * b, 1) if b else total)

    tail = pl.ds(count, quarter)
    part_ref[tail, :] = jnp.where(first, packed, part_ref[tail, :] + packed)

    def after(i, carry):
        r = pl.ds(pl.multiple_of(i * 128, 128), 128)
        sums = list(carry)
        for n in both:
            low = w_ref[n, r, :].astype(bf16)
            dpre_ref[r, n * 128:(n + 1) * 128] = low
            sums[n] = sums[n] + jnp.sum(low.astype(f32).reshape(16, 8, 128), axis=0)
        ddl = jnp.dot(dpre_ref[r, :], wdt_ref[...], preferred_element_type=f32)
        part_ref[r, :] = jnp.where(first, ddl, part_ref[r, :] + ddl)
        return tuple(sums)

    sums = lax.fori_loop(0, count // 128, after, (blank,) * tiles)

    gwdt_ref[...] = lax.dot_general(dpre_ref[...], dl_ref[...], (((0,), (0,)), ((), ())), preferred_element_type=f32)

    @pl.when(jnp.logical_not(first))
    def _():
        gather(2)
        gather(1)
        for end, source, at_z in ((1, left, 3), (2, right, 0)):
            @pl.when(z == end)
            def _():
                landed(recv_ref, lr, source)
                add_rows(acc_ref.at[at_z], [acc_ref.at[at_z], recv_ref])

        save = pltpu.make_async_copy(acc_ref, acc_out, loads.at[8])
        save.start()
        for at_z in range(4):
            sent(ups_ref.at[flip(c, 1), at_z], ss.at[at_z], sib)
        for end, target, at_z in ((0, right, 3), (3, left, 0)):
            @pl.when(z == end)
            def _():
                sent(acc_ref.at[at_z], ls, target)
        save.wait()

    stat_ref[...] = jnp.zeros_like(stat_ref)
    for n in both:
        lanes = slice(n * 128, (n + 1) * 128)
        stat_ref[0:1, lanes] = jnp.sum(seen[n], axis=0, keepdims=True)
        stat_ref[1:2, lanes] = jnp.max(seen[tiles + n], axis=0, keepdims=True)
        stat_ref[5:6, lanes] = jnp.sum(sums[n], axis=0, keepdims=True)
        stat_ref[6:7, lanes] = jnp.sum(tile_of(dskip, n), axis=0, keepdims=True)


def k2(dl, kq, smalls, vecs, masks, live, v, g, ups, wout, states):
    count, rank = dl.shape
    channels, model = wout.shape
    tiles = 2
    width = tiles * 128
    like = jax.ShapeDtypeStruct
    once = pl.Buffered(buffer_count=1)
    whole = lambda a: pl.BlockSpec(a.shape, lambda h: (0,) * a.ndim, pipeline_mode=once)
    deep = pl.BlockSpec((tiles, count, 128), lambda h: (h, 0, 0))
    flat = pl.BlockSpec((count, width), lambda h: (0, h))
    return pl.pallas_call(
        functools.partial(k2_kernel, states),
        grid=(channels // width,),
        out_shape=(
            like((4, count // 8, model), bf16),
            like((channels, count), bf16),
            like((count, channels), bf16),
            like((channels, rank), f32),
            like((2, 4, count // 8, model), bf16),
            like(v.shape, f32),
            like((count + count // 4, 128), f32),
            like((8, channels), f32),
        ),
        in_specs=[
            whole(dl), whole(kq),
            pl.BlockSpec((width, 128), lambda h: (h, 2)),
            pl.BlockSpec((8, width), lambda h: (0, h)),
            pl.BlockSpec((1, count, 128), lambda h: (0, 0, 0), pipeline_mode=once),
            pl.BlockSpec((1, count, 128), lambda h: (0, 0, 0), pipeline_mode=once),
            deep, deep, pl.BlockSpec(memory_space=pl.ANY),
            pl.BlockSpec(memory_space=pl.ANY),
        ],
        out_specs=(pl.BlockSpec(memory_space=pltpu.HBM), pl.BlockSpec((width, count), lambda h: (h, 0)), flat, pl.BlockSpec((width, rank), lambda h: (h, 0)), pl.BlockSpec(memory_space=pltpu.HBM), deep, pl.BlockSpec((count + count // 4, 128), lambda h: (0, 0)), pl.BlockSpec((8, width), lambda h: (0, h))),
        scratch_shapes=[
            pltpu.VMEM((2, 4, count // 8, model), bf16),
            pltpu.SemaphoreType.DMA((9,)),
            pltpu.SemaphoreType.DMA((8,)),
        ] + [pltpu.SemaphoreType.DMA(())] * 6 + [
            pltpu.SemaphoreType.DMA((4,)),
            pltpu.SemaphoreType.DMA((4,)),
            pltpu.VMEM((count, channels), bf16),
            pltpu.VMEM((channels, model), bf16),
            pltpu.VMEM((4, count // 8, model), bf16),
            pltpu.VMEM((count // 8, model), bf16),
            pltpu.VMEM((count, width), bf16),
            pltpu.VMEM((count // 8 // GROUP + 1, GROUP, states, 8, width), f32),
            pltpu.VMEM((states, 8, width), f32),
        ] + [pltpu.VMEM((tiles, count, 128), f32)] * 4
        + [pltpu.VMEM((count, 2 * states * 128), f32), pltpu.VMEM((128, 2 * states * 128), bf16), pltpu.VMEM((count, 128), f32)],
        compiler_params=pltpu.CompilerParams(collective_id=2, has_side_effects=True, vmem_limit_bytes=63400000),
    )(dl, kq, smalls, vecs, masks, live, v, g, ups, wout)


class Row:
    def __init__(self, part, sib, recv, sems, merged=False):
        self.part, self.sib, self.recv, self.merged = part, sib, recv, merged
        self.ss, self.sr, self.gs, self.lr, self.rr = sems
        d, c, z = place()
        self.c = c
        self.other = (d, flip(c, 1), z)
        self.to_left = (d, c, lax.rem(z + 3, 4))
        self.to_right = (d, c, lax.rem(z + 1, 4))

    def start(self):
        for zp in (3, 0, 2, 1):
            put(self.part.at[flip(self.c, 1), zp], self.sib.at[zp], self.ss.at[zp], self.sr.at[zp], self.other)

    def gather(self):
        for zp in (3, 0, 2, 1):
            landed(self.sib.at[zp], self.sr.at[zp], self.other)
            add_rows(self.sib.at[zp], [self.sib.at[zp], self.part.at[self.c, zp]])

    def release(self):
        for zp in range(4):
            sent(self.part.at[flip(self.c, 1), zp], self.ss.at[zp], self.other)

    def terms(self, zs, zp):
        found = [self.sib.at[zp]]
        if zp >= zs and zs > 0 and not (self.merged and (zs, zp) == (1, 3)):
            landed(self.recv.at[zp], self.lr.at[zp], self.to_left)
            found.append(self.recv.at[zp])
        if zp <= zs and zs < 3 and not (self.merged and (zs, zp) == (2, 0)):
            slot = self.recv.at[4 if zp == zs else zp]
            landed(slot, self.rr.at[zp], self.to_right)
            found.append(slot)
        return found

    def join(self, zs, zp):
        found = self.terms(zs, zp)
        if len(found) > 1:
            add_rows(self.sib.at[zp], found)

    def skips(self, zs, zp):
        return self.merged and (zs, zp) in ((0, 3), (3, 0))

    def step(self, zs, k):
        k = k + 1 if self.merged else k
        ends = 1 if self.merged else 0
        for zp in ((3, 2, 1, 0) if zs == 0 else (0, 1, 2, 3)):
            if zp > zs and not self.skips(zs, zp) and k == (ends if zs == 0 else 3 - zp + zs):
                self.join(zs, zp)
                put(self.sib.at[zp], self.recv.at[zp], self.gs.at[zp], self.lr.at[zp], self.to_right)
            if zp < zs and not self.skips(zs, zp) and k == (ends if zs == 3 else zp + 3 - zs):
                self.join(zs, zp)
                put(self.sib.at[zp], self.recv.at[4 if zp == zs - 1 else zp], self.gs.at[zp], self.rr.at[zp], self.to_left)

    def finish(self, zs):
        add_rows(self.sib.at[zs], self.terms(zs, zs), self.total)

    def close(self, zs):
        for zp in range(4):
            if zp != zs and not self.skips(zs, zp):
                sent(self.sib.at[zp], self.gs.at[zp], self.other)

    def along(self, k, total=None):
        self.total = total
        d, c, z = place()
        for zs in range(4):
            @pl.when(z == zs)
            def _():
                if k < (2 if self.merged else 3):
                    self.step(zs, k)
                else:
                    self.finish(zs)
                    self.close(zs)


def row_scratch(rows, columns):
    return [pltpu.VMEM((4, rows, columns), bf16), pltpu.VMEM((5, rows, columns), bf16)] + [pltpu.SemaphoreType.DMA((4,))] * 5


def add_rows(dst, sources, total=None):
    rows = (total if total is not None else dst).shape[0]
    step = 16

    def body(i, carry):
        r = pl.ds(pl.multiple_of(i * step, step), step)
        value = sources[0][r, :].astype(f32)
        for more in sources[1:]:
            value = value + more[r, :].astype(f32)
        if total is not None:
            total[r, :] = value
        else:
            dst[r, :] = value.astype(dst.dtype)
        return carry

    lax.fori_loop(0, rows // step, body, 0)


class Flat:
    def __init__(self, part, xa, yb, rx, ry, ss, rs):
        self.part, self.xa, self.yb, self.rx, self.ry, self.ss, self.rs = part, xa, yb, rx, ry, ss, rs
        d, c, z = place()
        self.d, self.dx, self.dy, self.dd = d, flip(d, 1), flip(d, 2), flip(flip(d, 1), 2)
        self.xn, self.yn = (self.dx, c, z), (self.dy, c, z)
        half = part.shape[1] // 2
        self.a, self.b = pl.ds(0, half), pl.ds(half, half)
        self.sends = []

    def start_far(self):
        p = self.part
        self.sends.append(put(p.at[self.dd, self.a], self.xa, self.ss.at[0], self.rs.at[0], self.xn))
        self.sends.append(put(p.at[self.dd, self.b], self.yb, self.ss.at[1], self.rs.at[1], self.yn))

    def start_near(self):
        p = self.part
        self.sends.append(put(p.at[self.dx, self.a], self.rx.at[self.a], self.ss.at[2], self.rs.at[2], self.xn))
        self.sends.append(put(p.at[self.dy, self.b], self.ry.at[self.b], self.ss.at[3], self.rs.at[3], self.yn))

    def middle(self):
        p = self.part
        landed(self.xa, self.rs.at[0], self.xn)
        add_rows(self.xa, [self.xa, p.at[self.dy, self.a]])
        self.sends.append(put(self.xa, self.ry.at[self.a], self.ss.at[4], self.rs.at[4], self.yn))
        landed(self.yb, self.rs.at[1], self.yn)
        add_rows(self.yb, [self.yb, p.at[self.dx, self.b]])
        self.sends.append(put(self.yb, self.rx.at[self.b], self.ss.at[5], self.rs.at[5], self.xn))

    def finish(self, out):
        landed(self.rx.at[self.a], self.rs.at[2], self.xn)
        landed(self.ry.at[self.b], self.rs.at[3], self.yn)
        landed(self.ry.at[self.a], self.rs.at[4], self.yn)
        landed(self.rx.at[self.b], self.rs.at[5], self.xn)
        add_rows(out, [self.part.at[self.d], self.rx, self.ry])

    def close(self):
        for copy in self.sends:
            copy.wait_send()


def flat_scratch(rows, columns, dtype):
    half = pltpu.VMEM((rows // 2, columns), dtype)
    full = pltpu.VMEM((rows, columns), dtype)
    return [half, half, full, full, pltpu.SemaphoreType.DMA((6,)), pltpu.SemaphoreType.DMA((6,))]


def k3_kernel(part_ref, stat_ref, smalls_ref, vecs_ref, gains_ref, gwdt_ref, masks_ref, tok_ref, up_ref,
              acc_any, mt_any, dg_any, dv_any, slope_any, u_any, vt_any, xnt_any, win_any, ups_any,
              block_out, gtok_out, gwin_out, gwout_out, small_out, tiny_out, *scratch):
    scratch = list(scratch)

    def take(n):
        found = scratch[:n]
        del scratch[:n]
        return found

    block_ref, gtok_ref, gwin_ref, gwout_ref, small_ref, tiny_ref, stores = take(7)
    outp, win_ref, up, gp, gwoutp, smallp = take(6)
    mt_ref, dz_ref, dc_ref, slope_ref, u_ref, xnt_ref, dp_ref, slots_ref, row_ref = take(9)
    near_ref, pairs_ref, sum_ref, far_ref = take(4)
    loads, as_, ar, ns, nr, fs, fr = take(7)
    totals = take(7)
    total_sems = take(8)
    out_row = Row(None, *take(2), take(5), True)
    dxn_row = Row(outp, *take(2), take(5))
    flats = [Flat(up, *take(6)), Flat(gp, *take(6))]
    gwout_flat = Flat(gwoutp, *take(6))
    small_flat = Flat(smallp, *take(6))
    d, c, z = place()
    j = c * 4 + z
    other = flip(c, 1)
    steps = mates()
    planes = [(flip(d, 1), c, z), (flip(d, 2), c, z), (flip(flip(d, 1), 2), c, z)]
    length, model = tok_ref.shape[1:]
    tiles, padded, _ = dc_ref.shape
    count = dz_ref.shape[0]
    width = tiles * 128
    rows_any = [(dg_any, dz_ref.at[:, pl.ds(width, width)]), (xnt_any, xnt_ref), (acc_any, out_row.sib), (mt_any, mt_ref), (ups_any, outp),
                (dv_any, dc_ref.at[:, pl.ds(0, count)]), (slope_any, slope_ref), (u_any, u_ref), (win_any, win_ref)]
    copies = [pltpu.make_async_copy(a, b, loads.at[i]) for i, (a, b) in enumerate(rows_any)]
    for copy in copies:
        copy.start()
    greet([mate(s) for s in steps] + planes)
    outs = [(block_ref, block_out), (gtok_ref, gtok_out), (gwin_ref, gwin_out), (gwout_ref, gwout_out), (small_ref, small_out), (tiny_ref, tiny_out)]
    outs = [pltpu.make_async_copy(a, b, stores.at[i]) for i, (a, b) in enumerate(outs)]
    tile = 256
    nt = (((1,), (1,)), ((), ()))

    def rows_product(half):
        def body(i, carry):
            value = win_ref[i // (512 // tile), pl.ds(pl.multiple_of((i % (512 // tile)) * tile, tile), tile), :]
            product = lax.dot_general(dz_ref[pl.ds(pl.multiple_of(half * 512, 512), 512), :], value, nt, preferred_element_type=f32)
            for zp in range(4):
                outp[half, zp, :, pl.ds(pl.multiple_of(i * tile, tile), tile)] = product[zp * length:(zp + 1) * length].astype(bf16)
            return carry

        lax.fori_loop(0, model // tile, body, 0)

    def weight_rows(holder, first, group):
        def body(i, carry):
            lanes = pl.ds(pl.multiple_of(i * tile, tile), tile)
            left = xnt_ref[pl.ds(pl.multiple_of(group * 512, 512), 512), :]
            value = dz_ref[:, pl.ds(pl.multiple_of(first + i * tile, tile), tile)]
            holder[group, :, lanes] = jnp.dot(left, value, preferred_element_type=f32).astype(bf16)
            return carry

        lax.fori_loop(0, width // tile, body, 0)

    def weight_part(k):
        flat = flats[k]
        holder, first = (up, 0) if k == 0 else (gp, width)
        weight_rows(holder, first, flat.dd)
        flat.start_far()
        weight_rows(holder, first, flat.dx)
        weight_rows(holder, first, flat.dy)
        flat.start_near()
        weight_rows(holder, first, d)

    def early():
        for copy in copies[0:2]:
            copy.wait()
        weight_part(1)

    def between():
        copies[2].wait()
        out_row.along(0)
        flats[1].middle()

    def late():
        for copy in copies[3:5]:
            copy.wait()

        def body(i, carry):
            lanes = pl.ds(pl.multiple_of(i * tile, tile), tile)
            product = jnp.dot(mt_ref[...], outp[:, :, :, lanes].reshape(count, tile), preferred_element_type=f32)
            for g in range(4):
                gwoutp[g, :, lanes] = product[g * 128:(g + 1) * 128].astype(bf16)
            return carry

        lax.fori_loop(0, model // tile, body, 0)
        gwout_flat.start_far()
        gwout_flat.start_near()

    seen = jnp.sum(stat_ref[0:1, :], axis=1, keepdims=True)
    peak = jnp.max(stat_ref[1:2, :], axis=1, keepdims=True)
    row8 = lax.broadcasted_iota(jnp.int32, (8, 128), 0)
    lane8 = lax.broadcasted_iota(jnp.int32, (8, 128), 1)
    pairs_ref[...] = jnp.where(lane8 == 0, seen, jnp.where(lane8 == 1, peak, 0.0))
    for i, s in enumerate(steps):
        put(pairs_ref, near_ref.at[i], ns.at[i], nr.at[i], mate(s))

    def join(a, b):
        return jnp.where(lane8 == 1, jnp.maximum(a, b), a + b)

    total_ref = totals[0]
    line_total(part_ref, *totals, *total_sems, early, between, late)
    vt_copy = pltpu.make_async_copy(vt_any, mt_ref, loads.at[9])
    vt_copy.start()
    block = gwin_ref.shape[0]
    pending = []

    def rows_of(k, rank):
        return flats[k].part.at[d, pl.ds(pl.multiple_of(rank * block, block), block)]

    def give(k):
        flats[k].finish(flats[k].part.at[d])
        for i, s in enumerate(steps):
            to = mate(s)
            pending.append(put(rows_of(k, rank_of(to)), slots_ref.at[k, i], as_.at[7 * k + i], ar.at[7 * k + i], to))

    value = pairs_ref[...]
    for i, s in enumerate(steps):
        landed(near_ref.at[i], nr.at[i], mate(s, -1))
        value = join(value, near_ref[i])
    sum_ref[...] = value
    for i, to in enumerate(planes):
        put(sum_ref, far_ref.at[i], fs.at[i], fr.at[i], to)
    quarter = count // 4
    lane = lax.broadcasted_iota(jnp.int32, (quarter, 128), 1)
    dp_ref[:, 0:128] = total_ref[0:count, :].astype(bf16)
    for b in range(4):
        packed = total_ref[count:count + quarter, :]
        packed = pltpu.roll(packed, 128 - 32 * b, 1) if b else packed
        dp_ref[b * quarter:(b + 1) * quarter, 128:256] = jnp.where(lane < 32, packed, 0.0).astype(bf16)
    for copy in copies[5:8]:
        copy.wait()
    dc_ref[:, count:, :] = jnp.zeros((tiles, padded - count, 128), f32)

    def slope_step(i, carry):
        r = pl.ds(pl.multiple_of(i * 256, 256), 256)
        product = lax.dot_general(dp_ref[r, :], smalls_ref[:, 0:256], nt, preferred_element_type=f32)
        for n in range(tiles):
            dc_ref[n, r, :] = (dc_ref[n, r, :] + product[:, n * 128:(n + 1) * 128]) * slope_ref[n, r, :]
        return carry

    lax.fori_loop(0, count // 256, slope_step, 0)
    give(1)
    out_row.along(1)
    taps = [vecs_ref[o:o + 1, :] for o in range(4)]
    lead = u_ref.shape[1] - count

    for n in range(tiles):
        lanes = slice(n * 128, (n + 1) * 128)
        tap = [t[:, lanes] for t in taps]

        def conv_step(i, carry):
            r = pl.ds(pl.multiple_of(i * 32, 32), 32)
            sums = list(carry)
            dc = dc_ref[n, r, :]
            du = tap[3] * dc
            fold8 = lambda x: x[0:8] + x[8:16] + x[16:24] + x[24:32]
            sums[4] = sums[4] + fold8(dc)
            sums[3] = sums[3] + fold8(dc * u_ref[n, pl.ds(pl.multiple_of(lead + i * 32, 8), 32), :])
            for o in range(1, 4):
                sums[3 - o] = sums[3 - o] + fold8(dc * (u_ref[n, pl.ds(pl.multiple_of(lead + i * 32 - 8 * o, 8), 32), :] * masks_ref[o - 1, pl.ds(pl.multiple_of(i * 32, 8), 32), :]))
                du = du + tap[3 - o] * (dc_ref[n, pl.ds(pl.multiple_of(i * 32 + 8 * o, 8), 32), :] * masks_ref[o - 1, pl.ds(pl.multiple_of(i * 32 + 8 * o, 8), 32), :])
            dc_ref[n, r, :] = du
            return tuple(sums)

        sums = lax.fori_loop(0, count // 32, conv_step, (jnp.zeros((8, 128), f32),) * 5)
        smallp[n, 128:160, :] = jnp.zeros((32, 384), f32)
        for k in range(5):
            smallp[n, 128 + k:129 + k, 0:128] = jnp.sum(sums[k], axis=0, keepdims=True)
        smallp[n, 133:134, 0:128] = stat_ref[5:6, lanes]
        smallp[n, 134:135, 0:128] = stat_ref[6:7, lanes]
        smallp[n, 0:128, 256:384] = gwdt_ref[n * 128:(n + 1) * 128, :]

    def by_row(i, carry):
        r = pl.ds(pl.multiple_of(i * length, length), length)
        for n in range(tiles):
            dz_ref[r, n * 128:(n + 1) * 128] = dc_ref[n, pl.ds(i, length, stride=8), :].astype(bf16)
        return carry

    lax.fori_loop(0, 8, by_row, 0)
    gwout_flat.middle()
    copies[8].wait()
    rows_product(other)
    dxn_row.start()
    weight_rows(up, 0, flats[0].dd)
    flats[0].start_far()
    rows_product(c)
    dxn_row.gather()
    dxn_row.along(0)
    weight_rows(up, 0, flats[0].dx)
    weight_rows(up, 0, flats[0].dy)
    flats[0].start_near()
    weight_rows(up, 0, d)
    vt_copy.wait()
    for n in range(tiles):
        smallp[n, 0:128, 0:256] = jnp.dot(mt_ref[n * 128:(n + 1) * 128, :], dp_ref[...], preferred_element_type=f32)
    small_flat.start_far()
    small_flat.start_near()
    flats[0].middle()
    out_row.along(2, row_ref)

    def block_step(i, carry):
        r = pl.ds(pl.multiple_of(i * 16, 16), 16)
        block_ref[r, :] = (tok_ref[0, r, :].astype(f32) + row_ref[r, :]).astype(bf16)
        return carry

    lax.fori_loop(0, length // 16, block_step, 0)
    outs[0].start()
    dxn_row.along(1)
    give(0)
    small_flat.middle()
    dxn_row.along(2)
    gwout_flat.finish(gwout_ref)
    outs[3].start()
    dxn_row.along(3, row_ref)
    dxn_row.release()
    def norm_step(i, carry):
        r = pl.ds(pl.multiple_of(i * 16, 16), 16)
        x = tok_ref[0, r, :].astype(f32)
        scale = lax.rsqrt(jnp.sum(x * x, axis=1, keepdims=True) * (1.0 / model) + EPS)
        dxn = row_ref[r, :]
        inner = dxn * gains_ref[...]
        dot = jnp.sum(inner * x, axis=1, keepdims=True) * (1.0 / model)
        dxx = scale * inner - x * (scale * scale * scale * dot)
        gtok_ref[r, :] = (up_ref[0, r, :].astype(f32) + dxx).astype(bf16)
        return carry

    lax.fori_loop(0, length // 16, norm_step, 0)
    outs[1].start()
    small_flat.finish(small_ref)
    outs[4].start()

    def settle(k, rank, source):
        for g in range(4):
            at = k * width * 8 + g * 1024
            gwin_ref[:, pl.ds(pl.multiple_of(at + rank * 128, 128), 128)] = source[:, g * 128:(g + 1) * 128]

    for k in (1, 0):
        settle(k, j, rows_of(k, j))
        for i, s in enumerate(steps):
            src = mate(s, -1)
            landed(slots_ref.at[k, i], ar.at[7 * k + i], src)
            settle(k, rank_of(src), slots_ref.at[k, i])
    outs[2].start()
    value = sum_ref[...]
    for i, to in enumerate(planes):
        landed(far_ref.at[i], fr.at[i], to)
        value = join(value, far_ref[i])
    tiny_ref[...] = value
    outs[5].start()
    for i, to in enumerate(planes):
        sent(sum_ref, fs.at[i], to)
    for i, s in enumerate(steps):
        sent(near_ref.at[i], ns.at[i], mate(s))
    for copy in pending:
        copy.wait_send()
    for flat in (*flats, gwout_flat, small_flat):
        flat.close()
    for copy in outs:
        copy.wait()


def k3(part, stat, smalls, vecs, gains, gwdt, masks, tokens, upstream, acc, mt, dg, dv, slope, u, vt, xnt, win, ups):
    like = jax.ShapeDtypeStruct
    length, model = tokens.shape[1:]
    channels, count = mt.shape
    tiles = channels // 128
    here = pl.BlockSpec(memory_space=pltpu.VMEM)
    far = pl.BlockSpec(memory_space=pl.ANY)
    dma = lambda n: pltpu.SemaphoreType.DMA((n,))
    own_d = model // 32
    packed = part.shape[0]
    return pl.pallas_call(
        k3_kernel,
        out_shape=(
            like((length, model), bf16),
            like((length, model), bf16),
            like((own_d, 16 * channels), bf16),
            like((128, model), f32),
            like((160, 384), f32),
            like((8, 128), f32),
        ),
        in_specs=[here] * 9 + [far] * 10,
        out_specs=(pl.BlockSpec(memory_space=pltpu.HBM),) * 6,
        scratch_shapes=[
            pltpu.VMEM((length, model), bf16),
            pltpu.VMEM((length, model), bf16),
            pltpu.VMEM((own_d, 16 * channels), bf16),
            pltpu.VMEM((128, model), f32),
            pltpu.VMEM((160, 384), f32),
            pltpu.VMEM((8, 128), f32),
            dma(6),
            pltpu.VMEM((2, 4, length, model), bf16),
            pltpu.VMEM((4, 512, 2 * channels), bf16),
            pltpu.VMEM((4, 512, channels), bf16),
            pltpu.VMEM((4, 512, channels), bf16),
            pltpu.VMEM((4, 128, model), bf16),
            pltpu.VMEM((4, 160, 384), f32),
            pltpu.VMEM((channels, count), bf16),
            pltpu.VMEM((count, 2 * channels), bf16),
            pltpu.VMEM((tiles, count + 32, 128), f32),
            pltpu.VMEM((tiles, count, 128), f32),
            pltpu.VMEM(u.shape, f32),
            pltpu.VMEM((model, count), bf16),
            pltpu.VMEM((count, 256), bf16),
            pltpu.VMEM((2, 7, own_d, channels), bf16),
            pltpu.VMEM((length, model), f32),
            pltpu.VMEM((7, 8, 128), f32),
            pltpu.VMEM((8, 128), f32),
            pltpu.VMEM((8, 128), f32),
            pltpu.VMEM((3, 8, 128), f32),
            dma(10), dma(14), dma(14), dma(7), dma(7), dma(3), dma(3),
            pltpu.VMEM((packed, 128), f32),
        ] + [pltpu.VMEM((packed // 2, 128), f32)] + [pltpu.VMEM((packed // 2, 128), LINE2)] * 5 + [dma(PIECES) for _ in range(8)]
        + row_scratch(length, model) * 2
        + flat_scratch(512, channels, bf16) * 2 + flat_scratch(128, model, bf16) + flat_scratch(160, 384, f32),
        compiler_params=pltpu.CompilerParams(collective_id=1, has_side_effects=True, vmem_limit_bytes=63400000),
    )(part, stat, smalls, vecs, gains, gwdt, masks, tokens, upstream, acc, mt, dg, dv, slope, u, vt, xnt, win, ups)


def k4_kernel(slots, block_in, gtok_in, gwin_in, gwout_in, small_in, tiny_in, win_ref, gain_ref,
              block_ref, gtok_ref, gain_out, gwin_ref, convw_ref, convb_ref, gwx_ref, gwdt_ref, dtb_ref, skip_ref, gwout_ref, mean_ref, peak_ref):
    block_ref[0] = block_in[...]
    gtok_ref[0] = gtok_in[...]
    gwout_ref[...] = gwout_in[...]
    depth, total = gwin_in.shape
    dot = jnp.zeros((depth, 128), f32)
    for at in range(0, total, 128):
        value = gwin_in[:, at:at + 128].astype(f32)
        gwin_ref[:, at:at + 128] = value
        dot = dot + value * win_ref[:, at:at + 128].astype(f32)
    column = jnp.broadcast_to(jnp.sum(dot, axis=1, keepdims=True), (depth, 128))
    gain_out[...] = column.T[0:1, :] / gain_ref[...].astype(f32)
    gwx_ref[...] = small_in[0:128, 0:256].T[0:gwx_ref.shape[0], :]
    gwdt_ref[...] = small_in[0:128, 256:384]
    convw_ref[...] = small_in[128:132, 0:128]
    convb_ref[...] = small_in[132:133, 0:128]
    dtb_ref[...] = small_in[133:134, 0:128]
    skip_ref[...] = small_in[134:135, 0:128]
    mean_ref[...] = tiny_in[0:1, 0:1] * (1.0 / slots)
    peak_ref[...] = tiny_in[0:1, 1:2]


def k4(slots, block, gtok, gwin, gwout, small, tiny, w_in, gain, columns):
    like = jax.ShapeDtypeStruct
    here = pl.BlockSpec(memory_space=pltpu.VMEM)
    row = like((1, 128), f32)
    return pl.pallas_call(
        functools.partial(k4_kernel, slots),
        out_shape=(
            like((1,) + block.shape, bf16), like((1,) + gtok.shape, bf16), like(gain.shape, f32), like(gwin.shape, f32),
            like((4, 128), f32), row, like((columns, 128), f32), like((128, 128), f32), row, row, like(gwout.shape, f32),
            like((1, 1), f32), like((1, 1), f32),
        ),
        in_specs=[here] * 8,
        out_specs=(here,) * 13,
        compiler_params=pltpu.CompilerParams(vmem_limit_bytes=63400000),
    )(block, gtok, gwin, gwout, small, tiny, w_in, gain)

def masks(lengths, count):
    ends = jnp.cumsum(lengths, axis=1)
    places = jnp.arange(count, dtype=jnp.int32)
    segment = jnp.sum((places[:, None, None] >= ends[None, :, :]).astype(jnp.int32), axis=2)
    same = []
    for offset in range(1, 4):
        before = jnp.pad(segment, ((offset, 0), (0, 0)), constant_values=-1)[:count]
        same.append((before == segment).astype(f32))
    return same, (segment < DOCS).astype(f32)


def columns(weights, ways):
    rows, total = weights.shape
    return weights.reshape(rows, 2, total // (2 * ways * 128), ways, 128)


def on_device(tokens, lengths, gain, w_in, conv_w, conv_b, w_x, w_dt, dt_bias, skip, w_out, grad_out):
    ways = lax.axis_size("core") * lax.axis_size("z")
    groups = lax.axis_size("dp")
    length, model = tokens.shape[1:]
    own_d = w_in.shape[0]
    own_e = conv_w.shape[0]
    inner = w_in.shape[1] // 2
    channels = inner // ways
    rank = w_dt.shape[1]
    states = (w_x.shape[1] - rank) // 2
    cols = w_in.reshape(own_d, 2, groups, ways, own_e).transpose(3, 0, 1, 2, 4).reshape(ways, own_d, 2 * channels)
    cols = lax.all_to_all(cols, TP, split_axis=0, concat_axis=0, tiled=True)
    win = lax.all_gather(cols, "dp", axis=0, tiled=True).reshape(model, 2 * channels)
    small = jnp.concatenate([w_x, w_dt, conv_w, conv_b[:, None], dt_bias[:, None], skip[:, None]], axis=1)
    small_width = small.shape[1]
    small = lax.all_gather(small, "dp", axis=0, tiled=True)
    wx = small[:, :rank + 2 * states]
    wdt = small[:, rank + 2 * states:2 * rank + 2 * states]
    rest = small[:, 2 * rank + 2 * states:].astype(f32)
    taps, bias, dtb, skips = rest[:, :4], rest[:, 4], rest[:, 5], rest[:, 6]
    wout = lax.all_gather(w_out, "dp", axis=0, tiled=True)
    gains = lax.all_gather(gain, ALL, axis=0, tiled=True).astype(f32)
    x = tokens[0].astype(f32)
    scale = lax.rsqrt(jnp.mean(x * x, axis=1, keepdims=True) + EPS)
    xn = (x * scale * gains).astype(bf16)
    xns = lax.all_gather(xn, TP, axis=0, tiled=True)
    ups = lax.all_gather(grad_out[0], TP, axis=0, tiled=True)
    lens = lax.all_gather(lengths, TP, axis=0, tiled=True)
    rows = lens.shape[0]
    tall = rows * length

    def time_major(a):
        return a.reshape(rows, length, -1).transpose(1, 0, 2).reshape(tall, -1)

    def row_major(a):
        return a.reshape(length, rows, -1).transpose(1, 0, 2).reshape(tall, -1)

    same, live = masks(lens, length)
    zz = time_major(jnp.dot(xns, win, preferred_element_type=f32))
    u = zz[:, :channels].reshape(length, rows, channels)
    g = zz[:, channels:]
    c = bias + taps[:, 3] * u
    shifted = []
    for offset in range(1, 4):
        earlier = jnp.pad(u, ((offset, 0), (0, 0), (0, 0)))[:length] * same[offset - 1][:, :, None]
        shifted.append(earlier)
        c = c + taps[:, 3 - offset] * earlier
    sig = jax.nn.sigmoid(c)
    v16 = (c * sig).astype(bf16).reshape(tall, channels)
    v = v16.astype(f32)
    p = lax.psum(jnp.dot(v16, wx, preferred_element_type=f32), TP)
    dl = p[:, :rank].astype(bf16)
    kq = p[:, rank:]
    dims_cols = (((1,), (1,)), ((), ()))
    dims_rows = (((0,), (0,)), ((), ()))
    pre = lax.dot_general(dl, wdt, dims_cols, preferred_element_type=f32) + dtb
    dm = time_major(lax.dot_general(ups, wout, dims_cols, preferred_element_type=f32))
    flags = jnp.pad(jnp.stack([same[0].reshape(tall), live.reshape(tall)], axis=1), ((0, 0), (0, 126)))
    hi = kq.astype(bf16)
    mid = (kq - hi.astype(f32)).astype(bf16)
    low = (kq - hi.astype(f32) - mid.astype(f32)).astype(bf16)
    kq3 = jnp.concatenate([hi, mid, low], axis=1)
    keys = kq[:, :states]
    sk = jnp.broadcast_to(jnp.sum(keys * keys, axis=1, keepdims=True), (tall, 8))
    m, dg, dpre, dv, dkq, stats = mixer(flags, kq3, sk, pre, v, g, dm, skips[None], states=states, width=256, unroll=4)
    stats = stats.transpose(1, 2, 0, 3).reshape(3, 8, channels)
    dskip = jnp.sum(stats[0], axis=0)
    total = lax.psum(jnp.sum(stats[1]), ALL)
    peak = lax.pmax(jnp.max(stats[2]), ALL)
    beta_mean = total / float(groups * ways * length * inner)
    m16 = row_major(m).astype(bf16)
    out = jnp.dot(m16, wout, preferred_element_type=f32).astype(bf16)
    out = lax.psum_scatter(out, TP, scatter_dimension=0, tiled=True)
    block_out = (x + out.astype(f32)).astype(bf16)
    grad_wout = lax.dot_general(m16, ups, dims_rows, preferred_element_type=f32).astype(bf16)
    grad_wout = lax.psum_scatter(grad_wout, "dp", scatter_dimension=0, tiled=True)
    dpre16 = dpre.astype(bf16)
    grad_dtb = jnp.sum(dpre16.astype(f32), axis=0)
    grad_wdt = lax.dot_general(dpre16, dl, dims_rows, preferred_element_type=f32)
    ddl = jnp.dot(dpre16, wdt, preferred_element_type=f32)
    dkq = dkq[:, :2 * states] + dkq[:, 2 * states:2 * states + 1] * jnp.pad(keys, ((0, 0), (0, states)))
    dp16 = lax.psum(jnp.concatenate([ddl, dkq], axis=1), TP).astype(bf16)
    grad_wx = lax.dot_general(v16, dp16, dims_rows, preferred_element_type=f32)
    dvt = dv + lax.dot_general(dp16, wx, dims_cols, preferred_element_type=f32)
    dc = (dvt * (sig.reshape(tall, channels) * (1.0 + c.reshape(tall, channels) * (1.0 - sig.reshape(tall, channels))))).reshape(length, rows, channels)
    du = taps[:, 3] * dc
    grad_taps = [jnp.sum(dc * u, axis=(0, 1))]
    for offset in range(1, 4):
        grad_taps.append(jnp.sum(dc * shifted[offset - 1], axis=(0, 1)))
        du = du + taps[:, 3 - offset] * jnp.pad((dc * same[offset - 1][:, :, None])[offset:], ((0, offset), (0, 0), (0, 0)))
    grad_conv = jnp.stack(grad_taps[::-1] + [jnp.sum(dc, axis=(0, 1)), grad_dtb, dskip], axis=1)
    dz = row_major(jnp.concatenate([du.reshape(tall, channels), dg], axis=1)).astype(bf16)
    gwin = lax.dot_general(xns, dz, dims_rows, preferred_element_type=f32).astype(bf16)
    gwin = lax.psum_scatter(gwin, "dp", scatter_dimension=0, tiled=True)
    gwin = lax.all_to_all(gwin.reshape(ways, own_d, 2 * channels), TP, split_axis=0, concat_axis=0, tiled=True)
    grad_win = gwin.reshape(ways, own_d, 2, groups, own_e).transpose(1, 2, 3, 0, 4).reshape(own_d, 2 * inner).astype(f32)
    dxn = lax.dot_general(dz, win, dims_cols, preferred_element_type=f32).astype(bf16)
    dxn = lax.psum_scatter(dxn, TP, scatter_dimension=0, tiled=True).astype(f32)
    small_grad = lax.psum_scatter(jnp.concatenate([grad_wx, grad_wdt, grad_conv], axis=1), "dp", scatter_dimension=0, tiled=True)
    inner_grad = dxn * gains
    dxx = scale * inner_grad - x * (scale * scale * scale) * (jnp.sum(inner_grad * x, axis=1, keepdims=True) / model)
    grad_tokens = (grad_out[0].astype(f32) + dxx).astype(bf16)
    grad_gain = lax.psum_scatter(jnp.sum(dxn * x * scale, axis=0), ALL, scatter_dimension=0, tiled=True)
    at = rank + 2 * states
    return (
        block_out[None],
        grad_tokens[None],
        grad_gain,
        grad_win,
        small_grad[:, at + rank:at + rank + 4],
        small_grad[:, at + rank + 4],
        small_grad[:, :at],
        small_grad[:, at:at + rank],
        small_grad[:, at + rank + 5],
        small_grad[:, at + rank + 6],
        grad_wout.astype(f32),
        beta_mean,
        peak,
    )


def on_device_direct(tokens, lengths, gain, w_in, conv_w, conv_b, w_x, w_dt, dt_bias, skip, w_out, grad_out):
    groups, ways = 4, 8
    length, model = tokens.shape[1:]
    own_d = w_in.shape[0]
    own_e = conv_w.shape[0]
    inner = w_in.shape[1] // 2
    channels = inner // ways
    rank = w_dt.shape[1]
    states = (w_x.shape[1] - rank) // 2
    gain = gain[None]
    xnt, ups, win, wout, smalls, vecs, gains, masks, live, u, g, v, vt, slope, dl, kq = k1(
        tokens, grad_out, w_in, w_out, w_x.T, w_dt, gain, lengths, conv_w.T, conv_b[None], dt_bias[None], skip[None])
    acc, mt, dg, gwdt, ups, dv, part, stat = k2(dl, kq, smalls, vecs, masks, live, v, g, ups, wout, states)
    sums = k3(
        part, stat, smalls, vecs, gains, gwdt, masks, tokens, grad_out, acc, mt, dg, dv, slope, u, vt, xnt,
        win.reshape(groups, ways * own_d, 2 * channels), ups)
    block_out, grad_tokens, grad_gain, grad_win, convw, convb, gwx, gwdt, dtb, dskip, grad_wout, mean, peak = k4(
        float(groups * ways * length * inner), *sums, w_in, gain, rank + 2 * states)
    return (
        block_out, grad_tokens, grad_gain[0], grad_win, convw.T, convb[0], gwx.T, gwdt, dtb[0], dskip[0], grad_wout, mean[0, 0], peak[0, 0],
    )


def on_device_any(*args):
    if lax.axis_size("dp") == 4 and lax.axis_size("z") == 4:
        return on_device_direct(*args)
    return on_device(*args)


def solution(mesh):
    wide, narrow = mesh.devices.shape
    fine = Mesh(mesh.devices.reshape(wide // 2, 2, narrow), ALL)
    cut = (P(ALL, None), P(ALL))
    in_specs = (P(ALL, None, None), cut[0], cut[1], cut[0], cut[0], cut[1], cut[0], cut[0], cut[1], cut[1], cut[0], P(ALL, None, None))
    out_specs = (P(ALL, None, None), P(ALL, None, None), cut[1], cut[0], cut[0], cut[1], cut[0], cut[0], cut[1], cut[1], cut[0], P(), P())
    return jax.shard_map(on_device_any, mesh=fine, in_specs=in_specs, out_specs=out_specs, check_vma=False)
```

```python
import functools
import jax, jax.numpy as jnp
from jax import lax
from jax.experimental import pallas as pl
from jax.experimental.pallas import tpu as pltpu
from jax.sharding import Mesh, PartitionSpec as P

DOCS = 4
EPS = 1e-05
ALL = ("dp", "core", "z")
TP = ("core", "z")

f32 = jnp.float32
bf16 = jnp.bfloat16

def fold(x):
    total = x[:, :128]
    for at in range(128, x.shape[1], 128):
        total = total + x[:, at:at+128]
    return total

def mixer_kernel(states, unroll, chunk, flags_ref, kq3_ref, sk_ref, pre_ref, v_ref, g_ref, dm_ref, skip_ref,
                 m_ref, dg_ref, dpre_ref, dv_ref, dkq_ref, stat_ref, s_ref, h_ref, rate_ref, rv_ref, kb_ref, drr_ref):
    rows = pre_ref.shape[0]
    width = pre_ref.shape[1]
    steps = rows // 8
    wide = states * 128
    spread_rows = kq3_ref.shape[1]
    def spread(i, c):
        r = pl.ds(pl.multiple_of(i * chunk, chunk), chunk)
        left = kq3_ref[r, :]
        for part in range(0, 2 * wide, 512):
            ids = lax.broadcasted_iota(jnp.int32, (spread_rows, 512), 0) % (2 * states)
            col = lax.broadcasted_iota(jnp.int32, (spread_rows, 512), 1) // 128 + part // 128
            hot = jnp.where(ids == col, 1.0, 0.0).astype(bf16)
            kb_ref[r, part:part+512] = jnp.dot(left, hot, preferred_element_type=f32)
        return c
    lax.fori_loop(0, rows // chunk, spread, 0)

    def before(i, c):
        r = pl.ds(pl.multiple_of(i * 64, 64), 64)
        live = flags_ref[r, 1:2]
        beta = jax.nn.sigmoid(pre_ref[r, :])
        part = 1.0 / (1.0 + beta * sk_ref[r, 0:1])
        rate = beta * part
        rate_ref[r, :] = rate
        v = v_ref[r, :]
        rv_ref[r, :] = rate * v
        dpre_ref[r, :] = part * part * beta * (1.0 - beta)
        g = g_ref[r, :]
        sg = jax.nn.sigmoid(g)
        dm = dm_ref[r, :] * live
        dv_ref[r, :] = dm * (g * sg)
        dg_ref[r, :] = dm * (sg * (1.0 + g * (1.0 - sg)))
        return c
    lax.fori_loop(0, rows // 64, before, 0)

    s_ref[0, 0] = jnp.zeros(s_ref.shape[2:], f32)

    group = unroll
    tile = lambda x: jnp.concatenate([x] * (width // 128), axis=1)
    span = group * 8
    at = [slice(j * 8, j * 8 + 8) for j in range(group)]
    def view(ref, i):
        return ref.at[pl.ds(pl.multiple_of(i * span, span), span)]

    def forward(i, carry):
        flags, rates, rvs, vs, kbs, ms = [view(x, i) for x in (flags_ref, rate_ref, rv_ref, v_ref, kb_ref, m_ref)]
        keep = [jnp.broadcast_to(flags[r, 0:1], (8, 128)) for r in at]
        rate = [rates[r, :] for r in at]
        rv = [rvs[r, :] for r in at]
        y = [skip_ref[...] * vs[r, :] for r in at]
        for n in range(states):
            state = s_ref[i, 0, n]
            for j, r in enumerate(at):
                kb = kbs[r, n*128:(n+1)*128]
                qb = kbs[r, wide+n*128:wide+(n+1)*128]
                state = (tile(keep[j]) - rate[j] * tile(kb * kb * keep[j])) * state + rv[j] * tile(kb)
                if j < group - 1:
                    s_ref[i, j + 1, n] = state
                else:
                    s_ref[i + 1, 0, n] = state
                y[j] = y[j] + state * tile(qb)
        for j, r in enumerate(at):
            ms[r, :] = y[j]
        return carry

    lax.fori_loop(0, steps // group, forward, 0)
    h_ref[...] = jnp.zeros_like(h_ref)

    def backward(step, carry):
        i = steps // group - 1 - step
        flags, rates, rvs, vs, kbs, dvs, dpres, drrs = [view(x, i) for x in (flags_ref, rate_ref, rv_ref, v_ref, kb_ref, dv_ref, dpre_ref, drr_ref)]
        keep = [jnp.broadcast_to(flags[r, 0:1], (8, 128)) for r in at]
        rate = [rates[r, :] for r in at]
        rv = [rvs[r, :] for r in at]
        dy = [dvs[r, :] for r in at]
        hk = [jnp.zeros((8, width), f32) for r in at]
        hs2 = [jnp.zeros((8, width), f32) for r in at]
        for n in range(states):
            ah = h_ref[n]
            after_ = s_ref[i + 1, 0, n]
            for j in range(group - 1, -1, -1):
                r = at[j]
                kb = kbs[r, n*128:(n+1)*128]
                qb = kbs[r, wide+n*128:wide+(n+1)*128]
                kk = kb * keep[j]
                held = tile(kb * kk)
                h = dy[j] * tile(qb) + ah
                prior = s_ref[i, j, n]
                hs = h * prior
                hk[j] = hk[j] + h * tile(kb)
                hs2[j] = hs2[j] + hs * held
                kbs[r, n*128:(n+1)*128] = fold(h * rv[j]) - 2.0 * kk * fold(hs * rate[j])
                kbs[r, wide+n*128:wide+(n+1)*128] = fold(dy[j] * after_)
                after_ = prior
                ah = (tile(keep[j]) - rate[j] * held) * h
            h_ref[n] = ah
        for j, r in enumerate(at):
            v = vs[r, :]
            drate = v * hk[j] - hs2[j]
            drrs[r, :] = fold(drate * rate[j] * rate[j]) * (-2.0)
            dpres[r, :] = drate * dpres[r, :]
            dvs[r, :] = rate[j] * hk[j] + skip_ref[...] * dy[j]
            stat_ref[0, 0] += dy[j] * v
        return carry

    stat_ref[...] = jnp.zeros_like(stat_ref)
    lax.fori_loop(0, steps // group, backward, 0)

    first = pl.program_id(0) == 0
    def gather(i, c):
        r = pl.ds(pl.multiple_of(i * chunk, chunk), chunk)
        total = jnp.zeros((chunk, 128), f32)
        for part in range(0, 2 * wide, 512):
            row = lax.broadcasted_iota(jnp.int32, (512, 128), 0) // 128 + part // 128
            col = lax.broadcasted_iota(jnp.int32, (512, 128), 1)
            hot = jnp.where(row == col, 1.0, 0.0).astype(bf16)
            total += jnp.dot(kb_ref[r, part:part+512].astype(bf16), hot, preferred_element_type=f32)
        col = lax.broadcasted_iota(jnp.int32, (128, 128), 1)
        hot = jnp.where(col == 2 * states, 1.0, 0.0).astype(bf16)
        total += jnp.dot(drr_ref[r, :].astype(bf16), hot, preferred_element_type=f32)
        dkq_ref[r, :] = jnp.where(first, total, dkq_ref[r, :] + total)
        return c
    lax.fori_loop(0, rows // chunk, gather, 0)

    def after(i, c):
        r = pl.ds(pl.multiple_of(i * 64, 64), 64)
        live = flags_ref[r, 1:2]
        y = m_ref[r, :]
        g = g_ref[r, :]
        m_ref[r, :] = y * (g * jax.nn.sigmoid(g)) * live
        dg_ref[r, :] = y * dg_ref[r, :]
        shown = (jax.nn.sigmoid(pre_ref[r, :]) * live).reshape(8, 8, width)
        stat_ref[0, 1] += jnp.sum(shown, axis=0)
        stat_ref[0, 2] = jnp.maximum(stat_ref[0, 2], jnp.max(shown, axis=0))
        return c
    lax.fori_loop(0, rows // 64, after, 0)

def mixer(flags, kq3, sk, pre, v, g, dm, skip, states=16, width=256, unroll=1):
    rows, total = pre.shape
    steps = rows // 8
    tiles = total // width
    big = jax.ShapeDtypeStruct((rows, total), f32)
    cut = pl.BlockSpec((rows, width), lambda h: (0, h))
    whole = lambda a: pl.BlockSpec(a.shape, lambda h: (0,) * a.ndim)
    return pl.pallas_call(
        functools.partial(mixer_kernel, states, unroll, min(256, rows)),
        grid=(tiles,),
        out_shape=(big, big, big, big, jax.ShapeDtypeStruct((rows, 128), f32), jax.ShapeDtypeStruct((tiles, 3, 8, width), f32)),
        in_specs=[whole(flags), whole(kq3), whole(sk), cut, cut, cut, cut, pl.BlockSpec((1, width), lambda h: (0, h))],
        out_specs=(cut, cut, cut, cut, pl.BlockSpec((rows, 128), lambda h: (0, 0)), pl.BlockSpec((1, 3, 8, width), lambda h: (h, 0, 0, 0))),
        scratch_shapes=[pltpu.VMEM((steps//unroll+1, unroll, states, 8, width), f32), pltpu.VMEM((states, 8, width), f32)] + [pltpu.VMEM((rows, width), f32)]*2
          + [pltpu.VMEM((rows, 2*states*128), f32), pltpu.VMEM((rows, 128), f32)],
        compiler_params=pltpu.CompilerParams(vmem_limit_bytes=60*1024*1024),
    )(flags, kq3, sk, pre, v, g, dm, skip)


MESH = pl.DeviceIdType.MESH


def flip(value, bit):
    return value + bit * (1 - 2 * ((value // bit) % 2))


def place():
    d, c, z = lax.axis_index("dp"), lax.axis_index("core"), lax.axis_index("z")
    return d, c, z


def put(src, dst, send, recv, device):
    copy = pltpu.make_async_remote_copy(src_ref=src, dst_ref=dst, send_sem=send, recv_sem=recv, device_id=device, device_id_type=MESH)
    copy.start()
    return copy


def landed(slot, sem, device):
    pltpu.make_async_remote_copy(src_ref=slot, dst_ref=slot, send_sem=sem, recv_sem=sem, device_id=device, device_id_type=MESH).wait_recv()


def sent(slot, sem, device):
    pltpu.make_async_remote_copy(src_ref=slot, dst_ref=slot, send_sem=sem, recv_sem=sem, device_id=device, device_id_type=MESH).wait_send()


def greet(devices):
    barrier = pltpu.get_barrier_semaphore()
    for device in devices:
        pl.semaphore_signal(barrier, inc=1, device_id=device, device_id_type=MESH)
    pl.semaphore_wait(barrier, len(devices))


def mates():
    return [(a, k) for k in (0, 1, 3, 2) for a in (1, 0) if (a, k) != (0, 0)]


def mate(step, sign=1):
    d, c, z = place()
    a, k = step
    return d, (flip(c, 1) if a else c), lax.rem(z + sign * k + 4, 4)


def rank_of(device):
    return device[1] * 4 + device[2]


PIECES = 2


UP_HOPS = 2
LINE1 = bf16
LINE2 = bf16


def k1_kernel(tok_ref, up_ref, w_ref, wout_ref, wx_ref, wdt_ref, gain_ref, lens_ref, convw_ref, convb_ref, dtb_ref, skip_ref,
              xnt_out, ups_ref, win_out, wouts_ref, smalls_ref, vecs_ref, gains_ref, masks_out, live_out,
              u_out, g_out, v_out, vt_out, slope_out, dl_ref, kq_ref,
              masks_ref, live_ref, u_ref, g_ref, v_ref, vt_ref, slope_ref, save_sem, cols_ref, meta_ref, small_ref,
              xs_ref, xn_ref, xnt_ref, win_ref, metas_ref, part_ref, out_ref, sib_ref, base_ref, left_ref, right_ref, tor_ref, tol_ref,
              own_sem, ms, mr, qs, qr, xls, xlr, xrs, xrr, xcs, xcr, as_, ar, ps, pr, rs, rr, ws, wr, ts, tr, tls, tlr, trs, trr, tos, tor):
    d, c, z = place()
    j = c * 4 + z
    dx, dy, dd = flip(d, 1), flip(d, 2), flip(flip(d, 1), 2)
    xn, yn, dn = (dx, c, z), (dy, c, z), (dd, c, z)
    sib = (d, flip(c, 1), z)
    left = (d, c, lax.rem(z + 3, 4))
    right = (d, c, lax.rem(z + 1, 4))
    steps = mates()
    length = tok_ref.shape[1]
    model = tok_ref.shape[2]
    depth = cols_ref.shape[1]
    for rank in range(8):
        for n in range(8):
            cols_ref[rank, :, n * 128:(n + 1) * 128] = w_ref[:, (n * 8 + rank) * 128:(n * 8 + rank + 1) * 128]
    meta_ref[...] = jnp.zeros_like(meta_ref)
    meta_ref[0:1, 0:depth] = gain_ref[...].astype(f32)
    meta_ref[0:1, depth:2 * depth] = gain_ref[...].astype(f32)
    meta_ref[1:2, 0:5] = lens_ref[...].astype(f32)
    meta_ref[8:12, :] = convw_ref[...].astype(f32)
    meta_ref[12:13, :] = convb_ref[...].astype(f32)
    meta_ref[13:14, :] = dtb_ref[...].astype(f32)
    meta_ref[14:15, :] = skip_ref[...].astype(f32)
    narrow_rows = wx_ref.shape[0]
    small_ref[:, 0:128] = wx_ref[0:128, :].astype(f32).T.astype(bf16)
    tail = jnp.concatenate([wx_ref[128:narrow_rows, :].astype(f32), jnp.zeros((256 - narrow_rows, 128), f32)], axis=0)
    small_ref[:, 128:256] = tail.T.astype(bf16)
    small_ref[:, 256:384] = wdt_ref[...]
    greet([mate(s) for s in steps] + [xn, yn, dn])
    tiles = u_ref.shape[0]
    width = tiles * 128
    count = g_ref.shape[1]

    def rows(rank):
        return pl.ds(pl.multiple_of(rank * length, length), length)

    def block(group, rank):
        return pl.ds(pl.multiple_of((group * 8 + rank) * depth, depth), depth)

    own_e = wout_ref.shape[0]
    half_w = cols_ref.shape[2] // 2

    def part_w(q):
        return pl.ds(q * half_w, half_w)

    def part_e(group, start=0, size=own_e):
        return pl.ds(pl.multiple_of(group * own_e + start, 16), size)

    own = [
        pltpu.make_async_copy(tok_ref.at[0], xs_ref.at[rows(j)], own_sem.at[0]),
        pltpu.make_async_copy(up_ref.at[0], ups_ref.at[rows(j)], own_sem.at[1]),
        pltpu.make_async_copy(cols_ref.at[j], win_ref.at[block(d, j)], own_sem.at[2]),
        pltpu.make_async_copy(wout_ref, wouts_ref.at[part_e(d)], own_sem.at[3]),
        pltpu.make_async_copy(small_ref, smalls_ref.at[part_e(d)], own_sem.at[4]),
        pltpu.make_async_copy(meta_ref, metas_ref.at[d, j], own_sem.at[5]),
    ]
    for copy in own:
        copy.start()
    pending = []
    for i, s in enumerate(steps):
        to = mate(s)
        pending.append(put(meta_ref, metas_ref.at[d, j], ms.at[i], mr.at[i], to))
    for i, s in enumerate(steps):
        to = mate(s)
        pending.append(put(cols_ref.at[rank_of(to), :, part_w(0)], win_ref.at[block(d, j), part_w(0)], as_.at[i], ar.at[i], to))
    for i, to in enumerate((xn, yn, dn)):
        pending.append(put(small_ref, smalls_ref.at[part_e(d)], ps.at[32 + i], pr.at[32 + i], to))
    halves = own_e // 2
    pending.append(put(wout_ref, wouts_ref.at[part_e(d)], ws.at[0], wr.at[0], xn))
    pending.append(put(wout_ref, wouts_ref.at[part_e(d)], ws.at[1], wr.at[1], yn))
    own[2].wait()

    def own_part(q):
        slot = win_ref.at[block(d, j), part_w(q)]
        pending.append(put(slot, slot, ps.at[16 * q + 7], pr.at[16 * q + 7], xn))
        pending.append(put(slot, slot, ps.at[16 * q + 15], pr.at[16 * q + 15], yn))

    own_part(0)

    def row_start(ref, out, base):
        pending.append(put(ref.at[0], out.at[rows(j)], xcs.at[base + z], xcr.at[base + z], sib))

        @pl.when(z < 3)
        def _():
            put(ref.at[0], out.at[rows(j)], xls.at[base], xlr.at[base], right)

        @pl.when(z > 0)
        def _():
            put(ref.at[0], out.at[rows(j)], xrs.at[base], xrr.at[base], left)

    def row_hop(out, base, i, then=None, hops=3):
        if i >= hops:
            return

        @pl.when(z > i)
        def _():
            at = z - 1 - i
            slot = out.at[rows(c * 4 + at)]
            landed(slot, xlr.at[base + i], left)
            if i < hops - 1:
                @pl.when(z < 3)
                def _():
                    put(slot, slot, xls.at[base + i + 1], xlr.at[base + i + 1], right)
            put(slot, slot, xcs.at[base + at], xcr.at[base + at], sib)
            if then is not None:
                then(c * 4 + at)

        @pl.when(z < 3 - i)
        def _():
            at = z + 1 + i
            slot = out.at[rows(c * 4 + at)]
            landed(slot, xrr.at[base + i], right)
            if i < hops - 1:
                @pl.when(z > 0)
                def _():
                    put(slot, slot, xrs.at[base + i + 1], xrr.at[base + i + 1], left)
            put(slot, slot, xcs.at[base + at], xcr.at[base + at], sib)
            if then is not None:
                then(c * 4 + at)

    def row_end(out, base, hops=3):
        for i in range(hops):
            @pl.when((z < 3) & (z >= i))
            def _():
                sent(out.at[rows(j)], xls.at[base + i], right)

            @pl.when((z > 0) & (z <= 3 - i))
            def _():
                sent(out.at[rows(j)], xrs.at[base + i], left)
        for at in range(4):
            @pl.when((z != at) & (z <= at + hops) & (at <= z + hops))
            def _():
                sent(out.at[rows(j)], xcs.at[base + at], sib)

    row_start(tok_ref, xs_ref, 0)
    own[5].wait()
    for i, s in enumerate(steps):
        landed(metas_ref.at[d, rank_of(mate(s, -1))], mr.at[i], xn)
    for i, to in enumerate((xn, yn, dn)):
        pending.append(put(metas_ref.at[d], metas_ref.at[d], qs.at[i], qr.at[i], to))
    slots = {7: j}
    for i, s in enumerate(steps):
        slots[i] = rank_of(mate(s, -1))
    order = [7] + list(range(7))

    def pass_on(i, q):
        src = mate(steps[i], -1)
        slot = win_ref.at[block(d, slots[i]), part_w(q)]
        landed(slot, ar.at[7 * q + i], src)
        pending.append(put(slot, slot, ps.at[16 * q + i], pr.at[16 * q + i], xn))
        pending.append(put(slot, slot, ps.at[16 * q + 8 + i], pr.at[16 * q + 8 + i], yn))

    def relay(k, q):
        i = order[k]
        slot = win_ref.at[block(dx, slots[i]), part_w(q)]
        landed(slot, pr.at[16 * q + i], xn)
        if k % 2 == 0:
            pending.append(put(slot, slot, rs.at[8 * q + k // 2], rr.at[8 * q + k // 2], yn))
        slot = win_ref.at[block(dy, slots[i]), part_w(q)]
        landed(slot, pr.at[16 * q + 8 + i], yn)
        if k % 2 == 1:
            pending.append(put(slot, slot, rs.at[8 * q + 4 + k // 2], rr.at[8 * q + 4 + k // 2], xn))

    def relayed(q):
        for k, i in enumerate(order):
            slot = win_ref.at[block(dd, slots[i]), part_w(q)]
            if k % 2 == 0:
                landed(slot, rr.at[8 * q + k // 2], yn)
            else:
                landed(slot, rr.at[8 * q + 4 + k // 2], xn)

    pass_on(0, 0)
    for i, (to, at) in enumerate(((xn, dx), (yn, dy), (dn, dd))):
        landed(metas_ref.at[at], qr.at[i], to)
    lens = jnp.concatenate([metas_ref[d, r, 1:2, :] for r in range(8)], axis=0)
    ends = []
    last = jnp.zeros((8, 1), f32)
    for i in range(5):
        last = last + lens[:, i:i + 1]
        ends.append(jnp.broadcast_to(last, (8, 128)))

    def mask_step(t, carry):
        here = t.astype(f32)

        def segment(at):
            total = jnp.zeros((8, 128), f32)
            for end in ends:
                total = total + jnp.where(end <= at, 1.0, 0.0)
            return total

        now = segment(here)
        r = pl.ds(pl.multiple_of(t * 8, 8), 8)
        for o in range(1, 4):
            same = jnp.where(segment(here - o) == now, 1.0, 0.0)
            masks_ref[o - 1, r, :] = jnp.where(here >= o, same, 0.0)
        live_ref[0, r, :] = jnp.where(now < DOCS, 1.0, 0.0)
        return carry

    lax.fori_loop(0, length, mask_step, 0)
    masks_ref[:, count:, :] = jnp.zeros((3, masks_ref.shape[1] - count, 128), f32)
    lane = lax.broadcasted_iota(jnp.int32, (1, 128), 1)
    for group in range(4):
        for pair in range(4):
            at = group * 512 + pair * 128
            gains_ref[:, at:at + 128] = jnp.where(lane < depth, metas_ref[group, 2 * pair, 0:1, :], metas_ref[group, 2 * pair + 1, 0:1, :])
        vecs_ref[:, group * own_e:(group + 1) * own_e] = metas_ref[group, j, 8:16, :]

    def normalize(rank):
        def body(i, carry):
            r = pl.ds(pl.multiple_of(rank * length + i * 16, 16), 16)
            x = xs_ref[r, :].astype(f32)
            scale = lax.rsqrt(jnp.sum(x * x, axis=1, keepdims=True) * (1.0 / model) + EPS)
            xn_ref[r, :] = (x * scale * gains_ref[...]).astype(bf16)
            return carry

        lax.fori_loop(0, length // 16, body, 0, unroll=4)

    for i in range(1, 4):
        pass_on(i, 0)
    slot = wouts_ref.at[part_e(dx)]
    landed(slot, wr.at[0], xn)
    slot = wouts_ref.at[part_e(dx, 0, halves)]
    pending.append(put(slot, slot, ws.at[2], wr.at[2], yn))
    slot = wouts_ref.at[part_e(dy)]
    landed(slot, wr.at[1], yn)
    slot = wouts_ref.at[part_e(dy, halves, halves)]
    pending.append(put(slot, slot, ws.at[3], wr.at[3], xn))

    for i in range(4, 7):
        pass_on(i, 0)
    own[0].wait()
    normalize(j)
    row_hop(xs_ref, 0, 0, normalize)
    for i, s in enumerate(steps):
        to = mate(s)
        pending.append(put(cols_ref.at[rank_of(to), :, part_w(1)], win_ref.at[block(d, j), part_w(1)], as_.at[7 + i], ar.at[7 + i], to))
    own_part(1)
    for k in range(8):
        relay(k, 0)
    row_hop(xs_ref, 0, 1, normalize)
    for i in range(7):
        pass_on(i, 1)
    row_start(up_ref, ups_ref, 4)
    row_hop(xs_ref, 0, 2, normalize)
    for at in range(4):
        rank = flip(c, 1) * 4 + at
        landed(xs_ref.at[rows(rank)], xcr.at[at], sib)
        normalize(rank)
    relayed(0)
    own += [pltpu.make_async_copy(xnt_ref, xnt_out, own_sem.at[6]), pltpu.make_async_copy(win_ref, win_out, own_sem.at[7])]
    lead = u_ref.shape[1] - count
    u_ref[:, 0:lead, :] = jnp.zeros((tiles, lead, 128), f32)

    tile = 256

    def spread(out, first, start):
        def body(i, carry):
            product = jnp.dot(xn_ref[...], win_ref[:, pl.ds(pl.multiple_of(start + i * tile, tile), tile)], preferred_element_type=f32)
            for r in range(8):
                for part in range(0, tile, 128):
                    out[i * (tile // 128) + part // 128, pl.ds(first + r, length, stride=8), :] = product[r * length:(r + 1) * length, part:part + 128]
            return carry

        lax.fori_loop(0, width // tile, body, 0)

    spread(u_ref, lead, 0)
    taps = [vecs_ref[o:o + 1, :] for o in range(4)]
    bias = vecs_ref[4:5, :]

    def conv_step(i, carry):
        r = pl.ds(pl.multiple_of(i * 32, 32), 32)
        for n in range(tiles):
            lanes = slice(n * 128, n * 128 + 128)
            total = bias[:, lanes] + taps[3][:, lanes] * u_ref[n, pl.ds(pl.multiple_of(lead + i * 32, 8), 32), :]
            for o in range(1, 4):
                total = total + taps[3 - o][:, lanes] * (u_ref[n, pl.ds(pl.multiple_of(lead + i * 32 - 8 * o, 8), 32), :] * masks_ref[o - 1, r, :])
            sig = jax.nn.sigmoid(total)
            v_ref[n, r, :] = (total * sig).astype(bf16).astype(f32)
            slope_ref[n, r, :] = sig * (1.0 + total * (1.0 - sig))
        return carry

    lax.fori_loop(0, count // 32, conv_step, 0, unroll=2)
    for k in range(8):
        relay(k, 1)
    for copy in own[3:5]:
        copy.wait()
    for i, (to, at) in enumerate(((xn, dx), (yn, dy), (dn, dd))):
        landed(smalls_ref.at[part_e(at)], pr.at[32 + i], to)
    quarter = count // 4
    narrow = smalls_ref[:, 128:256].astype(f32)
    packed = jnp.zeros((quarter, 128), f32)
    for b in range(4):
        r = slice(b * quarter, (b + 1) * quarter)
        values = jnp.concatenate([v_ref[n, r, :].astype(bf16) for n in range(tiles)], axis=1)
        part_ref[r, :] = jnp.dot(values, smalls_ref[:, 0:128], preferred_element_type=f32)
        turned = pltpu.roll(narrow, 32 * b, 1) if b else narrow
        packed = packed + jnp.dot(values, turned.astype(bf16), preferred_element_type=f32)
    part_ref[count:count + quarter, :] = packed
    saves = [(u_ref, u_out), (v_ref, v_out), (slope_ref, slope_out), (masks_ref, masks_out), (live_ref, live_out), (g_ref, g_out), (vt_ref, vt_out)]
    saves = [pltpu.make_async_copy(a, b, save_sem.at[i]) for i, (a, b) in enumerate(saves)]
    for copy in saves[:5]:
        copy.start()

    def early():
        row_hop(ups_ref, 4, 0, None, UP_HOPS)

    def between():
        relayed(1)
        own[7].start()
        spread(g_ref, 0, width)
        saves[5].start()

    def late():
        def turn_x(i, carry):
            part = pl.ds(pl.multiple_of(i * 128, 128), 128)
            for rank in range(8):
                r = slice(rank * length, (rank + 1) * length)
                xnt_ref[part, r] = xn_ref[r, part].T
            return carry

        lax.fori_loop(0, model // 128, turn_x, 0)
        own[6].start()
        row_hop(ups_ref, 4, 1, None, UP_HOPS)

        def turn_v(i, carry):
            r = pl.ds(pl.multiple_of(i * 128, 128), 128)
            for n in range(tiles):
                vt_ref[n * 128:(n + 1) * 128, r] = v_ref[n, r, :].T.astype(bf16)
            return carry

        lax.fori_loop(0, count // 128, turn_v, 0)
        saves[6].start()

    line_total(part_ref, out_ref, sib_ref, base_ref, left_ref, right_ref, tor_ref, tol_ref, ts, tr, tls, tlr, trs, trr, tos, tor, early, between, late)
    dl_ref[...] = out_ref[0:count, :].astype(bf16)
    for b in range(4):
        packed = out_ref[count:count + quarter, :]
        kq_ref[b * quarter:(b + 1) * quarter, :] = pltpu.roll(packed, 128 - 32 * b, 1) if b else packed
    row_hop(ups_ref, 4, 2, None, UP_HOPS)
    for at in range(4):
        @pl.when((z <= at + UP_HOPS) & (at <= z + UP_HOPS))
        def _():
            landed(ups_ref.at[rows(flip(c, 1) * 4 + at)], xcr.at[4 + at], sib)

    landed(wouts_ref.at[part_e(dd, 0, halves)], wr.at[2], yn)
    landed(wouts_ref.at[part_e(dd, halves, halves)], wr.at[3], xn)
    row_end(xs_ref, 0)
    row_end(ups_ref, 4, UP_HOPS)
    own[1].wait()
    for copy in saves:
        copy.wait()
    own[6].wait()
    own[7].wait()
    for copy in pending:
        copy.wait_send()


def line_total(part_ref, out_ref, sib_ref, base_ref, left_ref, right_ref, tor_ref, tol_ref, ss, sr, ls, lr, rs, rr, os_, or_, early, between, late):
    d, c, z = place()
    sib = (d, flip(c, 1), z)
    left = (d, c, lax.rem(z + 3, 4))
    right = (d, c, lax.rem(z + 1, 4))
    rows = part_ref.shape[0] // 2
    piece = rows // PIECES
    mine, theirs = c * rows, flip(c, 1) * rows

    def cut(p):
        return pl.ds(p * piece, piece)

    def far(base, p):
        return pl.ds(pl.multiple_of(base + p * piece, 8), piece)

    for p in range(PIECES):
        put(part_ref.at[far(theirs, p)], sib_ref.at[cut(p)], ss.at[p], sr.at[p], sib)
    for p in range(PIECES):
        landed(sib_ref.at[cut(p)], sr.at[p], sib)
        value = part_ref[far(mine, p), :] + sib_ref[cut(p), :]
        out_ref[far(mine, p), :] = value
        base_ref[cut(p), :] = value.astype(base_ref.dtype)

        @pl.when(z == 0)
        def _():
            put(base_ref.at[cut(p)], left_ref.at[cut(p)], rs.at[p], lr.at[p], right)

        @pl.when(z == 3)
        def _():
            put(base_ref.at[cut(p)], right_ref.at[cut(p)], ls.at[p], rr.at[p], left)

    early()

    def from_left(p):
        landed(left_ref.at[cut(p)], lr.at[p], left)

        @pl.when(z < 3)
        def _():
            tor_ref[cut(p), :] = (out_ref[far(mine, p), :] + left_ref[cut(p), :].astype(f32)).astype(tor_ref.dtype)
            put(tor_ref.at[cut(p)], left_ref.at[cut(p)], rs.at[p], lr.at[p], right)

    def from_right(p):
        landed(right_ref.at[cut(p)], rr.at[p], right)

        @pl.when(z > 0)
        def _():
            tol_ref[cut(p), :] = (out_ref[far(mine, p), :] + right_ref[cut(p), :].astype(f32)).astype(tol_ref.dtype)
            put(tol_ref.at[cut(p)], right_ref.at[cut(p)], ls.at[p], rr.at[p], left)

    @pl.when(z == 1)
    def _():
        for p in range(PIECES):
            from_left(p)

    @pl.when(z == 2)
    def _():
        for p in range(PIECES):
            from_right(p)

    between()

    @pl.when(z < 2)
    def _():
        for p in range(PIECES):
            from_right(p)

    @pl.when(z >= 2)
    def _():
        for p in range(PIECES):
            from_left(p)

    for p in range(PIECES):
        @pl.when(z > 0)
        def _():
            out_ref[far(mine, p), :] += left_ref[cut(p), :].astype(f32)

        @pl.when(z < 3)
        def _():
            out_ref[far(mine, p), :] += right_ref[cut(p), :].astype(f32)

        put(out_ref.at[far(mine, p)], out_ref.at[far(mine, p)], os_.at[p], or_.at[p], sib)
    late()
    for p in range(PIECES):
        landed(out_ref.at[far(theirs, p)], or_.at[p], sib)
        sent(out_ref.at[far(mine, p)], os_.at[p], sib)
        sent(part_ref.at[far(theirs, p)], ss.at[p], sib)

        @pl.when(z < 3)
        def _():
            sent(base_ref.at[cut(p)], rs.at[p], right)

        @pl.when(z > 0)
        def _():
            sent(base_ref.at[cut(p)], ls.at[p], left)


def k1(tokens, upstream, w_in, w_out, w_x, w_dt, gain, lengths, conv_w, conv_b, dt_bias, skip):
    groups, ways = 4, 8
    small = jax.ShapeDtypeStruct((128, 384), bf16)
    cols = jax.ShapeDtypeStruct((ways, w_in.shape[0], w_in.shape[1] // ways), bf16)
    meta = jax.ShapeDtypeStruct((16, 128), f32)
    like = jax.ShapeDtypeStruct
    length, model = tokens.shape[1:]
    count = ways * length
    channels = groups * w_out.shape[0]
    dma = lambda n: pltpu.SemaphoreType.DMA((n,))
    some = pl.BlockSpec(memory_space=pl.ANY)
    far = pl.BlockSpec(memory_space=pltpu.HBM)
    here = pl.BlockSpec(memory_space=pltpu.VMEM)
    packed = count + count // 4
    return pl.pallas_call(
        k1_kernel,
        out_shape=(
            like((model, count), bf16),
            like((count, model), bf16),
            like((groups * ways * cols.shape[1], cols.shape[2]), bf16),
            like((channels, model), bf16),
            like((channels, small.shape[1]), bf16),
            like((8, channels), f32),
            like((1, model), f32),
            like((3, count + 32, 128), f32),
            like((1, count, 128), f32),
            like((channels // 128, count + 24, 128), f32),
            like((channels // 128, count, 128), f32),
            like((channels // 128, count, 128), f32),
            like((channels, count), bf16),
            like((channels // 128, count, 128), f32),
            like((count, 128), bf16),
            like((count, 128), f32),
        ),
        in_specs=[some] * 2 + [here, some] + [here] * 8,
        out_specs=(far,) * 4 + (here,) * 3 + (far,) * 7 + (here,) * 2,
        scratch_shapes=[
            pltpu.VMEM((3, count + 32, 128), f32),
            pltpu.VMEM((1, count, 128), f32),
            pltpu.VMEM((channels // 128, count + 24, 128), f32),
            pltpu.VMEM((channels // 128, count, 128), f32),
            pltpu.VMEM((channels // 128, count, 128), f32),
            pltpu.VMEM((channels, count), bf16),
            pltpu.VMEM((channels // 128, count, 128), f32),
            dma(7),
            pltpu.VMEM(cols.shape, bf16),
            pltpu.VMEM(meta.shape, f32),
            pltpu.VMEM(small.shape, bf16),
            pltpu.VMEM((count, model), bf16),
            pltpu.VMEM((count, model), bf16),
            pltpu.VMEM((model, count), bf16),
            pltpu.VMEM((groups * ways * cols.shape[1], cols.shape[2]), bf16),
            pltpu.VMEM((groups, ways) + meta.shape, f32),
            pltpu.VMEM((packed, 128), f32),
            pltpu.VMEM((packed, 128), f32),
        ] + [pltpu.VMEM((packed // 2, 128), f32)] + [pltpu.VMEM((packed // 2, 128), LINE1)] * 5
        + [dma(8), dma(7), dma(7), dma(3), dma(3), dma(8), dma(8), dma(8), dma(8), dma(8), dma(8), dma(14), dma(14), dma(35), dma(35), dma(16), dma(16), dma(4), dma(4)]
        + [dma(PIECES) for _ in range(8)],
        compiler_params=pltpu.CompilerParams(collective_id=0, has_side_effects=True, vmem_limit_bytes=56 * 1024 * 1024),
    )(tokens, upstream, w_in, w_out, w_x, w_dt, gain, lengths, conv_w, conv_b, dt_bias, skip)


GROUP = 4


def k2_kernel(states, dl_ref, kq_ref, wdt_ref, vecs_ref, keep_ref, live_ref, v_ref, g_ref, ups_any, wout_any,
              acc_out, mt_ref, dg_ref, gwdt_ref, ups_out, dv_ref, part_ref, stat_ref,
              ups_ref, loads, stores, zs, zr, cs, cr, ls, lr, ss, sr, m_ref, wout_ref, acc_ref, recv_ref, dpre_ref, s_ref, h_ref, rate_ref, w_ref, y_ref, dm_ref, kb_ref, hot_ref, drr_ref):
    tiles, count = v_ref.shape[:2]
    steps = count // 8
    wide = states * 128
    chunk = 256
    first = pl.program_id(0) == 0
    half = pl.program_id(0)
    both = range(tiles)
    width = tiles * 128
    rank = wdt_ref.shape[1]

    length = count // 8
    d, c, z = place()
    sib = (d, flip(c, 1), z)
    left = (d, c, lax.rem(z + 3, 4))
    right = (d, c, lax.rem(z + 1, 4))

    def rows(rank):
        return pl.ds(pl.multiple_of(rank * length, length), length)

    keeps = [pltpu.make_async_copy(ups_ref.at[r // 4, r % 4], ups_out.at[r // 4, r % 4], stores.at[r]) for r in range(8)]

    def arrive(act):
        for rank in range(8):
            at = rank % 4
            here = jnp.logical_not(((z == 0) & (at == 3)) | ((z == 3) & (at == 0))) if at in (0, 3) else None
            copy = pltpu.make_async_copy(ups_any.at[rows(rank)], ups_ref.at[rank // 4, at], loads.at[rank])
            if here is None:
                act(copy)
            else:
                @pl.when(here)
                def _():
                    act(copy)

    @pl.when(first)
    def _():
        arrive(lambda copy: copy.start())
        pltpu.make_async_copy(wout_any, wout_ref, loads.at[8]).start()
        greet([sib, left, right])

        @pl.when(z == 1)
        def _():
            put(ups_any.at[rows(c * 4 + 3)], ups_ref.at[c, 3], zs, zr, left)

        @pl.when(z == 2)
        def _():
            put(ups_any.at[rows(c * 4)], ups_ref.at[c, 0], zs, zr, right)

    def complete():
        for end, source, at in ((0, right, 3), (3, left, 0)):
            @pl.when(z == end)
            def _():
                slot = ups_ref.at[c, at]
                landed(slot, zr, source)
                put(slot, slot, cs, cr, sib)
                landed(ups_ref.at[flip(c, 1), at], cr, sib)
                sent(slot, cs, sib)

        for end, target, at in ((1, left, 3), (2, right, 0)):
            @pl.when(z == end)
            def _():
                sent(ups_any.at[rows(c * 4 + at)], zs, target)

        arrive(lambda copy: copy.wait())
        pltpu.make_async_copy(wout_any, wout_ref, loads.at[8]).wait()
        for copy in keeps:
            copy.start()

    @pl.when(first)
    def _():
        row = lax.broadcasted_iota(jnp.int32, (128, 512), 0)
        col = lax.broadcasted_iota(jnp.int32, (128, 512), 1) // 128
        for part in range(0, 2 * wide, 512):
            hot_ref[:, part:part + 512] = jnp.where((row % 32 == col + part // 128) & (row < 96), 1.0, 0.0).astype(bf16)

    lane = lax.broadcasted_iota(jnp.int32, (512, 128), 1)

    def spread(i, carry):
        r = pl.ds(pl.multiple_of(i * 512, 512), 512)
        value = jnp.where(lane < 2 * states, kq_ref[r, :], 0.0)
        hi = value.astype(bf16).astype(f32)
        mid = (value - hi).astype(bf16).astype(f32)
        low = value - hi - mid
        left = (hi + pltpu.roll(mid, 32, 1) + pltpu.roll(low, 64, 1)).astype(bf16)
        for part in range(0, 2 * wide, 256):
            kb_ref[r, part:part + 256] = jnp.dot(left, hot_ref[:, part:part + 256], preferred_element_type=f32)
        return carry

    lax.fori_loop(0, count // 512, spread, 0)
    cols = (((1,), (1,)), ((), ()))

    def gate_step(i, carry):
        product = lax.dot_general(ups_ref[i].reshape(4 * length, wout_ref.shape[1]), wout_ref[pl.ds(pl.multiple_of(half * width, width), width), :], cols, preferred_element_type=f32)
        for j in range(4):
            for n in both:
                dm_ref[n, pl.ds(i * 4 + j, length, stride=8), :] = product[j * length:(j + 1) * length, n * 128:(n + 1) * 128]
        return carry

    bias = vecs_ref[5:6, :]
    skip = vecs_ref[6:7, :]
    tile_of = lambda x, n: x[:, n * 128:(n + 1) * 128]
    ks = lax.broadcasted_iota(jnp.int32, (128, 128), 1)

    def before(i, carry):
        seen = list(carry)
        r = pl.ds(pl.multiple_of(i * 128, 128), 128)
        live = live_ref[0, r, :]
        k = jnp.where(ks < states, kq_ref[r, :], 0.0)
        sk = jnp.sum(k * k, axis=1, keepdims=True)
        pre = lax.dot_general(dl_ref[r, :], wdt_ref[...], cols, preferred_element_type=f32) + bias
        for n in both:
            beta = jax.nn.sigmoid(tile_of(pre, n))
            part = 1.0 / (1.0 + beta * sk)
            rate_ref[n, r, :] = beta * part
            w_ref[n, r, :] = part * part * beta * (1.0 - beta)
            shown = (beta * live).reshape(16, 8, 128)
            seen[n] = seen[n] + jnp.sum(shown, axis=0)
            seen[tiles + n] = jnp.maximum(seen[tiles + n], jnp.max(shown, axis=0))
        return tuple(seen)

    blank = jnp.zeros((8, 128), f32)
    seen = lax.fori_loop(0, count // 128, before, (blank,) * (2 * tiles))
    s_ref[0, 0] = jnp.zeros(s_ref.shape[2:], f32)
    span = GROUP * 8
    at = [slice(j * 8, j * 8 + 8) for j in range(GROUP)]

    def view(ref, i):
        r = pl.ds(pl.multiple_of(i * span, span), span)
        return ref.at[:, r] if len(ref.shape) == 3 else ref.at[r]

    def pair(ref, r):
        return jnp.concatenate([ref[n, r, :] for n in both], axis=1)

    def keep_pair(ref, r, value):
        for n in both:
            ref[n, r, :] = tile_of(value, n)

    tile = lambda x: jnp.concatenate([x] * tiles, axis=1)

    def fold(x):
        total = tile_of(x, 0)
        for n in range(1, tiles):
            total = total + tile_of(x, n)
        return total

    def forward(i, carry):
        keeps, rates, vs, kbs, ys = [view(x, i) for x in (keep_ref, rate_ref, v_ref, kb_ref, y_ref)]
        keep = [keeps[0, r, :] for r in at]
        rate = [pair(rates, r) for r in at]
        value = [pair(vs, r) for r in at]
        rv = [a * b for a, b in zip(rate, value)]
        y = [skip * b for b in value]
        for n in range(states):
            state = s_ref[i, 0, n]
            for j, r in enumerate(at):
                kb = kbs[r, n * 128:(n + 1) * 128]
                qb = kbs[r, wide + n * 128:wide + (n + 1) * 128]
                state = (tile(keep[j]) - rate[j] * tile(kb * kb * keep[j])) * state + rv[j] * tile(kb)
                if j < GROUP - 1:
                    s_ref[i, j + 1, n] = state
                else:
                    s_ref[i + 1, 0, n] = state
                y[j] = y[j] + state * tile(qb)
        for j, r in enumerate(at):
            keep_pair(ys, r, y[j])
        return carry

    lax.fori_loop(0, steps // GROUP, forward, 0)
    h_ref[...] = jnp.zeros_like(h_ref)

    @pl.when(first)
    def _():
        complete()

    lax.fori_loop(0, 2, gate_step, 0)

    def gates(i, carry):
        r = pl.ds(pl.multiple_of(i * 32, 32), 32)
        live = live_ref[0, r, :]
        for n in both:
            g = g_ref[n, r, :]
            sg = jax.nn.sigmoid(g)
            silu = g * sg
            y = y_ref[n, r, :]
            dm = dm_ref[n, r, :] * live
            dv_ref[n, r, :] = dm * silu
            dm_ref[n, r, :] = dm * y * (sg * (1.0 + g * (1.0 - sg)))
            y_ref[n, r, :] = y * silu * live
        return carry

    lax.fori_loop(0, count // 32, gates, 0, unroll=2)

    def by_row(j, carry):
        r = pl.ds(pl.multiple_of(j * length, length), length)
        for n in both:
            value = y_ref[n, pl.ds(j, length, stride=8), :]
            m_ref[r, pl.ds(pl.multiple_of(half * width + n * 128, 128), 128)] = value.astype(bf16)
            mt_ref[n * 128:(n + 1) * 128, r] = value.T.astype(bf16)
            dg_ref[r, n * 128:(n + 1) * 128] = dm_ref[n, pl.ds(j, length, stride=8), :].astype(bf16)
        return carry

    lax.fori_loop(0, 8, by_row, 0)

    def rows_product(core):
        def body(i, carry):
            lanes = pl.ds(pl.multiple_of(i * chunk, chunk), chunk)
            product = jnp.dot(m_ref[pl.ds(pl.multiple_of(core * 4 * length, 4 * length), 4 * length), :], wout_ref[:, lanes], preferred_element_type=f32)
            for at_z in range(4):
                ups_ref[core, at_z, :, lanes] = product[at_z * length:(at_z + 1) * length].astype(bf16)
            return carry

        lax.fori_loop(0, wout_ref.shape[1] // chunk, body, 0)

    def gather(at_z):
        landed(acc_ref.at[at_z], sr.at[at_z], sib)
        add_rows(acc_ref.at[at_z], [acc_ref.at[at_z], ups_ref.at[c, at_z]])

    @pl.when(jnp.logical_not(first))
    def _():
        for copy in keeps:
            copy.wait()
        rows_product(flip(c, 1))
        for at_z in (3, 0, 2, 1):
            put(ups_ref.at[flip(c, 1), at_z], acc_ref.at[at_z], ss.at[at_z], sr.at[at_z], sib)
        rows_product(c)
        gather(3)
        gather(0)

        @pl.when(z == 0)
        def _():
            put(acc_ref.at[3], recv_ref, ls, lr, right)

        @pl.when(z == 3)
        def _():
            put(acc_ref.at[0], recv_ref, ls, lr, left)


    def backward(step, carry):
        i = steps // GROUP - 1 - step
        keeps, rates, vs, kbs, dvs, ws, drrs = [view(x, i) for x in (keep_ref, rate_ref, v_ref, kb_ref, dv_ref, w_ref, drr_ref)]
        keep = [keeps[0, r, :] for r in at]
        rate = [pair(rates, r) for r in at]
        value = [pair(vs, r) for r in at]
        rv = [a * b for a, b in zip(rate, value)]
        dy = [pair(dvs, r) for r in at]
        hk = [jnp.zeros((8, tiles * 128), f32) for r in at]
        hs2 = [jnp.zeros((8, tiles * 128), f32) for r in at]
        for n in range(states):
            ah = h_ref[n]
            later = s_ref[i + 1, 0, n]
            for j in range(GROUP - 1, -1, -1):
                r = at[j]
                kb = kbs[r, n * 128:(n + 1) * 128]
                qb = kbs[r, wide + n * 128:wide + (n + 1) * 128]
                kk = kb * keep[j]
                held = tile(kb * kk)
                h = dy[j] * tile(qb) + ah
                prior = s_ref[i, j, n]
                hs = h * prior
                hk[j] = hk[j] + h * tile(kb)
                hs2[j] = hs2[j] + hs * held
                kbs[r, n * 128:(n + 1) * 128] = fold(h * rv[j]) - 2.0 * kk * fold(hs * rate[j])
                kbs[r, wide + n * 128:wide + (n + 1) * 128] = fold(dy[j] * later)
                later = prior
                ah = (tile(keep[j]) - rate[j] * held) * h
            h_ref[n] = ah
        dskip = carry
        for j, r in enumerate(at):
            drate = value[j] * hk[j] - hs2[j]
            drrs[r, :] = fold(drate * rate[j] * rate[j]) * (-2.0)
            keep_pair(ws, r, drate * pair(ws, r))
            keep_pair(dvs, r, rate[j] * hk[j] + skip * dy[j])
            dskip = dskip + dy[j] * value[j]
        return dskip

    dskip = lax.fori_loop(0, steps // GROUP, backward, jnp.zeros((8, tiles * 128), f32))

    quarter = count // 4
    packed = jnp.zeros((quarter, 128), f32)
    for b in range(4):
        r = slice(b * quarter, (b + 1) * quarter)
        total = jnp.zeros((quarter, 128), f32)
        for part in range(0, 2 * wide, 512):
            total = total + lax.dot_general(kb_ref[r, part:part + 512].astype(bf16), hot_ref[:, part:part + 512], cols, preferred_element_type=f32)
        drr = jnp.sum(drr_ref[r, :], axis=1, keepdims=True)
        k = kq_ref[r, :]
        low = lax.broadcasted_iota(jnp.int32, (quarter, 128), 1)
        total = jnp.where(low < 2 * states, total, 0.0) + jnp.where(low < states, k * drr, 0.0)
        packed = packed + (pltpu.roll(total, 32 * b, 1) if b else total)

    tail = pl.ds(count, quarter)
    part_ref[tail, :] = jnp.where(first, packed, part_ref[tail, :] + packed)

    def after(i, carry):
        r = pl.ds(pl.multiple_of(i * 128, 128), 128)
        sums = list(carry)
        for n in both:
            low = w_ref[n, r, :].astype(bf16)
            dpre_ref[r, n * 128:(n + 1) * 128] = low
            sums[n] = sums[n] + jnp.sum(low.astype(f32).reshape(16, 8, 128), axis=0)
        ddl = jnp.dot(dpre_ref[r, :], wdt_ref[...], preferred_element_type=f32)
        part_ref[r, :] = jnp.where(first, ddl, part_ref[r, :] + ddl)
        return tuple(sums)

    sums = lax.fori_loop(0, count // 128, after, (blank,) * tiles)

    gwdt_ref[...] = lax.dot_general(dpre_ref[...], dl_ref[...], (((0,), (0,)), ((), ())), preferred_element_type=f32)

    @pl.when(jnp.logical_not(first))
    def _():
        gather(2)
        gather(1)
        for end, source, at_z in ((1, left, 3), (2, right, 0)):
            @pl.when(z == end)
            def _():
                landed(recv_ref, lr, source)
                add_rows(acc_ref.at[at_z], [acc_ref.at[at_z], recv_ref])

        save = pltpu.make_async_copy(acc_ref, acc_out, loads.at[8])
        save.start()
        for at_z in range(4):
            sent(ups_ref.at[flip(c, 1), at_z], ss.at[at_z], sib)
        for end, target, at_z in ((0, right, 3), (3, left, 0)):
            @pl.when(z == end)
            def _():
                sent(acc_ref.at[at_z], ls, target)
        save.wait()

    stat_ref[...] = jnp.zeros_like(stat_ref)
    for n in both:
        lanes = slice(n * 128, (n + 1) * 128)
        stat_ref[0:1, lanes] = jnp.sum(seen[n], axis=0, keepdims=True)
        stat_ref[1:2, lanes] = jnp.max(seen[tiles + n], axis=0, keepdims=True)
        stat_ref[5:6, lanes] = jnp.sum(sums[n], axis=0, keepdims=True)
        stat_ref[6:7, lanes] = jnp.sum(tile_of(dskip, n), axis=0, keepdims=True)


def k2(dl, kq, smalls, vecs, masks, live, v, g, ups, wout, states):
    count, rank = dl.shape
    channels, model = wout.shape
    tiles = 2
    width = tiles * 128
    like = jax.ShapeDtypeStruct
    once = pl.Buffered(buffer_count=1)
    whole = lambda a: pl.BlockSpec(a.shape, lambda h: (0,) * a.ndim, pipeline_mode=once)
    deep = pl.BlockSpec((tiles, count, 128), lambda h: (h, 0, 0))
    flat = pl.BlockSpec((count, width), lambda h: (0, h))
    return pl.pallas_call(
        functools.partial(k2_kernel, states),
        grid=(channels // width,),
        out_shape=(
            like((4, count // 8, model), bf16),
            like((channels, count), bf16),
            like((count, channels), bf16),
            like((channels, rank), f32),
            like((2, 4, count // 8, model), bf16),
            like(v.shape, f32),
            like((count + count // 4, 128), f32),
            like((8, channels), f32),
        ),
        in_specs=[
            whole(dl), whole(kq),
            pl.BlockSpec((width, 128), lambda h: (h, 2)),
            pl.BlockSpec((8, width), lambda h: (0, h)),
            pl.BlockSpec((1, count, 128), lambda h: (0, 0, 0), pipeline_mode=once),
            pl.BlockSpec((1, count, 128), lambda h: (0, 0, 0), pipeline_mode=once),
            deep, deep, pl.BlockSpec(memory_space=pl.ANY),
            pl.BlockSpec(memory_space=pl.ANY),
        ],
        out_specs=(pl.BlockSpec(memory_space=pltpu.HBM), pl.BlockSpec((width, count), lambda h: (h, 0)), flat, pl.BlockSpec((width, rank), lambda h: (h, 0)), pl.BlockSpec(memory_space=pltpu.HBM), deep, pl.BlockSpec((count + count // 4, 128), lambda h: (0, 0)), pl.BlockSpec((8, width), lambda h: (0, h))),
        scratch_shapes=[
            pltpu.VMEM((2, 4, count // 8, model), bf16),
            pltpu.SemaphoreType.DMA((9,)),
            pltpu.SemaphoreType.DMA((8,)),
        ] + [pltpu.SemaphoreType.DMA(())] * 6 + [
            pltpu.SemaphoreType.DMA((4,)),
            pltpu.SemaphoreType.DMA((4,)),
            pltpu.VMEM((count, channels), bf16),
            pltpu.VMEM((channels, model), bf16),
            pltpu.VMEM((4, count // 8, model), bf16),
            pltpu.VMEM((count // 8, model), bf16),
            pltpu.VMEM((count, width), bf16),
            pltpu.VMEM((count // 8 // GROUP + 1, GROUP, states, 8, width), f32),
            pltpu.VMEM((states, 8, width), f32),
        ] + [pltpu.VMEM((tiles, count, 128), f32)] * 4
        + [pltpu.VMEM((count, 2 * states * 128), f32), pltpu.VMEM((128, 2 * states * 128), bf16), pltpu.VMEM((count, 128), f32)],
        compiler_params=pltpu.CompilerParams(collective_id=2, has_side_effects=True, vmem_limit_bytes=63400000),
    )(dl, kq, smalls, vecs, masks, live, v, g, ups, wout)


class Row:
    def __init__(self, part, sib, recv, sems, merged=False):
        self.part, self.sib, self.recv, self.merged = part, sib, recv, merged
        self.ss, self.sr, self.gs, self.lr, self.rr = sems
        d, c, z = place()
        self.c = c
        self.other = (d, flip(c, 1), z)
        self.to_left = (d, c, lax.rem(z + 3, 4))
        self.to_right = (d, c, lax.rem(z + 1, 4))

    def start(self):
        for zp in (3, 0, 2, 1):
            put(self.part.at[flip(self.c, 1), zp], self.sib.at[zp], self.ss.at[zp], self.sr.at[zp], self.other)

    def gather(self):
        for zp in (3, 0, 2, 1):
            landed(self.sib.at[zp], self.sr.at[zp], self.other)
            add_rows(self.sib.at[zp], [self.sib.at[zp], self.part.at[self.c, zp]])

    def release(self):
        for zp in range(4):
            sent(self.part.at[flip(self.c, 1), zp], self.ss.at[zp], self.other)

    def terms(self, zs, zp):
        found = [self.sib.at[zp]]
        if zp >= zs and zs > 0 and not (self.merged and (zs, zp) == (1, 3)):
            landed(self.recv.at[zp], self.lr.at[zp], self.to_left)
            found.append(self.recv.at[zp])
        if zp <= zs and zs < 3 and not (self.merged and (zs, zp) == (2, 0)):
            slot = self.recv.at[4 if zp == zs else zp]
            landed(slot, self.rr.at[zp], self.to_right)
            found.append(slot)
        return found

    def join(self, zs, zp):
        found = self.terms(zs, zp)
        if len(found) > 1:
            add_rows(self.sib.at[zp], found)

    def skips(self, zs, zp):
        return self.merged and (zs, zp) in ((0, 3), (3, 0))

    def step(self, zs, k):
        k = k + 1 if self.merged else k
        ends = 1 if self.merged else 0
        for zp in ((3, 2, 1, 0) if zs == 0 else (0, 1, 2, 3)):
            if zp > zs and not self.skips(zs, zp) and k == (ends if zs == 0 else 3 - zp + zs):
                self.join(zs, zp)
                put(self.sib.at[zp], self.recv.at[zp], self.gs.at[zp], self.lr.at[zp], self.to_right)
            if zp < zs and not self.skips(zs, zp) and k == (ends if zs == 3 else zp + 3 - zs):
                self.join(zs, zp)
                put(self.sib.at[zp], self.recv.at[4 if zp == zs - 1 else zp], self.gs.at[zp], self.rr.at[zp], self.to_left)

    def finish(self, zs):
        add_rows(self.sib.at[zs], self.terms(zs, zs), self.total)

    def close(self, zs):
        for zp in range(4):
            if zp != zs and not self.skips(zs, zp):
                sent(self.sib.at[zp], self.gs.at[zp], self.other)

    def along(self, k, total=None):
        self.total = total
        d, c, z = place()
        for zs in range(4):
            @pl.when(z == zs)
            def _():
                if k < (2 if self.merged else 3):
                    self.step(zs, k)
                else:
                    self.finish(zs)
                    self.close(zs)


def row_scratch(rows, columns):
    return [pltpu.VMEM((4, rows, columns), bf16), pltpu.VMEM((5, rows, columns), bf16)] + [pltpu.SemaphoreType.DMA((4,))] * 5


def add_rows(dst, sources, total=None):
    rows = (total if total is not None else dst).shape[0]
    step = 16

    def body(i, carry):
        r = pl.ds(pl.multiple_of(i * step, step), step)
        value = sources[0][r, :].astype(f32)
        for more in sources[1:]:
            value = value + more[r, :].astype(f32)
        if total is not None:
            total[r, :] = value
        else:
            dst[r, :] = value.astype(dst.dtype)
        return carry

    lax.fori_loop(0, rows // step, body, 0, unroll=2)


class Flat:
    def __init__(self, part, xa, yb, rx, ry, ss, rs):
        self.part, self.xa, self.yb, self.rx, self.ry, self.ss, self.rs = part, xa, yb, rx, ry, ss, rs
        d, c, z = place()
        self.d, self.dx, self.dy, self.dd = d, flip(d, 1), flip(d, 2), flip(flip(d, 1), 2)
        self.xn, self.yn = (self.dx, c, z), (self.dy, c, z)
        half = part.shape[1] // 2
        self.a, self.b = pl.ds(0, half), pl.ds(half, half)
        self.sends = []

    def start_far(self):
        p = self.part
        self.sends.append(put(p.at[self.dd, self.a], self.xa, self.ss.at[0], self.rs.at[0], self.xn))
        self.sends.append(put(p.at[self.dd, self.b], self.yb, self.ss.at[1], self.rs.at[1], self.yn))

    def start_near(self):
        p = self.part
        self.sends.append(put(p.at[self.dx, self.a], self.rx.at[self.a], self.ss.at[2], self.rs.at[2], self.xn))
        self.sends.append(put(p.at[self.dy, self.b], self.ry.at[self.b], self.ss.at[3], self.rs.at[3], self.yn))

    def middle(self):
        p = self.part
        landed(self.xa, self.rs.at[0], self.xn)
        add_rows(self.xa, [self.xa, p.at[self.dy, self.a]])
        self.sends.append(put(self.xa, self.ry.at[self.a], self.ss.at[4], self.rs.at[4], self.yn))
        landed(self.yb, self.rs.at[1], self.yn)
        add_rows(self.yb, [self.yb, p.at[self.dx, self.b]])
        self.sends.append(put(self.yb, self.rx.at[self.b], self.ss.at[5], self.rs.at[5], self.xn))

    def finish(self, out):
        landed(self.rx.at[self.a], self.rs.at[2], self.xn)
        landed(self.ry.at[self.b], self.rs.at[3], self.yn)
        landed(self.ry.at[self.a], self.rs.at[4], self.yn)
        landed(self.rx.at[self.b], self.rs.at[5], self.xn)
        add_rows(out, [self.part.at[self.d], self.rx, self.ry])

    def close(self):
        for copy in self.sends:
            copy.wait_send()


def flat_scratch(rows, columns, dtype):
    half = pltpu.VMEM((rows // 2, columns), dtype)
    full = pltpu.VMEM((rows, columns), dtype)
    return [half, half, full, full, pltpu.SemaphoreType.DMA((6,)), pltpu.SemaphoreType.DMA((6,))]


def k3_kernel(part_ref, stat_ref, smalls_ref, vecs_ref, gains_ref, gwdt_ref, masks_ref, tok_ref, up_ref,
              acc_any, mt_any, dg_any, dv_any, slope_any, u_any, vt_any, xnt_any, win_any, ups_any,
              block_out, gtok_out, gwin_out, gwout_out, small_out, tiny_out, *scratch):
    scratch = list(scratch)

    def take(n):
        found = scratch[:n]
        del scratch[:n]
        return found

    block_ref, gtok_ref, gwin_ref, gwout_ref, small_ref, tiny_ref, stores = take(7)
    outp, win_ref, up, gp, gwoutp, smallp = take(6)
    mt_ref, dz_ref, dc_ref, slope_ref, u_ref, xnt_ref, dp_ref, slots_ref, row_ref = take(9)
    near_ref, pairs_ref, sum_ref, far_ref = take(4)
    loads, as_, ar, ns, nr, fs, fr = take(7)
    totals = take(7)
    total_sems = take(8)
    out_row = Row(None, *take(2), take(5), True)
    dxn_row = Row(outp, *take(2), take(5))
    flats = [Flat(up, *take(6)), Flat(gp, *take(6))]
    gwout_flat = Flat(gwoutp, *take(6))
    small_flat = Flat(smallp, *take(6))
    d, c, z = place()
    j = c * 4 + z
    other = flip(c, 1)
    steps = mates()
    planes = [(flip(d, 1), c, z), (flip(d, 2), c, z), (flip(flip(d, 1), 2), c, z)]
    length, model = tok_ref.shape[1:]
    tiles, padded, _ = dc_ref.shape
    count = dz_ref.shape[0]
    width = tiles * 128
    rows_any = [(dg_any, dz_ref.at[:, pl.ds(width, width)]), (xnt_any, xnt_ref), (acc_any, out_row.sib), (mt_any, mt_ref), (ups_any, outp),
                (dv_any, dc_ref.at[:, pl.ds(0, count)]), (slope_any, slope_ref), (u_any, u_ref), (win_any, win_ref)]
    copies = [pltpu.make_async_copy(a, b, loads.at[i]) for i, (a, b) in enumerate(rows_any)]
    for copy in copies:
        copy.start()
    greet([mate(s) for s in steps] + planes)
    outs = [(block_ref, block_out), (gtok_ref, gtok_out), (gwin_ref, gwin_out), (gwout_ref, gwout_out), (small_ref, small_out), (tiny_ref, tiny_out)]
    outs = [pltpu.make_async_copy(a, b, stores.at[i]) for i, (a, b) in enumerate(outs)]
    tile = 256
    nt = (((1,), (1,)), ((), ()))

    def rows_product(half):
        def body(i, carry):
            value = win_ref[i // (512 // tile), pl.ds(pl.multiple_of((i % (512 // tile)) * tile, tile), tile), :]
            product = lax.dot_general(dz_ref[pl.ds(pl.multiple_of(half * 512, 512), 512), :], value, nt, preferred_element_type=f32)
            for zp in range(4):
                outp[half, zp, :, pl.ds(pl.multiple_of(i * tile, tile), tile)] = product[zp * length:(zp + 1) * length].astype(bf16)
            return carry

        lax.fori_loop(0, model // tile, body, 0)

    def weight_rows(holder, first, group):
        def body(i, carry):
            lanes = pl.ds(pl.multiple_of(i * tile, tile), tile)
            left = xnt_ref[pl.ds(pl.multiple_of(group * 512, 512), 512), :]
            value = dz_ref[:, pl.ds(pl.multiple_of(first + i * tile, tile), tile)]
            holder[group, :, lanes] = jnp.dot(left, value, preferred_element_type=f32).astype(bf16)
            return carry

        lax.fori_loop(0, width // tile, body, 0)

    def weight_part(k):
        flat = flats[k]
        holder, first = (up, 0) if k == 0 else (gp, width)
        weight_rows(holder, first, flat.dd)
        flat.start_far()
        weight_rows(holder, first, flat.dx)
        weight_rows(holder, first, flat.dy)
        flat.start_near()
        weight_rows(holder, first, d)

    def early():
        for copy in copies[0:2]:
            copy.wait()
        weight_part(1)

    def between():
        copies[2].wait()
        out_row.along(0)
        flats[1].middle()

    def late():
        for copy in copies[3:5]:
            copy.wait()

        def body(i, carry):
            lanes = pl.ds(pl.multiple_of(i * tile, tile), tile)
            product = jnp.dot(mt_ref[...], outp[:, :, :, lanes].reshape(count, tile), preferred_element_type=f32)
            for g in range(4):
                gwoutp[g, :, lanes] = product[g * 128:(g + 1) * 128].astype(bf16)
            return carry

        lax.fori_loop(0, model // tile, body, 0)
        gwout_flat.start_far()
        gwout_flat.start_near()

    seen = jnp.sum(stat_ref[0:1, :], axis=1, keepdims=True)
    peak = jnp.max(stat_ref[1:2, :], axis=1, keepdims=True)
    row8 = lax.broadcasted_iota(jnp.int32, (8, 128), 0)
    lane8 = lax.broadcasted_iota(jnp.int32, (8, 128), 1)
    pairs_ref[...] = jnp.where(lane8 == 0, seen, jnp.where(lane8 == 1, peak, 0.0))
    for i, s in enumerate(steps):
        put(pairs_ref, near_ref.at[i], ns.at[i], nr.at[i], mate(s))

    def join(a, b):
        return jnp.where(lane8 == 1, jnp.maximum(a, b), a + b)

    total_ref = totals[0]
    line_total(part_ref, *totals, *total_sems, early, between, late)
    vt_copy = pltpu.make_async_copy(vt_any, mt_ref, loads.at[9])
    vt_copy.start()
    block = gwin_ref.shape[0]
    pending = []

    def rows_of(k, rank):
        return flats[k].part.at[d, pl.ds(pl.multiple_of(rank * block, block), block)]

    def give(k):
        flats[k].finish(flats[k].part.at[d])
        for i, s in enumerate(steps):
            to = mate(s)
            pending.append(put(rows_of(k, rank_of(to)), slots_ref.at[k, i], as_.at[7 * k + i], ar.at[7 * k + i], to))

    value = pairs_ref[...]
    for i, s in enumerate(steps):
        landed(near_ref.at[i], nr.at[i], mate(s, -1))
        value = join(value, near_ref[i])
    sum_ref[...] = value
    for i, to in enumerate(planes):
        put(sum_ref, far_ref.at[i], fs.at[i], fr.at[i], to)
    quarter = count // 4
    lane = lax.broadcasted_iota(jnp.int32, (quarter, 128), 1)
    dp_ref[:, 0:128] = total_ref[0:count, :].astype(bf16)
    for b in range(4):
        packed = total_ref[count:count + quarter, :]
        packed = pltpu.roll(packed, 128 - 32 * b, 1) if b else packed
        dp_ref[b * quarter:(b + 1) * quarter, 128:256] = jnp.where(lane < 32, packed, 0.0).astype(bf16)
    for copy in copies[5:8]:
        copy.wait()
    dc_ref[:, count:, :] = jnp.zeros((tiles, padded - count, 128), f32)

    def slope_step(i, carry):
        r = pl.ds(pl.multiple_of(i * 256, 256), 256)
        product = lax.dot_general(dp_ref[r, :], smalls_ref[:, 0:256], nt, preferred_element_type=f32)
        for n in range(tiles):
            dc_ref[n, r, :] = (dc_ref[n, r, :] + product[:, n * 128:(n + 1) * 128]) * slope_ref[n, r, :]
        return carry

    lax.fori_loop(0, count // 256, slope_step, 0)
    give(1)
    out_row.along(1)
    taps = [vecs_ref[o:o + 1, :] for o in range(4)]
    lead = u_ref.shape[1] - count

    for n in range(tiles):
        lanes = slice(n * 128, (n + 1) * 128)
        tap = [t[:, lanes] for t in taps]

        def conv_step(i, carry):
            r = pl.ds(pl.multiple_of(i * 32, 32), 32)
            sums = list(carry)
            dc = dc_ref[n, r, :]
            du = tap[3] * dc
            fold8 = lambda x: x[0:8] + x[8:16] + x[16:24] + x[24:32]
            sums[4] = sums[4] + fold8(dc)
            sums[3] = sums[3] + fold8(dc * u_ref[n, pl.ds(pl.multiple_of(lead + i * 32, 8), 32), :])
            for o in range(1, 4):
                sums[3 - o] = sums[3 - o] + fold8(dc * (u_ref[n, pl.ds(pl.multiple_of(lead + i * 32 - 8 * o, 8), 32), :] * masks_ref[o - 1, pl.ds(pl.multiple_of(i * 32, 8), 32), :]))
                du = du + tap[3 - o] * (dc_ref[n, pl.ds(pl.multiple_of(i * 32 + 8 * o, 8), 32), :] * masks_ref[o - 1, pl.ds(pl.multiple_of(i * 32 + 8 * o, 8), 32), :])
            dc_ref[n, r, :] = du
            return tuple(sums)

        sums = lax.fori_loop(0, count // 32, conv_step, (jnp.zeros((8, 128), f32),) * 5, unroll=2)
        tops = jnp.concatenate([jnp.sum(sums[k], axis=0, keepdims=True) for k in range(5)] + [stat_ref[5:6, lanes], stat_ref[6:7, lanes], jnp.zeros((25, 128), f32)], axis=0)
        smallp[n, 128:160, :] = jnp.zeros((32, 384), bf16)
        smallp[n, 128:160, 0:128] = tops.astype(bf16)
        smallp[n, 0:128, 256:384] = gwdt_ref[n * 128:(n + 1) * 128, :].astype(bf16)

    def by_row(i, carry):
        r = pl.ds(pl.multiple_of(i * length, length), length)
        for n in range(tiles):
            dz_ref[r, n * 128:(n + 1) * 128] = dc_ref[n, pl.ds(i, length, stride=8), :].astype(bf16)
        return carry

    lax.fori_loop(0, 8, by_row, 0)
    gwout_flat.middle()
    copies[8].wait()
    rows_product(other)
    dxn_row.start()
    weight_rows(up, 0, flats[0].dd)
    flats[0].start_far()
    rows_product(c)
    dxn_row.gather()
    dxn_row.along(0)
    weight_rows(up, 0, flats[0].dx)
    weight_rows(up, 0, flats[0].dy)
    flats[0].start_near()
    weight_rows(up, 0, d)
    vt_copy.wait()
    for n in range(tiles):
        smallp[n, 0:128, 0:256] = jnp.dot(mt_ref[n * 128:(n + 1) * 128, :], dp_ref[...], preferred_element_type=f32).astype(bf16)
    flats[0].middle()
    small_flat.start_far()
    small_flat.start_near()
    out_row.along(2, row_ref)

    def block_step(i, carry):
        r = pl.ds(pl.multiple_of(i * 16, 16), 16)
        block_ref[r, :] = (tok_ref[0, r, :].astype(f32) + row_ref[r, :]).astype(bf16)
        return carry

    lax.fori_loop(0, length // 16, block_step, 0)
    outs[0].start()
    dxn_row.along(1)
    give(0)
    small_flat.middle()
    dxn_row.along(2)
    gwout_flat.finish(gwout_ref)
    outs[3].start()
    dxn_row.along(3, row_ref)
    dxn_row.release()
    def norm_step(i, carry):
        r = pl.ds(pl.multiple_of(i * 16, 16), 16)
        x = tok_ref[0, r, :].astype(f32)
        scale = lax.rsqrt(jnp.sum(x * x, axis=1, keepdims=True) * (1.0 / model) + EPS)
        dxn = row_ref[r, :]
        inner = dxn * gains_ref[...]
        dot = jnp.sum(inner * x, axis=1, keepdims=True) * (1.0 / model)
        dxx = scale * inner - x * (scale * scale * scale * dot)
        gtok_ref[r, :] = (up_ref[0, r, :].astype(f32) + dxx).astype(bf16)
        return carry

    lax.fori_loop(0, length // 16, norm_step, 0, unroll=2)
    outs[1].start()
    small_flat.finish(small_ref)
    outs[4].start()

    def settle(k, rank, source):
        for g in range(4):
            at = k * width * 8 + g * 1024
            gwin_ref[:, pl.ds(pl.multiple_of(at + rank * 128, 128), 128)] = source[:, g * 128:(g + 1) * 128]

    for k in (1, 0):
        settle(k, j, rows_of(k, j))
        for i, s in enumerate(steps):
            src = mate(s, -1)
            landed(slots_ref.at[k, i], ar.at[7 * k + i], src)
            settle(k, rank_of(src), slots_ref.at[k, i])
    outs[2].start()
    value = sum_ref[...]
    for i, to in enumerate(planes):
        landed(far_ref.at[i], fr.at[i], to)
        value = join(value, far_ref[i])
    tiny_ref[...] = value
    outs[5].start()
    for i, to in enumerate(planes):
        sent(sum_ref, fs.at[i], to)
    for i, s in enumerate(steps):
        sent(near_ref.at[i], ns.at[i], mate(s))
    for copy in pending:
        copy.wait_send()
    for flat in (*flats, gwout_flat, small_flat):
        flat.close()
    for copy in outs:
        copy.wait()


def k3(part, stat, smalls, vecs, gains, gwdt, masks, tokens, upstream, acc, mt, dg, dv, slope, u, vt, xnt, win, ups):
    like = jax.ShapeDtypeStruct
    length, model = tokens.shape[1:]
    channels, count = mt.shape
    tiles = channels // 128
    here = pl.BlockSpec(memory_space=pltpu.VMEM)
    far = pl.BlockSpec(memory_space=pl.ANY)
    dma = lambda n: pltpu.SemaphoreType.DMA((n,))
    own_d = model // 32
    packed = part.shape[0]
    return pl.pallas_call(
        k3_kernel,
        out_shape=(
            like((length, model), bf16),
            like((length, model), bf16),
            like((own_d, 16 * channels), bf16),
            like((128, model), f32),
            like((160, 384), f32),
            like((8, 128), f32),
        ),
        in_specs=[here] * 9 + [far] * 10,
        out_specs=(pl.BlockSpec(memory_space=pltpu.HBM),) * 6,
        scratch_shapes=[
            pltpu.VMEM((length, model), bf16),
            pltpu.VMEM((length, model), bf16),
            pltpu.VMEM((own_d, 16 * channels), bf16),
            pltpu.VMEM((128, model), f32),
            pltpu.VMEM((160, 384), f32),
            pltpu.VMEM((8, 128), f32),
            dma(6),
            pltpu.VMEM((2, 4, length, model), bf16),
            pltpu.VMEM((4, 512, 2 * channels), bf16),
            pltpu.VMEM((4, 512, channels), bf16),
            pltpu.VMEM((4, 512, channels), bf16),
            pltpu.VMEM((4, 128, model), bf16),
            pltpu.VMEM((4, 160, 384), bf16),
            pltpu.VMEM((channels, count), bf16),
            pltpu.VMEM((count, 2 * channels), bf16),
            pltpu.VMEM((tiles, count + 32, 128), f32),
            pltpu.VMEM((tiles, count, 128), f32),
            pltpu.VMEM(u.shape, f32),
            pltpu.VMEM((model, count), bf16),
            pltpu.VMEM((count, 256), bf16),
            pltpu.VMEM((2, 7, own_d, channels), bf16),
            pltpu.VMEM((length, model), f32),
            pltpu.VMEM((7, 8, 128), f32),
            pltpu.VMEM((8, 128), f32),
            pltpu.VMEM((8, 128), f32),
            pltpu.VMEM((3, 8, 128), f32),
            dma(10), dma(14), dma(14), dma(7), dma(7), dma(3), dma(3),
            pltpu.VMEM((packed, 128), f32),
        ] + [pltpu.VMEM((packed // 2, 128), f32)] + [pltpu.VMEM((packed // 2, 128), LINE2)] * 5 + [dma(PIECES) for _ in range(8)]
        + row_scratch(length, model) * 2
        + flat_scratch(512, channels, bf16) * 2 + flat_scratch(128, model, bf16) + flat_scratch(160, 384, bf16),
        compiler_params=pltpu.CompilerParams(collective_id=1, has_side_effects=True, vmem_limit_bytes=63400000),
    )(part, stat, smalls, vecs, gains, gwdt, masks, tokens, upstream, acc, mt, dg, dv, slope, u, vt, xnt, win, ups)


def k4_kernel(slots, block_in, gtok_in, gwin_in, gwout_in, small_in, tiny_in, win_ref, gain_ref,
              block_ref, gtok_ref, gain_out, gwin_ref, convw_ref, convb_ref, gwx_ref, gwdt_ref, dtb_ref, skip_ref, gwout_ref, mean_ref, peak_ref):
    block_ref[0] = block_in[...]
    gtok_ref[0] = gtok_in[...]
    gwout_ref[...] = gwout_in[...]
    depth, total = gwin_in.shape
    dot = jnp.zeros((depth, 128), f32)
    for at in range(0, total, 128):
        value = gwin_in[:, at:at + 128].astype(f32)
        gwin_ref[:, at:at + 128] = value
        dot = dot + value * win_ref[:, at:at + 128].astype(f32)
    column = jnp.broadcast_to(jnp.sum(dot, axis=1, keepdims=True), (depth, 128))
    gain_out[...] = column.T[0:1, :] / gain_ref[...].astype(f32)
    gwx_ref[...] = small_in[0:128, 0:256].T[0:gwx_ref.shape[0], :]
    gwdt_ref[...] = small_in[0:128, 256:384]
    convw_ref[...] = small_in[128:132, 0:128]
    convb_ref[...] = small_in[132:133, 0:128]
    dtb_ref[...] = small_in[133:134, 0:128]
    skip_ref[...] = small_in[134:135, 0:128]
    mean_ref[...] = tiny_in[0:1, 0:1] * (1.0 / slots)
    peak_ref[...] = tiny_in[0:1, 1:2]


def k4(slots, block, gtok, gwin, gwout, small, tiny, w_in, gain, columns):
    like = jax.ShapeDtypeStruct
    here = pl.BlockSpec(memory_space=pltpu.VMEM)
    row = like((1, 128), f32)
    return pl.pallas_call(
        functools.partial(k4_kernel, slots),
        out_shape=(
            like((1,) + block.shape, bf16), like((1,) + gtok.shape, bf16), like(gain.shape, f32), like(gwin.shape, f32),
            like((4, 128), f32), row, like((columns, 128), f32), like((128, 128), f32), row, row, like(gwout.shape, f32),
            like((1, 1), f32), like((1, 1), f32),
        ),
        in_specs=[here] * 8,
        out_specs=(here,) * 13,
        compiler_params=pltpu.CompilerParams(vmem_limit_bytes=63400000),
    )(block, gtok, gwin, gwout, small, tiny, w_in, gain)

def masks(lengths, count):
    ends = jnp.cumsum(lengths, axis=1)
    places = jnp.arange(count, dtype=jnp.int32)
    segment = jnp.sum((places[:, None, None] >= ends[None, :, :]).astype(jnp.int32), axis=2)
    same = []
    for offset in range(1, 4):
        before = jnp.pad(segment, ((offset, 0), (0, 0)), constant_values=-1)[:count]
        same.append((before == segment).astype(f32))
    return same, (segment < DOCS).astype(f32)


def columns(weights, ways):
    rows, total = weights.shape
    return weights.reshape(rows, 2, total // (2 * ways * 128), ways, 128)


def on_device(tokens, lengths, gain, w_in, conv_w, conv_b, w_x, w_dt, dt_bias, skip, w_out, grad_out):
    ways = lax.axis_size("core") * lax.axis_size("z")
    groups = lax.axis_size("dp")
    length, model = tokens.shape[1:]
    own_d = w_in.shape[0]
    own_e = conv_w.shape[0]
    inner = w_in.shape[1] // 2
    channels = inner // ways
    rank = w_dt.shape[1]
    states = (w_x.shape[1] - rank) // 2
    cols = w_in.reshape(own_d, 2, groups, ways, own_e).transpose(3, 0, 1, 2, 4).reshape(ways, own_d, 2 * channels)
    cols = lax.all_to_all(cols, TP, split_axis=0, concat_axis=0, tiled=True)
    win = lax.all_gather(cols, "dp", axis=0, tiled=True).reshape(model, 2 * channels)
    small = jnp.concatenate([w_x, w_dt, conv_w, conv_b[:, None], dt_bias[:, None], skip[:, None]], axis=1)
    small_width = small.shape[1]
    small = lax.all_gather(small, "dp", axis=0, tiled=True)
    wx = small[:, :rank + 2 * states]
    wdt = small[:, rank + 2 * states:2 * rank + 2 * states]
    rest = small[:, 2 * rank + 2 * states:].astype(f32)
    taps, bias, dtb, skips = rest[:, :4], rest[:, 4], rest[:, 5], rest[:, 6]
    wout = lax.all_gather(w_out, "dp", axis=0, tiled=True)
    gains = lax.all_gather(gain, ALL, axis=0, tiled=True).astype(f32)
    x = tokens[0].astype(f32)
    scale = lax.rsqrt(jnp.mean(x * x, axis=1, keepdims=True) + EPS)
    xn = (x * scale * gains).astype(bf16)
    xns = lax.all_gather(xn, TP, axis=0, tiled=True)
    ups = lax.all_gather(grad_out[0], TP, axis=0, tiled=True)
    lens = lax.all_gather(lengths, TP, axis=0, tiled=True)
    rows = lens.shape[0]
    tall = rows * length

    def time_major(a):
        return a.reshape(rows, length, -1).transpose(1, 0, 2).reshape(tall, -1)

    def row_major(a):
        return a.reshape(length, rows, -1).transpose(1, 0, 2).reshape(tall, -1)

    same, live = masks(lens, length)
    zz = time_major(jnp.dot(xns, win, preferred_element_type=f32))
    u = zz[:, :channels].reshape(length, rows, channels)
    g = zz[:, channels:]
    c = bias + taps[:, 3] * u
    shifted = []
    for offset in range(1, 4):
        earlier = jnp.pad(u, ((offset, 0), (0, 0), (0, 0)))[:length] * same[offset - 1][:, :, None]
        shifted.append(earlier)
        c = c + taps[:, 3 - offset] * earlier
    sig = jax.nn.sigmoid(c)
    v16 = (c * sig).astype(bf16).reshape(tall, channels)
    v = v16.astype(f32)
    p = lax.psum(jnp.dot(v16, wx, preferred_element_type=f32), TP)
    dl = p[:, :rank].astype(bf16)
    kq = p[:, rank:]
    dims_cols = (((1,), (1,)), ((), ()))
    dims_rows = (((0,), (0,)), ((), ()))
    pre = lax.dot_general(dl, wdt, dims_cols, preferred_element_type=f32) + dtb
    dm = time_major(lax.dot_general(ups, wout, dims_cols, preferred_element_type=f32))
    flags = jnp.pad(jnp.stack([same[0].reshape(tall), live.reshape(tall)], axis=1), ((0, 0), (0, 126)))
    hi = kq.astype(bf16)
    mid = (kq - hi.astype(f32)).astype(bf16)
    low = (kq - hi.astype(f32) - mid.astype(f32)).astype(bf16)
    kq3 = jnp.concatenate([hi, mid, low], axis=1)
    keys = kq[:, :states]
    sk = jnp.broadcast_to(jnp.sum(keys * keys, axis=1, keepdims=True), (tall, 8))
    m, dg, dpre, dv, dkq, stats = mixer(flags, kq3, sk, pre, v, g, dm, skips[None], states=states, width=256, unroll=4)
    stats = stats.transpose(1, 2, 0, 3).reshape(3, 8, channels)
    dskip = jnp.sum(stats[0], axis=0)
    total = lax.psum(jnp.sum(stats[1]), ALL)
    peak = lax.pmax(jnp.max(stats[2]), ALL)
    beta_mean = total / float(groups * ways * length * inner)
    m16 = row_major(m).astype(bf16)
    out = jnp.dot(m16, wout, preferred_element_type=f32).astype(bf16)
    out = lax.psum_scatter(out, TP, scatter_dimension=0, tiled=True)
    block_out = (x + out.astype(f32)).astype(bf16)
    grad_wout = lax.dot_general(m16, ups, dims_rows, preferred_element_type=f32).astype(bf16)
    grad_wout = lax.psum_scatter(grad_wout, "dp", scatter_dimension=0, tiled=True)
    dpre16 = dpre.astype(bf16)
    grad_dtb = jnp.sum(dpre16.astype(f32), axis=0)
    grad_wdt = lax.dot_general(dpre16, dl, dims_rows, preferred_element_type=f32)
    ddl = jnp.dot(dpre16, wdt, preferred_element_type=f32)
    dkq = dkq[:, :2 * states] + dkq[:, 2 * states:2 * states + 1] * jnp.pad(keys, ((0, 0), (0, states)))
    dp16 = lax.psum(jnp.concatenate([ddl, dkq], axis=1), TP).astype(bf16)
    grad_wx = lax.dot_general(v16, dp16, dims_rows, preferred_element_type=f32)
    dvt = dv + lax.dot_general(dp16, wx, dims_cols, preferred_element_type=f32)
    dc = (dvt * (sig.reshape(tall, channels) * (1.0 + c.reshape(tall, channels) * (1.0 - sig.reshape(tall, channels))))).reshape(length, rows, channels)
    du = taps[:, 3] * dc
    grad_taps = [jnp.sum(dc * u, axis=(0, 1))]
    for offset in range(1, 4):
        grad_taps.append(jnp.sum(dc * shifted[offset - 1], axis=(0, 1)))
        du = du + taps[:, 3 - offset] * jnp.pad((dc * same[offset - 1][:, :, None])[offset:], ((0, offset), (0, 0), (0, 0)))
    grad_conv = jnp.stack(grad_taps[::-1] + [jnp.sum(dc, axis=(0, 1)), grad_dtb, dskip], axis=1)
    dz = row_major(jnp.concatenate([du.reshape(tall, channels), dg], axis=1)).astype(bf16)
    gwin = lax.dot_general(xns, dz, dims_rows, preferred_element_type=f32).astype(bf16)
    gwin = lax.psum_scatter(gwin, "dp", scatter_dimension=0, tiled=True)
    gwin = lax.all_to_all(gwin.reshape(ways, own_d, 2 * channels), TP, split_axis=0, concat_axis=0, tiled=True)
    grad_win = gwin.reshape(ways, own_d, 2, groups, own_e).transpose(1, 2, 3, 0, 4).reshape(own_d, 2 * inner).astype(f32)
    dxn = lax.dot_general(dz, win, dims_cols, preferred_element_type=f32).astype(bf16)
    dxn = lax.psum_scatter(dxn, TP, scatter_dimension=0, tiled=True).astype(f32)
    small_grad = lax.psum_scatter(jnp.concatenate([grad_wx, grad_wdt, grad_conv], axis=1), "dp", scatter_dimension=0, tiled=True)
    inner_grad = dxn * gains
    dxx = scale * inner_grad - x * (scale * scale * scale) * (jnp.sum(inner_grad * x, axis=1, keepdims=True) / model)
    grad_tokens = (grad_out[0].astype(f32) + dxx).astype(bf16)
    grad_gain = lax.psum_scatter(jnp.sum(dxn * x * scale, axis=0), ALL, scatter_dimension=0, tiled=True)
    at = rank + 2 * states
    return (
        block_out[None],
        grad_tokens[None],
        grad_gain,
        grad_win,
        small_grad[:, at + rank:at + rank + 4],
        small_grad[:, at + rank + 4],
        small_grad[:, :at],
        small_grad[:, at:at + rank],
        small_grad[:, at + rank + 5],
        small_grad[:, at + rank + 6],
        grad_wout.astype(f32),
        beta_mean,
        peak,
    )


def on_device_direct(tokens, lengths, gain, w_in, conv_w, conv_b, w_x, w_dt, dt_bias, skip, w_out, grad_out):
    groups, ways = 4, 8
    length, model = tokens.shape[1:]
    own_d = w_in.shape[0]
    own_e = conv_w.shape[0]
    inner = w_in.shape[1] // 2
    channels = inner // ways
    rank = w_dt.shape[1]
    states = (w_x.shape[1] - rank) // 2
    gain = gain[None]
    xnt, ups, win, wout, smalls, vecs, gains, masks, live, u, g, v, vt, slope, dl, kq = k1(
        tokens, grad_out, w_in, w_out, w_x.T, w_dt, gain, lengths, conv_w.T, conv_b[None], dt_bias[None], skip[None])
    acc, mt, dg, gwdt, ups, dv, part, stat = k2(dl, kq, smalls, vecs, masks, live, v, g, ups, wout, states)
    sums = k3(
        part, stat, smalls, vecs, gains, gwdt, masks, tokens, grad_out, acc, mt, dg, dv, slope, u, vt, xnt,
        win.reshape(groups, ways * own_d, 2 * channels), ups)
    block_out, grad_tokens, grad_gain, grad_win, convw, convb, gwx, gwdt, dtb, dskip, grad_wout, mean, peak = k4(
        float(groups * ways * length * inner), *sums, w_in, gain, rank + 2 * states)
    return (
        block_out, grad_tokens, grad_gain[0], grad_win, convw.T, convb[0], gwx.T, gwdt, dtb[0], dskip[0], grad_wout, mean[0, 0], peak[0, 0],
    )


def on_device_any(*args):
    if lax.axis_size("dp") == 4 and lax.axis_size("z") == 4:
        return on_device_direct(*args)
    return on_device(*args)


def solution(mesh):
    wide, narrow = mesh.devices.shape
    fine = Mesh(mesh.devices.reshape(wide // 2, 2, narrow), ALL)
    cut = (P(ALL, None), P(ALL))
    in_specs = (P(ALL, None, None), cut[0], cut[1], cut[0], cut[0], cut[1], cut[0], cut[0], cut[1], cut[1], cut[0], P(ALL, None, None))
    out_specs = (P(ALL, None, None), P(ALL, None, None), cut[1], cut[0], cut[0], cut[1], cut[0], cut[0], cut[1], cut[1], cut[0], P(), P())
    return jax.shard_map(on_device_any, mesh=fine, in_specs=in_specs, out_specs=out_specs, check_vma=False)
```
